32 devices in a mesh: comp: 4 (over y, x), gx: 4 (over z), gy: 2 (over core).
Axes of the slice: x: 2, y: 2, z: 4, core: 2. Of those that a mesh axis runs over, the one named last changes fastest.
Arguments:
- zonal_flow_speed: float32 [64, 64, 256], P('comp', 'gx', 'gy'), may hold values from -5 to 5
- meridional_flow_speed: float32 [64, 64, 256], P('comp', 'gx', 'gy'), may hold values from -5 to 5
- thermal_anomaly: float32 [64, 64, 256], P('comp', 'gx', 'gy'), may hold values from -6 to 6
- brine_anomaly_values: float32 [64, 64, 256], P('comp', 'gx', 'gy'), may hold values from -6 to 6
- marine_indicator: int32 [64, 256], P('gx', 'gy'), may hold values 0 or 1
- seafloor_layer: int32 [64, 256], P('gx', 'gy'), may hold values from 1 to 64
- dissolved_species: float32 [24, 64, 4, 4, 4, 256], P(None, None, 'gx', 'comp', None, 'gy'), may hold values from 0.05 to 2
- topmost_sunshine: float32 [4, 4, 4, 256], P('gx', 'comp', None, 'gy'), may hold values from 0.3 to 3
- attenuation_coefficient: float32 [24], replicated, may hold values from 0.01 to 0.1
- peak_intake_speed: float32 [24], replicated, may hold values from 0.2 to 2
- feedstock_midpoint_constant: float32 [24], replicated, may hold values from 0.05 to 1
- photon_midpoint_constant: float32 [24], replicated, may hold values from 0.05 to 1
- stoichiometry_matrix: float32 [24, 24], replicated, may hold values from -1.25 to 1.25
Outputs:
- east_new: float32 [64, 64, 256], P('comp', 'gx', 'gy')
- north_new: float32 [64, 64, 256], P('comp', 'gx', 'gy')
- warmed_result: float32 [64, 64, 256], P('comp', 'gx', 'gy')
- salt_mixed: float32 [64, 64, 256], P('comp', 'gx', 'gy')
- buoyancy: float32 [64, 64, 256], P('comp', 'gx', 'gy')
- result: float32 [24, 64, 4, 4, 4, 256], P(None, None, 'gx', 'comp', None, 'gy')
The draws below stay inside these ranges and needn't reach their ends.
All inputs are finite; a program needn't handle non-finite values. No bound on the sum of `marine_indicator` on one device may be relied on, other than what follows from the above.
Results may differ from the reference program's by a relative error of at most 0.00007.
Values sent between devices are 32-bit elements; how exact they have to be, the bound alone decides.
No kernel may reach another device: no remote copies, remote signals or barrier semaphores. Data moves between devices by JAX's collectives and lax.ppermute only.
A program may use at most 128 MiB of HBM per device.

```python
import math
import jax
import jax.numpy as jnp
from jax import lax

LAYER_COUNT = 64
NTR = 24
SUBX = 4
NSUB = 2
MESH_HEIGHT = 64
MESH_WIDTH = 256
N_COMP = 4
N_GX = 4


def plant(values, own_key, low, largest):
    longest = values.shape.index(max(values.shape))
    spots = []
    for shift in (0, 1):
        where = [jax.random.randint(jax.random.fold_in(own_key, axis), (), 0, length) for axis, length in enumerate(values.shape)]
        where[longest] = (where[longest] + shift) % values.shape[longest]
        spots.append(tuple(where))
    return values.at[spots[0]].set(low).at[spots[1]].set(largest)


def steps_of(stream_key, extent, shards, smallest, high):
    loudness = 1.0
    for axis_at, parts in shards:
        draws = jax.random.uniform(jax.random.fold_in(jax.random.fold_in(stream_key, 6), axis_at), (parts,), jnp.float32, smallest / len(shards), high / len(shards))
        loudness = loudness * jnp.repeat(jnp.exp(draws), extent[axis_at] // parts).reshape((-1,) + (1,) * (len(extent) - 1 - axis_at))
    return loudness


def bell_draw(stream_key, extent, deviation, reach, split=(), kind=jnp.bfloat16):
    entries = deviation * jax.random.normal(stream_key, extent, jnp.float32)
    if split:
        entries = entries * steps_of(stream_key, extent, split, -0.22, 0.18)
    return jnp.clip(entries, -reach, reach).astype(kind)


def setup_inputs(seed: int = 0) -> dict:
    key_of = jax.random.split(jax.random.key(seed), 14)
    return {
        "zonal_flow_speed": bell_draw(key_of[0], (LAYER_COUNT, MESH_HEIGHT, MESH_WIDTH), 1.0, 5.0, ((0, 4), (1, 4), (2, 2)), jnp.float32),
        "meridional_flow_speed": bell_draw(key_of[1], (LAYER_COUNT, MESH_HEIGHT, MESH_WIDTH), 1.0, 5.0, ((0, 4), (1, 4), (2, 2)), jnp.float32),
        "thermal_anomaly": bell_draw(key_of[2], (LAYER_COUNT, MESH_HEIGHT, MESH_WIDTH), 1.0, 6.0, ((0, 4), (1, 4), (2, 2)), jnp.float32),
        "brine_anomaly_values": bell_draw(key_of[3], (LAYER_COUNT, MESH_HEIGHT, MESH_WIDTH), 1.0, 6.0, ((0, 4), (1, 4), (2, 2)), jnp.float32),
        "marine_indicator": plant((jax.random.randint(key_of[4], (MESH_HEIGHT, MESH_WIDTH), 0, 5) < 4).astype(jnp.int32), jax.random.fold_in(key_of[4], 1), 0, 1),
        "seafloor_layer": plant(jax.random.randint(key_of[5], (MESH_HEIGHT, MESH_WIDTH), 1, LAYER_COUNT + 1), jax.random.fold_in(key_of[5], 1), 1, LAYER_COUNT).astype(jnp.int32),
        "dissolved_species": jnp.clip(jnp.exp(math.log(2.0) - 3.6888794 * jax.random.uniform(key_of[6], (NTR, LAYER_COUNT, N_GX, N_COMP, SUBX, MESH_WIDTH), jnp.float32) ** steps_of(key_of[6], (NTR, LAYER_COUNT, N_GX, N_COMP, SUBX, MESH_WIDTH), ((2, 4), (3, 4), (5, 2)), -0.2, 0.2)), 0.05, 2.0),
        "topmost_sunshine": jnp.clip(jnp.exp(math.log(3.0) - 2.3025851 * jax.random.uniform(key_of[7], (N_GX, N_COMP, SUBX, MESH_WIDTH), jnp.float32) ** steps_of(key_of[7], (N_GX, N_COMP, SUBX, MESH_WIDTH), ((0, 4), (1, 4), (3, 2)), -0.2, 0.2)), 0.3, 3.0),
        "attenuation_coefficient": jnp.clip(jnp.exp(jax.random.uniform(key_of[8], (NTR,), jnp.float32, math.log(0.01), math.log(0.1))), 0.01, 0.1),
        "peak_intake_speed": jnp.clip(jnp.exp(jax.random.uniform(key_of[9], (NTR,), jnp.float32, math.log(0.2), math.log(2.0))), 0.2, 2.0),
        "feedstock_midpoint_constant": jnp.clip(jnp.exp(jax.random.uniform(key_of[10], (NTR,), jnp.float32, math.log(0.05), math.log(1.0))), 0.05, 1.0),
        "photon_midpoint_constant": jnp.clip(jnp.exp(jax.random.uniform(key_of[11], (NTR,), jnp.float32, math.log(0.05), math.log(1.0))), 0.05, 1.0),
        "stoichiometry_matrix": bell_draw(key_of[12], (NTR, NTR), NTR ** -0.5, 1.25, (), jnp.float32),
    }


DT_FLOW = 0.1
CORIOLIS = 0.3
MIXING = 0.15
COURANT = 0.24
DT_BIO = 0.5
WARMING_FACTOR = 0.5
CLEAR_WATER = 0.5
HIGHEST = lax.Precision.HIGHEST


def forward_cell(values, direction):
    widths = [(0, 0)] * values.ndim
    widths[direction] = (0, 1)
    padded_field = jnp.pad(values, widths)
    return lax.slice_in_dim(padded_field, 1, values.shape[direction] + 1, axis=direction)


def backward_cell(values, direction):
    widths = [(0, 0)] * values.ndim
    widths[direction] = (1, 0)
    padded_field = jnp.pad(values, widths)
    return lax.slice_in_dim(padded_field, 0, values.shape[direction], axis=direction)


def reference(zonal_flow_speed, meridional_flow_speed, thermal_anomaly, brine_anomaly_values, marine_indicator, seafloor_layer, dissolved_species, topmost_sunshine, attenuation_coefficient, peak_intake_speed, feedstock_midpoint_constant, photon_midpoint_constant, stoichiometry_matrix):
    depth_index = jnp.arange(LAYER_COUNT, dtype=jnp.int32)[:, None, None]
    submerged_indicator = ((marine_indicator[None] == 1) & (depth_index < seafloor_layer[None])).astype(jnp.float32)
    open_east = submerged_indicator * forward_cell(submerged_indicator, 1)
    open_north = submerged_indicator * forward_cell(submerged_indicator, 2)
    seawater_heaviness = submerged_indicator * (-0.2 * thermal_anomaly + 0.8 * brine_anomaly_values)
    strict_lower = (jnp.arange(LAYER_COUNT)[:, None] > jnp.arange(LAYER_COUNT)[None, :]).astype(jnp.float32)
    depth_above = jnp.dot(strict_lower, seawater_heaviness.reshape(LAYER_COUNT, -1), precision=HIGHEST).reshape(seawater_heaviness.shape)
    weight_of_overlying = depth_above + 0.5 * seawater_heaviness
    east_new = open_east * (zonal_flow_speed + DT_FLOW * (CORIOLIS * meridional_flow_speed - (forward_cell(weight_of_overlying, 1) - weight_of_overlying)))
    north_new = open_north * (meridional_flow_speed + DT_FLOW * (-CORIOLIS * zonal_flow_speed - (forward_cell(weight_of_overlying, 2) - weight_of_overlying)))

    def diapycnal_diffusion(values):
        flux_east = open_east * (forward_cell(values, 1) - values)
        flux_north = open_north * (forward_cell(values, 2) - values)
        return values + MIXING * ((flux_east - backward_cell(flux_east, 1)) + (flux_north - backward_cell(flux_north, 2)))

    thermal_blended = diapycnal_diffusion(thermal_anomaly)
    salt_mixed = diapycnal_diffusion(brine_anomaly_values)
    courant_east = COURANT * jnp.tanh(east_new)
    courant_north = COURANT * jnp.tanh(north_new)
    whole_field = dissolved_species.reshape(NTR, LAYER_COUNT, MESH_HEIGHT, MESH_WIDTH)

    def advect(tracer_field):
        for substep in range(NSUB):
            flux_east = jnp.maximum(courant_east, 0.0) * tracer_field + jnp.minimum(courant_east, 0.0) * forward_cell(tracer_field, 1)
            flux_north = jnp.maximum(courant_north, 0.0) * tracer_field + jnp.minimum(courant_north, 0.0) * forward_cell(tracer_field, 2)
            tracer_field = submerged_indicator * (tracer_field - (flux_east - backward_cell(flux_east, 1)) - (flux_north - backward_cell(flux_north, 2)))
        return tracer_field

    advected = lax.map(advect, whole_field)
    layer_depth = 2.0 / LAYER_COUNT
    optical_step = layer_depth * (CLEAR_WATER + jnp.tensordot(attenuation_coefficient, advected, axes=1, precision=HIGHEST))
    optical_above = jnp.dot(strict_lower, optical_step.reshape(LAYER_COUNT, -1), precision=HIGHEST).reshape(optical_step.shape)
    transmitted = jnp.exp(-optical_above)
    surface = topmost_sunshine.reshape(MESH_HEIGHT, MESH_WIDTH)[None]
    light_level = surface * transmitted * jnp.exp(-0.5 * optical_step)
    warming_step = submerged_indicator * surface * transmitted * (1.0 - jnp.exp(-optical_step)) / layer_depth
    nutrient = advected[0]

    def uptake(inputs):
        tracer_field, rate_max, nutrient_half, light_sat = inputs
        return rate_max * (nutrient / (nutrient_half + nutrient)) * (light_level / (light_level + light_sat)) * tracer_field

    uptake_rates = lax.map(uptake, (advected, peak_intake_speed, feedstock_midpoint_constant, photon_midpoint_constant))
    change = jnp.tensordot(stoichiometry_matrix, uptake_rates, axes=1, precision=HIGHEST)
    result = advected + DT_BIO * submerged_indicator * change
    warmed_result = thermal_blended + WARMING_FACTOR * warming_step
    buoyancy = submerged_indicator * (0.2 * warmed_result - 0.8 * salt_mixed)
    return east_new, north_new, warmed_result, salt_mixed, buoyancy, result.reshape(dissolved_species.shape)
```

```python
import functools

import jax
import jax.numpy as jnp
from jax import lax
from jax.experimental import pallas as pl
from jax.experimental.pallas import tpu as pltpu
from jax.sharding import PartitionSpec as P

NSUB = 2
SLOTS = 4 * NSUB

DT_FLOW = 0.1
CORIOLIS = 0.3
MIXING = 0.15
COURANT = 0.24
DT_BIO = 0.5
WARMING_FACTOR = 0.5
CLEAR_WATER = 0.5
HIGHEST = lax.Precision.HIGHEST
VMEM_LIMIT = 48 * 1024 * 1024


def lanes_of(shape):
    return lax.broadcasted_iota(jnp.int32, shape, len(shape) - 1)


def rows_of(shape):
    return lax.broadcasted_iota(jnp.int32, shape, len(shape) - 2)


def turn(x, by, axis):
    by = by % x.shape[axis]
    return x if by == 0 else pltpu.roll(x, by, axis)


def params(**more):
    return pltpu.CompilerParams(vmem_limit_bytes=VMEM_LIMIT, **more)


def pack_tracers_kernel(blocks, group, q_ref, *outs):
    lows, highs, packed_ref = outs[:blocks], outs[blocks : 2 * blocks], outs[2 * blocks]
    sub = rows_of((8, 128))
    lane = lanes_of((8, 128))
    pairs = 128 // (2 * SLOTS)
    for t in range(group):
        for b in range(blocks):
            v = [q_ref[t, (b * pairs + p) * 8 : (b * pairs + p + 1) * 8, :] for p in range(pairs)]
            for i in range(pairs // 2):
                v0, v1 = v[2 * i], v[2 * i + 1]
                v0_2, v0_4, v1_4, v1_2 = turn(v0, -2, 0), turn(v0, 4, 0), turn(v1, 4, 0), turn(v1, 2, 0)
                low = jnp.where(
                    sub < 4, jnp.where(sub < 2, v0, v0_2), jnp.where(sub < 6, v1_4, v1_2)
                )
                high = jnp.where(
                    sub < 4, jnp.where(sub < 2, v0_2, v0_4), jnp.where(sub < 6, v1_2, v1)
                )
                lows[b][t, 8 * i : 8 * i + 8, :] = low
                highs[b][t, 8 * i : 8 * i + 8, :] = high
            acc = jnp.zeros((8, 128), jnp.float32)
            for p in range(pairs):
                acc = jnp.where(lane // (2 * SLOTS) == p, turn(v[p], 2 * SLOTS * p + 2, 1), acc)
            acc = jnp.where(lane % SLOTS < SLOTS // 2, acc, turn(acc, SLOTS // 2, 1))
            later = turn(turn(acc, SLOTS, 1), 4, 0)
            acc = jnp.where(lane % (2 * SLOTS) < SLOTS, acc, later)
            packed_ref[b, t] = acc[0:4]


def pack_tracers(q, blocks, levels_dev, sub_rows):
    tracers, _, cols = q.shape
    group = 4
    rows = levels_dev * sub_rows
    edge = jax.ShapeDtypeStruct((tracers, levels_dev * NSUB, cols), jnp.float32)
    edge_spec = pl.BlockSpec((group, levels_dev * NSUB, cols), lambda i: (i, 0, 0))
    return pl.pallas_call(
        functools.partial(pack_tracers_kernel, blocks, group),
        grid=(tracers // group,),
        in_specs=[pl.BlockSpec((group, blocks * rows, cols), lambda i: (i, 0, 0))],
        out_specs=[edge_spec] * (2 * blocks)
        + [pl.BlockSpec((blocks, group, sub_rows, cols), lambda i: (0, i, 0, 0))],
        out_shape=[edge] * (2 * blocks)
        + [jax.ShapeDtypeStruct((blocks, tracers, sub_rows, cols), jnp.float32)],
        compiler_params=params(),
    )(q)


def pack_ocean_kernel(u_ref, v_ref, t_ref, s_ref, sea_ref, floor_ref, packed_ref, low_ref, high_ref):
    levels, rows, cols = u_ref.shape
    lane = lanes_of((rows, cols))

    def packed(layer):
        acc = jnp.zeros((rows, cols), jnp.float32)
        for k in range(levels):
            acc = jnp.where(lane // SLOTS == k, turn(layer(k), SLOTS * k + 2, 1), acc)
        return jnp.where(lane % SLOTS < SLOTS // 2, acc, turn(acc, SLOTS // 2, 1))

    fields = (u_ref, v_ref, t_ref, s_ref)
    for f, ref in enumerate(fields):
        packed_ref[f] = packed(lambda k: ref[k])
        for k in range(levels):
            low_ref[f * levels + k] = ref[k, 0:2, :]
            high_ref[f * levels + k] = ref[k, rows - 2 : rows, :]
    depth = jnp.where(sea_ref[...] == 1, floor_ref[...], 0).astype(jnp.float32)
    packed_ref[len(fields)] = packed(lambda k: depth)
    low_ref[len(fields) * levels] = depth[0:2]
    high_ref[len(fields) * levels] = depth[rows - 2 : rows]


def pack_ocean(u, v, t, s, sea, floor):
    levels, rows, cols = u.shape
    edge = jax.ShapeDtypeStruct((4 * levels + 1, NSUB, cols), jnp.float32)
    return pl.pallas_call(
        pack_ocean_kernel,
        out_shape=[jax.ShapeDtypeStruct((5, rows, cols), jnp.float32), edge, edge],
        compiler_params=params(),
    )(u, v, t, s, sea, floor)


def density_kernel(
    base_ref, t_ref, s_ref, sea_ref, floor_ref, packed_ref, after_ref, before_ref, rim_ref, total_ref
):
    levels, rows, cols = t_ref.shape
    rim_ref[...] = jnp.zeros_like(rim_ref)
    rim_ref[:, 0:2, :] = after_ref[...]
    rim_ref[:, 6:8, :] = before_ref[...]
    base = base_ref[0]
    depth = jnp.where(sea_ref[...] == 1, floor_ref[...], 0).astype(jnp.float32)
    depth = jnp.concatenate([depth, rim_ref[4 * levels]], axis=0)
    total = jnp.zeros((rows + 8, cols), jnp.float32)
    for k in range(levels):
        heat = jnp.concatenate([t_ref[k], rim_ref[2 * levels + k]], axis=0)
        salt = jnp.concatenate([s_ref[k], rim_ref[3 * levels + k]], axis=0)
        wet = ((base + k).astype(jnp.float32) < depth).astype(jnp.float32)
        total = total + wet * (-0.2 * heat + 0.8 * salt)
    total_ref[0 : rows + 8, :] = total
    side = [jnp.concatenate([packed_ref[f], rim_ref[4 * levels + 1 + f]], axis=0) for f in (2, 3, 4)]
    level = (base + lanes_of(side[0].shape) // SLOTS).astype(jnp.float32)
    wet = (level < side[2]).astype(jnp.float32)
    total = wet * (-0.2 * side[0] + 0.8 * side[1])
    by = SLOTS
    while by < cols:
        total = total + turn(total, by, 1)
        by *= 2
    total_ref[rows + 8 :, :] = total


def density(base, t, s, sea, floor, packed, after, before):
    levels, rows, cols = t.shape
    vmem = pl.BlockSpec(memory_space=pltpu.VMEM)
    return pl.pallas_call(
        density_kernel,
        in_specs=[pl.BlockSpec(memory_space=pltpu.SMEM)] + [vmem] * 7,
        out_shape=[
            jax.ShapeDtypeStruct((after.shape[0], 8, cols), jnp.float32),
            jax.ShapeDtypeStruct((2 * (rows + 8), cols), jnp.float32),
        ],
        compiler_params=params(),
    )(base, t, s, sea, floor, packed, after, before)


def flow_kernel(blocks, *refs):
    base_ref, u_ref, v_ref, t_ref, s_ref, sea_ref, floor_ref, packed_ref, rim_ref = refs[:9]
    above_refs = refs[9 : 9 + blocks - 1]
    east_ref, north_ref, tmix_ref, smix_ref, send_ref, depth_ref = refs[9 + blocks - 1 :]
    levels, rows, cols = t_ref.shape
    tall = rows + 8
    sub_rows = rows // blocks
    shape = (tall, cols)
    lane = lanes_of(shape)
    slot = lane % SLOTS
    base = base_ref[0]
    above = jnp.zeros((2 * tall, cols), jnp.float32)
    for ref in above_refs:
        above = above + ref[...]

    def row_after(x):
        return turn(x, -1, 0)

    def row_before(x):
        return turn(x, 1, 0)

    def window(x, g):
        rolled = turn(x, -sub_rows * g, 0)
        row = rows_of((8, cols))
        return jnp.where(row < 6, rolled[0:8], rolled[tall - 8 : tall])

    def to_first(x):
        return turn(x, -6, 1)

    up, vp, tp, sp, dp = [
        jnp.concatenate([packed_ref[f], rim_ref[4 * levels + 1 + f]], axis=0) for f in range(5)
    ]
    wet_p = ((base + lane // SLOTS).astype(jnp.float32) < dp).astype(jnp.float32)
    heavy = wet_p * (-0.2 * tp + 0.8 * sp)
    running = heavy
    by = 1
    while by < levels:
        running = running + jnp.where(lane // SLOTS >= by, turn(running, SLOTS * by, 1), 0.0)
        by *= 2
    before = jnp.where(lane >= SLOTS, turn(running, SLOTS, 1), 0.0)
    press_p = above[tall:] + before + 0.5 * heavy
    open_e = wet_p * row_after(wet_p)
    open_n = wet_p * turn(wet_p, -1, 1)
    east = open_e * (up + DT_FLOW * (CORIOLIS * vp - (row_after(press_p) - press_p)))
    north = open_n * (vp + DT_FLOW * (-CORIOLIS * up - (turn(press_p, -1, 1) - press_p)))
    ce, cn = COURANT * jnp.tanh(east), COURANT * jnp.tanh(north)
    for g in range(blocks):
        send_ref[g, levels, 0:8, :] = window(ce, g)
        send_ref[g, levels, 8:16, :] = window(cn, g)
        depth_ref[g, 8:16, :] = window(dp, g)
    flux_t = open_n * (turn(tp, -1, 1) - tp)
    flux_s = open_n * (turn(sp, -1, 1) - sp)
    side_t = jnp.where(slot == 0, to_first(tp), flux_t)
    side_s = jnp.where(slot == 0, to_first(sp), flux_s)
    side_p = to_first(press_p)
    side_w = to_first(wet_p)

    depth = jnp.where(sea_ref[...] == 1, floor_ref[...], 0).astype(jnp.float32)
    depth = jnp.concatenate([depth, rim_ref[4 * levels]], axis=0)
    for g in range(blocks):
        depth_ref[g, 0:8, :] = window(depth, g)
    last = lane == cols - 1
    first = lane == 0
    running = above[:tall]
    for k in range(levels):
        by = -(SLOTS * k + 1)
        u, v, t, s = [
            jnp.concatenate([ref[k], rim_ref[f * levels + k]], axis=0)
            for f, ref in enumerate((u_ref, v_ref, t_ref, s_ref))
        ]
        wet = ((base + k).astype(jnp.float32) < depth).astype(jnp.float32)
        heavy = wet * (-0.2 * t + 0.8 * s)
        press = running + 0.5 * heavy
        running = running + heavy
        edge_t, edge_s = turn(side_t, by, 1), turn(side_s, by, 1)
        press_n = jnp.where(last, turn(side_p, by, 1), turn(press, -1, 1))
        wet_n = jnp.where(last, turn(side_w, by, 1), turn(wet, -1, 1))
        t_n = jnp.where(last, edge_t, turn(t, -1, 1))
        s_n = jnp.where(last, edge_s, turn(s, -1, 1))
        open_e = wet * row_after(wet)
        open_n = wet * wet_n
        east = open_e * (u + DT_FLOW * (CORIOLIS * v - (row_after(press) - press)))
        north = open_n * (v + DT_FLOW * (-CORIOLIS * u - (press_n - press)))
        east_ref[k] = east[0:rows]
        north_ref[k] = north[0:rows]
        ce, cn = COURANT * jnp.tanh(east), COURANT * jnp.tanh(north)
        for g in range(blocks):
            send_ref[g, k, 0:8, :] = window(ce, g)
            send_ref[g, k, 8:16, :] = window(cn, g)
        for out_ref, field, field_n, edge in ((tmix_ref, t, t_n, edge_t), (smix_ref, s, s_n, edge_s)):
            flux_e = open_e * (row_after(field) - field)
            flux_n = open_n * (field_n - field)
            flux_b = jnp.where(first, edge, turn(flux_n, 1, 1))
            mixed = field + MIXING * ((flux_e - row_before(flux_e)) + (flux_n - flux_b))
            out_ref[k] = mixed[0:rows]


def flow(blocks, base, u, v, t, s, sea, floor, packed, rim, above):
    levels, rows, cols = t.shape
    vmem = pl.BlockSpec(memory_space=pltpu.VMEM)
    field = jax.ShapeDtypeStruct((levels, rows, cols), jnp.float32)
    return pl.pallas_call(
        functools.partial(flow_kernel, blocks),
        in_specs=[pl.BlockSpec(memory_space=pltpu.SMEM)] + [vmem] * (8 + len(above)),
        out_shape=[field] * 4
        + [
            jax.ShapeDtypeStruct((blocks, levels + 1, 16, cols), jnp.float32),
            jax.ShapeDtypeStruct((blocks, 16, cols), jnp.float32),
        ],
        compiler_params=params(),
    )(base, u, v, t, s, sea, floor, packed, rim, *above)


def tracer_kernel(block, level_count, has_before, *refs):
    (
        absorb_ref,
        growth_ref,
        half_ref,
        dim_ref,
        matrix_ref,
        surface_ref,
        depth_ref,
        courant_ref,
        q_ref,
        after_ref,
        before_ref,
        side_ref,
        carry_ref,
    ) = refs[:13]
    result_ref, heat_ref, carry_out_ref, coef_ref, edge_ref, moved_ref, uptake_ref = refs[
        13 + 2 * has_before :
    ]
    tracers = q_ref.shape[0]
    cols = q_ref.shape[2]
    levels = courant_ref.shape[1] - 1
    shape = (8, cols)
    sub, lane = rows_of(shape), lanes_of(shape)
    slot = lane % SLOTS
    first, last = lane == 0, lane == cols - 1
    upper = sub < 4
    base = block * levels
    depth = depth_ref[0:8, :]
    depth_pair = jnp.where(upper, depth, turn(depth, 4, 0))

    packed_cn = courant_ref[0, levels, 8:16, :]
    for k in range(levels + 1):
        ce, cn = courant_ref[0, k, 0:8, :], courant_ref[0, k, 8:16, :]
        ce_b, cn_b = turn(ce, 1, 0), turn(cn, 1, 1)
        if k < levels:
            cn_b = jnp.where(first, turn(packed_cn, -(SLOTS * k + 1), 1), cn_b)
            wet = (float(base + k) < depth).astype(jnp.float32)
        else:
            wet = ((base + lane // SLOTS).astype(jnp.float32) < depth_ref[8:16, :]).astype(jnp.float32)
        coef_ref[k, 0] = wet * (
            1.0
            - jnp.maximum(ce, 0.0)
            + jnp.minimum(ce_b, 0.0)
            - jnp.maximum(cn, 0.0)
            + jnp.minimum(cn_b, 0.0)
        )
        coef_ref[k, 1] = -wet * jnp.minimum(ce, 0.0)
        coef_ref[k, 2] = wet * jnp.maximum(ce_b, 0.0)
        coef_ref[k, 3] = -wet * jnp.minimum(cn, 0.0)
        coef_ref[k, 4] = wet * jnp.maximum(cn_b, 0.0)

    def stencil(q, coef, edge=None):
        north, south = turn(q, -1, 1), turn(q, 1, 1)
        if edge is not None:
            north, south = jnp.where(last, edge, north), jnp.where(first, edge, south)
        return (
            (coef[0] * q + coef[1] * turn(q, -1, 0))
            + (coef[2] * turn(q, 1, 0) + coef[3] * north)
            + coef[4] * south
        )

    def paired(q):
        return jnp.where(slot == 0, turn(q, -6, 1), q)

    packed_coef = [coef_ref[levels, i] for i in range(5)]

    def side_step(t, _):
        q = side_ref[0, t]
        edge_ref[t, 0] = paired(q)
        edge_ref[t, 1] = paired(stencil(q, packed_coef))
        return _

    lax.fori_loop(0, tracers, side_step, 0)

    layer = 2.0 / level_count
    surface = surface_ref[...]
    carry = carry_ref[...]
    for g in range(levels // 4):
        coefs = [[coef_ref[4 * g + j, i] for i in range(5)] for j in range(4)]

        def advect(t, sums):
            v = [q_ref[t, 16 * g + 8 * p : 16 * g + 8 * p + 8, :] for p in range(2)]
            after = after_ref[t, 8 * g : 8 * g + 8, :]
            before = before_ref[t, 8 * g : 8 * g + 8, :]
            edge0, edge1 = edge_ref[t, 0], edge_ref[t, 1]
            r = []
            for j in range(4):
                own = turn(v[j // 2], 4 * (j % 2), 0)
                rim = jnp.where(sub < 6, turn(after, 4 - 2 * j, 0), turn(before, 6 - 2 * j, 0))
                q = jnp.where(upper, own, rim)
                by = -(SLOTS * (4 * g + j) + 1)
                q = stencil(q, coefs[j], turn(edge0, by, 1))
                r.append(stencil(q, coefs[j], turn(edge1, by, 1)))
            out = []
            for p in range(2):
                pair = jnp.where(upper, r[2 * p], turn(r[2 * p + 1], 4, 0))
                moved_ref[t, p] = pair
                out.append(sums[p] + absorb_ref[t] * pair)
            return tuple(out)

        zero = jnp.zeros(shape, jnp.float32)
        sums = lax.fori_loop(0, tracers, advect, (zero, zero), unroll=2)
        lights, wets = [], []
        for p in range(2):
            step = layer * (CLEAR_WATER + sums[p])
            other = turn(step, 4, 0)
            through = jnp.exp(-(carry + jnp.where(upper, 0.0, other)))
            carry = carry + step + other
            level = (base + 4 * g + 2 * p) + jnp.where(upper, 0, 1)
            wet = (level.astype(jnp.float32) < depth_pair).astype(jnp.float32)
            lights.append(surface * through * jnp.exp(-0.5 * step))
            wets.append(wet)
            heat = wet * surface * through * (1.0 - jnp.exp(-step)) / layer
            heat_ref[16 * g + 8 * p : 16 * g + 8 * p + 8, :] = heat
        food = [moved_ref[0, p] for p in range(2)]
        both = [food[p] * lights[p] for p in range(2)]

        def uptake(t, _):
            for p in range(2):
                scale = (half_ref[t] + food[p]) * (lights[p] + dim_ref[t])
                value = growth_ref[t] * moved_ref[t, p] * (both[p] / scale)
                uptake_ref[pl.ds(t * 8, 8), p * cols : (p + 1) * cols] = value
            return _

        lax.fori_loop(0, tracers, uptake, 0, unroll=4)
        change = jnp.dot(
            matrix_ref[...], uptake_ref[...], precision=HIGHEST, preferred_element_type=jnp.float32
        )
        for t in range(tracers):
            for p in range(2):
                result_ref[t, 16 * g + 8 * p : 16 * g + 8 * p + 8, :] = (
                    moved_ref[t, p]
                    + DT_BIO * wets[p] * change[8 * t : 8 * t + 8, p * cols : (p + 1) * cols]
                )
    carry_out_ref[...] = carry


def tracer_block(block, level_count, scalars, matrix, surface, depth, courant, q, after, before, side, carry, held):
    tracers, all_rows, cols = q.shape
    levels = courant.shape[1] - 1
    rows = all_rows * levels // level_count
    vmem = pl.BlockSpec(memory_space=pltpu.VMEM)
    smem = pl.BlockSpec(memory_space=pltpu.SMEM)
    own = pl.BlockSpec((tracers, rows, cols), lambda i: (0, block, 0))
    has_before = held is not None
    operands = [*scalars, matrix, surface, depth, courant, q, after, before, side, carry]
    in_specs = [smem] * 4 + [
        vmem,
        vmem,
        vmem,
        pl.BlockSpec((1,) + courant.shape[1:], lambda i: (block, 0, 0, 0)),
        own,
        vmem,
        vmem,
        pl.BlockSpec((1,) + side.shape[1:], lambda i: (block, 0, 0, 0)),
        vmem,
    ]
    aliases = {}
    if has_before:
        aliases = {len(operands): 0, len(operands) + 1: 1}
        operands += list(held)
        in_specs += [pl.BlockSpec(memory_space=pl.ANY)] * 2
    return pl.pallas_call(
        functools.partial(tracer_kernel, block, level_count, has_before),
        grid=(1,),
        in_specs=in_specs,
        out_specs=[own, pl.BlockSpec((rows, cols), lambda i: (block, 0)), vmem],
        out_shape=[
            jax.ShapeDtypeStruct(q.shape, jnp.float32),
            jax.ShapeDtypeStruct((all_rows, cols), jnp.float32),
            jax.ShapeDtypeStruct((8, cols), jnp.float32),
        ],
        scratch_shapes=[
            pltpu.VMEM((levels + 1, 5, 8, cols), jnp.float32),
            pltpu.VMEM((tracers, 2, 8, cols), jnp.float32),
            pltpu.VMEM((tracers, 2, 8, cols), jnp.float32),
            pltpu.VMEM((tracers * 8, 2 * cols), jnp.float32),
        ],
        input_output_aliases=aliases,
        compiler_params=params(),
    )(*operands)


def from_before(x, axis, by=1):
    count = lax.axis_size(axis)
    return lax.ppermute(x, axis, [(i, i + by) for i in range(count - by)])


def from_after(x, axis, by=1):
    count = lax.axis_size(axis)
    return lax.ppermute(x, axis, [(i + by, i) for i in range(count - by)])


def row_pairs():
    blocks, tiles = lax.axis_size("comp"), lax.axis_size("gx")
    places = [b * tiles + tile for tile in range(tiles) for b in range(blocks)]
    return list(zip(places[:-1], places[1:]))


def from_block_before(x):
    return lax.ppermute(x, ("comp", "gx"), row_pairs())


def from_block_after(x):
    return lax.ppermute(x, ("comp", "gx"), [(later, own) for own, later in row_pairs()])


def with_sides(x):
    count = lax.axis_size("gy")
    if count == 2:
        left = right = lax.ppermute(x, "gy", [(0, 1), (1, 0)])
    else:
        left, right = from_before(x, "gy"), from_after(x, "gy")
    slot = lanes_of(x.shape) % SLOTS
    return jnp.where(slot < NSUB, left, jnp.where(slot >= SLOTS - NSUB, right, x))


def on_device(
    zonal_flow_speed,
    meridional_flow_speed,
    thermal_anomaly,
    brine_anomaly_values,
    marine_indicator,
    seafloor_layer,
    dissolved_species,
    topmost_sunshine,
    attenuation_coefficient,
    peak_intake_speed,
    feedstock_midpoint_constant,
    photon_midpoint_constant,
    stoichiometry_matrix,
):
    group_index = lax.axis_index("comp")
    blocks = lax.axis_size("comp")
    levels_dev, tile_rows, tile_cols = zonal_flow_speed.shape
    tracer_count, level_count = dissolved_species.shape[:2]
    sub_rows = dissolved_species.shape[4]
    ocean = (zonal_flow_speed, meridional_flow_speed, thermal_anomaly, brine_anomaly_values)
    sea = (marine_indicator, seafloor_layer)

    q = dissolved_species.reshape(tracer_count, level_count * sub_rows, tile_cols)
    *edges, packed_q = pack_tracers(q, blocks, levels_dev, sub_rows)
    lows, highs = edges[:blocks], edges[blocks:]
    afters = [from_block_after(low) for low in lows]
    befores = [from_block_before(high) for high in highs]

    packed, low, high = pack_ocean(*ocean, *sea)
    packed = with_sides(packed)
    slot = lanes_of((1, tile_cols)) % SLOTS
    place, ends = lax.axis_index("gy"), lax.axis_size("gy") - 1
    beyond = ((slot < NSUB) & (place == 0)) | ((slot >= SLOTS - NSUB) & (place == ends))
    packed = jnp.concatenate([packed[:4], jnp.where(beyond, 0.0, packed[4:])], axis=0)
    after = from_after(jnp.concatenate([low, packed[:, :NSUB]], axis=0), "gx")
    before = from_before(jnp.concatenate([high, packed[:, tile_rows - NSUB :]], axis=0), "gx")
    base = (group_index * levels_dev).astype(jnp.int32).reshape(1)
    rim, total = density(base, *ocean[2:], *sea, packed, after, before)
    above = [from_before(total, "comp", by) for by in range(1, blocks)]
    east_new, north_new, temp_mixed, salt_mixed, courant, depths = flow(
        blocks, base, *ocean, *sea, packed, rim, above
    )
    courant = lax.all_to_all(courant, "comp", split_axis=0, concat_axis=0, tiled=True)
    depth = lax.dynamic_index_in_dim(depths, group_index, 0, False)

    packed_q = with_sides(packed_q)
    side_after = from_block_after(packed_q[:, :, :1])
    side_before = from_block_before(packed_q[:, :, -1:])
    nothing = jnp.zeros(packed_q.shape[:2] + (2,) + packed_q.shape[3:], jnp.float32)
    side = jnp.concatenate([packed_q, side_after, nothing, side_before], axis=2)

    matrix = (
        stoichiometry_matrix[:, None, :, None] * jnp.eye(8, dtype=jnp.float32)[None, :, None, :]
    ).reshape(8 * tracer_count, 8 * tracer_count)
    surface = jnp.tile(topmost_sunshine.reshape(sub_rows, tile_cols), (2, 1))
    scalars = (
        attenuation_coefficient,
        peak_intake_speed,
        feedstock_midpoint_constant,
        photon_midpoint_constant,
    )
    carry = jnp.zeros((8, tile_cols), jnp.float32)
    held = None
    for block in range(blocks):
        result, heating, carry = tracer_block(
            block,
            level_count,
            scalars,
            matrix,
            surface,
            depth,
            courant,
            q,
            afters[block],
            befores[block],
            side,
            carry,
            held,
        )
        held = (result, heating)

    heating = lax.all_to_all(
        heating.reshape(blocks, levels_dev, sub_rows, tile_cols),
        "comp",
        split_axis=0,
        concat_axis=0,
        tiled=True,
    )
    heating = heating.transpose(1, 0, 2, 3).reshape(levels_dev, tile_rows, tile_cols)
    warmed_result = temp_mixed + WARMING_FACTOR * heating
    depth_index = base[0] + jnp.arange(levels_dev, dtype=jnp.int32)[:, None, None]
    wet = ((marine_indicator[None] == 1) & (depth_index < seafloor_layer[None])).astype(jnp.float32)
    buoyancy = wet * (0.2 * warmed_result - 0.8 * salt_mixed)
    return (
        east_new,
        north_new,
        warmed_result,
        salt_mixed,
        buoyancy,
        result.reshape(dissolved_species.shape),
    )


def solution(mesh):
    return jax.shard_map(
        on_device,
        mesh=mesh,
        in_specs=(
            P("comp", "gx", "gy"),
            P("comp", "gx", "gy"),
            P("comp", "gx", "gy"),
            P("comp", "gx", "gy"),
            P("gx", "gy"),
            P("gx", "gy"),
            P(None, None, "gx", "comp", None, "gy"),
            P("gx", "comp", None, "gy"),
            P(),
            P(),
            P(),
            P(),
            P(),
        ),
        out_specs=(
            P("comp", "gx", "gy"),
            P("comp", "gx", "gy"),
            P("comp", "gx", "gy"),
            P("comp", "gx", "gy"),
            P("comp", "gx", "gy"),
            P(None, None, "gx", "comp", None, "gy"),
        ),
        check_vma=False,
    )
```

```python
import functools

import jax
import jax.numpy as jnp
from jax import lax
from jax.experimental import pallas as pl
from jax.experimental.pallas import tpu as pltpu
from jax.sharding import PartitionSpec as P

NSUB = 2
SLOTS = 4 * NSUB
SUB = 8
HALF = 64
ENTRIES = 18

DT_FLOW = 0.1
CORIOLIS = 0.3
MIXING = 0.15
COURANT = 0.24
DT_BIO = 0.5
WARMING_FACTOR = 0.5
CLEAR_WATER = 0.5
VMEM_LIMIT = 48 * 1024 * 1024


def lanes_of(shape):
    return lax.broadcasted_iota(jnp.int32, shape, len(shape) - 1)


def subs_of(shape):
    return lax.broadcasted_iota(jnp.int32, shape, len(shape) - 2)


def turn(x, by, axis):
    by = by % x.shape[axis]
    return x if by == 0 else pltpu.roll(x, by, axis)


def params(**more):
    return pltpu.CompilerParams(vmem_limit_bytes=VMEM_LIMIT, **more)


def whole(shape):
    return pl.BlockSpec(shape, lambda *_: (0,) * len(shape))


def smem():
    return pl.BlockSpec(memory_space=pltpu.SMEM)


def shaped(*shape):
    return jax.ShapeDtypeStruct(shape, jnp.float32)


def sums_above(x):
    sub = subs_of(x.shape)
    running, total = x, x
    by = 1
    while by < x.shape[0]:
        running = running + jnp.where(sub >= by, turn(running, by, 0), 0.0)
        total = total + turn(total, by, 0)
        by *= 2
    return jnp.where(sub >= 1, turn(running, 1, 0), 0.0), total


def pack_kernel(levels, sub_rows, cuts, group, *refs):
    u_ref, v_ref, t_ref, s_ref, sea_ref, floor_ref, q_ref = refs[:7]
    chunks = len(cuts)
    low_refs, high_refs = refs[7 : 7 + chunks], refs[7 + chunks : 7 + 2 * chunks]
    packed_ref, edge_low_ref, edge_high_ref = refs[7 + 2 * chunks :]
    step = pl.program_id(0)
    cols = q_ref.shape[2]
    level_count = q_ref.shape[1] // sub_rows
    tracers = group * pl.num_programs(0)
    tile_rows = sea_ref.shape[0]
    lane = lanes_of((SUB, cols))

    def both_ends(acc):
        return jnp.where(lanes_of(acc.shape) % SLOTS < SLOTS // 2, acc, turn(acc, SLOTS // 2, 1))

    for pair in range(group // 2):
        for chunk, (start, size) in enumerate(cuts):
            for k in range(start, start + size, SUB):
                acc = jnp.zeros((SUB, cols), jnp.float32)
                for odd in range(2):
                    t = 2 * pair + odd
                    for r in range(sub_rows):
                        x = q_ref[t, pl.ds(sub_rows * k + r, SUB, stride=sub_rows), :]
                        if r < NSUB:
                            low_refs[chunk][t, r, k - start : k - start + SUB, :] = x
                        if r >= sub_rows - NSUB:
                            high_refs[chunk][t, r - sub_rows + NSUB, k - start : k - start + SUB, :] = x
                        at = HALF * odd + SLOTS * (r + NSUB)
                        acc = jnp.where(lane // SLOTS == at // SLOTS, turn(x, at + NSUB, 1), acc)
                row = (step * (group // 2) + pair) * level_count + k
                packed_ref[pl.ds(row, SUB), :] = both_ends(acc)

    @pl.when(step == 0)
    def _():
        first = (group * pl.num_programs(0)) // 2 * level_count
        lane = lanes_of((levels, cols))
        edge_low_ref[...] = jnp.zeros_like(edge_low_ref)
        edge_high_ref[...] = jnp.zeros_like(edge_high_ref)
        for f, ref in enumerate((u_ref, v_ref, t_ref, s_ref)):
            acc = jnp.zeros((levels, cols), jnp.float32)
            for r in range(tile_rows):
                x = ref[pl.ds(r, levels, stride=tile_rows), :]
                acc = jnp.where(lane // SLOTS == r, turn(x, SLOTS * r + NSUB, 1), acc)
                if r < NSUB:
                    edge_low_ref[NSUB * f + r] = x
                if r >= tile_rows - NSUB:
                    edge_high_ref[NSUB * f + r - tile_rows + NSUB] = x
            packed_ref[pl.ds(first + f * levels, levels), :] = both_ends(acc)
        depth = jnp.where(sea_ref[...] == 1, floor_ref[...], 0).astype(jnp.float32)
        acc = jnp.zeros((levels, cols), jnp.float32)
        for r in range(tile_rows):
            x = jnp.broadcast_to(depth[r : r + 1], (levels, cols))
            acc = jnp.where(lane // SLOTS == r, turn(x, SLOTS * r + NSUB, 1), acc)
        packed_ref[pl.ds(first + 4 * levels, levels), :] = both_ends(acc)
        edge_low_ref[4 * NSUB, 0:NSUB, :] = depth[0:NSUB]
        edge_high_ref[4 * NSUB, 0:NSUB, :] = depth[tile_rows - NSUB :]


def pack(ocean, sea, q, levels, sub_rows, cuts):
    tracers, rows, cols = q.shape
    group = 4
    tile_rows = sea[0].shape[0]
    flat = [x.reshape(levels * tile_rows, cols) for x in ocean]
    rims = [shaped(tracers, NSUB, size, cols) for _, size in cuts]
    rim_specs = [pl.BlockSpec((group, NSUB, size, cols), lambda i: (i, 0, 0, 0)) for _, size in cuts]
    packed = shaped(tracers // 2 * (rows // sub_rows) + 5 * levels, cols)
    edge = shaped(4 * NSUB + 1, levels, cols)
    out = pl.pallas_call(
        functools.partial(pack_kernel, levels, sub_rows, cuts, group),
        grid=(tracers // group,),
        in_specs=[whole(x.shape) for x in flat]
        + [whole(x.shape) for x in sea]
        + [pl.BlockSpec((group, rows, cols), lambda i: (i, 0, 0))],
        out_specs=rim_specs * 2 + [whole(packed.shape), whole(edge.shape), whole(edge.shape)],
        out_shape=rims * 2 + [packed, edge, edge],
        compiler_params=params(),
    )(*flat, *sea, q)
    n = len(cuts)
    return out[:n], out[n : 2 * n], *out[2 * n :]


def sides_kernel(levels, level_count, place_ref, *refs):
    own_ref, left_ref, right_ref, low_ref, high_ref = refs[:5]
    up_ref, down_ref, ocean_ref, side_ref, side_low_ref, side_high_ref = refs[5:]
    cols = own_ref.shape[1]
    pairs = side_ref.shape[0]
    rows = low_ref.shape[0]

    def with_sides(start, size):
        at = slice(start, start + size)
        slot = lanes_of((size, cols)) % SLOTS
        ends = jnp.where(slot < NSUB, left_ref[at], right_ref[at])
        return jnp.where((slot < NSUB) | (slot >= SLOTS - NSUB), ends, own_ref[at])

    lane = lanes_of((level_count, cols))
    for v in range(side_low_ref.shape[0]):
        low = jnp.zeros((level_count, cols), jnp.float32)
        high = jnp.zeros((level_count, cols), jnp.float32)
        for m in range(min(SUB, pairs - v * SUB)):
            x = with_sides((v * SUB + m) * level_count, level_count)
            side_ref[v * SUB + m] = x
            for odd in range(2):
                to = 2 * SLOTS * m + SLOTS * odd
                here = lane // SLOTS == to // SLOTS
                low = jnp.where(here, turn(x, to - HALF * odd - SLOTS * 2, 1), low)
                high = jnp.where(here, turn(x, to - HALF * odd - SLOTS * 5, 1), high)
        side_low_ref[v] = low
        side_high_ref[v] = high
    up_ref[0:rows] = low_ref[...]
    down_ref[0:rows] = high_ref[...]
    slot = lanes_of((levels, cols)) % SLOTS
    first, last = place_ref[0] == 0, place_ref[0] == place_ref[1] - 1
    for f in range(5):
        x = with_sides(pairs * level_count + f * levels, levels)
        if f == 4:
            x = jnp.where((slot < NSUB) & first, 0.0, x)
            x = jnp.where((slot >= SLOTS - NSUB) & last, 0.0, x)
        ocean_ref[f] = x
        up_ref[rows + f] = x
        down_ref[rows + f] = x


def sides(place, own, left, right, low, high, levels, level_count, tracers):
    cols = own.shape[1]
    pairs = tracers // 2
    edge = shaped(low.shape[0] + 5, levels, cols)
    packed_edge = shaped(-(-pairs // SUB), level_count, cols)
    outs = [edge, edge, shaped(5, levels, cols), shaped(pairs, level_count, cols), packed_edge, packed_edge]
    ins = [own, left, right, low, high]
    return pl.pallas_call(
        functools.partial(sides_kernel, levels, level_count),
        grid=(1,),
        in_specs=[smem()] + [whole(x.shape) for x in ins],
        out_specs=[whole(x.shape) for x in outs],
        out_shape=outs,
        compiler_params=params(),
    )(place, *ins)


def ocean_kernel(blocks, levels, base_ref, *refs):
    u_ref, v_ref, t_ref, s_ref, sea_ref, floor_ref, packed_ref, after_ref, before_ref = refs[:9]
    tmix_ref, smix_ref, send_ref, local_ref, faces_ref, depths_ref, press_ref, total_ref = refs[9:]
    tile_rows, cols = sea_ref.shape
    sub_rows = tile_rows // blocks
    shape = (levels, cols)
    lane = lanes_of(shape)
    first, last = lane == 0, lane == cols - 1
    level = (base_ref[0] + subs_of(shape)).astype(jnp.float32)
    rims = after_ref.shape[0] - 5
    refs_of = (u_ref, v_ref, t_ref, s_ref)

    def packed(f):
        after, before = after_ref[rims + f], before_ref[rims + f]
        rim = jnp.where(lane < NSUB * SLOTS, after, jnp.where(lane >= cols - NSUB * SLOTS, before, 0.0))
        return jnp.concatenate([packed_ref[f], rim], axis=1)

    def row_after(x):
        return turn(x, -SLOTS, 1)

    def row_before(x):
        return turn(x, SLOTS, 1)

    up, vp, tp, sp, dp = [packed(f) for f in range(5)]
    wide = jnp.concatenate([level, level], axis=1)
    wet = (wide < dp).astype(jnp.float32)
    heavy = wet * (-0.2 * tp + 0.8 * sp)
    above, total = sums_above(heavy)
    press = above + 0.5 * heavy
    east = up + DT_FLOW * (CORIOLIS * vp - (row_after(press) - press))
    north = vp + DT_FLOW * (-CORIOLIS * up - (turn(press, -1, 1) - press))
    open_n = wet * turn(wet, -1, 1)
    flux_t = open_n * (turn(tp, -1, 1) - tp)
    flux_s = open_n * (turn(sp, -1, 1) - sp)
    total_e, total_n = row_after(total) - total, turn(total, -1, 1) - total
    depth_e, depth_n = jnp.minimum(dp, row_after(dp)), jnp.minimum(dp, turn(dp, -1, 1))

    def window(x, g):
        x = turn(x, -SLOTS * (sub_rows * g - NSUB), 1)[:, 0:cols]
        return jnp.where(lane < HALF, x, turn(x, HALF, 1))

    for g in range(blocks):
        send_ref[g, 13] = window(east, g)
        send_ref[g, 14] = window(north, g)
        send_ref[g, 15, 13:14, :] = window(total_e, g)[0:1]
        send_ref[g, 15, 14:15, :] = window(total_n, g)[0:1]
        send_ref[g, 15, 15:16, :] = jnp.zeros((1, cols), jnp.float32)
        depths_ref[g, 24:25, :] = window(depth_e, g)[0:1]
        depths_ref[g, 25:26, :] = window(depth_n, g)[0:1]
        depths_ref[g, 26:27, :] = window(dp, g)[0:1]

    slot = lanes_of(tp.shape) % SLOTS

    def edges(x, other):
        x = jnp.where(slot == 0, turn(x, -6, 1), other)
        return x[:, 0:cols], x[:, cols:]

    edge_p, edge_w = edges(press, press), edges(wet, wet)
    edge_t, edge_s = edges(tp, flux_t), edges(sp, flux_s)
    edge_total, edge_depth = edges(total, total), edges(dp, dp)

    def edge(pair, r):
        at = r % tile_rows
        return turn(pair[0] if 0 <= r < tile_rows else pair[1], -(SLOTS * at + 1), 1)

    depth = jnp.where(sea_ref[...] == 1, floor_ref[...], 0).astype(jnp.float32)

    def row_of(f, r):
        if r < 0:
            return before_ref[NSUB * f + r + NSUB]
        if r >= tile_rows:
            return after_ref[NSUB * f + r - tile_rows]
        return refs_of[f][pl.ds(r, levels, stride=tile_rows), :]

    def depth_of(r):
        if r < 0:
            x = before_ref[4 * NSUB, r + NSUB : r + NSUB + 1, :]
        elif r >= tile_rows:
            x = after_ref[4 * NSUB, r - tile_rows : r - tile_rows + 1, :]
        else:
            x = depth[r : r + 1]
        return jnp.broadcast_to(x, shape)

    lo, hi = -NSUB, tile_rows + NSUB
    for r in range(lo, hi):
        heavy = (level < depth_of(r)).astype(jnp.float32) * (-0.2 * row_of(2, r) + 0.8 * row_of(3, r))
        above, total = sums_above(heavy)
        press_ref[r - lo] = above + 0.5 * heavy
        total_ref[r - lo] = total

    def windows(r, before):
        for g in range(blocks):
            j = r - (sub_rows * g - before)
            if 0 <= j < sub_rows + 1 + before:
                yield g, j

    flux_before = [None, None]
    for r in range(lo, hi - 1):
        press, press_e = press_ref[r - lo], press_ref[r - lo + 1]
        total, total_a = total_ref[r - lo], total_ref[r - lo + 1]
        d, d_e = depth_of(r), depth_of(r + 1)
        d_n = jnp.where(last, edge(edge_depth, r), turn(d, -1, 1))
        face_e, face_n = jnp.minimum(d, d_e), jnp.minimum(d, d_n)
        u, v = row_of(0, r), row_of(1, r)
        east = u + DT_FLOW * (CORIOLIS * v - (press_e - press))
        press_n = jnp.where(last, edge(edge_p, r), turn(press, -1, 1))
        north = v + DT_FLOW * (-CORIOLIS * u - (press_n - press))
        total_e = total_a - total
        total_n = jnp.where(last, edge(edge_total, r), turn(total, -1, 1)) - total
        for g, j in windows(r, 2):
            send_ref[g, j] = east
            send_ref[g, 15, j : j + 1, :] = total_e[0:1]
            depths_ref[g, j : j + 1, :] = face_e[0:1]
        for g, j in windows(r, 1):
            send_ref[g, 7 + j] = north
            send_ref[g, 15, 7 + j : 8 + j, :] = total_n[0:1]
            depths_ref[g, 8 + j : 9 + j, :] = face_n[0:1]
            depths_ref[g, 16 + j : 17 + j, :] = d[0:1]
        if 0 <= r < tile_rows:
            local_ref[0, r] = east
            local_ref[1, r] = north
            faces_ref[0, r : r + 1, :] = face_e[0:1]
            faces_ref[1, r : r + 1, :] = face_n[0:1]
            for g in range(blocks):
                send_ref[g, 16, r : r + 1, :] = total_e[0:1]
                send_ref[g, 17, r : r + 1, :] = total_n[0:1]
        if r < -1 or r >= tile_rows:
            continue
        open_e = (level < face_e).astype(jnp.float32)
        open_n = (level < face_n).astype(jnp.float32)
        for i, (f, ends, out_ref) in enumerate(((2, edge_t, tmix_ref), (3, edge_s, smix_ref))):
            x = row_of(f, r)
            flux_e = open_e * (row_of(f, r + 1) - x)
            if r >= 0:
                ending = edge(ends, r)
                flux_n = open_n * (jnp.where(last, ending, turn(x, -1, 1)) - x)
                flux_b = jnp.where(first, ending, turn(flux_n, 1, 1))
                mixed = x + MIXING * ((flux_e - flux_before[i]) + (flux_n - flux_b))
                out_ref[pl.ds(r, levels, stride=tile_rows), :] = mixed
            flux_before[i] = flux_e


def ocean_phase(blocks, levels, base, ocean, sea, packed, after, before):
    tile_rows, cols = sea[0].shape
    flat = [x.reshape(levels * tile_rows, cols) for x in ocean]
    ins = [*flat, *sea, packed, after, before]
    outs = [
        shaped(levels * tile_rows, cols),
        shaped(levels * tile_rows, cols),
        shaped(blocks, ENTRIES, levels, cols),
        shaped(2, tile_rows, levels, cols),
        shaped(2, tile_rows, cols),
        shaped(blocks, 32, cols),
    ]
    tall = tile_rows + 2 * NSUB
    return pl.pallas_call(
        functools.partial(ocean_kernel, blocks, levels),
        grid=(1,),
        in_specs=[smem()] + [whole(x.shape) for x in ins],
        out_specs=[whole(x.shape) for x in outs],
        out_shape=outs,
        scratch_shapes=[pltpu.VMEM((tall, levels, cols), jnp.float32)] * 2,
        compiler_params=params(),
    )(base, *ins)


def velocity_kernel(group_ref, local_ref, faces_ref, received_ref, east_ref, north_ref):
    blocks = received_ref.shape[0]
    _, tile_rows, levels, cols = local_ref.shape
    group = group_ref[0]
    level = (group * levels + subs_of((levels, cols))).astype(jnp.float32)
    for f, out_ref in enumerate((east_ref, north_ref)):
        above = jnp.zeros((tile_rows, cols), jnp.float32)
        for s in range(blocks - 1):
            above = above + jnp.where(s < group, received_ref[s, 16 + f], 0.0)
        for r in range(tile_rows):
            x = local_ref[f, r] - DT_FLOW * jnp.broadcast_to(above[r : r + 1], (levels, cols))
            x = jnp.where(level < faces_ref[f, r : r + 1, :], x, 0.0)
            out_ref[pl.ds(r, levels, stride=tile_rows), :] = x


def velocities(group, local, faces, received):
    _, tile_rows, levels, cols = local.shape
    ins = [local, faces, received]
    out = shaped(levels * tile_rows, cols)
    return pl.pallas_call(
        velocity_kernel,
        grid=(1,),
        in_specs=[smem()] + [whole(x.shape) for x in ins],
        out_specs=[whole(out.shape)] * 2,
        out_shape=[out] * 2,
        compiler_params=params(),
    )(group, *ins)


def advection_kernel(first_block, level_count, *refs):
    (
        absorb_ref,
        surface_ref,
        depth_ref,
        totals_ref,
        courant_ref,
        q_ref,
        after_ref,
        before_ref,
        side_ref,
        side_after_ref,
        side_before_ref,
        carry_ref,
    ) = refs[:12]
    moved_ref, light_ref, heat_ref, carry_out_ref = refs[-9:-5]
    coef_ref, side_coef_ref, edge_ref, running_ref, above_ref = refs[-5:]
    step = pl.program_id(0)
    tracers, _, cols = q_ref.shape
    levels = courant_ref.shape[2]
    sub_rows = surface_ref.shape[0]
    rows = sub_rows + 2
    shape = (levels, cols)
    lane = lanes_of(shape)
    first, last = lane == 0, lane == cols - 1
    first8, last8 = first[0:SUB], last[0:SUB]
    slot = lane % SLOTS

    @pl.when(step == 0)
    def _():
        running_ref[...] = carry_ref[...]
        above = jnp.zeros(shape, jnp.float32)
        for s in range(first_block):
            above = above + totals_ref[s, 0]
        above_ref[...] = above

    level = ((first_block + step) * levels + subs_of(shape)).astype(jnp.float32)

    def spread(ref, r):
        return jnp.broadcast_to(ref[r : r + 1, :], shape)

    def courant(entry, face):
        x = courant_ref[0, entry] - DT_FLOW * spread(above_ref, entry)
        return COURANT * jnp.tanh(jnp.where(level < spread(depth_ref, face), x, 0.0))

    def coefficients(wet, ce, ce_b, cn, cn_b):
        return (
            wet
            * (
                1.0
                - jnp.maximum(ce, 0.0)
                + jnp.minimum(ce_b, 0.0)
                - jnp.maximum(cn, 0.0)
                + jnp.minimum(cn_b, 0.0)
            ),
            -wet * jnp.minimum(ce, 0.0),
            wet * jnp.maximum(ce_b, 0.0),
            -wet * jnp.minimum(cn, 0.0),
            wet * jnp.maximum(cn_b, 0.0),
        )

    side_e, side_n = courant(13, 24), courant(14, 25)
    wet = (level < spread(depth_ref, 26)).astype(jnp.float32)
    packed_coef = coefficients(wet, side_e, turn(side_e, SLOTS, 1), side_n, turn(side_n, 1, 1))
    for i in range(5):
        side_coef_ref[i] = packed_coef[i]
    ce_b = courant(0, 0)
    for j in range(rows):
        ce, cn = courant(1 + j, 1 + j), courant(7 + j, 8 + j)
        cn_b = jnp.where(first, turn(side_n, -(SLOTS * (j + 1) + 1), 1), turn(cn, 1, 1))
        wet = (level < spread(depth_ref, 16 + j)).astype(jnp.float32)
        for i, x in enumerate(coefficients(wet, ce, ce_b, cn, cn_b)):
            coef_ref[5 * j + i] = x
        ce_b = ce
    above_ref[...] = above_ref[...] + totals_ref[first_block + step, 0]

    place = lane // SLOTS
    for i in range(side_ref.shape[0]):
        x = side_ref[i]
        v, m = i // SUB, i % SUB
        for odd in range(2):
            start = SLOTS * (2 * m + odd)
            for ref, row in ((side_after_ref, 6), (side_before_ref, 1)):
                to = HALF * odd + SLOTS * row
                x = jnp.where(place == to // SLOTS, turn(ref[v], to - start, 1), x)
        edge_ref[i, 0] = jnp.where(slot == 0, turn(x, -6, 1), x)
        x = (
            (side_coef_ref[0] * x + side_coef_ref[1] * turn(x, -SLOTS, 1))
            + (side_coef_ref[2] * turn(x, SLOTS, 1) + side_coef_ref[3] * turn(x, -1, 1))
            + side_coef_ref[4] * turn(x, 1, 1)
        )
        edge_ref[i, 1] = jnp.where(slot == 0, turn(x, -6, 1), x)

    layer = 2.0 / level_count
    zero = jnp.zeros((SUB, cols), jnp.float32)
    for k in range(0, levels, SUB):
        at = slice(k, k + SUB)

        def stencil(x, j, edge):
            north = jnp.where(last8, edge, turn(x[1], -1, 1))
            south = jnp.where(first8, edge, turn(x[1], 1, 1))
            return (
                (coef_ref[5 * j, at] * x[1] + coef_ref[5 * j + 1, at] * x[2])
                + (coef_ref[5 * j + 2, at] * x[0] + coef_ref[5 * j + 3, at] * north)
                + coef_ref[5 * j + 4, at] * south
            )

        def advect(i, sums):
            edge0, edge1 = edge_ref[i, 0, at], edge_ref[i, 1, at]
            sums = list(sums)
            for odd in range(2):
                t = 2 * i + odd
                x = [before_ref[t, n, at] for n in range(NSUB)]
                x += [
                    q_ref[t, pl.ds(sub_rows * k + r, SUB, stride=sub_rows), :]
                    for r in range(sub_rows)
                ]
                x += [after_ref[t, n, at] for n in range(NSUB)]

                def edge(source, j):
                    return turn(source, -(HALF * odd + SLOTS * (j + 1) + 1), 1)

                x = [stencil(x[j : j + 3], j, edge(edge0, j)) for j in range(rows)]
                x = [stencil(x[j - 1 : j + 2], j, edge(edge1, j)) for j in range(1, rows - 1)]
                for r in range(sub_rows):
                    moved_ref[t, r, at] = x[r]
                    sums[r] = sums[r] + absorb_ref[t] * x[r]
            return tuple(sums)

        sums = lax.fori_loop(0, tracers // 2, advect, (zero,) * sub_rows, unroll=2)
        for r in range(sub_rows):
            optical = layer * (CLEAR_WATER + sums[r])
            above, total = sums_above(optical)
            through = jnp.exp(-(running_ref[r] + above))
            running_ref[r] = running_ref[r] + total
            surface = jnp.broadcast_to(surface_ref[r : r + 1, :], (SUB, cols))
            light_ref[r, at] = surface * through * jnp.exp(-0.5 * optical)
            wet = (level[at] < jnp.broadcast_to(depth_ref[17 + r : 18 + r, :], (SUB, cols))).astype(
                jnp.float32
            )
            heat_ref[0, r, at] = wet * surface * through * (1.0 - jnp.exp(-optical)) / layer
    carry_out_ref[...] = running_ref[...]


def advection(cut, level_count, absorb, surface, depth, received, q, after, before, side, side_after, side_before, carry, heat):
    first_block, blocks = cut
    tracers, all_rows, cols = q.shape
    every, _, levels, _ = received.shape
    sub_rows = surface.shape[0]
    rows = levels * sub_rows
    rim = pl.BlockSpec((tracers, NSUB, levels, cols), lambda i: (0, 0, i, 0))
    by_level = lambda x: pl.BlockSpec(
        (x.shape[0], levels, cols), lambda i: (0, first_block + i, 0)
    )
    operands = [absorb, surface, depth, received, received, q, after, before, side, side_after, side_before, carry]
    in_specs = [
        smem(),
        whole(surface.shape),
        whole(depth.shape),
        pl.BlockSpec((every, 1, levels, cols), lambda i: (0, 15, 0, 0)),
        pl.BlockSpec((1, ENTRIES, levels, cols), lambda i: (first_block + i, 0, 0, 0)),
        pl.BlockSpec((tracers, rows, cols), lambda i: (0, first_block + i, 0)),
        rim,
        rim,
        by_level(side),
        by_level(side_after),
        by_level(side_before),
        whole(carry.shape),
    ]
    aliases = {}
    if heat is not None:
        aliases = {len(operands): 2}
        operands.append(heat)
        in_specs.append(pl.BlockSpec(memory_space=pl.ANY))
    outs = [
        shaped(tracers, sub_rows, blocks * levels, cols),
        shaped(sub_rows, blocks * levels, cols),
        shaped(every, sub_rows, levels, cols),
        shaped(*carry.shape),
    ]
    return pl.pallas_call(
        functools.partial(advection_kernel, first_block, level_count),
        grid=(blocks,),
        in_specs=in_specs,
        out_specs=[
            pl.BlockSpec((tracers, sub_rows, levels, cols), lambda i: (0, 0, i, 0)),
            pl.BlockSpec((sub_rows, levels, cols), lambda i: (0, i, 0)),
            pl.BlockSpec((1, sub_rows, levels, cols), lambda i: (first_block + i, 0, 0, 0)),
            whole(carry.shape),
        ],
        out_shape=outs,
        scratch_shapes=[
            pltpu.VMEM((5 * (sub_rows + 2), levels, cols), jnp.float32),
            pltpu.VMEM((5, levels, cols), jnp.float32),
            pltpu.VMEM((tracers // 2, 2, levels, cols), jnp.float32),
            pltpu.VMEM((sub_rows, SUB, cols), jnp.float32),
            pltpu.VMEM((levels, cols), jnp.float32),
        ],
        input_output_aliases=aliases,
        compiler_params=params(),
    )(*operands)


def uptake_kernel(first_level, *refs):
    growth_ref, half_ref, dim_ref, matrix_ref, depth_ref, moved_ref, light_ref = refs[:7]
    result_ref, uptake_ref = refs[-2:]
    tracers, sub_rows, levels, cols = moved_ref.shape
    step = pl.program_id(0)
    matrix = matrix_ref[...]
    matrix_high = matrix.astype(jnp.bfloat16)
    matrix_low = (matrix - matrix_high.astype(jnp.float32)).astype(jnp.bfloat16)
    for k in range(0, levels, SUB):
        at = slice(k, k + SUB)
        level = (first_level + step * levels + k + subs_of((SUB, cols))).astype(jnp.float32)
        light = [light_ref[r, at] for r in range(sub_rows)]
        food = [moved_ref[0, r, at] for r in range(sub_rows)]
        both = [light[r] * food[r] for r in range(sub_rows)]

        def uptake(t, _):
            for r in range(sub_rows):
                scale = (half_ref[t] + food[r]) * (light[r] + dim_ref[t])
                value = growth_ref[t] * moved_ref[t, r, at] * (both[r] / scale)
                uptake_ref[pl.ds(t * SUB, SUB), r * cols : (r + 1) * cols] = value
            return _

        lax.fori_loop(0, tracers, uptake, 0, unroll=4)
        amount = uptake_ref[...]
        high = amount.astype(jnp.bfloat16)
        low = (amount - high.astype(jnp.float32)).astype(jnp.bfloat16)
        dot = functools.partial(jnp.dot, preferred_element_type=jnp.float32)
        change = dot(matrix_high, high) + (dot(matrix_high, low) + dot(matrix_low, high))
        for r in range(sub_rows):
            depth = jnp.broadcast_to(depth_ref[17 + r : 18 + r, :], (SUB, cols))
            scale = DT_BIO * (level < depth).astype(jnp.float32)
            for t in range(tracers):
                result_ref[t, pl.ds(sub_rows * k + r, SUB, stride=sub_rows), :] = (
                    moved_ref[t, r, at]
                    + scale * change[SUB * t : SUB * (t + 1), r * cols : (r + 1) * cols]
                )


def uptake(cut, levels, all_rows, scalars, matrix, depth, moved, light, result):
    first_block, blocks = cut
    tracers, sub_rows, _, cols = moved.shape
    rows = levels * sub_rows
    operands = [*scalars, matrix, depth, moved, light]
    in_specs = [smem()] * 3 + [
        whole(matrix.shape),
        whole(depth.shape),
        pl.BlockSpec((tracers, sub_rows, levels, cols), lambda i: (0, 0, i, 0)),
        pl.BlockSpec((sub_rows, levels, cols), lambda i: (0, i, 0)),
    ]
    aliases = {}
    if result is not None:
        aliases = {len(operands): 0}
        operands.append(result)
        in_specs.append(pl.BlockSpec(memory_space=pl.ANY))
    return pl.pallas_call(
        functools.partial(uptake_kernel, first_block * levels),
        grid=(blocks,),
        in_specs=in_specs,
        out_specs=pl.BlockSpec((tracers, rows, cols), lambda i: (0, first_block + i, 0)),
        out_shape=shaped(tracers, all_rows, cols),
        scratch_shapes=[pltpu.VMEM((tracers * SUB, sub_rows * cols), jnp.float32)],
        input_output_aliases=aliases,
        compiler_params=params(),
    )(*operands)


def warming_kernel(base_ref, heat_ref, tmix_ref, smix_ref, sea_ref, floor_ref, warm_ref, buoyant_ref):
    blocks, sub_rows, levels, cols = heat_ref.shape
    tile_rows = blocks * sub_rows
    level = (base_ref[0] + subs_of((levels, cols))).astype(jnp.float32)
    depth = jnp.where(sea_ref[...] == 1, floor_ref[...], 0).astype(jnp.float32)
    for r in range(tile_rows):
        at = pl.ds(r, levels, stride=tile_rows)
        warm = tmix_ref[at, :] + WARMING_FACTOR * heat_ref[r // sub_rows, r % sub_rows]
        wet = (level < depth[r : r + 1]).astype(jnp.float32)
        warm_ref[at, :] = warm
        buoyant_ref[at, :] = wet * (0.2 * warm - 0.8 * smix_ref[at, :])


def warming(base, heat, tmix, smix, sea):
    ins = [heat, tmix, smix, *sea]
    return pl.pallas_call(
        warming_kernel,
        grid=(1,),
        in_specs=[smem()] + [whole(x.shape) for x in ins],
        out_specs=[whole(tmix.shape)] * 2,
        out_shape=[shaped(*tmix.shape)] * 2,
        compiler_params=params(),
    )(base, *ins)


def from_before(x, axis):
    return lax.ppermute(x, axis, [(i, i + 1) for i in range(lax.axis_size(axis) - 1)])


def from_after(x, axis):
    return lax.ppermute(x, axis, [(i + 1, i) for i in range(lax.axis_size(axis) - 1)])


def row_pairs():
    blocks, tiles = lax.axis_size("comp"), lax.axis_size("gx")
    places = [b * tiles + tile for tile in range(tiles) for b in range(blocks)]
    return list(zip(places[:-1], places[1:]))


def from_block_before(x):
    return lax.ppermute(x, ("comp", "gx"), row_pairs())


def from_block_after(x):
    return lax.ppermute(x, ("comp", "gx"), [(later, own) for own, later in row_pairs()])


def from_sides(x):
    if lax.axis_size("gy") == 2:
        other = lax.ppermute(x, "gy", [(0, 1), (1, 0)])
        return other, other
    return from_before(x, "gy"), from_after(x, "gy")


def on_device(
    zonal_flow_speed,
    meridional_flow_speed,
    thermal_anomaly,
    brine_anomaly_values,
    marine_indicator,
    seafloor_layer,
    dissolved_species,
    topmost_sunshine,
    attenuation_coefficient,
    peak_intake_speed,
    feedstock_midpoint_constant,
    photon_midpoint_constant,
    stoichiometry_matrix,
):
    group_index = lax.axis_index("comp")
    blocks = lax.axis_size("comp")
    levels, tile_rows, tile_cols = zonal_flow_speed.shape
    tracer_count, level_count = dissolved_species.shape[:2]
    sub_rows = dissolved_species.shape[4]
    ocean = (zonal_flow_speed, meridional_flow_speed, thermal_anomaly, brine_anomaly_values)
    sea = (marine_indicator, seafloor_layer)
    group = group_index.astype(jnp.int32).reshape(1)
    base = group * levels
    place = jnp.stack([lax.axis_index("gy"), lax.axis_size("gy")]).astype(jnp.int32)

    half = blocks // 2
    cuts = [(0, half), (half, blocks - half)]
    q = dissolved_species.reshape(tracer_count, level_count * sub_rows, tile_cols)
    lows, highs, packed, edge_low, edge_high = pack(
        ocean, sea, q, levels, sub_rows, [(start * levels, size * levels) for start, size in cuts]
    )
    left, right = from_sides(packed)
    afters = [from_block_after(lows[0])]
    befores = [from_block_before(highs[0])]

    up, down, packed, side, side_low, side_high = sides(
        place, packed, left, right, edge_low, edge_high, levels, level_count, tracer_count
    )
    after, before = from_after(up, "gx"), from_before(down, "gx")
    tmix, smix, send, local, faces, depths = ocean_phase(
        blocks, levels, base, ocean, sea, packed, after, before
    )
    received = lax.all_to_all(send, "comp", split_axis=0, concat_axis=0, tiled=True)
    depth = lax.dynamic_index_in_dim(depths, group_index, 0, False)
    side_after, side_before = from_block_after(side_low), from_block_before(side_high)
    afters.append(from_block_after(lows[1]))
    befores.append(from_block_before(highs[1]))
    east_new, north_new = velocities(group, local, faces, received)

    matrix = (
        stoichiometry_matrix[:, None, :, None] * jnp.eye(SUB, dtype=jnp.float32)[None, :, None, :]
    ).reshape(SUB * tracer_count, SUB * tracer_count)
    surface = topmost_sunshine.reshape(sub_rows, tile_cols)
    scalars = (peak_intake_speed, feedstock_midpoint_constant, photon_midpoint_constant)
    carry = jnp.zeros((sub_rows, SUB, tile_cols), jnp.float32)
    heat, result = None, None
    for cut, rim_after, rim_before in zip(cuts, afters, befores):
        moved, light, heat, carry = advection(
            cut,
            level_count,
            attenuation_coefficient,
            surface,
            depth,
            received,
            q,
            rim_after,
            rim_before,
            side,
            side_after,
            side_before,
            carry,
            heat,
        )
        result = uptake(
            cut, levels, level_count * sub_rows, scalars, matrix, depth, moved, light, result
        )
    heat = lax.all_to_all(heat, "comp", split_axis=0, concat_axis=0, tiled=True)
    warmed_result, buoyancy = warming(base, heat, tmix, smix, sea)
    fields = (east_new, north_new, warmed_result, smix, buoyancy)
    return (
        *[x.reshape(zonal_flow_speed.shape) for x in fields],
        result.reshape(dissolved_species.shape),
    )


def solution(mesh):
    return jax.shard_map(
        on_device,
        mesh=mesh,
        in_specs=(
            P("comp", "gx", "gy"),
            P("comp", "gx", "gy"),
            P("comp", "gx", "gy"),
            P("comp", "gx", "gy"),
            P("gx", "gy"),
            P("gx", "gy"),
            P(None, None, "gx", "comp", None, "gy"),
            P("gx", "comp", None, "gy"),
            P(),
            P(),
            P(),
            P(),
            P(),
        ),
        out_specs=(
            P("comp", "gx", "gy"),
            P("comp", "gx", "gy"),
            P("comp", "gx", "gy"),
            P("comp", "gx", "gy"),
            P("comp", "gx", "gy"),
            P(None, None, "gx", "comp", None, "gy"),
        ),
        check_vma=False,
    )
```

```python
import functools

import jax
import jax.numpy as jnp
from jax import lax
from jax.experimental import pallas as pl
from jax.experimental.pallas import tpu as pltpu
from jax.sharding import PartitionSpec as P

NSUB = 2
SLOTS = 4 * NSUB
SUB = 8
HALF = 64
ENTRIES = 18

DT_FLOW = 0.1
CORIOLIS = 0.3
MIXING = 0.15
COURANT = 0.24
DT_BIO = 0.5
WARMING_FACTOR = 0.5
CLEAR_WATER = 0.5
VMEM_LIMIT = 48 * 1024 * 1024


def lanes_of(shape):
    return lax.broadcasted_iota(jnp.int32, shape, len(shape) - 1)


def subs_of(shape):
    return lax.broadcasted_iota(jnp.int32, shape, len(shape) - 2)


def turn(x, by, axis):
    by = by % x.shape[axis]
    return x if by == 0 else pltpu.roll(x, by, axis)


def params(**more):
    return pltpu.CompilerParams(vmem_limit_bytes=VMEM_LIMIT, **more)


def whole(shape):
    return pl.BlockSpec(shape, lambda *_: (0,) * len(shape))


def smem():
    return pl.BlockSpec(memory_space=pltpu.SMEM)


def shaped(*shape):
    return jax.ShapeDtypeStruct(shape, jnp.float32)


def sums_above(x):
    sub = subs_of(x.shape)
    running, total = x, x
    by = 1
    while by < x.shape[0]:
        running = running + jnp.where(sub >= by, turn(running, by, 0), 0.0)
        total = total + turn(total, by, 0)
        by *= 2
    return jnp.where(sub >= 1, turn(running, 1, 0), 0.0), total


def cut_kernel(start, size, q_ref, *refs):
    low_ref, high_ref, sems = refs[-3:]
    ends = q_ref.shape[2] - 1
    copies = [
        pltpu.make_async_copy(q_ref.at[:, pl.ds(start, size), at], out_ref, sems.at[i])
        for i, (at, out_ref) in enumerate(((0, low_ref), (ends, high_ref)))
    ]
    for copy in copies:
        copy.start()
    for copy in copies:
        copy.wait()


def cut_rows(q, start, size, after):
    tracers, _, _, _, cols = q.shape
    anywhere = pl.BlockSpec(memory_space=pl.ANY)
    return pl.pallas_call(
        functools.partial(cut_kernel, start, size),
        in_specs=[anywhere] * (1 + len(after)),
        out_specs=[anywhere] * 2,
        out_shape=[shaped(tracers, size, NSUB, cols)] * 2,
        scratch_shapes=[pltpu.SemaphoreType.DMA((2,))],
        compiler_params=params(),
    )(q, *after)


def both_ends(acc):
    return jnp.where(lanes_of(acc.shape) % SLOTS < SLOTS // 2, acc, turn(acc, SLOTS // 2, 1))


def pack_tracers_kernel(sub_rows, group, q_ref, packed_ref):
    cols = q_ref.shape[2]
    level_count = q_ref.shape[1] // sub_rows
    lane = lanes_of((SUB, cols))
    for pair in range(group // 2):
        for k in range(0, level_count, SUB):
            acc = jnp.zeros((SUB, cols), jnp.float32)
            for odd in range(2):
                for r in range(sub_rows):
                    x = q_ref[2 * pair + odd, pl.ds(sub_rows * k + r, SUB, stride=sub_rows), :]
                    at = HALF * odd + SLOTS * (r + NSUB)
                    acc = jnp.where(lane // SLOTS == at // SLOTS, turn(x, at + NSUB, 1), acc)
            packed_ref[pair, k : k + SUB, :] = both_ends(acc)


def pack_tracers(q, sub_rows):
    tracers, rows, cols = q.shape
    group = 4
    levels = rows // sub_rows
    return pl.pallas_call(
        functools.partial(pack_tracers_kernel, sub_rows, group),
        grid=(tracers // group,),
        in_specs=[pl.BlockSpec((group, rows, cols), lambda i: (i, 0, 0))],
        out_specs=pl.BlockSpec((group // 2, levels, cols), lambda i: (i, 0, 0)),
        out_shape=shaped(tracers // 2, levels, cols),
        compiler_params=params(),
    )(q)


def fetched(kernel, count, *refs):
    far, refs, near, sems = refs[:count], refs[count : -count - 1], refs[-count - 1 : -1], refs[-1]
    copies = [pltpu.make_async_copy(far[i], near[i], sems.at[i]) for i in range(count)]
    for copy in copies:
        copy.start()
    for copy in copies:
        copy.wait()
    kernel(*near, *refs)


def call_fetching(kernel, far, near, outs, scratch=(), scalars=()):
    hbm = pl.BlockSpec(memory_space=pltpu.HBM)
    return pl.pallas_call(
        functools.partial(fetched, kernel, len(far)),
        in_specs=[hbm] * len(far)
        + [smem()] * len(scalars)
        + [pl.BlockSpec(memory_space=pltpu.VMEM)] * len(near),
        out_shape=outs,
        scratch_shapes=list(scratch)
        + [pltpu.VMEM(x.shape, x.dtype) for x in far]
        + [pltpu.SemaphoreType.DMA((len(far),))],
        compiler_params=params(),
    )(*far, *scalars, *near)


def pack_ocean_kernel(levels, *refs):
    u_ref, v_ref, t_ref, s_ref, sea_ref, floor_ref, packed_ref, edge_low_ref, edge_high_ref = refs
    tile_rows, cols = sea_ref.shape
    lane = lanes_of((levels, cols))
    edge_low_ref[4 * NSUB] = jnp.zeros((levels, cols), jnp.float32)
    edge_high_ref[4 * NSUB] = jnp.zeros((levels, cols), jnp.float32)
    for f, ref in enumerate((u_ref, v_ref, t_ref, s_ref)):
        acc = jnp.zeros((levels, cols), jnp.float32)
        for r in range(tile_rows):
            x = ref[pl.ds(r, levels, stride=tile_rows), :]
            acc = jnp.where(lane // SLOTS == r, turn(x, SLOTS * r + NSUB, 1), acc)
            if r < NSUB:
                edge_low_ref[NSUB * f + r] = x
            if r >= tile_rows - NSUB:
                edge_high_ref[NSUB * f + r - tile_rows + NSUB] = x
        packed_ref[f] = both_ends(acc)
    depth = jnp.where(sea_ref[...] == 1, floor_ref[...], 0).astype(jnp.float32)
    acc = jnp.zeros((levels, cols), jnp.float32)
    for r in range(tile_rows):
        x = jnp.broadcast_to(depth[r : r + 1], (levels, cols))
        acc = jnp.where(lane // SLOTS == r, turn(x, SLOTS * r + NSUB, 1), acc)
    packed_ref[4] = both_ends(acc)
    edge_low_ref[4 * NSUB, 0:NSUB, :] = depth[0:NSUB]
    edge_high_ref[4 * NSUB, 0:NSUB, :] = depth[tile_rows - NSUB :]


def pack_ocean(flat, sea, levels):
    cols = sea[0].shape[1]
    edge = shaped(4 * NSUB + 1, levels, cols)
    return call_fetching(
        functools.partial(pack_ocean_kernel, levels),
        [*flat, *sea],
        [],
        [shaped(5, levels, cols), edge, edge],
    )


def with_sides(own, left, right):
    slot = lanes_of(own.shape) % SLOTS
    ends = jnp.where(slot < NSUB, left, right)
    return jnp.where((slot < NSUB) | (slot >= SLOTS - NSUB), ends, own)


def ocean_sides_kernel(place_ref, own_ref, left_ref, right_ref, low_ref, high_ref, up_ref, down_ref, out_ref):
    _, levels, cols = own_ref.shape
    rows = low_ref.shape[0]
    up_ref[0:rows] = low_ref[...]
    down_ref[0:rows] = high_ref[...]
    slot = lanes_of((levels, cols)) % SLOTS
    first, last = place_ref[0] == 0, place_ref[0] == place_ref[1] - 1
    for f in range(5):
        x = with_sides(own_ref[f], left_ref[f], right_ref[f])
        if f == 4:
            x = jnp.where((slot < NSUB) & first, 0.0, x)
            x = jnp.where((slot >= SLOTS - NSUB) & last, 0.0, x)
        out_ref[f] = x
        up_ref[rows + f] = x
        down_ref[rows + f] = x


def ocean_sides(place, own, left, right, low, high):
    edge = shaped(low.shape[0] + 5, *low.shape[1:])
    return pl.pallas_call(
        ocean_sides_kernel,
        in_specs=[smem()] + [pl.BlockSpec(memory_space=pltpu.VMEM)] * 5,
        out_shape=[edge, edge, shaped(*own.shape)],
        compiler_params=params(),
    )(place, own, left, right, low, high)


def tracer_sides_kernel(own_ref, left_ref, right_ref, side_ref, low_ref, high_ref):
    pairs, level_count, cols = own_ref.shape
    lane = lanes_of((level_count, cols))
    for v in range(low_ref.shape[0]):
        low = jnp.zeros((level_count, cols), jnp.float32)
        high = jnp.zeros((level_count, cols), jnp.float32)
        for m in range(min(SUB, pairs - v * SUB)):
            at = v * SUB + m
            x = with_sides(own_ref[at], left_ref[at], right_ref[at])
            side_ref[at] = x
            for odd in range(2):
                to = 2 * SLOTS * m + SLOTS * odd
                here = lane // SLOTS == to // SLOTS
                low = jnp.where(here, turn(x, to - HALF * odd - SLOTS * 2, 1), low)
                high = jnp.where(here, turn(x, to - HALF * odd - SLOTS * 5, 1), high)
        low_ref[v] = low
        high_ref[v] = high


def tracer_sides(own, left, right):
    pairs, level_count, cols = own.shape
    edge = shaped(-(-pairs // SUB), level_count, cols)
    return pl.pallas_call(
        tracer_sides_kernel,
        in_specs=[pl.BlockSpec(memory_space=pltpu.VMEM)] * 3,
        out_shape=[shaped(*own.shape), edge, edge],
        compiler_params=params(),
    )(own, left, right)


def ocean_kernel(blocks, levels, *refs):
    u_ref, v_ref, t_ref, s_ref, sea_ref, floor_ref = refs[:6]
    base_ref, packed_ref, after_ref, before_ref = refs[6:10]
    tmix_ref, smix_ref, send_ref, local_ref, faces_ref, depths_ref, press_ref, total_ref = refs[10:]
    tile_rows, cols = sea_ref.shape
    sub_rows = tile_rows // blocks
    shape = (levels, cols)
    lane = lanes_of(shape)
    first, last = lane == 0, lane == cols - 1
    level = (base_ref[0] + subs_of(shape)).astype(jnp.float32)
    rims = after_ref.shape[0] - 5
    refs_of = (u_ref, v_ref, t_ref, s_ref)

    def packed(f):
        after, before = after_ref[rims + f], before_ref[rims + f]
        rim = jnp.where(lane < NSUB * SLOTS, after, jnp.where(lane >= cols - NSUB * SLOTS, before, 0.0))
        return jnp.concatenate([packed_ref[f], rim], axis=1)

    def row_after(x):
        return turn(x, -SLOTS, 1)

    def row_before(x):
        return turn(x, SLOTS, 1)

    up, vp, tp, sp, dp = [packed(f) for f in range(5)]
    wide = jnp.concatenate([level, level], axis=1)
    wet = (wide < dp).astype(jnp.float32)
    heavy = wet * (-0.2 * tp + 0.8 * sp)
    above, total = sums_above(heavy)
    press = above + 0.5 * heavy
    east = up + DT_FLOW * (CORIOLIS * vp - (row_after(press) - press))
    north = vp + DT_FLOW * (-CORIOLIS * up - (turn(press, -1, 1) - press))
    open_n = wet * turn(wet, -1, 1)
    flux_t = open_n * (turn(tp, -1, 1) - tp)
    flux_s = open_n * (turn(sp, -1, 1) - sp)
    total_e, total_n = row_after(total) - total, turn(total, -1, 1) - total
    depth_e, depth_n = jnp.minimum(dp, row_after(dp)), jnp.minimum(dp, turn(dp, -1, 1))

    def window(x, g):
        x = turn(x, -SLOTS * (sub_rows * g - NSUB), 1)[:, 0:cols]
        return jnp.where(lane < HALF, x, turn(x, HALF, 1))

    for g in range(blocks):
        send_ref[g, 13] = window(east, g)
        send_ref[g, 14] = window(north, g)
        send_ref[g, 15, 13:14, :] = window(total_e, g)[0:1]
        send_ref[g, 15, 14:15, :] = window(total_n, g)[0:1]
        send_ref[g, 15, 15:16, :] = jnp.zeros((1, cols), jnp.float32)
        depths_ref[g, 24:25, :] = window(depth_e, g)[0:1]
        depths_ref[g, 25:26, :] = window(depth_n, g)[0:1]
        depths_ref[g, 26:27, :] = window(dp, g)[0:1]

    slot = lanes_of(tp.shape) % SLOTS

    def edges(x, other):
        x = jnp.where(slot == 0, turn(x, -6, 1), other)
        return x[:, 0:cols], x[:, cols:]

    edge_p, edge_w = edges(press, press), edges(wet, wet)
    edge_t, edge_s = edges(tp, flux_t), edges(sp, flux_s)
    edge_total, edge_depth = edges(total, total), edges(dp, dp)

    def edge(pair, r):
        at = r % tile_rows
        return turn(pair[0] if 0 <= r < tile_rows else pair[1], -(SLOTS * at + 1), 1)

    depth = jnp.where(sea_ref[...] == 1, floor_ref[...], 0).astype(jnp.float32)

    def row_of(f, r):
        if r < 0:
            return before_ref[NSUB * f + r + NSUB]
        if r >= tile_rows:
            return after_ref[NSUB * f + r - tile_rows]
        return refs_of[f][pl.ds(r, levels, stride=tile_rows), :]

    def depth_of(r):
        if r < 0:
            x = before_ref[4 * NSUB, r + NSUB : r + NSUB + 1, :]
        elif r >= tile_rows:
            x = after_ref[4 * NSUB, r - tile_rows : r - tile_rows + 1, :]
        else:
            x = depth[r : r + 1]
        return jnp.broadcast_to(x, shape)

    lo, hi = -NSUB, tile_rows + NSUB
    for r in range(lo, hi):
        heavy = (level < depth_of(r)).astype(jnp.float32) * (-0.2 * row_of(2, r) + 0.8 * row_of(3, r))
        above, total = sums_above(heavy)
        press_ref[r - lo] = above + 0.5 * heavy
        total_ref[r - lo] = total

    def windows(r, before):
        for g in range(blocks):
            j = r - (sub_rows * g - before)
            if 0 <= j < sub_rows + 1 + before:
                yield g, j

    flux_before = [None, None]
    for r in range(lo, hi - 1):
        press, press_e = press_ref[r - lo], press_ref[r - lo + 1]
        total, total_a = total_ref[r - lo], total_ref[r - lo + 1]
        d, d_e = depth_of(r), depth_of(r + 1)
        d_n = jnp.where(last, edge(edge_depth, r), turn(d, -1, 1))
        face_e, face_n = jnp.minimum(d, d_e), jnp.minimum(d, d_n)
        u, v = row_of(0, r), row_of(1, r)
        east = u + DT_FLOW * (CORIOLIS * v - (press_e - press))
        press_n = jnp.where(last, edge(edge_p, r), turn(press, -1, 1))
        north = v + DT_FLOW * (-CORIOLIS * u - (press_n - press))
        total_e = total_a - total
        total_n = jnp.where(last, edge(edge_total, r), turn(total, -1, 1)) - total
        for g, j in windows(r, 2):
            send_ref[g, j] = east
            send_ref[g, 15, j : j + 1, :] = total_e[0:1]
            depths_ref[g, j : j + 1, :] = face_e[0:1]
        for g, j in windows(r, 1):
            send_ref[g, 7 + j] = north
            send_ref[g, 15, 7 + j : 8 + j, :] = total_n[0:1]
            depths_ref[g, 8 + j : 9 + j, :] = face_n[0:1]
            depths_ref[g, 16 + j : 17 + j, :] = d[0:1]
        if 0 <= r < tile_rows:
            local_ref[0, r] = east
            local_ref[1, r] = north
            faces_ref[0, r : r + 1, :] = face_e[0:1]
            faces_ref[1, r : r + 1, :] = face_n[0:1]
            for g in range(blocks):
                send_ref[g, 16, r : r + 1, :] = total_e[0:1]
                send_ref[g, 17, r : r + 1, :] = total_n[0:1]
        if r < -1 or r >= tile_rows:
            continue
        open_e = (level < face_e).astype(jnp.float32)
        open_n = (level < face_n).astype(jnp.float32)
        for i, (f, ends, out_ref) in enumerate(((2, edge_t, tmix_ref), (3, edge_s, smix_ref))):
            x = row_of(f, r)
            flux_e = open_e * (row_of(f, r + 1) - x)
            if r >= 0:
                ending = edge(ends, r)
                flux_n = open_n * (jnp.where(last, ending, turn(x, -1, 1)) - x)
                flux_b = jnp.where(first, ending, turn(flux_n, 1, 1))
                mixed = x + MIXING * ((flux_e - flux_before[i]) + (flux_n - flux_b))
                out_ref[pl.ds(r, levels, stride=tile_rows), :] = mixed
            flux_before[i] = flux_e


def ocean_phase(blocks, levels, base, flat, sea, packed, after, before):
    tile_rows, cols = sea[0].shape
    outs = [
        shaped(levels * tile_rows, cols),
        shaped(levels * tile_rows, cols),
        shaped(blocks, ENTRIES, levels, cols),
        shaped(2, tile_rows, levels, cols),
        shaped(2, tile_rows, cols),
        shaped(blocks, 32, cols),
    ]
    tall = tile_rows + 2 * NSUB
    return call_fetching(
        functools.partial(ocean_kernel, blocks, levels),
        [*flat, *sea],
        [packed, after, before],
        outs,
        [pltpu.VMEM((tall, levels, cols), jnp.float32)] * 2,
        [base],
    )


def velocity_kernel(group_ref, local_ref, faces_ref, received_ref, east_ref, north_ref):
    blocks = received_ref.shape[0]
    _, tile_rows, levels, cols = local_ref.shape
    group = group_ref[0]
    level = (group * levels + subs_of((levels, cols))).astype(jnp.float32)
    for f, out_ref in enumerate((east_ref, north_ref)):
        above = jnp.zeros((tile_rows, cols), jnp.float32)
        for s in range(blocks - 1):
            above = above + jnp.where(s < group, received_ref[s, 16 + f], 0.0)
        for r in range(tile_rows):
            x = local_ref[f, r] - DT_FLOW * jnp.broadcast_to(above[r : r + 1], (levels, cols))
            x = jnp.where(level < faces_ref[f, r : r + 1, :], x, 0.0)
            out_ref[pl.ds(r, levels, stride=tile_rows), :] = x


def velocities(group, local, faces, received):
    _, tile_rows, levels, cols = local.shape
    ins = [local, faces, received]
    out = shaped(levels * tile_rows, cols)
    return pl.pallas_call(
        velocity_kernel,
        grid=(1,),
        in_specs=[smem()] + [whole(x.shape) for x in ins],
        out_specs=[whole(out.shape)] * 2,
        out_shape=[out] * 2,
        compiler_params=params(),
    )(group, *ins)


def advection_kernel(first_part, parts, level_count, *refs):
    (
        absorb_ref,
        surface_ref,
        depth_ref,
        totals_ref,
        courant_ref,
        q_ref,
        after_ref,
        before_ref,
        side_ref,
        side_after_ref,
        side_before_ref,
        carry_ref,
    ) = refs[:12]
    moved_ref, light_ref, heat_ref, carry_out_ref = refs[-9:-5]
    coef_ref, side_coef_ref, edge_ref, running_ref, above_ref = refs[-5:]
    step = pl.program_id(0)
    tracers, _, cols = q_ref.shape
    levels = courant_ref.shape[2]
    sub_rows = surface_ref.shape[0]
    rows = sub_rows + 2
    shape = (levels, cols)
    lane = lanes_of(shape)
    first, last = lane == 0, lane == cols - 1
    first8, last8 = first[0:SUB], last[0:SUB]
    slot = lane % SLOTS

    @pl.when(step == 0)
    def _():
        running_ref[...] = carry_ref[...]

    part = first_part + step
    above = jnp.zeros(above_ref.shape, jnp.float32)
    for s in range(totals_ref.shape[0] - 1):
        above = above + jnp.where(s < part // parts, totals_ref[s, 0], 0.0)
    above_ref[...] = above
    level = (part * levels + subs_of(shape)).astype(jnp.float32)

    def spread(ref, r):
        return jnp.broadcast_to(ref[r : r + 1, :], shape)

    def courant(entry, face):
        x = courant_ref[0, entry] - DT_FLOW * spread(above_ref, entry)
        return COURANT * jnp.tanh(jnp.where(level < spread(depth_ref, face), x, 0.0))

    def coefficients(wet, ce, ce_b, cn, cn_b):
        return (
            wet
            * (
                1.0
                - jnp.maximum(ce, 0.0)
                + jnp.minimum(ce_b, 0.0)
                - jnp.maximum(cn, 0.0)
                + jnp.minimum(cn_b, 0.0)
            ),
            -wet * jnp.minimum(ce, 0.0),
            wet * jnp.maximum(ce_b, 0.0),
            -wet * jnp.minimum(cn, 0.0),
            wet * jnp.maximum(cn_b, 0.0),
        )

    side_e, side_n = courant(13, 24), courant(14, 25)
    wet = (level < spread(depth_ref, 26)).astype(jnp.float32)
    packed_coef = coefficients(wet, side_e, turn(side_e, SLOTS, 1), side_n, turn(side_n, 1, 1))
    for i in range(5):
        side_coef_ref[i] = packed_coef[i]
    ce_b = courant(0, 0)
    for j in range(rows):
        ce, cn = courant(1 + j, 1 + j), courant(7 + j, 8 + j)
        cn_b = jnp.where(first, turn(side_n, -(SLOTS * (j + 1) + 1), 1), turn(cn, 1, 1))
        wet = (level < spread(depth_ref, 16 + j)).astype(jnp.float32)
        for i, x in enumerate(coefficients(wet, ce, ce_b, cn, cn_b)):
            coef_ref[5 * j + i] = x
        ce_b = ce
    place = lane // SLOTS
    for i in range(side_ref.shape[0]):
        x = side_ref[i]
        v, m = i // SUB, i % SUB
        for odd in range(2):
            start = SLOTS * (2 * m + odd)
            for ref, row in ((side_after_ref, 6), (side_before_ref, 1)):
                to = HALF * odd + SLOTS * row
                x = jnp.where(place == to // SLOTS, turn(ref[v], to - start, 1), x)
        edge_ref[i, 0] = jnp.where(slot == 0, turn(x, -6, 1), x)
        x = (
            (side_coef_ref[0] * x + side_coef_ref[1] * turn(x, -SLOTS, 1))
            + (side_coef_ref[2] * turn(x, SLOTS, 1) + side_coef_ref[3] * turn(x, -1, 1))
            + side_coef_ref[4] * turn(x, 1, 1)
        )
        edge_ref[i, 1] = jnp.where(slot == 0, turn(x, -6, 1), x)

    layer = 2.0 / level_count
    zero = jnp.zeros((SUB, cols), jnp.float32)
    for k in range(0, levels, SUB):
        at = slice(k, k + SUB)

        def stencil(x, j, edge):
            north = jnp.where(last8, edge, turn(x[1], -1, 1))
            south = jnp.where(first8, edge, turn(x[1], 1, 1))
            return (
                (coef_ref[5 * j, at] * x[1] + coef_ref[5 * j + 1, at] * x[2])
                + (coef_ref[5 * j + 2, at] * x[0] + coef_ref[5 * j + 3, at] * north)
                + coef_ref[5 * j + 4, at] * south
            )

        def advect(i, sums):
            edge0, edge1 = edge_ref[i, 0, at], edge_ref[i, 1, at]
            sums = list(sums)
            for odd in range(2):
                t = 2 * i + odd
                x = [before_ref[t, pl.ds(n, SUB, stride=NSUB), :] for n in range(NSUB)]
                x += [
                    q_ref[t, pl.ds(sub_rows * k + r, SUB, stride=sub_rows), :]
                    for r in range(sub_rows)
                ]
                x += [after_ref[t, pl.ds(n, SUB, stride=NSUB), :] for n in range(NSUB)]

                def edge(source, j):
                    return turn(source, -(HALF * odd + SLOTS * (j + 1) + 1), 1)

                x = [stencil(x[j : j + 3], j, edge(edge0, j)) for j in range(rows)]
                x = [stencil(x[j - 1 : j + 2], j, edge(edge1, j)) for j in range(1, rows - 1)]
                for r in range(sub_rows):
                    moved_ref[t, r, at] = x[r]
                    sums[r] = sums[r] + absorb_ref[t] * x[r]
            return tuple(sums)

        sums = lax.fori_loop(0, tracers // 2, advect, (zero,) * sub_rows, unroll=2)
        for r in range(sub_rows):
            optical = layer * (CLEAR_WATER + sums[r])
            above, total = sums_above(optical)
            through = jnp.exp(-(running_ref[r] + above))
            running_ref[r] = running_ref[r] + total
            surface = jnp.broadcast_to(surface_ref[r : r + 1, :], (SUB, cols))
            light_ref[r, at] = surface * through * jnp.exp(-0.5 * optical)
            wet = (level[at] < jnp.broadcast_to(depth_ref[17 + r : 18 + r, :], (SUB, cols))).astype(
                jnp.float32
            )
            heat_ref[0, r, at] = wet * surface * through * (1.0 - jnp.exp(-optical)) / layer
    carry_out_ref[...] = running_ref[...]


def advection(cut, level_count, absorb, surface, depth, received, q, after, before, side, side_after, side_before, carry, heat):
    first_part, count = cut
    tracers, all_rows, cols = q.shape
    every, _, levels, _ = received.shape
    parts = levels // SUB
    sub_rows = surface.shape[0]
    rim = pl.BlockSpec((tracers, SUB * NSUB, cols), lambda i: (0, i, 0))
    by_level = lambda x: pl.BlockSpec((x.shape[0], SUB, cols), lambda i: (0, first_part + i, 0))
    operands = [absorb, surface, depth, received, received, q, after, before, side, side_after, side_before, carry]
    in_specs = [
        smem(),
        whole(surface.shape),
        whole(depth.shape),
        pl.BlockSpec((every, 1, levels, cols), lambda i: (0, 15, 0, 0)),
        pl.BlockSpec(
            (1, ENTRIES, SUB, cols),
            lambda i: ((first_part + i) // parts, 0, (first_part + i) % parts, 0),
        ),
        pl.BlockSpec((tracers, SUB * sub_rows, cols), lambda i: (0, first_part + i, 0)),
        rim,
        rim,
        by_level(side),
        by_level(side_after),
        by_level(side_before),
        whole(carry.shape),
    ]
    aliases = {}
    if heat is not None:
        aliases = {len(operands): 2}
        operands.append(heat)
        in_specs.append(pl.BlockSpec(memory_space=pl.ANY))
    outs = [
        shaped(tracers, sub_rows, count * SUB, cols),
        shaped(sub_rows, count * SUB, cols),
        shaped(every, sub_rows, levels, cols),
        shaped(*carry.shape),
    ]
    return pl.pallas_call(
        functools.partial(advection_kernel, first_part, parts, level_count),
        grid=(count,),
        in_specs=in_specs,
        out_specs=[
            pl.BlockSpec((tracers, sub_rows, SUB, cols), lambda i: (0, 0, i, 0)),
            pl.BlockSpec((sub_rows, SUB, cols), lambda i: (0, i, 0)),
            pl.BlockSpec(
                (1, sub_rows, SUB, cols),
                lambda i: ((first_part + i) // parts, 0, (first_part + i) % parts, 0),
            ),
            whole(carry.shape),
        ],
        out_shape=outs,
        scratch_shapes=[
            pltpu.VMEM((5 * (sub_rows + 2), SUB, cols), jnp.float32),
            pltpu.VMEM((5, SUB, cols), jnp.float32),
            pltpu.VMEM((tracers // 2, 2, SUB, cols), jnp.float32),
            pltpu.VMEM((sub_rows, SUB, cols), jnp.float32),
            pltpu.VMEM((levels, cols), jnp.float32),
        ],
        input_output_aliases=aliases,
        compiler_params=params(),
    )(*operands)


def uptake_kernel(first_level, *refs):
    growth_ref, half_ref, dim_ref, matrix_ref, depth_ref, moved_ref, light_ref = refs[:7]
    result_ref, uptake_ref = refs[-2:]
    tracers, sub_rows, levels, cols = moved_ref.shape
    step = pl.program_id(0)
    matrix = matrix_ref[...]
    matrix_high = matrix.astype(jnp.bfloat16)
    matrix_low = (matrix - matrix_high.astype(jnp.float32)).astype(jnp.bfloat16)
    for k in range(0, levels, SUB):
        at = slice(k, k + SUB)
        level = (first_level + step * levels + k + subs_of((SUB, cols))).astype(jnp.float32)
        light = [light_ref[r, at] for r in range(sub_rows)]
        food = [moved_ref[0, r, at] for r in range(sub_rows)]
        both = [light[r] * food[r] for r in range(sub_rows)]

        def uptake(t, _):
            for r in range(sub_rows):
                scale = (half_ref[t] + food[r]) * (light[r] + dim_ref[t])
                value = growth_ref[t] * moved_ref[t, r, at] * (both[r] / scale)
                uptake_ref[pl.ds(t * SUB, SUB), r * cols : (r + 1) * cols] = value
            return _

        lax.fori_loop(0, tracers, uptake, 0, unroll=4)
        amount = uptake_ref[...]
        high = amount.astype(jnp.bfloat16)
        low = (amount - high.astype(jnp.float32)).astype(jnp.bfloat16)
        dot = functools.partial(jnp.dot, preferred_element_type=jnp.float32)
        change = dot(matrix_high, high) + (dot(matrix_high, low) + dot(matrix_low, high))
        for r in range(sub_rows):
            depth = jnp.broadcast_to(depth_ref[17 + r : 18 + r, :], (SUB, cols))
            scale = DT_BIO * (level < depth).astype(jnp.float32)
            for t in range(tracers):
                result_ref[t, pl.ds(sub_rows * k + r, SUB, stride=sub_rows), :] = (
                    moved_ref[t, r, at]
                    + scale * change[SUB * t : SUB * (t + 1), r * cols : (r + 1) * cols]
                )


def uptake(cut, all_rows, scalars, matrix, depth, moved, light, result):
    first_part, count = cut
    tracers, sub_rows, _, cols = moved.shape
    operands = [*scalars, matrix, depth, moved, light]
    in_specs = [smem()] * 3 + [
        whole(matrix.shape),
        whole(depth.shape),
        pl.BlockSpec((tracers, sub_rows, SUB, cols), lambda i: (0, 0, i, 0)),
        pl.BlockSpec((sub_rows, SUB, cols), lambda i: (0, i, 0)),
    ]
    aliases = {}
    if result is not None:
        aliases = {len(operands): 0}
        operands.append(result)
        in_specs.append(pl.BlockSpec(memory_space=pl.ANY))
    return pl.pallas_call(
        functools.partial(uptake_kernel, first_part * SUB),
        grid=(count,),
        in_specs=in_specs,
        out_specs=pl.BlockSpec((tracers, SUB * sub_rows, cols), lambda i: (0, first_part + i, 0)),
        out_shape=shaped(tracers, all_rows, cols),
        scratch_shapes=[pltpu.VMEM((tracers * SUB, sub_rows * cols), jnp.float32)],
        input_output_aliases=aliases,
        compiler_params=params(),
    )(*operands)


def warming_kernel(sea_ref, floor_ref, base_ref, heat_ref, tmix_ref, smix_ref, warm_ref, buoyant_ref):
    blocks, sub_rows, levels, cols = heat_ref.shape
    tile_rows = blocks * sub_rows
    level = (base_ref[0] + subs_of((levels, cols))).astype(jnp.float32)
    depth = jnp.where(sea_ref[...] == 1, floor_ref[...], 0).astype(jnp.float32)
    for r in range(tile_rows):
        at = pl.ds(r, levels, stride=tile_rows)
        warm = tmix_ref[at, :] + WARMING_FACTOR * heat_ref[r // sub_rows, r % sub_rows]
        wet = (level < depth[r : r + 1]).astype(jnp.float32)
        warm_ref[at, :] = warm
        buoyant_ref[at, :] = wet * (0.2 * warm - 0.8 * smix_ref[at, :])


def warming(base, heat, tmix, smix, sea):
    return call_fetching(
        warming_kernel, sea, [heat, tmix, smix], [shaped(*tmix.shape)] * 2, scalars=[base]
    )


def from_before(x, axis):
    return lax.ppermute(x, axis, [(i, i + 1) for i in range(lax.axis_size(axis) - 1)])


def from_after(x, axis):
    return lax.ppermute(x, axis, [(i + 1, i) for i in range(lax.axis_size(axis) - 1)])


def row_pairs():
    blocks, tiles = lax.axis_size("comp"), lax.axis_size("gx")
    places = [b * tiles + tile for tile in range(tiles) for b in range(blocks)]
    return list(zip(places[:-1], places[1:]))


def from_block_before(x):
    return lax.ppermute(x, ("comp", "gx"), row_pairs())


def from_block_after(x):
    return lax.ppermute(x, ("comp", "gx"), [(later, own) for own, later in row_pairs()])


def from_sides(x):
    if lax.axis_size("gy") == 2:
        other = lax.ppermute(x, "gy", [(0, 1), (1, 0)])
        return other, other
    return from_before(x, "gy"), from_after(x, "gy")


def sided(x):
    return (x, *from_sides(x))


def on_device(
    zonal_flow_speed,
    meridional_flow_speed,
    thermal_anomaly,
    brine_anomaly_values,
    marine_indicator,
    seafloor_layer,
    dissolved_species,
    topmost_sunshine,
    attenuation_coefficient,
    peak_intake_speed,
    feedstock_midpoint_constant,
    photon_midpoint_constant,
    stoichiometry_matrix,
):
    group_index = lax.axis_index("comp")
    blocks = lax.axis_size("comp")
    levels, tile_rows, tile_cols = zonal_flow_speed.shape
    tracer_count, level_count = dissolved_species.shape[:2]
    sub_rows = dissolved_species.shape[4]
    ocean = (zonal_flow_speed, meridional_flow_speed, thermal_anomaly, brine_anomaly_values)
    sea = (marine_indicator, seafloor_layer)
    group = group_index.astype(jnp.int32).reshape(1)
    base = group * levels
    place = jnp.stack([lax.axis_index("gy"), lax.axis_size("gy")]).astype(jnp.int32)

    flat = [x.reshape(levels * tile_rows, tile_cols) for x in ocean]
    q = dissolved_species.reshape(tracer_count, level_count * sub_rows, tile_cols)
    rows_of_q = dissolved_species.reshape(
        tracer_count, level_count, sub_rows // NSUB, NSUB, tile_cols
    )
    parts = levels // SUB
    cuts = [(parts * b, parts) for b in range(blocks - 1)]
    cuts += [(parts * (blocks - 1) + p, 1) for p in range(parts)]

    def rims(cut, *after):
        low, high = cut_rows(rows_of_q, cut[0] * SUB, cut[1] * SUB, after)
        shape = (tracer_count, cut[1] * SUB * NSUB, tile_cols)
        return from_block_after(low).reshape(shape), from_block_before(high).reshape(shape)

    edges = [rims(cuts[0])]
    packed, edge_low, edge_high = pack_ocean(flat, sea, levels)
    up, down, packed = ocean_sides(place, packed, *from_sides(packed), edge_low, edge_high)
    after, before = from_after(up, "gx"), from_before(down, "gx")
    edges.append(rims(cuts[1], packed))
    side, side_low, side_high = tracer_sides(*sided(pack_tracers(q, sub_rows)))
    side_after, side_before = from_block_after(side_low), from_block_before(side_high)
    tmix, smix, send, local, faces, depths = ocean_phase(
        blocks, levels, base, flat, sea, packed, after, before
    )
    received = lax.all_to_all(send, "comp", split_axis=0, concat_axis=0, tiled=True)
    depth = lax.dynamic_index_in_dim(depths, group_index, 0, False)
    edges.append(rims(cuts[2], depths, side_low, *edges[0]))
    east_new, north_new = velocities(group, local, faces, received)

    matrix = (
        stoichiometry_matrix[:, None, :, None] * jnp.eye(SUB, dtype=jnp.float32)[None, :, None, :]
    ).reshape(SUB * tracer_count, SUB * tracer_count)
    surface = topmost_sunshine.reshape(sub_rows, tile_cols)
    scalars = (peak_intake_speed, feedstock_midpoint_constant, photon_midpoint_constant)
    carry = jnp.zeros((sub_rows, SUB, tile_cols), jnp.float32)
    heat, result = None, None
    for i, cut in enumerate(cuts):
        if i >= len(edges):
            edges.append(rims(cut, *held))
        rim_after, rim_before = edges[i]
        moved, light, heat, carry = advection(
            cut,
            level_count,
            attenuation_coefficient,
            surface,
            depth,
            received,
            q,
            rim_after,
            rim_before,
            side,
            side_after,
            side_before,
            carry,
            heat,
        )
        held = (carry,) if i == 0 else held
        result = uptake(
            cut, level_count * sub_rows, scalars, matrix, depth, moved, light, result
        )
    heat = lax.all_to_all(heat, "comp", split_axis=0, concat_axis=0, tiled=True)
    warmed_result, buoyancy = warming(base, heat, tmix, smix, sea)
    fields = (east_new, north_new, warmed_result, smix, buoyancy)
    return (
        *[x.reshape(zonal_flow_speed.shape) for x in fields],
        result.reshape(dissolved_species.shape),
    )


def solution(mesh):
    return jax.shard_map(
        on_device,
        mesh=mesh,
        in_specs=(
            P("comp", "gx", "gy"),
            P("comp", "gx", "gy"),
            P("comp", "gx", "gy"),
            P("comp", "gx", "gy"),
            P("gx", "gy"),
            P("gx", "gy"),
            P(None, None, "gx", "comp", None, "gy"),
            P("gx", "comp", None, "gy"),
            P(),
            P(),
            P(),
            P(),
            P(),
        ),
        out_specs=(
            P("comp", "gx", "gy"),
            P("comp", "gx", "gy"),
            P("comp", "gx", "gy"),
            P("comp", "gx", "gy"),
            P("comp", "gx", "gy"),
            P(None, None, "gx", "comp", None, "gy"),
        ),
        check_vma=False,
    )
```

```python
import functools

import jax
import jax.numpy as jnp
from jax import lax
from jax.experimental import pallas as pl
from jax.experimental.pallas import tpu as pltpu
from jax.sharding import PartitionSpec as P

NSUB = 2
SLOTS = 4 * NSUB
SUB = 8
HALF = 64
ENTRIES = 18

DT_FLOW = 0.1
CORIOLIS = 0.3
MIXING = 0.15
COURANT = 0.24
DT_BIO = 0.5
WARMING_FACTOR = 0.5
CLEAR_WATER = 0.5
VMEM_LIMIT = 16 * 1024 * 1024


def lanes_of(shape):
    return lax.broadcasted_iota(jnp.int32, shape, len(shape) - 1)


def subs_of(shape):
    return lax.broadcasted_iota(jnp.int32, shape, len(shape) - 2)


def turn(x, by, axis):
    by = by % x.shape[axis]
    return x if by == 0 else pltpu.roll(x, by, axis)


def params(**more):
    return pltpu.CompilerParams(vmem_limit_bytes=VMEM_LIMIT, **more)


def whole(shape):
    return pl.BlockSpec(shape, lambda *_: (0,) * len(shape))


def smem():
    return pl.BlockSpec(memory_space=pltpu.SMEM)


def shaped(*shape):
    return jax.ShapeDtypeStruct(shape, jnp.float32)


def sums_above(x):
    sub = subs_of(x.shape)
    running, total = x, x
    by = 1
    while by < x.shape[0]:
        running = running + jnp.where(sub >= by, turn(running, by, 0), 0.0)
        total = total + turn(total, by, 0)
        by *= 2
    return jnp.where(sub >= 1, turn(running, 1, 0), 0.0), total


def cut_kernel(start, size, q_ref, *refs):
    low_ref, high_ref, sems = refs[-3:]
    ends = q_ref.shape[2] - 1
    copies = [
        pltpu.make_async_copy(q_ref.at[:, pl.ds(start, size), at], out_ref, sems.at[i])
        for i, (at, out_ref) in enumerate(((0, low_ref), (ends, high_ref)))
    ]
    for copy in copies:
        copy.start()
    for copy in copies:
        copy.wait()


def cut_rows(q, start, size, after):
    tracers, _, _, _, cols = q.shape
    anywhere = pl.BlockSpec(memory_space=pl.ANY)
    return pl.pallas_call(
        functools.partial(cut_kernel, start, size),
        in_specs=[anywhere] * (1 + len(after)),
        out_specs=[anywhere] * 2,
        out_shape=[shaped(tracers, size, NSUB, cols)] * 2,
        scratch_shapes=[pltpu.SemaphoreType.DMA((2,))],
        compiler_params=params(),
    )(q, *after)


def both_ends(acc):
    return jnp.where(lanes_of(acc.shape) % SLOTS < SLOTS // 2, acc, turn(acc, SLOTS // 2, 1))


def pack_tracers_kernel(sub_rows, group, q_ref, after_ref, before_ref, packed_ref):
    cols = q_ref.shape[2]
    levels = q_ref.shape[1] // sub_rows
    lane = lanes_of((SUB, cols))
    for pair in range(group // 2):
        for k in range(0, levels, SUB):
            acc = jnp.zeros((SUB, cols), jnp.float32)
            for odd in range(2):
                t = 2 * pair + odd
                for r in range(-1, sub_rows + 1):
                    if r < 0:
                        x = before_ref[t, pl.ds(NSUB * k + NSUB + r, SUB, stride=NSUB), :]
                    elif r >= sub_rows:
                        x = after_ref[t, pl.ds(NSUB * k + r - sub_rows, SUB, stride=NSUB), :]
                    else:
                        x = q_ref[t, pl.ds(sub_rows * k + r, SUB, stride=sub_rows), :]
                    at = HALF * odd + SLOTS * (r + NSUB)
                    acc = jnp.where(lane // SLOTS == at // SLOTS, turn(x, at + NSUB, 1), acc)
            packed_ref[pair, k : k + SUB, :] = both_ends(acc)


def pack_tracers(q, rim_after, rim_before, cut, sub_rows, after):
    tracers, _, cols = q.shape
    group = 12
    part, count = cut
    levels = count * SUB
    rim = pl.BlockSpec((group, levels * NSUB, cols), lambda i: (i, 0, 0))
    return pl.pallas_call(
        functools.partial(ignoring, len(after), functools.partial(pack_tracers_kernel, sub_rows, group)),
        grid=(tracers // group,),
        in_specs=[pl.BlockSpec(memory_space=pl.ANY)] * len(after)
        + [pl.BlockSpec((group, levels * sub_rows, cols), lambda i: (i, part // count, 0)), rim, rim],
        out_specs=pl.BlockSpec((group // 2, levels, cols), lambda i: (i, 0, 0)),
        out_shape=shaped(tracers // 2, levels, cols),
        compiler_params=params(),
    )(*after, q, rim_after, rim_before)


def ignoring(count, kernel, *refs):
    kernel(*refs[count:])


def call_once(kernel, operands, outs, scratch=(), scalars=(), after=()):
    return pl.pallas_call(
        functools.partial(ignoring, len(after), kernel),
        grid=(1,),
        in_specs=[pl.BlockSpec(memory_space=pl.ANY)] * len(after)
        + [smem()] * len(scalars)
        + [whole(x.shape) for x in operands],
        out_specs=[whole(x.shape) for x in outs],
        out_shape=outs,
        scratch_shapes=list(scratch),
        compiler_params=params(),
    )(*after, *scalars, *operands)


def pack_ocean_kernel(levels, *refs):
    u_ref, v_ref, t_ref, s_ref, sea_ref, floor_ref, packed_ref, edge_low_ref, edge_high_ref = refs
    tile_rows, cols = sea_ref.shape
    lane = lanes_of((levels, cols))
    edge_low_ref[4 * NSUB] = jnp.zeros((levels, cols), jnp.float32)
    edge_high_ref[4 * NSUB] = jnp.zeros((levels, cols), jnp.float32)
    for f, ref in enumerate((u_ref, v_ref, t_ref, s_ref)):
        acc = jnp.zeros((levels, cols), jnp.float32)
        for r in range(tile_rows):
            x = ref[pl.ds(r, levels, stride=tile_rows), :]
            acc = jnp.where(lane // SLOTS == r, turn(x, SLOTS * r + NSUB, 1), acc)
            if r < NSUB:
                edge_low_ref[NSUB * f + r] = x
            if r >= tile_rows - NSUB:
                edge_high_ref[NSUB * f + r - tile_rows + NSUB] = x
        packed_ref[f] = both_ends(acc)
    depth = jnp.where(sea_ref[...] == 1, floor_ref[...], 0).astype(jnp.float32)
    acc = jnp.zeros((levels, cols), jnp.float32)
    for r in range(tile_rows):
        x = jnp.broadcast_to(depth[r : r + 1], (levels, cols))
        acc = jnp.where(lane // SLOTS == r, turn(x, SLOTS * r + NSUB, 1), acc)
    packed_ref[4] = both_ends(acc)
    edge_low_ref[4 * NSUB, 0:NSUB, :] = depth[0:NSUB]
    edge_high_ref[4 * NSUB, 0:NSUB, :] = depth[tile_rows - NSUB :]


def pack_ocean(flat, sea, levels, after):
    cols = sea[0].shape[1]
    edge = shaped(4 * NSUB + 1, levels, cols)
    return call_once(
        functools.partial(pack_ocean_kernel, levels),
        [*flat, *sea],
        [shaped(5, levels, cols), edge, edge],
        after=after,
    )


def with_sides(own, left, right):
    slot = lanes_of(own.shape) % SLOTS
    ends = jnp.where(slot < NSUB, left, right)
    return jnp.where((slot < NSUB) | (slot >= SLOTS - NSUB), ends, own)


def ocean_sides_kernel(place_ref, own_ref, left_ref, right_ref, low_ref, high_ref, up_ref, down_ref, out_ref):
    _, levels, cols = own_ref.shape
    rows = low_ref.shape[0]
    up_ref[0:rows] = low_ref[...]
    down_ref[0:rows] = high_ref[...]
    slot = lanes_of((levels, cols)) % SLOTS
    first, last = place_ref[0] == 0, place_ref[0] == place_ref[1] - 1
    for f in range(5):
        x = with_sides(own_ref[f], left_ref[f], right_ref[f])
        if f == 4:
            x = jnp.where((slot < NSUB) & first, 0.0, x)
            x = jnp.where((slot >= SLOTS - NSUB) & last, 0.0, x)
        out_ref[f] = x
        up_ref[rows + f] = x
        down_ref[rows + f] = x


def ocean_sides(place, own, left, right, low, high):
    edge = shaped(low.shape[0] + 5, *low.shape[1:])
    return call_once(
        ocean_sides_kernel,
        [own, left, right, low, high],
        [edge, edge, shaped(*own.shape)],
        scalars=[place],
    )


def ocean_kernel(blocks, levels, *refs):
    base_ref, u_ref, v_ref, t_ref, s_ref, sea_ref, floor_ref = refs[:7]
    packed_ref, after_ref, before_ref = refs[7:10]
    tmix_ref, smix_ref, send_ref, local_ref, faces_ref, depths_ref, press_ref, total_ref = refs[10:]
    tile_rows, cols = sea_ref.shape
    sub_rows = tile_rows // blocks
    shape = (levels, cols)
    lane = lanes_of(shape)
    first, last = lane == 0, lane == cols - 1
    level = (base_ref[0] + subs_of(shape)).astype(jnp.float32)
    rims = after_ref.shape[0] - 5
    refs_of = (u_ref, v_ref, t_ref, s_ref)

    def packed(f):
        after, before = after_ref[rims + f], before_ref[rims + f]
        rim = jnp.where(lane < NSUB * SLOTS, after, jnp.where(lane >= cols - NSUB * SLOTS, before, 0.0))
        return jnp.concatenate([packed_ref[f], rim], axis=1)

    def row_after(x):
        return turn(x, -SLOTS, 1)

    def row_before(x):
        return turn(x, SLOTS, 1)

    up, vp, tp, sp, dp = [packed(f) for f in range(5)]
    wide = jnp.concatenate([level, level], axis=1)
    wet = (wide < dp).astype(jnp.float32)
    heavy = wet * (-0.2 * tp + 0.8 * sp)
    above, total = sums_above(heavy)
    press = above + 0.5 * heavy
    east = up + DT_FLOW * (CORIOLIS * vp - (row_after(press) - press))
    north = vp + DT_FLOW * (-CORIOLIS * up - (turn(press, -1, 1) - press))
    open_n = wet * turn(wet, -1, 1)
    flux_t = open_n * (turn(tp, -1, 1) - tp)
    flux_s = open_n * (turn(sp, -1, 1) - sp)
    total_e, total_n = row_after(total) - total, turn(total, -1, 1) - total
    depth_e, depth_n = jnp.minimum(dp, row_after(dp)), jnp.minimum(dp, turn(dp, -1, 1))

    def window(x, g):
        x = turn(x, -SLOTS * (sub_rows * g - NSUB), 1)[:, 0:cols]
        return jnp.where(lane < HALF, x, turn(x, HALF, 1))

    for g in range(blocks):
        send_ref[g, 13] = window(east, g)
        send_ref[g, 14] = window(north, g)
        send_ref[g, 15, 13:14, :] = window(total_e, g)[0:1]
        send_ref[g, 15, 14:15, :] = window(total_n, g)[0:1]
        send_ref[g, 15, 15:16, :] = jnp.zeros((1, cols), jnp.float32)
        depths_ref[g, 24:25, :] = window(depth_e, g)[0:1]
        depths_ref[g, 25:26, :] = window(depth_n, g)[0:1]
        depths_ref[g, 26:27, :] = window(dp, g)[0:1]

    slot = lanes_of(tp.shape) % SLOTS

    def edges(x, other):
        x = jnp.where(slot == 0, turn(x, -6, 1), other)
        return x[:, 0:cols], x[:, cols:]

    edge_p, edge_w = edges(press, press), edges(wet, wet)
    edge_t, edge_s = edges(tp, flux_t), edges(sp, flux_s)
    edge_total, edge_depth = edges(total, total), edges(dp, dp)

    def edge(pair, r):
        at = r % tile_rows
        return turn(pair[0] if 0 <= r < tile_rows else pair[1], -(SLOTS * at + 1), 1)

    depth = jnp.where(sea_ref[...] == 1, floor_ref[...], 0).astype(jnp.float32)

    def row_of(f, r):
        if r < 0:
            return before_ref[NSUB * f + r + NSUB]
        if r >= tile_rows:
            return after_ref[NSUB * f + r - tile_rows]
        return refs_of[f][pl.ds(r, levels, stride=tile_rows), :]

    def depth_of(r):
        if r < 0:
            x = before_ref[4 * NSUB, r + NSUB : r + NSUB + 1, :]
        elif r >= tile_rows:
            x = after_ref[4 * NSUB, r - tile_rows : r - tile_rows + 1, :]
        else:
            x = depth[r : r + 1]
        return jnp.broadcast_to(x, shape)

    lo, hi = -NSUB, tile_rows + NSUB
    for r in range(lo, hi):
        heavy = (level < depth_of(r)).astype(jnp.float32) * (-0.2 * row_of(2, r) + 0.8 * row_of(3, r))
        above, total = sums_above(heavy)
        press_ref[r - lo] = above + 0.5 * heavy
        total_ref[r - lo] = total

    def windows(r, before):
        for g in range(blocks):
            j = r - (sub_rows * g - before)
            if 0 <= j < sub_rows + 1 + before:
                yield g, j

    flux_before = [None, None]
    for r in range(lo, hi - 1):
        press, press_e = press_ref[r - lo], press_ref[r - lo + 1]
        total, total_a = total_ref[r - lo], total_ref[r - lo + 1]
        d, d_e = depth_of(r), depth_of(r + 1)
        d_n = jnp.where(last, edge(edge_depth, r), turn(d, -1, 1))
        face_e, face_n = jnp.minimum(d, d_e), jnp.minimum(d, d_n)
        u, v = row_of(0, r), row_of(1, r)
        east = u + DT_FLOW * (CORIOLIS * v - (press_e - press))
        press_n = jnp.where(last, edge(edge_p, r), turn(press, -1, 1))
        north = v + DT_FLOW * (-CORIOLIS * u - (press_n - press))
        total_e = total_a - total
        total_n = jnp.where(last, edge(edge_total, r), turn(total, -1, 1)) - total
        for g, j in windows(r, 2):
            send_ref[g, j] = east
            send_ref[g, 15, j : j + 1, :] = total_e[0:1]
            depths_ref[g, j : j + 1, :] = face_e[0:1]
        for g, j in windows(r, 1):
            send_ref[g, 7 + j] = north
            send_ref[g, 15, 7 + j : 8 + j, :] = total_n[0:1]
            depths_ref[g, 8 + j : 9 + j, :] = face_n[0:1]
            depths_ref[g, 16 + j : 17 + j, :] = d[0:1]
        if 0 <= r < tile_rows:
            local_ref[0, r] = east
            local_ref[1, r] = north
            faces_ref[0, r : r + 1, :] = face_e[0:1]
            faces_ref[1, r : r + 1, :] = face_n[0:1]
            for g in range(blocks):
                send_ref[g, 16, r : r + 1, :] = total_e[0:1]
                send_ref[g, 17, r : r + 1, :] = total_n[0:1]
        if r < -1 or r >= tile_rows:
            continue
        open_e = (level < face_e).astype(jnp.float32)
        open_n = (level < face_n).astype(jnp.float32)
        for i, (f, ends, out_ref) in enumerate(((2, edge_t, tmix_ref), (3, edge_s, smix_ref))):
            x = row_of(f, r)
            flux_e = open_e * (row_of(f, r + 1) - x)
            if r >= 0:
                ending = edge(ends, r)
                flux_n = open_n * (jnp.where(last, ending, turn(x, -1, 1)) - x)
                flux_b = jnp.where(first, ending, turn(flux_n, 1, 1))
                mixed = x + MIXING * ((flux_e - flux_before[i]) + (flux_n - flux_b))
                out_ref[pl.ds(r, levels, stride=tile_rows), :] = mixed
            flux_before[i] = flux_e


def ocean_phase(blocks, levels, base, flat, sea, packed, rim_after, rim_before, after):
    tile_rows, cols = sea[0].shape
    outs = [
        shaped(levels * tile_rows, cols),
        shaped(levels * tile_rows, cols),
        shaped(blocks, ENTRIES, levels, cols),
        shaped(2, tile_rows, levels, cols),
        shaped(2, tile_rows, cols),
        shaped(blocks, 32, cols),
    ]
    tall = tile_rows + 2 * NSUB
    return call_once(
        functools.partial(ocean_kernel, blocks, levels),
        [*flat, *sea, packed, rim_after, rim_before],
        outs,
        [pltpu.VMEM((tall, levels, cols), jnp.float32)] * 2,
        [base],
        after,
    )


def velocity_kernel(group_ref, local_ref, faces_ref, received_ref, east_ref, north_ref):
    blocks = received_ref.shape[0]
    _, tile_rows, levels, cols = local_ref.shape
    group = group_ref[0]
    level = (group * levels + subs_of((levels, cols))).astype(jnp.float32)
    for f, out_ref in enumerate((east_ref, north_ref)):
        above = jnp.zeros((tile_rows, cols), jnp.float32)
        for s in range(blocks - 1):
            above = above + jnp.where(s < group, received_ref[s, 16 + f], 0.0)
        for r in range(tile_rows):
            x = local_ref[f, r] - DT_FLOW * jnp.broadcast_to(above[r : r + 1], (levels, cols))
            x = jnp.where(level < faces_ref[f, r : r + 1, :], x, 0.0)
            out_ref[pl.ds(r, levels, stride=tile_rows), :] = x


def velocities(group, local, faces, received):
    _, tile_rows, levels, cols = local.shape
    outs = [shaped(levels * tile_rows, cols)] * 2
    return call_once(velocity_kernel, [local, faces, received], outs, scalars=[group])


def advection_kernel(first_part, parts, level_count, *refs):
    (
        absorb_ref,
        surface_ref,
        depth_ref,
        totals_ref,
        courant_ref,
        q_ref,
        after_ref,
        before_ref,
        side_ref,
        left_ref,
        right_ref,
        carry_ref,
    ) = refs[:12]
    moved_ref, light_ref, heat_ref, carry_out_ref = refs[-9:-5]
    coef_ref, side_coef_ref, edge_ref, running_ref, above_ref = refs[-5:]
    step = pl.program_id(0)
    tracers, _, cols = q_ref.shape
    levels = courant_ref.shape[2]
    sub_rows = surface_ref.shape[0]
    rows = sub_rows + 2
    shape = (levels, cols)
    lane = lanes_of(shape)
    first, last = lane == 0, lane == cols - 1
    first8, last8 = first[0:SUB], last[0:SUB]
    slot = lane % SLOTS

    @pl.when(step == 0)
    def _():
        running_ref[...] = carry_ref[...]

    part = first_part + step
    above = jnp.zeros(above_ref.shape, jnp.float32)
    for s in range(totals_ref.shape[0] - 1):
        above = above + jnp.where(s < part // parts, totals_ref[s, 0], 0.0)
    above_ref[...] = above
    level = (part * levels + subs_of(shape)).astype(jnp.float32)

    def spread(ref, r):
        return jnp.broadcast_to(ref[r : r + 1, :], shape)

    def courant(entry, face):
        x = courant_ref[0, entry] - DT_FLOW * spread(above_ref, entry)
        return COURANT * jnp.tanh(jnp.where(level < spread(depth_ref, face), x, 0.0))

    def coefficients(wet, ce, ce_b, cn, cn_b):
        return (
            wet
            * (
                1.0
                - jnp.maximum(ce, 0.0)
                + jnp.minimum(ce_b, 0.0)
                - jnp.maximum(cn, 0.0)
                + jnp.minimum(cn_b, 0.0)
            ),
            -wet * jnp.minimum(ce, 0.0),
            wet * jnp.maximum(ce_b, 0.0),
            -wet * jnp.minimum(cn, 0.0),
            wet * jnp.maximum(cn_b, 0.0),
        )

    side_e, side_n = courant(13, 24), courant(14, 25)
    wet = (level < spread(depth_ref, 26)).astype(jnp.float32)
    packed_coef = coefficients(wet, side_e, turn(side_e, SLOTS, 1), side_n, turn(side_n, 1, 1))
    for i in range(5):
        side_coef_ref[i] = packed_coef[i]
    ce_b = courant(0, 0)
    for j in range(rows):
        ce, cn = courant(1 + j, 1 + j), courant(7 + j, 8 + j)
        cn_b = jnp.where(first, turn(side_n, -(SLOTS * (j + 1) + 1), 1), turn(cn, 1, 1))
        wet = (level < spread(depth_ref, 16 + j)).astype(jnp.float32)
        for i, x in enumerate(coefficients(wet, ce, ce_b, cn, cn_b)):
            coef_ref[5 * j + i] = x
        ce_b = ce
    for i in range(side_ref.shape[0]):
        x = with_sides(side_ref[i], left_ref[i], right_ref[i])
        edge_ref[i, 0] = jnp.where(slot == 0, turn(x, -6, 1), x)
        x = (
            (side_coef_ref[0] * x + side_coef_ref[1] * turn(x, -SLOTS, 1))
            + (side_coef_ref[2] * turn(x, SLOTS, 1) + side_coef_ref[3] * turn(x, -1, 1))
            + side_coef_ref[4] * turn(x, 1, 1)
        )
        edge_ref[i, 1] = jnp.where(slot == 0, turn(x, -6, 1), x)

    layer = 2.0 / level_count
    zero = jnp.zeros((SUB, cols), jnp.float32)
    for k in range(0, levels, SUB):
        at = slice(k, k + SUB)

        def stencil(x, j, edge):
            north = jnp.where(last8, edge, turn(x[1], -1, 1))
            south = jnp.where(first8, edge, turn(x[1], 1, 1))
            return (
                (coef_ref[5 * j, at] * x[1] + coef_ref[5 * j + 1, at] * x[2])
                + (coef_ref[5 * j + 2, at] * x[0] + coef_ref[5 * j + 3, at] * north)
                + coef_ref[5 * j + 4, at] * south
            )

        def advect(i, sums):
            edge0, edge1 = edge_ref[i, 0, at], edge_ref[i, 1, at]
            sums = list(sums)
            for odd in range(2):
                t = 2 * i + odd
                x = [before_ref[t, pl.ds(n, SUB, stride=NSUB), :] for n in range(NSUB)]
                x += [
                    q_ref[t, pl.ds(sub_rows * k + r, SUB, stride=sub_rows), :]
                    for r in range(sub_rows)
                ]
                x += [after_ref[t, pl.ds(n, SUB, stride=NSUB), :] for n in range(NSUB)]

                def edge(source, j):
                    return turn(source, -(HALF * odd + SLOTS * (j + 1) + 1), 1)

                x = [stencil(x[j : j + 3], j, edge(edge0, j)) for j in range(rows)]
                x = [stencil(x[j - 1 : j + 2], j, edge(edge1, j)) for j in range(1, rows - 1)]
                for r in range(sub_rows):
                    moved_ref[t, r, at] = x[r]
                    sums[r] = sums[r] + absorb_ref[t] * x[r]
            return tuple(sums)

        sums = lax.fori_loop(0, tracers // 2, advect, (zero,) * sub_rows, unroll=2)
        for r in range(sub_rows):
            optical = layer * (CLEAR_WATER + sums[r])
            above, total = sums_above(optical)
            through = jnp.exp(-(running_ref[r] + above))
            running_ref[r] = running_ref[r] + total
            surface = jnp.broadcast_to(surface_ref[r : r + 1, :], (SUB, cols))
            light_ref[r, at] = surface * through * jnp.exp(-0.5 * optical)
            wet = (level[at] < jnp.broadcast_to(depth_ref[17 + r : 18 + r, :], (SUB, cols))).astype(
                jnp.float32
            )
            heat_ref[0, r, at] = wet * surface * through * (1.0 - jnp.exp(-optical)) / layer
    carry_out_ref[...] = running_ref[...]


def advection(cut, level_count, absorb, surface, depth, received, q, rim_after, rim_before, sides, carry, heat, after):
    first_part, count = cut
    tracers, all_rows, cols = q.shape
    every, _, levels, _ = received.shape
    parts = levels // SUB
    sub_rows = surface.shape[0]
    rim = pl.BlockSpec((tracers, SUB * NSUB, cols), lambda i: (0, i, 0))
    side = pl.BlockSpec((tracers // 2, SUB, cols), lambda i: (0, i, 0))
    operands = [absorb, surface, depth, received, received, q, rim_after, rim_before, *sides, carry]
    in_specs = [
        smem(),
        whole(surface.shape),
        whole(depth.shape),
        pl.BlockSpec((every, 1, levels, cols), lambda i: (0, 15, 0, 0)),
        pl.BlockSpec(
            (1, ENTRIES, SUB, cols),
            lambda i: ((first_part + i) // parts, 0, (first_part + i) % parts, 0),
        ),
        pl.BlockSpec((tracers, SUB * sub_rows, cols), lambda i: (0, first_part + i, 0)),
        rim,
        rim,
        side,
        side,
        side,
        whole(carry.shape),
    ]
    aliases = {}
    if heat is not None:
        aliases = {len(operands): 2}
        operands.append(heat)
    operands += after
    in_specs += [pl.BlockSpec(memory_space=pl.ANY)] * (len(operands) - len(in_specs))
    outs = [
        shaped(tracers, sub_rows, count * SUB, cols),
        shaped(sub_rows, count * SUB, cols),
        shaped(every, sub_rows, levels, cols),
        shaped(*carry.shape),
    ]
    return pl.pallas_call(
        functools.partial(advection_kernel, first_part, parts, level_count),
        grid=(count,),
        in_specs=in_specs,
        out_specs=[
            pl.BlockSpec((tracers, sub_rows, SUB, cols), lambda i: (0, 0, i, 0)),
            pl.BlockSpec((sub_rows, SUB, cols), lambda i: (0, i, 0)),
            pl.BlockSpec(
                (1, sub_rows, SUB, cols),
                lambda i: ((first_part + i) // parts, 0, (first_part + i) % parts, 0),
            ),
            whole(carry.shape),
        ],
        out_shape=outs,
        scratch_shapes=[
            pltpu.VMEM((5 * (sub_rows + 2), SUB, cols), jnp.float32),
            pltpu.VMEM((5, SUB, cols), jnp.float32),
            pltpu.VMEM((tracers // 2, 2, SUB, cols), jnp.float32),
            pltpu.VMEM((sub_rows, SUB, cols), jnp.float32),
            pltpu.VMEM((levels, cols), jnp.float32),
        ],
        input_output_aliases=aliases,
        compiler_params=params(),
    )(*operands)


def uptake_kernel(first_level, *refs):
    growth_ref, half_ref, dim_ref, matrix_ref, depth_ref, moved_ref, light_ref = refs[:7]
    result_ref, token_ref, uptake_ref = refs[-3:]
    token_ref[...] = jnp.zeros_like(token_ref)
    tracers, sub_rows, levels, cols = moved_ref.shape
    step = pl.program_id(0)
    size = tracers * SUB
    tall = (subs_of((size, tracers)) // SUB == lanes_of((size, tracers))).astype(jnp.float32)
    wide = (lanes_of((tracers, size)) // SUB == subs_of((tracers, size))).astype(jnp.float32)
    exact = functools.partial(
        jnp.dot, precision=lax.Precision.HIGHEST, preferred_element_type=jnp.float32
    )
    same = subs_of((size, size)) % SUB == lanes_of((size, size)) % SUB
    matrix = jnp.where(same, exact(exact(tall, matrix_ref[...]), wide), 0.0)
    matrix_high = matrix.astype(jnp.bfloat16)
    matrix_low = (matrix - matrix_high.astype(jnp.float32)).astype(jnp.bfloat16)
    for k in range(0, levels, SUB):
        at = slice(k, k + SUB)
        level = (first_level + step * levels + k + subs_of((SUB, cols))).astype(jnp.float32)
        light = [light_ref[r, at] for r in range(sub_rows)]
        food = [moved_ref[0, r, at] for r in range(sub_rows)]
        both = [light[r] * food[r] for r in range(sub_rows)]

        def uptake(t, _):
            for r in range(sub_rows):
                scale = (half_ref[t] + food[r]) * (light[r] + dim_ref[t])
                value = growth_ref[t] * moved_ref[t, r, at] * (both[r] / scale)
                uptake_ref[pl.ds(t * SUB, SUB), r * cols : (r + 1) * cols] = value
            return _

        lax.fori_loop(0, tracers, uptake, 0, unroll=4)
        amount = uptake_ref[...]
        high = amount.astype(jnp.bfloat16)
        low = (amount - high.astype(jnp.float32)).astype(jnp.bfloat16)
        dot = functools.partial(jnp.dot, preferred_element_type=jnp.float32)
        change = dot(matrix_high, high) + (dot(matrix_high, low) + dot(matrix_low, high))
        for r in range(sub_rows):
            depth = jnp.broadcast_to(depth_ref[17 + r : 18 + r, :], (SUB, cols))
            scale = DT_BIO * (level < depth).astype(jnp.float32)
            for t in range(tracers):
                result_ref[t, pl.ds(sub_rows * k + r, SUB, stride=sub_rows), :] = (
                    moved_ref[t, r, at]
                    + scale * change[SUB * t : SUB * (t + 1), r * cols : (r + 1) * cols]
                )


def uptake(cut, all_rows, scalars, matrix, depth, moved, light, result):
    first_part, count = cut
    tracers, sub_rows, _, cols = moved.shape
    operands = [*scalars, matrix, depth, moved, light]
    in_specs = [smem()] * 3 + [
        whole(matrix.shape),
        whole(depth.shape),
        pl.BlockSpec((tracers, sub_rows, SUB, cols), lambda i: (0, 0, i, 0)),
        pl.BlockSpec((sub_rows, SUB, cols), lambda i: (0, i, 0)),
    ]
    aliases = {}
    if result is not None:
        aliases = {len(operands): 0}
        operands.append(result)
        in_specs.append(pl.BlockSpec(memory_space=pl.ANY))
    return pl.pallas_call(
        functools.partial(uptake_kernel, first_part * SUB),
        grid=(count,),
        in_specs=in_specs,
        out_specs=[
            pl.BlockSpec((tracers, SUB * sub_rows, cols), lambda i: (0, first_part + i, 0)),
            whole((SUB, cols)),
        ],
        out_shape=[shaped(tracers, all_rows, cols), shaped(SUB, cols)],
        scratch_shapes=[pltpu.VMEM((tracers * SUB, sub_rows * cols), jnp.float32)],
        input_output_aliases=aliases,
        compiler_params=params(),
    )(*operands)


def warming_kernel(base_ref, sea_ref, floor_ref, heat_ref, tmix_ref, smix_ref, warm_ref, buoyant_ref):
    blocks, sub_rows, levels, cols = heat_ref.shape
    tile_rows = blocks * sub_rows
    level = (base_ref[0] + subs_of((levels, cols))).astype(jnp.float32)
    depth = jnp.where(sea_ref[...] == 1, floor_ref[...], 0).astype(jnp.float32)
    for r in range(tile_rows):
        at = pl.ds(r, levels, stride=tile_rows)
        warm = tmix_ref[at, :] + WARMING_FACTOR * heat_ref[r // sub_rows, r % sub_rows]
        wet = (level < depth[r : r + 1]).astype(jnp.float32)
        warm_ref[at, :] = warm
        buoyant_ref[at, :] = wet * (0.2 * warm - 0.8 * smix_ref[at, :])


def warming(base, heat, tmix, smix, sea):
    outs = [shaped(*tmix.shape)] * 2
    return call_once(warming_kernel, [*sea, heat, tmix, smix], outs, scalars=[base])


def from_before(x, axis):
    return lax.ppermute(x, axis, [(i, i + 1) for i in range(lax.axis_size(axis) - 1)])


def from_after(x, axis):
    return lax.ppermute(x, axis, [(i + 1, i) for i in range(lax.axis_size(axis) - 1)])


def row_pairs():
    blocks, tiles = lax.axis_size("comp"), lax.axis_size("gx")
    places = [b * tiles + tile for tile in range(tiles) for b in range(blocks)]
    return list(zip(places[:-1], places[1:]))


def from_block_before(x):
    return lax.ppermute(x, ("comp", "gx"), row_pairs())


def from_block_after(x):
    return lax.ppermute(x, ("comp", "gx"), [(later, own) for own, later in row_pairs()])


def from_sides(x):
    if lax.axis_size("gy") == 2:
        other = lax.ppermute(x, "gy", [(0, 1), (1, 0)])
        return other, other
    return from_before(x, "gy"), from_after(x, "gy")


def on_device(
    zonal_flow_speed,
    meridional_flow_speed,
    thermal_anomaly,
    brine_anomaly_values,
    marine_indicator,
    seafloor_layer,
    dissolved_species,
    topmost_sunshine,
    attenuation_coefficient,
    peak_intake_speed,
    feedstock_midpoint_constant,
    photon_midpoint_constant,
    stoichiometry_matrix,
):
    group_index = lax.axis_index("comp")
    blocks = lax.axis_size("comp")
    levels, tile_rows, tile_cols = zonal_flow_speed.shape
    tracer_count, level_count = dissolved_species.shape[:2]
    sub_rows = dissolved_species.shape[4]
    ocean = (zonal_flow_speed, meridional_flow_speed, thermal_anomaly, brine_anomaly_values)
    sea = (marine_indicator, seafloor_layer)
    group = group_index.astype(jnp.int32).reshape(1)
    base = group * levels
    place = jnp.stack([lax.axis_index("gy"), lax.axis_size("gy")]).astype(jnp.int32)

    flat = [x.reshape(levels * tile_rows, tile_cols) for x in ocean]
    q = dissolved_species.reshape(tracer_count, level_count * sub_rows, tile_cols)
    rows_of_q = dissolved_species.reshape(
        tracer_count, level_count, sub_rows // NSUB, NSUB, tile_cols
    )
    parts = levels // SUB
    cuts = [(parts * b, parts) for b in range(blocks)]
    scalars_of_uptake = (
        peak_intake_speed,
        feedstock_midpoint_constant,
        photon_midpoint_constant,
    )

    def rims(cut, *after):
        low, high = cut_rows(rows_of_q, cut[0] * SUB, cut[1] * SUB, after)
        shape = (tracer_count, cut[1] * SUB * NSUB, tile_cols)
        moved = from_block_after(low).reshape(shape), from_block_before(high).reshape(shape)
        return (low, high), moved

    def sides(x):
        return (x, *from_sides(x))

    cut0, rims0 = rims(cuts[0])
    packed, edge_low, edge_high = pack_ocean(flat, sea, levels, cut0)
    up, down, packed = ocean_sides(place, packed, *from_sides(packed), edge_low, edge_high)
    after, before = from_after(up, "gx"), from_before(down, "gx")
    cut1, rims1 = rims(cuts[1], up)
    tmix, smix, send, local, faces, depths = ocean_phase(
        blocks, levels, base, flat, sea, packed, after, before, cut1
    )
    received = lax.all_to_all(send, "comp", split_axis=0, concat_axis=0, tiled=True)
    depth = lax.dynamic_index_in_dim(depths, group_index, 0, False)
    east_new, north_new = velocities(group, local, faces, received)
    ahead = [(cut0, rims0), (cut1, rims1), rims(cuts[2], depths)]

    surface = topmost_sunshine.reshape(sub_rows, tile_cols)
    carry = jnp.zeros((sub_rows, SUB, tile_cols), jnp.float32)
    heat, result = None, None
    for i, cut in enumerate(cuts):
        waits = list(ahead[i + 2][0]) if i + 2 < len(cuts) else []
        if i == len(cuts) - 1:
            waits.append(token)
        near = sides(pack_tracers(q, *ahead[i][1], cut, sub_rows, waits))
        moved, light, heat, carry = advection(
            cut,
            level_count,
            attenuation_coefficient,
            surface,
            depth,
            received,
            q,
            *ahead[i][1],
            near,
            carry,
            heat,
            [],
        )
        if i + 3 < len(cuts):
            ahead.append(rims(cuts[i + 3], carry))
        result, token = uptake(
            cut,
            level_count * sub_rows,
            scalars_of_uptake,
            stoichiometry_matrix,
            depth,
            moved,
            light,
            result,
        )
    heat = lax.all_to_all(heat, "comp", split_axis=0, concat_axis=0, tiled=True)
    warmed_result, buoyancy = warming(base, heat, tmix, smix, sea)
    fields = (east_new, north_new, warmed_result, smix, buoyancy)
    return (
        *[x.reshape(zonal_flow_speed.shape) for x in fields],
        result.reshape(dissolved_species.shape),
    )


def solution(mesh):
    return jax.shard_map(
        on_device,
        mesh=mesh,
        in_specs=(
            P("comp", "gx", "gy"),
            P("comp", "gx", "gy"),
            P("comp", "gx", "gy"),
            P("comp", "gx", "gy"),
            P("gx", "gy"),
            P("gx", "gy"),
            P(None, None, "gx", "comp", None, "gy"),
            P("gx", "comp", None, "gy"),
            P(),
            P(),
            P(),
            P(),
            P(),
        ),
        out_specs=(
            P("comp", "gx", "gy"),
            P("comp", "gx", "gy"),
            P("comp", "gx", "gy"),
            P("comp", "gx", "gy"),
            P("comp", "gx", "gy"),
            P(None, None, "gx", "comp", None, "gy"),
        ),
        check_vma=False,
    )
```

```python
import functools

import jax
import jax.numpy as jnp
from jax import lax
from jax.experimental import pallas as pl
from jax.experimental.pallas import tpu as pltpu
from jax.sharding import PartitionSpec as P

NSUB = 2
SLOTS = 4 * NSUB
SUB = 8
GROUP = 6
HALF = 64
ENTRIES = 18

DT_FLOW = 0.1
CORIOLIS = 0.3
MIXING = 0.15
COURANT = 0.24
DT_BIO = 0.5
WARMING_FACTOR = 0.5
CLEAR_WATER = 0.5
VMEM_LIMIT = 16 * 1024 * 1024
VMEM_MOST = 62 * 1024 * 1024


def lanes_of(shape):
    return lax.broadcasted_iota(jnp.int32, shape, len(shape) - 1)


def subs_of(shape):
    return lax.broadcasted_iota(jnp.int32, shape, len(shape) - 2)


def turn(x, by, axis):
    by = by % x.shape[axis]
    return x if by == 0 else pltpu.roll(x, by, axis)


def params(limit=VMEM_LIMIT):
    return pltpu.CompilerParams(vmem_limit_bytes=limit)


def whole(shape):
    return pl.BlockSpec(shape, lambda *_: (0,) * len(shape))


def smem():
    return pl.BlockSpec(memory_space=pltpu.SMEM)


def shaped(*shape):
    return jax.ShapeDtypeStruct(shape, jnp.float32)


def halves(x):
    high = x.astype(jnp.bfloat16)
    return high, (x - high.astype(jnp.float32)).astype(jnp.bfloat16)


def sums_above(x):
    sub = subs_of(x.shape)
    running, total = x, x
    by = 1
    while by < x.shape[0]:
        running = running + jnp.where(sub >= by, turn(running, by, 0), 0.0)
        total = total + turn(total, by, 0)
        by *= 2
    return jnp.where(sub >= 1, turn(running, 1, 0), 0.0), total


def cut_kernel(start, size, q_ref, *refs):
    low_ref, high_ref, sems = refs[-3:]
    ends = q_ref.shape[2] - 1
    copies = [
        pltpu.make_async_copy(q_ref.at[:, pl.ds(start, size), at], out_ref, sems.at[i])
        for i, (at, out_ref) in enumerate(((0, low_ref), (ends, high_ref)))
    ]
    for copy in copies:
        copy.start()
    for copy in copies:
        copy.wait()


def cut_rows(q, start, size, after):
    tracers, _, _, _, cols = q.shape
    anywhere = pl.BlockSpec(memory_space=pl.ANY)
    return pl.pallas_call(
        functools.partial(cut_kernel, start, size),
        in_specs=[anywhere] * (1 + len(after)),
        out_specs=[anywhere] * 2,
        out_shape=[shaped(tracers, size, NSUB, cols)] * 2,
        scratch_shapes=[pltpu.SemaphoreType.DMA((2,))],
        compiler_params=params(VMEM_MOST),
    )(q, *after)


def both_ends(acc):
    return jnp.where(lanes_of(acc.shape) % SLOTS < SLOTS // 2, acc, turn(acc, SLOTS // 2, 1))


def pack_tracers_kernel(sub_rows, group, q_ref, after_ref, before_ref, packed_ref):
    cols = q_ref.shape[2]
    levels = q_ref.shape[1] // sub_rows
    lane = lanes_of((SUB, cols))
    for pair in range(group // 2):
        for k in range(0, levels, SUB):
            acc = jnp.zeros((SUB, cols), jnp.float32)
            for odd in range(2):
                t = 2 * pair + odd
                for r in range(-1, sub_rows + 1):
                    if r < 0:
                        x = before_ref[t, pl.ds(NSUB * k + NSUB + r, SUB, stride=NSUB), :]
                    elif r >= sub_rows:
                        x = after_ref[t, pl.ds(NSUB * k + r - sub_rows, SUB, stride=NSUB), :]
                    else:
                        x = q_ref[t, pl.ds(sub_rows * k + r, SUB, stride=sub_rows), :]
                    at = HALF * odd + SLOTS * (r + NSUB)
                    acc = jnp.where(lane // SLOTS == at // SLOTS, turn(x, at + NSUB, 1), acc)
            packed_ref[pair, k : k + SUB, :] = both_ends(acc)


def pack_tracers(q, rim_after, rim_before, cut, sub_rows, after):
    tracers, _, cols = q.shape
    part, count = cut
    rim = pl.BlockSpec((tracers, SUB * NSUB, cols), lambda i: (0, i, 0))
    return pl.pallas_call(
        functools.partial(ignoring, len(after), functools.partial(pack_tracers_kernel, sub_rows, tracers)),
        grid=(count,),
        in_specs=[pl.BlockSpec(memory_space=pl.ANY)] * len(after)
        + [pl.BlockSpec((tracers, SUB * sub_rows, cols), lambda i: (0, part + i, 0)), rim, rim],
        out_specs=pl.BlockSpec((tracers // 2, SUB, cols), lambda i: (0, i, 0)),
        out_shape=shaped(tracers // 2, count * SUB, cols),
        compiler_params=params(),
    )(*after, q, rim_after, rim_before)


def ignoring(count, kernel, *refs):
    kernel(*refs[count:])


def call_once(kernel, operands, outs, scratch=(), scalars=(), after=(), limit=VMEM_LIMIT):
    return pl.pallas_call(
        functools.partial(ignoring, len(after), kernel),
        grid=(1,),
        in_specs=[pl.BlockSpec(memory_space=pl.ANY)] * len(after)
        + [smem()] * len(scalars)
        + [whole(x.shape) for x in operands],
        out_specs=[whole(x.shape) for x in outs],
        out_shape=outs,
        scratch_shapes=list(scratch),
        compiler_params=params(limit),
    )(*after, *scalars, *operands)


def pack_ocean_kernel(levels, *refs):
    u_ref, v_ref, t_ref, s_ref, sea_ref, floor_ref, packed_ref, edge_low_ref, edge_high_ref = refs
    tile_rows, cols = sea_ref.shape
    lane = lanes_of((levels, cols))
    edge_low_ref[4 * NSUB] = jnp.zeros((levels, cols), jnp.float32)
    edge_high_ref[4 * NSUB] = jnp.zeros((levels, cols), jnp.float32)
    for f, ref in enumerate((u_ref, v_ref, t_ref, s_ref)):
        acc = jnp.zeros((levels, cols), jnp.float32)
        for r in range(tile_rows):
            x = ref[pl.ds(r, levels, stride=tile_rows), :]
            acc = jnp.where(lane // SLOTS == r, turn(x, SLOTS * r + NSUB, 1), acc)
            if r < NSUB:
                edge_low_ref[NSUB * f + r] = x
            if r >= tile_rows - NSUB:
                edge_high_ref[NSUB * f + r - tile_rows + NSUB] = x
        packed_ref[f] = both_ends(acc)
    depth = jnp.where(sea_ref[...] == 1, floor_ref[...], 0).astype(jnp.float32)
    acc = jnp.zeros((levels, cols), jnp.float32)
    for r in range(tile_rows):
        x = jnp.broadcast_to(depth[r : r + 1], (levels, cols))
        acc = jnp.where(lane // SLOTS == r, turn(x, SLOTS * r + NSUB, 1), acc)
    packed_ref[4] = both_ends(acc)
    edge_low_ref[4 * NSUB, 0:NSUB, :] = depth[0:NSUB]
    edge_high_ref[4 * NSUB, 0:NSUB, :] = depth[tile_rows - NSUB :]


def pack_ocean(flat, sea, levels, after):
    cols = sea[0].shape[1]
    edge = shaped(4 * NSUB + 1, levels, cols)
    return call_once(
        functools.partial(pack_ocean_kernel, levels),
        [*flat, *sea],
        [shaped(5, levels, cols), edge, edge],
        after=after,
        limit=VMEM_MOST,
    )


def with_sides(own, left, right):
    slot = lanes_of(own.shape) % SLOTS
    ends = jnp.where(slot < NSUB, left, right)
    return jnp.where((slot < NSUB) | (slot >= SLOTS - NSUB), ends, own)


def ocean_sides_kernel(place_ref, own_ref, left_ref, right_ref, low_ref, high_ref, up_ref, down_ref, out_ref):
    _, levels, cols = own_ref.shape
    rows = low_ref.shape[0]
    up_ref[0:rows] = low_ref[...]
    down_ref[0:rows] = high_ref[...]
    slot = lanes_of((levels, cols)) % SLOTS
    first, last = place_ref[0] == 0, place_ref[0] == place_ref[1] - 1
    for f in range(5):
        x = with_sides(own_ref[f], left_ref[f], right_ref[f])
        if f == 4:
            x = jnp.where((slot < NSUB) & first, 0.0, x)
            x = jnp.where((slot >= SLOTS - NSUB) & last, 0.0, x)
        out_ref[f] = x
        up_ref[rows + f] = x
        down_ref[rows + f] = x


def ocean_sides(place, own, left, right, low, high):
    edge = shaped(low.shape[0] + 5, *low.shape[1:])
    return call_once(
        ocean_sides_kernel,
        [own, left, right, low, high],
        [edge, edge, shaped(*own.shape)],
        scalars=[place],
        limit=VMEM_MOST,
    )


def ocean_kernel(blocks, levels, *refs):
    base_ref, u_ref, v_ref, t_ref, s_ref, sea_ref, floor_ref = refs[:7]
    packed_ref, after_ref, before_ref = refs[7:10]
    tmix_ref, smix_ref, send_ref, local_ref, faces_ref, depths_ref, press_ref, total_ref = refs[10:]
    tile_rows, cols = sea_ref.shape
    sub_rows = tile_rows // blocks
    shape = (levels, cols)
    lane = lanes_of(shape)
    first, last = lane == 0, lane == cols - 1
    level = (base_ref[0] + subs_of(shape)).astype(jnp.float32)
    rims = after_ref.shape[0] - 5
    refs_of = (u_ref, v_ref, t_ref, s_ref)

    def packed(f):
        after, before = after_ref[rims + f], before_ref[rims + f]
        rim = jnp.where(lane < NSUB * SLOTS, after, jnp.where(lane >= cols - NSUB * SLOTS, before, 0.0))
        return jnp.concatenate([packed_ref[f], rim], axis=1)

    def row_after(x):
        return turn(x, -SLOTS, 1)

    def row_before(x):
        return turn(x, SLOTS, 1)

    up, vp, tp, sp, dp = [packed(f) for f in range(5)]
    wide = jnp.concatenate([level, level], axis=1)
    wet = (wide < dp).astype(jnp.float32)
    heavy = wet * (-0.2 * tp + 0.8 * sp)
    above, total = sums_above(heavy)
    press = above + 0.5 * heavy
    east = up + DT_FLOW * (CORIOLIS * vp - (row_after(press) - press))
    north = vp + DT_FLOW * (-CORIOLIS * up - (turn(press, -1, 1) - press))
    open_n = wet * turn(wet, -1, 1)
    flux_t = open_n * (turn(tp, -1, 1) - tp)
    flux_s = open_n * (turn(sp, -1, 1) - sp)
    total_e, total_n = row_after(total) - total, turn(total, -1, 1) - total
    depth_e, depth_n = jnp.minimum(dp, row_after(dp)), jnp.minimum(dp, turn(dp, -1, 1))

    def window(x, g):
        x = turn(x, -SLOTS * (sub_rows * g - NSUB), 1)[:, 0:cols]
        return jnp.where(lane < HALF, x, turn(x, HALF, 1))

    for g in range(blocks):
        send_ref[g, 13] = window(east, g)
        send_ref[g, 14] = window(north, g)
        send_ref[g, 15, 13:14, :] = window(total_e, g)[0:1]
        send_ref[g, 15, 14:15, :] = window(total_n, g)[0:1]
        send_ref[g, 15, 15:16, :] = jnp.zeros((1, cols), jnp.float32)
        depths_ref[g, 24:25, :] = window(depth_e, g)[0:1]
        depths_ref[g, 25:26, :] = window(depth_n, g)[0:1]
        depths_ref[g, 26:27, :] = window(dp, g)[0:1]

    slot = lanes_of(tp.shape) % SLOTS

    def edges(x, other):
        x = jnp.where(slot == 0, turn(x, -6, 1), other)
        return x[:, 0:cols], x[:, cols:]

    edge_p, edge_w = edges(press, press), edges(wet, wet)
    edge_t, edge_s = edges(tp, flux_t), edges(sp, flux_s)
    edge_total, edge_depth = edges(total, total), edges(dp, dp)

    def edge(pair, r):
        at = r % tile_rows
        return turn(pair[0] if 0 <= r < tile_rows else pair[1], -(SLOTS * at + 1), 1)

    depth = jnp.where(sea_ref[...] == 1, floor_ref[...], 0).astype(jnp.float32)

    def row_of(f, r):
        if r < 0:
            return before_ref[NSUB * f + r + NSUB]
        if r >= tile_rows:
            return after_ref[NSUB * f + r - tile_rows]
        return refs_of[f][pl.ds(r, levels, stride=tile_rows), :]

    def depth_of(r):
        if r < 0:
            x = before_ref[4 * NSUB, r + NSUB : r + NSUB + 1, :]
        elif r >= tile_rows:
            x = after_ref[4 * NSUB, r - tile_rows : r - tile_rows + 1, :]
        else:
            x = depth[r : r + 1]
        return jnp.broadcast_to(x, shape)

    lo, hi = -NSUB, tile_rows + NSUB
    for r in range(lo, hi):
        heavy = (level < depth_of(r)).astype(jnp.float32) * (-0.2 * row_of(2, r) + 0.8 * row_of(3, r))
        above, total = sums_above(heavy)
        press_ref[r - lo] = above + 0.5 * heavy
        total_ref[r - lo] = total

    def windows(r, before):
        for g in range(blocks):
            j = r - (sub_rows * g - before)
            if 0 <= j < sub_rows + 1 + before:
                yield g, j

    flux_before = [None, None]
    for r in range(lo, hi - 1):
        press, press_e = press_ref[r - lo], press_ref[r - lo + 1]
        total, total_a = total_ref[r - lo], total_ref[r - lo + 1]
        d, d_e = depth_of(r), depth_of(r + 1)
        d_n = jnp.where(last, edge(edge_depth, r), turn(d, -1, 1))
        face_e, face_n = jnp.minimum(d, d_e), jnp.minimum(d, d_n)
        u, v = row_of(0, r), row_of(1, r)
        east = u + DT_FLOW * (CORIOLIS * v - (press_e - press))
        press_n = jnp.where(last, edge(edge_p, r), turn(press, -1, 1))
        north = v + DT_FLOW * (-CORIOLIS * u - (press_n - press))
        total_e = total_a - total
        total_n = jnp.where(last, edge(edge_total, r), turn(total, -1, 1)) - total
        for g, j in windows(r, 2):
            send_ref[g, j] = east
            send_ref[g, 15, j : j + 1, :] = total_e[0:1]
            depths_ref[g, j : j + 1, :] = face_e[0:1]
        for g, j in windows(r, 1):
            send_ref[g, 7 + j] = north
            send_ref[g, 15, 7 + j : 8 + j, :] = total_n[0:1]
            depths_ref[g, 8 + j : 9 + j, :] = face_n[0:1]
            depths_ref[g, 16 + j : 17 + j, :] = d[0:1]
        if 0 <= r < tile_rows:
            local_ref[0, r] = east
            local_ref[1, r] = north
            faces_ref[0, r : r + 1, :] = face_e[0:1]
            faces_ref[1, r : r + 1, :] = face_n[0:1]
            for g in range(blocks):
                send_ref[g, 16, r : r + 1, :] = total_e[0:1]
                send_ref[g, 17, r : r + 1, :] = total_n[0:1]
        if r < -1 or r >= tile_rows:
            continue
        open_e = (level < face_e).astype(jnp.float32)
        open_n = (level < face_n).astype(jnp.float32)
        for i, (f, ends, out_ref) in enumerate(((2, edge_t, tmix_ref), (3, edge_s, smix_ref))):
            x = row_of(f, r)
            flux_e = open_e * (row_of(f, r + 1) - x)
            if r >= 0:
                ending = edge(ends, r)
                flux_n = open_n * (jnp.where(last, ending, turn(x, -1, 1)) - x)
                flux_b = jnp.where(first, ending, turn(flux_n, 1, 1))
                mixed = x + MIXING * ((flux_e - flux_before[i]) + (flux_n - flux_b))
                out_ref[pl.ds(r, levels, stride=tile_rows), :] = mixed
            flux_before[i] = flux_e


def ocean_phase(blocks, levels, base, flat, sea, packed, rim_after, rim_before, after):
    tile_rows, cols = sea[0].shape
    outs = [
        shaped(levels * tile_rows, cols),
        shaped(levels * tile_rows, cols),
        shaped(blocks, ENTRIES, levels, cols),
        shaped(2, tile_rows, levels, cols),
        shaped(2, tile_rows, cols),
        shaped(blocks, 32, cols),
    ]
    tall = tile_rows + 2 * NSUB
    return call_once(
        functools.partial(ocean_kernel, blocks, levels),
        [*flat, *sea, packed, rim_after, rim_before],
        outs,
        [pltpu.VMEM((tall, levels, cols), jnp.float32)] * 2,
        [base],
        after,
        VMEM_MOST,
    )


def velocity_kernel(group_ref, local_ref, faces_ref, received_ref, east_ref, north_ref):
    blocks = received_ref.shape[0]
    _, tile_rows, levels, cols = local_ref.shape
    group = group_ref[0]
    level = (group * levels + subs_of((levels, cols))).astype(jnp.float32)
    for f, out_ref in enumerate((east_ref, north_ref)):
        above = jnp.zeros((tile_rows, cols), jnp.float32)
        for s in range(blocks - 1):
            above = above + jnp.where(s < group, received_ref[s, 16 + f], 0.0)
        for r in range(tile_rows):
            x = local_ref[f, r] - DT_FLOW * jnp.broadcast_to(above[r : r + 1], (levels, cols))
            x = jnp.where(level < faces_ref[f, r : r + 1, :], x, 0.0)
            out_ref[pl.ds(r, levels, stride=tile_rows), :] = x


def velocities(group, local, faces, received):
    _, tile_rows, levels, cols = local.shape
    outs = [shaped(levels * tile_rows, cols)] * 2
    return call_once(velocity_kernel, [local, faces, received], outs, scalars=[group])


def advection_kernel(first_part, parts, level_count, *refs):
    (
        absorb_ref,
        surface_ref,
        depth_ref,
        totals_ref,
        courant_ref,
        q_ref,
        after_ref,
        before_ref,
        side_ref,
        left_ref,
        right_ref,
        carry_ref,
    ) = refs[:12]
    moved_ref, light_ref, heat_ref, carry_out_ref = refs[-10:-6]
    coef_ref, side_coef_ref, edge_ref, running_ref, above_ref, shift_ref = refs[-6:]
    step = pl.program_id(0)
    tracers, _, cols = q_ref.shape
    levels = courant_ref.shape[2]
    sub_rows = surface_ref.shape[0]
    rows = sub_rows + 2
    shape = (levels, cols)
    lane = lanes_of(shape)
    first, last = lane == 0, lane == cols - 1
    first8, last8 = first[0:SUB], last[0:SUB]
    slot = lane % SLOTS

    @pl.when(step == 0)
    def _():
        running_ref[...] = carry_ref[...]
        size = (2 * cols, 2 * cols)
        source, to = subs_of(size) % cols, lanes_of(size)
        hit = ((to < cols) & (source == to + 1)) | ((to >= cols) & (source == to - cols - 1))
        shift_ref[...] = hit.astype(jnp.float32).astype(jnp.bfloat16)

    part = first_part + step
    above = jnp.zeros(above_ref.shape, jnp.float32)
    for s in range(totals_ref.shape[0] - 1):
        above = above + jnp.where(s < part // parts, totals_ref[s, 0], 0.0)
    above_ref[...] = above
    level = (part * levels + subs_of(shape)).astype(jnp.float32)

    def spread(ref, r):
        return jnp.broadcast_to(ref[r : r + 1, :], shape)

    def courant(entry, face):
        x = courant_ref[0, entry] - DT_FLOW * spread(above_ref, entry)
        return COURANT * jnp.tanh(jnp.where(level < spread(depth_ref, face), x, 0.0))

    def coefficients(wet, ce, ce_b, cn, cn_b):
        return (
            wet
            * (
                1.0
                - jnp.maximum(ce, 0.0)
                + jnp.minimum(ce_b, 0.0)
                - jnp.maximum(cn, 0.0)
                + jnp.minimum(cn_b, 0.0)
            ),
            -wet * jnp.minimum(ce, 0.0),
            wet * jnp.maximum(ce_b, 0.0),
            -wet * jnp.minimum(cn, 0.0),
            wet * jnp.maximum(cn_b, 0.0),
        )

    side_e, side_n = courant(13, 24), courant(14, 25)
    wet = (level < spread(depth_ref, 26)).astype(jnp.float32)
    packed_coef = coefficients(wet, side_e, turn(side_e, SLOTS, 1), side_n, turn(side_n, 1, 1))
    for i in range(5):
        side_coef_ref[i] = packed_coef[i]
    ce_b = courant(0, 0)
    for j in range(rows):
        ce, cn = courant(1 + j, 1 + j), courant(7 + j, 8 + j)
        cn_b = jnp.where(first, turn(side_n, -(SLOTS * (j + 1) + 1), 1), turn(cn, 1, 1))
        wet = (level < spread(depth_ref, 16 + j)).astype(jnp.float32)
        for i, x in enumerate(coefficients(wet, ce, ce_b, cn, cn_b)):
            coef_ref[5 * j + i] = x
        ce_b = ce
    for i in range(side_ref.shape[0]):
        x = with_sides(side_ref[i], left_ref[i], right_ref[i])
        edge_ref[i, 0] = jnp.where(slot == 0, turn(x, -6, 1), x)
        x = (
            (side_coef_ref[0] * x + side_coef_ref[1] * turn(x, -SLOTS, 1))
            + (side_coef_ref[2] * turn(x, SLOTS, 1) + side_coef_ref[3] * turn(x, -1, 1))
            + side_coef_ref[4] * turn(x, 1, 1)
        )
        edge_ref[i, 1] = jnp.where(slot == 0, turn(x, -6, 1), x)

    layer = 2.0 / level_count
    zero = jnp.zeros((SUB, cols), jnp.float32)
    for k in range(0, levels, SUB):
        at = slice(k, k + SUB)

        def shifted(tiles):
            high, low = halves(jnp.concatenate(tiles, axis=0))
            return jnp.dot(
                jnp.concatenate([high, low], axis=1),
                shift_ref[...],
                preferred_element_type=jnp.float32,
            )

        def stencil(x, j, edge, beside):
            north = jnp.where(last8, edge, beside[:, :cols])
            south = jnp.where(first8, edge, beside[:, cols:])
            return (
                (coef_ref[5 * j, at] * x[1] + coef_ref[5 * j + 1, at] * x[2])
                + (coef_ref[5 * j + 2, at] * x[0] + coef_ref[5 * j + 3, at] * north)
                + coef_ref[5 * j + 4, at] * south
            )

        def advect(i, sums):
            sums = list(sums)
            fields = []
            for t in range(GROUP):
                t = GROUP * i + t
                x = [before_ref[t, pl.ds(n, SUB, stride=NSUB), :] for n in range(NSUB)]
                x += [
                    q_ref[t, pl.ds(sub_rows * k + r, SUB, stride=sub_rows), :]
                    for r in range(sub_rows)
                ]
                x += [after_ref[t, pl.ds(n, SUB, stride=NSUB), :] for n in range(NSUB)]
                fields.append(x)
            for stage in range(NSUB):
                inner = range(1 + stage, rows + 1 - stage)
                beside = shifted([x[j - stage] for x in fields for j in inner])
                for t, x in enumerate(fields):
                    edges = edge_ref[GROUP // 2 * i + t // 2, stage, at]
                    fresh = []
                    for n, j in enumerate(inner):
                        edge = turn(edges, -(HALF * (t % 2) + SLOTS * j + 1), 1)
                        row = SUB * (len(inner) * t + n)
                        fresh.append(
                            stencil(x[n : n + 3], j - 1, edge, beside[row : row + SUB])
                        )
                    fields[t] = fresh
            for t, x in enumerate(fields):
                for r in range(sub_rows):
                    moved_ref[GROUP * i + t, r, at] = x[r]
                    sums[r] = sums[r] + absorb_ref[GROUP * i + t] * x[r]
            return tuple(sums)

        sums = lax.fori_loop(0, tracers // GROUP, advect, (zero,) * sub_rows)
        for r in range(sub_rows):
            optical = layer * (CLEAR_WATER + sums[r])
            above, total = sums_above(optical)
            through = jnp.exp(-(running_ref[r] + above))
            running_ref[r] = running_ref[r] + total
            surface = jnp.broadcast_to(surface_ref[r : r + 1, :], (SUB, cols))
            light_ref[r, at] = surface * through * jnp.exp(-0.5 * optical)
            wet = (level[at] < jnp.broadcast_to(depth_ref[17 + r : 18 + r, :], (SUB, cols))).astype(
                jnp.float32
            )
            heat_ref[0, r, at] = wet * surface * through * (1.0 - jnp.exp(-optical)) / layer
    carry_out_ref[...] = running_ref[...]


def advection(cut, level_count, absorb, surface, depth, received, q, rim_after, rim_before, sides, carry, heat, after):
    first_part, count = cut
    tracers, all_rows, cols = q.shape
    every, _, levels, _ = received.shape
    parts = levels // SUB
    sub_rows = surface.shape[0]
    rim = pl.BlockSpec((tracers, SUB * NSUB, cols), lambda i: (0, i, 0))
    side = pl.BlockSpec((tracers // 2, SUB, cols), lambda i: (0, i, 0))
    operands = [absorb, surface, depth, received, received, q, rim_after, rim_before, *sides, carry]
    in_specs = [
        smem(),
        whole(surface.shape),
        whole(depth.shape),
        pl.BlockSpec((every, 1, levels, cols), lambda i: (0, 15, 0, 0)),
        pl.BlockSpec(
            (1, ENTRIES, SUB, cols),
            lambda i: ((first_part + i) // parts, 0, (first_part + i) % parts, 0),
        ),
        pl.BlockSpec((tracers, SUB * sub_rows, cols), lambda i: (0, first_part + i, 0)),
        rim,
        rim,
        side,
        side,
        side,
        whole(carry.shape),
    ]
    aliases = {}
    if heat is not None:
        aliases = {len(operands): 2}
        operands.append(heat)
    operands += after
    in_specs += [pl.BlockSpec(memory_space=pl.ANY)] * (len(operands) - len(in_specs))
    outs = [
        shaped(tracers, sub_rows, count * SUB, cols),
        shaped(sub_rows, count * SUB, cols),
        shaped(every, sub_rows, levels, cols),
        shaped(*carry.shape),
    ]
    return pl.pallas_call(
        functools.partial(advection_kernel, first_part, parts, level_count),
        grid=(count,),
        in_specs=in_specs,
        out_specs=[
            pl.BlockSpec((tracers, sub_rows, SUB, cols), lambda i: (0, 0, i, 0)),
            pl.BlockSpec((sub_rows, SUB, cols), lambda i: (0, i, 0)),
            pl.BlockSpec(
                (1, sub_rows, SUB, cols),
                lambda i: ((first_part + i) // parts, 0, (first_part + i) % parts, 0),
            ),
            whole(carry.shape),
        ],
        out_shape=outs,
        scratch_shapes=[
            pltpu.VMEM((5 * (sub_rows + 2), SUB, cols), jnp.float32),
            pltpu.VMEM((5, SUB, cols), jnp.float32),
            pltpu.VMEM((tracers // 2, 2, SUB, cols), jnp.float32),
            pltpu.VMEM((sub_rows, SUB, cols), jnp.float32),
            pltpu.VMEM((levels, cols), jnp.float32),
            pltpu.VMEM((2 * cols, 2 * cols), jnp.bfloat16),
        ],
        input_output_aliases=aliases,
        compiler_params=params(),
    )(*operands)


def spread_kernel(matrix_ref, out_ref):
    tracers = matrix_ref.shape[0]
    size = tracers * SUB
    tall = (subs_of((size, tracers)) // SUB == lanes_of((size, tracers))).astype(jnp.float32)
    wide = (lanes_of((tracers, size)) // SUB == subs_of((tracers, size))).astype(jnp.float32)
    exact = functools.partial(
        jnp.dot, precision=lax.Precision.HIGHEST, preferred_element_type=jnp.float32
    )
    same = subs_of((size, size)) % SUB == lanes_of((size, size)) % SUB
    out_ref[...] = jnp.where(same, exact(exact(tall, matrix_ref[...]), wide), 0.0)


def uptake_kernel(first_level, *refs):
    growth_ref, half_ref, dim_ref, matrix_ref, depth_ref, moved_ref, light_ref = refs[:7]
    result_ref, token_ref, uptake_ref = refs[-3:]
    token_ref[...] = jnp.zeros_like(token_ref)
    tracers, sub_rows, levels, cols = moved_ref.shape
    step = pl.program_id(0)
    matrix_high, matrix_low = halves(matrix_ref[...])
    for k in range(0, levels, SUB):
        at = slice(k, k + SUB)
        level = (first_level + step * levels + k + subs_of((SUB, cols))).astype(jnp.float32)
        light = [light_ref[r, at] for r in range(sub_rows)]
        food = [moved_ref[0, r, at] for r in range(sub_rows)]
        both = [light[r] * food[r] for r in range(sub_rows)]

        def uptake(t, _):
            for r in range(sub_rows):
                scale = (half_ref[t] + food[r]) * (light[r] + dim_ref[t])
                value = growth_ref[t] * moved_ref[t, r, at] * (both[r] / scale)
                uptake_ref[pl.ds(t * SUB, SUB), r * cols : (r + 1) * cols] = value
            return _

        lax.fori_loop(0, tracers, uptake, 0, unroll=4)
        amount = uptake_ref[...]
        high, low = halves(amount)
        dot = functools.partial(jnp.dot, preferred_element_type=jnp.float32)
        change = dot(matrix_high, high) + (dot(matrix_high, low) + dot(matrix_low, high))
        for r in range(sub_rows):
            depth = jnp.broadcast_to(depth_ref[17 + r : 18 + r, :], (SUB, cols))
            scale = DT_BIO * (level < depth).astype(jnp.float32)
            for t in range(tracers):
                result_ref[t, pl.ds(sub_rows * k + r, SUB, stride=sub_rows), :] = (
                    moved_ref[t, r, at]
                    + scale * change[SUB * t : SUB * (t + 1), r * cols : (r + 1) * cols]
                )


def uptake(cut, all_rows, scalars, matrix, depth, moved, light, result):
    first_part, count = cut
    tracers, sub_rows, _, cols = moved.shape
    operands = [*scalars, matrix, depth, moved, light]
    in_specs = [smem()] * 3 + [
        whole(matrix.shape),
        whole(depth.shape),
        pl.BlockSpec((tracers, sub_rows, SUB, cols), lambda i: (0, 0, i, 0)),
        pl.BlockSpec((sub_rows, SUB, cols), lambda i: (0, i, 0)),
    ]
    aliases = {}
    if result is not None:
        aliases = {len(operands): 0}
        operands.append(result)
        in_specs.append(pl.BlockSpec(memory_space=pl.ANY))
    return pl.pallas_call(
        functools.partial(uptake_kernel, first_part * SUB),
        grid=(count,),
        in_specs=in_specs,
        out_specs=[
            pl.BlockSpec((tracers, SUB * sub_rows, cols), lambda i: (0, first_part + i, 0)),
            whole((SUB, cols)),
        ],
        out_shape=[shaped(tracers, all_rows, cols), shaped(SUB, cols)],
        scratch_shapes=[pltpu.VMEM((tracers * SUB, sub_rows * cols), jnp.float32)],
        input_output_aliases=aliases,
        compiler_params=params(),
    )(*operands)


def warming_kernel(base_ref, sea_ref, floor_ref, heat_ref, tmix_ref, smix_ref, warm_ref, buoyant_ref):
    blocks, sub_rows, levels, cols = heat_ref.shape
    tile_rows = blocks * sub_rows
    level = (base_ref[0] + subs_of((levels, cols))).astype(jnp.float32)
    depth = jnp.where(sea_ref[...] == 1, floor_ref[...], 0).astype(jnp.float32)
    for r in range(tile_rows):
        at = pl.ds(r, levels, stride=tile_rows)
        warm = tmix_ref[at, :] + WARMING_FACTOR * heat_ref[r // sub_rows, r % sub_rows]
        wet = (level < depth[r : r + 1]).astype(jnp.float32)
        warm_ref[at, :] = warm
        buoyant_ref[at, :] = wet * (0.2 * warm - 0.8 * smix_ref[at, :])


def warming(base, heat, tmix, smix, sea):
    outs = [shaped(*tmix.shape)] * 2
    return call_once(warming_kernel, [*sea, heat, tmix, smix], outs, scalars=[base])


def from_before(x, axis):
    return lax.ppermute(x, axis, [(i, i + 1) for i in range(lax.axis_size(axis) - 1)])


def from_after(x, axis):
    return lax.ppermute(x, axis, [(i + 1, i) for i in range(lax.axis_size(axis) - 1)])


def row_pairs():
    blocks, tiles = lax.axis_size("comp"), lax.axis_size("gx")
    places = [b * tiles + tile for tile in range(tiles) for b in range(blocks)]
    return list(zip(places[:-1], places[1:]))


def from_block_before(x):
    return lax.ppermute(x, ("comp", "gx"), row_pairs())


def from_block_after(x):
    return lax.ppermute(x, ("comp", "gx"), [(later, own) for own, later in row_pairs()])


def from_sides(x):
    if lax.axis_size("gy") == 2:
        other = lax.ppermute(x, "gy", [(0, 1), (1, 0)])
        return other, other
    return from_before(x, "gy"), from_after(x, "gy")


def on_device(
    zonal_flow_speed,
    meridional_flow_speed,
    thermal_anomaly,
    brine_anomaly_values,
    marine_indicator,
    seafloor_layer,
    dissolved_species,
    topmost_sunshine,
    attenuation_coefficient,
    peak_intake_speed,
    feedstock_midpoint_constant,
    photon_midpoint_constant,
    stoichiometry_matrix,
):
    group_index = lax.axis_index("comp")
    blocks = lax.axis_size("comp")
    levels, tile_rows, tile_cols = zonal_flow_speed.shape
    tracer_count, level_count = dissolved_species.shape[:2]
    sub_rows = dissolved_species.shape[4]
    ocean = (zonal_flow_speed, meridional_flow_speed, thermal_anomaly, brine_anomaly_values)
    sea = (marine_indicator, seafloor_layer)
    group = group_index.astype(jnp.int32).reshape(1)
    base = group * levels
    place = jnp.stack([lax.axis_index("gy"), lax.axis_size("gy")]).astype(jnp.int32)

    flat = [x.reshape(levels * tile_rows, tile_cols) for x in ocean]
    q = dissolved_species.reshape(tracer_count, level_count * sub_rows, tile_cols)
    rows_of_q = dissolved_species.reshape(
        tracer_count, level_count, sub_rows // NSUB, NSUB, tile_cols
    )
    parts = levels // SUB
    every = parts * blocks
    sizes = [every - every // 4 - 3 * every // 8, 3 * every // 8, every // 4]
    cuts = [(sum(sizes[:i]), size) for i, size in enumerate(sizes)]
    matrix = call_once(
        spread_kernel,
        [stoichiometry_matrix],
        [shaped(SUB * tracer_count, SUB * tracer_count)],
    )[0]
    scalars_of_uptake = (
        peak_intake_speed,
        feedstock_midpoint_constant,
        photon_midpoint_constant,
    )

    def rims(cut, *after):
        low, high = cut_rows(rows_of_q, cut[0] * SUB, cut[1] * SUB, after)
        shape = (tracer_count, cut[1] * SUB * NSUB, tile_cols)
        moved = from_block_after(low).reshape(shape), from_block_before(high).reshape(shape)
        return (low, high), moved

    def sides(x):
        return (x, *from_sides(x))

    cut0, rims0 = rims(cuts[0])
    packed, edge_low, edge_high = pack_ocean(flat, sea, levels, cut0)
    up, down, packed = ocean_sides(place, packed, *from_sides(packed), edge_low, edge_high)
    after, before = from_after(up, "gx"), from_before(down, "gx")
    cut1, rims1 = rims(cuts[1], up)
    tmix, smix, send, local, faces, depths = ocean_phase(
        blocks, levels, base, flat, sea, packed, after, before, cut1
    )
    received = lax.all_to_all(send, "comp", split_axis=0, concat_axis=0, tiled=True)
    depth = lax.dynamic_index_in_dim(depths, group_index, 0, False)
    east_new, north_new = velocities(group, local, faces, received)
    ahead = [(cut0, rims0), (cut1, rims1), rims(cuts[2], depths)]

    surface = topmost_sunshine.reshape(sub_rows, tile_cols)
    carry = jnp.zeros((sub_rows, SUB, tile_cols), jnp.float32)
    heat, result = None, None
    for i, cut in enumerate(cuts):
        waits = list(ahead[i + 2][0]) if i + 2 < len(cuts) else []
        if i == len(cuts) - 1:
            waits.append(token)
        near = sides(pack_tracers(q, *ahead[i][1], cut, sub_rows, waits))
        moved, light, heat, carry = advection(
            cut,
            level_count,
            attenuation_coefficient,
            surface,
            depth,
            received,
            q,
            *ahead[i][1],
            near,
            carry,
            heat,
            [],
        )
        if i + 3 < len(cuts):
            ahead.append(rims(cuts[i + 3], carry))
        result, token = uptake(
            cut,
            level_count * sub_rows,
            scalars_of_uptake,
            matrix,
            depth,
            moved,
            light,
            result,
        )
    heat = lax.all_to_all(heat, "comp", split_axis=0, concat_axis=0, tiled=True)
    warmed_result, buoyancy = warming(base, heat, tmix, smix, sea)
    fields = (east_new, north_new, warmed_result, smix, buoyancy)
    return (
        *[x.reshape(zonal_flow_speed.shape) for x in fields],
        result.reshape(dissolved_species.shape),
    )


def solution(mesh):
    return jax.shard_map(
        on_device,
        mesh=mesh,
        in_specs=(
            P("comp", "gx", "gy"),
            P("comp", "gx", "gy"),
            P("comp", "gx", "gy"),
            P("comp", "gx", "gy"),
            P("gx", "gy"),
            P("gx", "gy"),
            P(None, None, "gx", "comp", None, "gy"),
            P("gx", "comp", None, "gy"),
            P(),
            P(),
            P(),
            P(),
            P(),
        ),
        out_specs=(
            P("comp", "gx", "gy"),
            P("comp", "gx", "gy"),
            P("comp", "gx", "gy"),
            P("comp", "gx", "gy"),
            P("comp", "gx", "gy"),
            P(None, None, "gx", "comp", None, "gy"),
        ),
        check_vma=False,
    )
```

```python
import functools

import jax
import jax.numpy as jnp
from jax import lax
from jax.experimental import pallas as pl
from jax.experimental.pallas import tpu as pltpu
from jax.sharding import PartitionSpec as P

NSUB = 2
SLOTS = 4 * NSUB
SUB = 8
GROUP = 6
HALF = 64
ENTRIES = 18

DT_FLOW = 0.1
CORIOLIS = 0.3
MIXING = 0.15
COURANT = 0.24
DT_BIO = 0.5
WARMING_FACTOR = 0.5
CLEAR_WATER = 0.5
VMEM_LIMIT = 16 * 1024 * 1024
VMEM_MOST = 62 * 1024 * 1024


def lanes_of(shape):
    return lax.broadcasted_iota(jnp.int32, shape, len(shape) - 1)


def subs_of(shape):
    return lax.broadcasted_iota(jnp.int32, shape, len(shape) - 2)


def turn(x, by, axis):
    by = by % x.shape[axis]
    return x if by == 0 else pltpu.roll(x, by, axis)


def params(limit=VMEM_LIMIT):
    return pltpu.CompilerParams(vmem_limit_bytes=limit)


def whole(shape):
    return pl.BlockSpec(shape, lambda *_: (0,) * len(shape))


def smem():
    return pl.BlockSpec(memory_space=pltpu.SMEM)


def shaped(*shape):
    return jax.ShapeDtypeStruct(shape, jnp.float32)


def halves(x):
    high = x.astype(jnp.bfloat16)
    return high, (x - high.astype(jnp.float32)).astype(jnp.bfloat16)


def sums_above(x):
    sub = subs_of(x.shape)
    running, total = x, x
    by = 1
    while by < x.shape[0]:
        running = running + jnp.where(sub >= by, turn(running, by, 0), 0.0)
        total = total + turn(total, by, 0)
        by *= 2
    return jnp.where(sub >= 1, turn(running, 1, 0), 0.0), total


def cut_kernel(start, size, q_ref, *refs):
    outs, sems = refs[-3:-1], refs[-1]
    rows = q_ref.shape[2]
    copies = [
        pltpu.make_async_copy(
            q_ref.at[:, pl.ds(start, size), r], outs[r // NSUB].at[:, r % NSUB], sems.at[r]
        )
        for r in range(rows)
    ]
    for copy in copies:
        copy.start()
    for copy in copies:
        copy.wait()


def cut_rows(q, start, size, after):
    tracers, _, rows, _, cols = q.shape
    anywhere = pl.BlockSpec(memory_space=pl.ANY)
    return pl.pallas_call(
        functools.partial(cut_kernel, start, size),
        in_specs=[anywhere] * (1 + len(after)),
        out_specs=[anywhere] * 2,
        out_shape=[shaped(tracers, NSUB, size, 1, cols)] * 2,
        scratch_shapes=[pltpu.SemaphoreType.DMA((rows,))],
        compiler_params=params(),
    )(q, *after)


def both_ends(acc):
    return jnp.where(lanes_of(acc.shape) % SLOTS < SLOTS // 2, acc, turn(acc, SLOTS // 2, 1))


def pack_tracers_kernel(low_ref, high_ref, after_ref, before_ref, packed_ref):
    tracers, _, _, cols = low_ref.shape
    lane = lanes_of((SUB, cols))
    for pair in range(tracers // 2):
        acc = jnp.zeros((SUB, cols), jnp.float32)
        for odd in range(2):
            t = 2 * pair + odd
            rows = [before_ref[t, 1], low_ref[t, 0], low_ref[t, 1], high_ref[t, 0], high_ref[t, 1]]
            for r, x in enumerate(rows + [after_ref[t, 0]]):
                at = HALF * odd + SLOTS * (r + 1)
                acc = jnp.where(lane // SLOTS == at // SLOTS, turn(x, at + NSUB, 1), acc)
        packed_ref[pair] = both_ends(acc)


def pack_tracers(own, rim, after):
    tracers, _, levels, cols = own[0].shape
    rows = pl.BlockSpec((tracers, NSUB, SUB, cols), lambda i: (0, 0, i, 0))
    return pl.pallas_call(
        functools.partial(ignoring, len(after), pack_tracers_kernel),
        grid=(levels // SUB,),
        in_specs=[pl.BlockSpec(memory_space=pl.ANY)] * len(after) + [rows] * 4,
        out_specs=pl.BlockSpec((tracers // 2, SUB, cols), lambda i: (0, i, 0)),
        out_shape=shaped(tracers // 2, levels, cols),
        compiler_params=params(),
    )(*after, *own, *rim)


def ignoring(count, kernel, *refs):
    kernel(*refs[count:])


def call_once(kernel, operands, outs, scratch=(), scalars=(), after=(), limit=VMEM_LIMIT):
    return pl.pallas_call(
        functools.partial(ignoring, len(after), kernel),
        grid=(1,),
        in_specs=[pl.BlockSpec(memory_space=pl.ANY)] * len(after)
        + [smem()] * len(scalars)
        + [whole(x.shape) for x in operands],
        out_specs=[whole(x.shape) for x in outs],
        out_shape=outs,
        scratch_shapes=list(scratch),
        compiler_params=params(limit),
    )(*after, *scalars, *operands)


def pack_ocean_kernel(levels, *refs):
    u_ref, v_ref, t_ref, s_ref, sea_ref, floor_ref, packed_ref, edge_low_ref, edge_high_ref, row_ref = refs
    tile_rows, cols = sea_ref.shape
    lane = lanes_of((levels, cols))
    edge_low_ref[4 * NSUB] = jnp.zeros((levels, cols), jnp.float32)
    edge_high_ref[4 * NSUB] = jnp.zeros((levels, cols), jnp.float32)
    for f, ref in enumerate((u_ref, v_ref, t_ref, s_ref)):
        acc = jnp.zeros((levels, cols), jnp.float32)
        for r in range(tile_rows):
            x = ref[pl.ds(r, levels, stride=tile_rows), :]
            row_ref[f, r] = x
            acc = jnp.where(lane // SLOTS == r, turn(x, SLOTS * r + NSUB, 1), acc)
            if r < NSUB:
                edge_low_ref[NSUB * f + r] = x
            if r >= tile_rows - NSUB:
                edge_high_ref[NSUB * f + r - tile_rows + NSUB] = x
        packed_ref[f] = both_ends(acc)
    depth = jnp.where(sea_ref[...] == 1, floor_ref[...], 0).astype(jnp.float32)
    acc = jnp.zeros((levels, cols), jnp.float32)
    for r in range(tile_rows):
        x = jnp.broadcast_to(depth[r : r + 1], (levels, cols))
        acc = jnp.where(lane // SLOTS == r, turn(x, SLOTS * r + NSUB, 1), acc)
    packed_ref[4] = both_ends(acc)
    edge_low_ref[4 * NSUB, 0:NSUB, :] = depth[0:NSUB]
    edge_high_ref[4 * NSUB, 0:NSUB, :] = depth[tile_rows - NSUB :]


def pack_ocean(flat, sea, levels):
    cols = sea[0].shape[1]
    edge = shaped(4 * NSUB + 1, levels, cols)
    return call_once(
        functools.partial(pack_ocean_kernel, levels),
        [*flat, *sea],
        [shaped(5, levels, cols), edge, edge, shaped(4, sea[0].shape[0], levels, cols)],
        limit=VMEM_MOST,
    )


def with_sides(own, left, right):
    slot = lanes_of(own.shape) % SLOTS
    ends = jnp.where(slot < NSUB, left, right)
    return jnp.where((slot < NSUB) | (slot >= SLOTS - NSUB), ends, own)


def ocean_sides_kernel(place_ref, own_ref, left_ref, right_ref, low_ref, high_ref, up_ref, down_ref, out_ref):
    _, levels, cols = own_ref.shape
    rows = low_ref.shape[0]
    up_ref[0:rows] = low_ref[...]
    down_ref[0:rows] = high_ref[...]
    slot = lanes_of((levels, cols)) % SLOTS
    first, last = place_ref[0] == 0, place_ref[0] == place_ref[1] - 1
    for f in range(5):
        x = with_sides(own_ref[f], left_ref[f], right_ref[f])
        if f == 4:
            x = jnp.where((slot < NSUB) & first, 0.0, x)
            x = jnp.where((slot >= SLOTS - NSUB) & last, 0.0, x)
        out_ref[f] = x
        up_ref[rows + f] = x
        down_ref[rows + f] = x


def ocean_sides(place, own, left, right, low, high):
    edge = shaped(low.shape[0] + 5, *low.shape[1:])
    return call_once(
        ocean_sides_kernel,
        [own, left, right, low, high],
        [edge, edge, shaped(*own.shape)],
        scalars=[place],
    )


def ocean_kernel(blocks, levels, *refs):
    base_ref, own_ref, sea_ref, floor_ref, packed_ref, after_ref, before_ref = refs[:7]
    smix_ref, mixed_ref, send_ref, local_ref, faces_ref, depths_ref, press_ref, total_ref = refs[7:]
    tile_rows, cols = sea_ref.shape
    sub_rows = tile_rows // blocks
    shape = (levels, cols)
    lane = lanes_of(shape)
    first, last = lane == 0, lane == cols - 1
    level = (base_ref[0] + subs_of(shape)).astype(jnp.float32)
    rims = after_ref.shape[0] - 5

    def packed(f):
        after, before = after_ref[rims + f], before_ref[rims + f]
        rim = jnp.where(lane < NSUB * SLOTS, after, jnp.where(lane >= cols - NSUB * SLOTS, before, 0.0))
        return jnp.concatenate([packed_ref[f], rim], axis=1)

    def row_after(x):
        return turn(x, -SLOTS, 1)

    def row_before(x):
        return turn(x, SLOTS, 1)

    up, vp, tp, sp, dp = [packed(f) for f in range(5)]
    wide = jnp.concatenate([level, level], axis=1)
    wet = (wide < dp).astype(jnp.float32)
    heavy = wet * (-0.2 * tp + 0.8 * sp)
    above, total = sums_above(heavy)
    press = above + 0.5 * heavy
    east = up + DT_FLOW * (CORIOLIS * vp - (row_after(press) - press))
    north = vp + DT_FLOW * (-CORIOLIS * up - (turn(press, -1, 1) - press))
    open_n = wet * turn(wet, -1, 1)
    flux_t = open_n * (turn(tp, -1, 1) - tp)
    flux_s = open_n * (turn(sp, -1, 1) - sp)
    total_e, total_n = row_after(total) - total, turn(total, -1, 1) - total
    depth_e, depth_n = jnp.minimum(dp, row_after(dp)), jnp.minimum(dp, turn(dp, -1, 1))

    def window(x, g):
        x = turn(x, -SLOTS * (sub_rows * g - NSUB), 1)[:, 0:cols]
        return jnp.where(lane < HALF, x, turn(x, HALF, 1))

    for g in range(blocks):
        send_ref[g, 13] = window(east, g)
        send_ref[g, 14] = window(north, g)
        send_ref[g, 15, 13:14, :] = window(total_e, g)[0:1]
        send_ref[g, 15, 14:15, :] = window(total_n, g)[0:1]
        send_ref[g, 15, 15:16, :] = jnp.zeros((1, cols), jnp.float32)
        depths_ref[g, 24:25, :] = window(depth_e, g)[0:1]
        depths_ref[g, 25:26, :] = window(depth_n, g)[0:1]
        depths_ref[g, 26:27, :] = window(dp, g)[0:1]

    slot = lanes_of(tp.shape) % SLOTS

    def edges(x, other):
        x = jnp.where(slot == 0, turn(x, -6, 1), other)
        return x[:, 0:cols], x[:, cols:]

    edge_p, edge_w = edges(press, press), edges(wet, wet)
    edge_t, edge_s = edges(tp, flux_t), edges(sp, flux_s)
    edge_total, edge_depth = edges(total, total), edges(dp, dp)

    def edge(pair, r):
        at = r % tile_rows
        return turn(pair[0] if 0 <= r < tile_rows else pair[1], -(SLOTS * at + 1), 1)

    depth = jnp.where(sea_ref[...] == 1, floor_ref[...], 0).astype(jnp.float32)

    def row_of(f, r):
        if r < 0:
            return before_ref[NSUB * f + r + NSUB]
        if r >= tile_rows:
            return after_ref[NSUB * f + r - tile_rows]
        return own_ref[f, r]

    def depth_of(r):
        if r < 0:
            x = before_ref[4 * NSUB, r + NSUB : r + NSUB + 1, :]
        elif r >= tile_rows:
            x = after_ref[4 * NSUB, r - tile_rows : r - tile_rows + 1, :]
        else:
            x = depth[r : r + 1]
        return jnp.broadcast_to(x, shape)

    lo, hi = -NSUB, tile_rows + NSUB
    for r in range(lo, hi):
        heavy = (level < depth_of(r)).astype(jnp.float32) * (-0.2 * row_of(2, r) + 0.8 * row_of(3, r))
        above, total = sums_above(heavy)
        press_ref[r - lo] = above + 0.5 * heavy
        total_ref[r - lo] = total

    def windows(r, before):
        for g in range(blocks):
            j = r - (sub_rows * g - before)
            if 0 <= j < sub_rows + 1 + before:
                yield g, j

    flux_before = [None, None]
    for r in range(lo, hi - 1):
        press, press_e = press_ref[r - lo], press_ref[r - lo + 1]
        total, total_a = total_ref[r - lo], total_ref[r - lo + 1]
        d, d_e = depth_of(r), depth_of(r + 1)
        d_n = jnp.where(last, edge(edge_depth, r), turn(d, -1, 1))
        face_e, face_n = jnp.minimum(d, d_e), jnp.minimum(d, d_n)
        u, v = row_of(0, r), row_of(1, r)
        east = u + DT_FLOW * (CORIOLIS * v - (press_e - press))
        press_n = jnp.where(last, edge(edge_p, r), turn(press, -1, 1))
        north = v + DT_FLOW * (-CORIOLIS * u - (press_n - press))
        total_e = total_a - total
        total_n = jnp.where(last, edge(edge_total, r), turn(total, -1, 1)) - total
        for g, j in windows(r, 2):
            send_ref[g, j] = east
            send_ref[g, 15, j : j + 1, :] = total_e[0:1]
            depths_ref[g, j : j + 1, :] = face_e[0:1]
        for g, j in windows(r, 1):
            send_ref[g, 7 + j] = north
            send_ref[g, 15, 7 + j : 8 + j, :] = total_n[0:1]
            depths_ref[g, 8 + j : 9 + j, :] = face_n[0:1]
            depths_ref[g, 16 + j : 17 + j, :] = d[0:1]
        if 0 <= r < tile_rows:
            local_ref[0, r] = east
            local_ref[1, r] = north
            faces_ref[0, r : r + 1, :] = face_e[0:1]
            faces_ref[1, r : r + 1, :] = face_n[0:1]
            for g in range(blocks):
                send_ref[g, 16, r : r + 1, :] = total_e[0:1]
                send_ref[g, 17, r : r + 1, :] = total_n[0:1]
        if r < -1 or r >= tile_rows:
            continue
        open_e = (level < face_e).astype(jnp.float32)
        open_n = (level < face_n).astype(jnp.float32)
        for i, (f, ends) in enumerate(((2, edge_t), (3, edge_s))):
            x = row_of(f, r)
            flux_e = open_e * (row_of(f, r + 1) - x)
            if r >= 0:
                ending = edge(ends, r)
                flux_n = open_n * (jnp.where(last, ending, turn(x, -1, 1)) - x)
                flux_b = jnp.where(first, ending, turn(flux_n, 1, 1))
                mixed = x + MIXING * ((flux_e - flux_before[i]) + (flux_n - flux_b))
                mixed_ref[i, r] = mixed
                if i == 1:
                    smix_ref[pl.ds(r, levels, stride=tile_rows), :] = mixed
            flux_before[i] = flux_e


def ocean_phase(blocks, levels, base, own, sea, packed, rim_after, rim_before, after):
    tile_rows, cols = sea[0].shape
    outs = [
        shaped(levels * tile_rows, cols),
        shaped(2, tile_rows, levels, cols),
        shaped(blocks, ENTRIES, levels, cols),
        shaped(2, tile_rows, levels, cols),
        shaped(2, tile_rows, cols),
        shaped(blocks, 32, cols),
    ]
    tall = tile_rows + 2 * NSUB
    return call_once(
        functools.partial(ocean_kernel, blocks, levels),
        [own, *sea, packed, rim_after, rim_before],
        outs,
        [pltpu.VMEM((tall, levels, cols), jnp.float32)] * 2,
        [base],
        after,
    )


def velocity_kernel(group_ref, local_ref, faces_ref, received_ref, east_ref, north_ref):
    blocks = received_ref.shape[0]
    _, tile_rows, levels, cols = local_ref.shape
    group = group_ref[0]
    level = (group * levels + subs_of((levels, cols))).astype(jnp.float32)
    for f, out_ref in enumerate((east_ref, north_ref)):
        above = jnp.zeros((tile_rows, cols), jnp.float32)
        for s in range(blocks - 1):
            above = above + jnp.where(s < group, received_ref[s, f], 0.0)
        for r in range(tile_rows):
            x = local_ref[f, r] - DT_FLOW * jnp.broadcast_to(above[r : r + 1], (levels, cols))
            x = jnp.where(level < faces_ref[f, r : r + 1, :], x, 0.0)
            out_ref[pl.ds(r, levels, stride=tile_rows), :] = x


def velocities(group, local, faces, received):
    blocks = received.shape[0]
    _, tile_rows, levels, cols = local.shape
    out = shaped(levels * tile_rows, cols)
    return pl.pallas_call(
        velocity_kernel,
        grid=(1,),
        in_specs=[
            smem(),
            whole(local.shape),
            whole(faces.shape),
            pl.BlockSpec((blocks, 2, levels, cols), lambda i: (0, ENTRIES // 2 - 1, 0, 0)),
        ],
        out_specs=[whole(out.shape)] * 2,
        out_shape=[out] * 2,
        compiler_params=params(),
    )(group, local, faces, received)


def advection_kernel(first_part, parts, level_count, *refs):
    (
        absorb_ref,
        surface_ref,
        depth_ref,
        totals_ref,
        courant_ref,
        low_ref,
        high_ref,
        after_ref,
        before_ref,
        side_ref,
        left_ref,
        right_ref,
        carry_ref,
    ) = refs[:13]
    moved_ref, light_ref, heat_ref, carry_out_ref = refs[-10:-6]
    coef_ref, side_coef_ref, edge_ref, running_ref, above_ref, shift_ref = refs[-6:]
    step = pl.program_id(0)
    tracers, _, _, cols = low_ref.shape
    levels = courant_ref.shape[2]
    sub_rows = surface_ref.shape[0]
    rows = sub_rows + 2
    shape = (levels, cols)
    lane = lanes_of(shape)
    first, last = lane == 0, lane == cols - 1
    first8, last8 = first[0:SUB], last[0:SUB]
    slot = lane % SLOTS

    @pl.when(step == 0)
    def _():
        running_ref[...] = carry_ref[...]
        size = (2 * cols, 2 * cols)
        source, to = subs_of(size) % cols, lanes_of(size)
        hit = ((to < cols) & (source == to + 1)) | ((to >= cols) & (source == to - cols - 1))
        shift_ref[...] = hit.astype(jnp.float32).astype(jnp.bfloat16)

    part = first_part + step
    above = jnp.zeros(above_ref.shape, jnp.float32)
    for s in range(totals_ref.shape[0] - 1):
        above = above + jnp.where(s < part // parts, totals_ref[s, 0], 0.0)
    above_ref[...] = above
    level = (part * levels + subs_of(shape)).astype(jnp.float32)

    def spread(ref, r):
        return jnp.broadcast_to(ref[r : r + 1, :], shape)

    def courant(entry, face):
        x = courant_ref[0, entry] - DT_FLOW * spread(above_ref, entry)
        return COURANT * jnp.tanh(jnp.where(level < spread(depth_ref, face), x, 0.0))

    def coefficients(wet, ce, ce_b, cn, cn_b):
        return (
            wet
            * (
                1.0
                - jnp.maximum(ce, 0.0)
                + jnp.minimum(ce_b, 0.0)
                - jnp.maximum(cn, 0.0)
                + jnp.minimum(cn_b, 0.0)
            ),
            -wet * jnp.minimum(ce, 0.0),
            wet * jnp.maximum(ce_b, 0.0),
            -wet * jnp.minimum(cn, 0.0),
            wet * jnp.maximum(cn_b, 0.0),
        )

    side_e, side_n = courant(13, 24), courant(14, 25)
    wet = (level < spread(depth_ref, 26)).astype(jnp.float32)
    packed_coef = coefficients(wet, side_e, turn(side_e, SLOTS, 1), side_n, turn(side_n, 1, 1))
    for i in range(5):
        side_coef_ref[i] = packed_coef[i]
    ce_b = courant(0, 0)
    for j in range(rows):
        ce, cn = courant(1 + j, 1 + j), courant(7 + j, 8 + j)
        cn_b = jnp.where(first, turn(side_n, -(SLOTS * (j + 1) + 1), 1), turn(cn, 1, 1))
        wet = (level < spread(depth_ref, 16 + j)).astype(jnp.float32)
        for i, x in enumerate(coefficients(wet, ce, ce_b, cn, cn_b)):
            coef_ref[5 * j + i] = x
        ce_b = ce
    for i in range(side_ref.shape[0]):
        x = with_sides(side_ref[i], left_ref[i], right_ref[i])
        edge_ref[i, 0] = jnp.where(slot == 0, turn(x, -6, 1), x)
        x = (
            (side_coef_ref[0] * x + side_coef_ref[1] * turn(x, -SLOTS, 1))
            + (side_coef_ref[2] * turn(x, SLOTS, 1) + side_coef_ref[3] * turn(x, -1, 1))
            + side_coef_ref[4] * turn(x, 1, 1)
        )
        edge_ref[i, 1] = jnp.where(slot == 0, turn(x, -6, 1), x)

    layer = 2.0 / level_count
    zero = jnp.zeros((SUB, cols), jnp.float32)
    for k in range(0, levels, SUB):
        at = slice(k, k + SUB)

        def shifted(tiles):
            high, low = halves(jnp.concatenate(tiles, axis=0))
            return jnp.dot(
                jnp.concatenate([high, low], axis=1),
                shift_ref[...],
                preferred_element_type=jnp.float32,
            )

        def stencil(x, j, edge, beside):
            north = jnp.where(last8, edge, beside[:, :cols])
            south = jnp.where(first8, edge, beside[:, cols:])
            return (
                (coef_ref[5 * j, at] * x[1] + coef_ref[5 * j + 1, at] * x[2])
                + (coef_ref[5 * j + 2, at] * x[0] + coef_ref[5 * j + 3, at] * north)
                + coef_ref[5 * j + 4, at] * south
            )

        def advect(i, sums):
            sums = list(sums)
            fields = []
            for t in range(GROUP):
                t = GROUP * i + t
                rows_of = (before_ref, low_ref, high_ref, after_ref)
                x = [ref[t, n, at] for ref in rows_of for n in range(NSUB)]
                fields.append(x)
            for stage in range(NSUB):
                inner = range(1 + stage, rows + 1 - stage)
                beside = shifted([x[j - stage] for x in fields for j in inner])
                for t, x in enumerate(fields):
                    edges = edge_ref[GROUP // 2 * i + t // 2, stage, at]
                    fresh = []
                    for n, j in enumerate(inner):
                        edge = turn(edges, -(HALF * (t % 2) + SLOTS * j + 1), 1)
                        row = SUB * (len(inner) * t + n)
                        fresh.append(
                            stencil(x[n : n + 3], j - 1, edge, beside[row : row + SUB])
                        )
                    fields[t] = fresh
            for t, x in enumerate(fields):
                for r in range(sub_rows):
                    moved_ref[GROUP * i + t, r, at] = x[r]
                    sums[r] = sums[r] + absorb_ref[GROUP * i + t] * x[r]
            return tuple(sums)

        sums = lax.fori_loop(0, tracers // GROUP, advect, (zero,) * sub_rows)
        for r in range(sub_rows):
            optical = layer * (CLEAR_WATER + sums[r])
            above, total = sums_above(optical)
            through = jnp.exp(-(running_ref[r] + above))
            running_ref[r] = running_ref[r] + total
            surface = jnp.broadcast_to(surface_ref[r : r + 1, :], (SUB, cols))
            light_ref[r, at] = surface * through * jnp.exp(-0.5 * optical)
            wet = (level[at] < jnp.broadcast_to(depth_ref[17 + r : 18 + r, :], (SUB, cols))).astype(
                jnp.float32
            )
            heat_ref[0, r, at] = wet * surface * through * (1.0 - jnp.exp(-optical)) / layer
    carry_out_ref[...] = running_ref[...]


def advection(cut, level_count, absorb, surface, depth, received, own, rim, sides, carry, heat, after):
    first_part, count = cut
    tracers, _, _, cols = own[0].shape
    every, _, levels, _ = received.shape
    parts = levels // SUB
    sub_rows = surface.shape[0]
    rows = pl.BlockSpec((tracers, NSUB, SUB, cols), lambda i: (0, 0, i, 0))
    side = pl.BlockSpec((tracers // 2, SUB, cols), lambda i: (0, i, 0))
    operands = [absorb, surface, depth, received, received, *own, *rim, *sides, carry]
    in_specs = [
        smem(),
        whole(surface.shape),
        whole(depth.shape),
        pl.BlockSpec((every, 1, levels, cols), lambda i: (0, 15, 0, 0)),
        pl.BlockSpec(
            (1, ENTRIES, SUB, cols),
            lambda i: ((first_part + i) // parts, 0, (first_part + i) % parts, 0),
        ),
        rows,
        rows,
        rows,
        rows,
        side,
        side,
        side,
        whole(carry.shape),
    ]
    aliases = {}
    if heat is not None:
        aliases = {len(operands): 2}
        operands.append(heat)
    operands += after
    in_specs += [pl.BlockSpec(memory_space=pl.ANY)] * (len(operands) - len(in_specs))
    outs = [
        shaped(tracers, sub_rows, count * SUB, cols),
        shaped(sub_rows, count * SUB, cols),
        shaped(every, sub_rows, levels, cols),
        shaped(*carry.shape),
    ]
    return pl.pallas_call(
        functools.partial(advection_kernel, first_part, parts, level_count),
        grid=(count,),
        in_specs=in_specs,
        out_specs=[
            pl.BlockSpec((tracers, sub_rows, SUB, cols), lambda i: (0, 0, i, 0)),
            pl.BlockSpec((sub_rows, SUB, cols), lambda i: (0, i, 0)),
            pl.BlockSpec(
                (1, sub_rows, SUB, cols),
                lambda i: ((first_part + i) // parts, 0, (first_part + i) % parts, 0),
            ),
            whole(carry.shape),
        ],
        out_shape=outs,
        scratch_shapes=[
            pltpu.VMEM((5 * (sub_rows + 2), SUB, cols), jnp.float32),
            pltpu.VMEM((5, SUB, cols), jnp.float32),
            pltpu.VMEM((tracers // 2, 2, SUB, cols), jnp.float32),
            pltpu.VMEM((sub_rows, SUB, cols), jnp.float32),
            pltpu.VMEM((levels, cols), jnp.float32),
            pltpu.VMEM((2 * cols, 2 * cols), jnp.bfloat16),
        ],
        input_output_aliases=aliases,
        compiler_params=params(),
    )(*operands)


def spread_kernel(matrix_ref, out_ref):
    tracers = matrix_ref.shape[0]
    size = tracers * SUB
    tall = (subs_of((size, tracers)) // SUB == lanes_of((size, tracers))).astype(jnp.float32)
    wide = (lanes_of((tracers, size)) // SUB == subs_of((tracers, size))).astype(jnp.float32)
    exact = functools.partial(
        jnp.dot, precision=lax.Precision.HIGHEST, preferred_element_type=jnp.float32
    )
    same = subs_of((size, size)) % SUB == lanes_of((size, size)) % SUB
    out_ref[...] = jnp.where(same, exact(exact(tall, matrix_ref[...]), wide), 0.0)


def uptake_kernel(first_level, *refs):
    growth_ref, half_ref, dim_ref, matrix_ref, depth_ref, moved_ref, light_ref = refs[:7]
    result_ref, token_ref, uptake_ref = refs[-3:]
    token_ref[...] = jnp.zeros_like(token_ref)
    tracers, sub_rows, levels, cols = moved_ref.shape
    step = pl.program_id(0)
    matrix_high, matrix_low = halves(matrix_ref[...])
    for k in range(0, levels, SUB):
        at = slice(k, k + SUB)
        level = (first_level + step * levels + k + subs_of((SUB, cols))).astype(jnp.float32)
        light = [light_ref[r, at] for r in range(sub_rows)]
        food = [moved_ref[0, r, at] for r in range(sub_rows)]
        both = [light[r] * food[r] for r in range(sub_rows)]

        def uptake(t, _):
            for r in range(sub_rows):
                scale = (half_ref[t] + food[r]) * (light[r] + dim_ref[t])
                value = growth_ref[t] * moved_ref[t, r, at] * (both[r] / scale)
                uptake_ref[pl.ds(t * SUB, SUB), r * cols : (r + 1) * cols] = value
            return _

        lax.fori_loop(0, tracers, uptake, 0, unroll=4)
        amount = uptake_ref[...]
        high, low = halves(amount)
        dot = functools.partial(jnp.dot, preferred_element_type=jnp.float32)
        change = dot(matrix_high, high) + (dot(matrix_high, low) + dot(matrix_low, high))
        for r in range(sub_rows):
            depth = jnp.broadcast_to(depth_ref[17 + r : 18 + r, :], (SUB, cols))
            scale = DT_BIO * (level < depth).astype(jnp.float32)
            for t in range(tracers):
                result_ref[t, pl.ds(sub_rows * k + r, SUB, stride=sub_rows), :] = (
                    moved_ref[t, r, at]
                    + scale * change[SUB * t : SUB * (t + 1), r * cols : (r + 1) * cols]
                )


def uptake(cut, all_rows, scalars, matrix, depth, moved, light, result):
    first_part, count = cut
    tracers, sub_rows, _, cols = moved.shape
    operands = [*scalars, matrix, depth, moved, light]
    in_specs = [smem()] * 3 + [
        whole(matrix.shape),
        whole(depth.shape),
        pl.BlockSpec((tracers, sub_rows, SUB, cols), lambda i: (0, 0, i, 0)),
        pl.BlockSpec((sub_rows, SUB, cols), lambda i: (0, i, 0)),
    ]
    aliases = {}
    if result is not None:
        aliases = {len(operands): 0}
        operands.append(result)
        in_specs.append(pl.BlockSpec(memory_space=pl.ANY))
    return pl.pallas_call(
        functools.partial(uptake_kernel, first_part * SUB),
        grid=(count,),
        in_specs=in_specs,
        out_specs=[
            pl.BlockSpec((tracers, SUB * sub_rows, cols), lambda i: (0, first_part + i, 0)),
            whole((SUB, cols)),
        ],
        out_shape=[shaped(tracers, all_rows, cols), shaped(SUB, cols)],
        scratch_shapes=[pltpu.VMEM((tracers * SUB, sub_rows * cols), jnp.float32)],
        input_output_aliases=aliases,
        compiler_params=params(),
    )(*operands)


def warming_kernel(base_ref, sea_ref, floor_ref, heat_ref, mixed_ref, warm_ref, buoyant_ref):
    blocks, sub_rows, levels, cols = heat_ref.shape
    tile_rows = blocks * sub_rows
    level = (base_ref[0] + subs_of((levels, cols))).astype(jnp.float32)
    depth = jnp.where(sea_ref[...] == 1, floor_ref[...], 0).astype(jnp.float32)
    for r in range(tile_rows):
        at = pl.ds(r, levels, stride=tile_rows)
        warm = mixed_ref[0, r] + WARMING_FACTOR * heat_ref[r // sub_rows, r % sub_rows]
        wet = (level < depth[r : r + 1]).astype(jnp.float32)
        warm_ref[at, :] = warm
        buoyant_ref[at, :] = wet * (0.2 * warm - 0.8 * mixed_ref[1, r])


def warming(base, heat, mixed, sea):
    _, tile_rows, levels, cols = mixed.shape
    outs = [shaped(levels * tile_rows, cols)] * 2
    return call_once(warming_kernel, [*sea, heat, mixed], outs, scalars=[base])


def from_before(x, axis):
    return lax.ppermute(x, axis, [(i, i + 1) for i in range(lax.axis_size(axis) - 1)])


def from_after(x, axis):
    return lax.ppermute(x, axis, [(i + 1, i) for i in range(lax.axis_size(axis) - 1)])


def row_pairs():
    blocks, tiles = lax.axis_size("comp"), lax.axis_size("gx")
    places = [b * tiles + tile for tile in range(tiles) for b in range(blocks)]
    return list(zip(places[:-1], places[1:]))


def from_block_before(x):
    return lax.ppermute(x, ("comp", "gx"), row_pairs())


def from_block_after(x):
    return lax.ppermute(x, ("comp", "gx"), [(later, own) for own, later in row_pairs()])


def from_sides(x):
    if lax.axis_size("gy") == 2:
        other = lax.ppermute(x, "gy", [(0, 1), (1, 0)])
        return other, other
    return from_before(x, "gy"), from_after(x, "gy")


def on_device(
    zonal_flow_speed,
    meridional_flow_speed,
    thermal_anomaly,
    brine_anomaly_values,
    marine_indicator,
    seafloor_layer,
    dissolved_species,
    topmost_sunshine,
    attenuation_coefficient,
    peak_intake_speed,
    feedstock_midpoint_constant,
    photon_midpoint_constant,
    stoichiometry_matrix,
):
    group_index = lax.axis_index("comp")
    blocks = lax.axis_size("comp")
    levels, tile_rows, tile_cols = zonal_flow_speed.shape
    tracer_count, level_count = dissolved_species.shape[:2]
    sub_rows = dissolved_species.shape[4]
    ocean = (zonal_flow_speed, meridional_flow_speed, thermal_anomaly, brine_anomaly_values)
    sea = (marine_indicator, seafloor_layer)
    group = group_index.astype(jnp.int32).reshape(1)
    base = group * levels
    place = jnp.stack([lax.axis_index("gy"), lax.axis_size("gy")]).astype(jnp.int32)

    flat = [x.reshape(levels * tile_rows, tile_cols) for x in ocean]
    q = dissolved_species.reshape(tracer_count, level_count, sub_rows, 1, tile_cols)
    parts = levels // SUB
    every = parts * blocks
    sizes = [every - every // 4 - 3 * every // 8, 3 * every // 8, every // 4]
    cuts = [(sum(sizes[:i]), size) for i, size in enumerate(sizes)]
    matrix = call_once(
        spread_kernel,
        [stoichiometry_matrix],
        [shaped(SUB * tracer_count, SUB * tracer_count)],
    )[0]
    scalars_of_uptake = (
        peak_intake_speed,
        feedstock_midpoint_constant,
        photon_midpoint_constant,
    )

    def rims(cut, *after):
        low, high = cut_rows(q, cut[0] * SUB, cut[1] * SUB, after)
        own = [x.reshape(tracer_count, NSUB, cut[1] * SUB, tile_cols) for x in (low, high)]
        return own, (from_block_after(own[0]), from_block_before(own[1]))

    def sides(x):
        return (x, *from_sides(x))

    packed, edge_low, edge_high, ocean_rows = pack_ocean(flat, sea, levels)
    cut0, rims0 = rims(cuts[0], packed)
    up, down, packed = ocean_sides(place, packed, *from_sides(packed), edge_low, edge_high)
    after, before = from_after(up, "gx"), from_before(down, "gx")
    cut1, rims1 = rims(cuts[1], up)
    smix, mixed, send, local, faces, depths = ocean_phase(
        blocks, levels, base, ocean_rows, sea, packed, after, before, cut1
    )
    received = lax.all_to_all(send, "comp", split_axis=0, concat_axis=0, tiled=True)
    depth = lax.dynamic_index_in_dim(depths, group_index, 0, False)
    east_new, north_new = velocities(group, local, faces, received)
    ahead = [(cut0, rims0), (cut1, rims1), rims(cuts[2], depths)]

    surface = topmost_sunshine.reshape(sub_rows, tile_cols)
    carry = jnp.zeros((sub_rows, SUB, tile_cols), jnp.float32)
    heat, result = None, None
    for i, cut in enumerate(cuts):
        waits = list(ahead[i + 2][0]) if i + 2 < len(cuts) else []
        if i > 0:
            waits.append(token)
        near = sides(pack_tracers(*ahead[i], waits))
        moved, light, heat, carry = advection(
            cut,
            level_count,
            attenuation_coefficient,
            surface,
            depth,
            received,
            *ahead[i],
            near,
            carry,
            heat,
            [],
        )
        if i + 3 < len(cuts):
            ahead.append(rims(cuts[i + 3], carry))
        result, token = uptake(
            cut,
            level_count * sub_rows,
            scalars_of_uptake,
            matrix,
            depth,
            moved,
            light,
            result,
        )
    heat = lax.all_to_all(heat, "comp", split_axis=0, concat_axis=0, tiled=True)
    warmed_result, buoyancy = warming(base, heat, mixed, sea)
    fields = (east_new, north_new, warmed_result, smix, buoyancy)
    return (
        *[x.reshape(zonal_flow_speed.shape) for x in fields],
        result.reshape(dissolved_species.shape),
    )


def solution(mesh):
    return jax.shard_map(
        on_device,
        mesh=mesh,
        in_specs=(
            P("comp", "gx", "gy"),
            P("comp", "gx", "gy"),
            P("comp", "gx", "gy"),
            P("comp", "gx", "gy"),
            P("gx", "gy"),
            P("gx", "gy"),
            P(None, None, "gx", "comp", None, "gy"),
            P("gx", "comp", None, "gy"),
            P(),
            P(),
            P(),
            P(),
            P(),
        ),
        out_specs=(
            P("comp", "gx", "gy"),
            P("comp", "gx", "gy"),
            P("comp", "gx", "gy"),
            P("comp", "gx", "gy"),
            P("comp", "gx", "gy"),
            P(None, None, "gx", "comp", None, "gy"),
        ),
        check_vma=False,
    )
```

```python
import functools

import jax
import jax.numpy as jnp
from jax import lax
from jax.experimental import pallas as pl
from jax.experimental.pallas import tpu as pltpu
from jax.sharding import PartitionSpec as P

NSUB = 2
SLOTS = 4 * NSUB
SUB = 8
GROUP = 24
HALF = 64
ENTRIES = 18

DT_FLOW = 0.1
CORIOLIS = 0.3
MIXING = 0.15
COURANT = 0.24
DT_BIO = 0.5
WARMING_FACTOR = 0.5
CLEAR_WATER = 0.5
VMEM_LIMIT = 16 * 1024 * 1024
VMEM_MOST = 62 * 1024 * 1024


def lanes_of(shape):
    return lax.broadcasted_iota(jnp.int32, shape, len(shape) - 1)


def subs_of(shape):
    return lax.broadcasted_iota(jnp.int32, shape, len(shape) - 2)


def turn(x, by, axis):
    by = by % x.shape[axis]
    return x if by == 0 else pltpu.roll(x, by, axis)


def params(limit=VMEM_LIMIT):
    return pltpu.CompilerParams(vmem_limit_bytes=limit)


def whole(shape):
    return pl.BlockSpec(shape, lambda *_: (0,) * len(shape))


def smem():
    return pl.BlockSpec(memory_space=pltpu.SMEM)


def shaped(*shape):
    return jax.ShapeDtypeStruct(shape, jnp.float32)


def halves(x):
    high = x.astype(jnp.bfloat16)
    return high, (x - high.astype(jnp.float32)).astype(jnp.bfloat16)


def sums_above(x):
    sub = subs_of(x.shape)
    running, total = x, x
    by = 1
    while by < x.shape[0]:
        running = running + jnp.where(sub >= by, turn(running, by, 0), 0.0)
        total = total + turn(total, by, 0)
        by *= 2
    return jnp.where(sub >= 1, turn(running, 1, 0), 0.0), total


def cut_kernel(start, size, q_ref, *refs):
    outs, sems = refs[-3:-1], refs[-1]
    rows = q_ref.shape[2]
    copies = [
        pltpu.make_async_copy(
            q_ref.at[:, pl.ds(start, size), r], outs[r // NSUB].at[:, r % NSUB], sems.at[r]
        )
        for r in range(rows)
    ]
    for copy in copies:
        copy.start()
    for copy in copies:
        copy.wait()


def cut_rows(q, start, size, after):
    tracers, _, rows, _, cols = q.shape
    anywhere = pl.BlockSpec(memory_space=pl.ANY)
    return pl.pallas_call(
        functools.partial(cut_kernel, start, size),
        in_specs=[anywhere] * (1 + len(after)),
        out_specs=[anywhere] * 2,
        out_shape=[shaped(tracers, NSUB, size, 1, cols)] * 2,
        scratch_shapes=[pltpu.SemaphoreType.DMA((rows,))],
        compiler_params=params(),
    )(q, *after)


def both_ends(acc):
    return jnp.where(lanes_of(acc.shape) % SLOTS < SLOTS // 2, acc, turn(acc, SLOTS // 2, 1))


def pack_tracers_kernel(low_ref, high_ref, after_ref, before_ref, packed_ref):
    tracers, _, _, cols = low_ref.shape
    lane = lanes_of((SUB, cols))
    for pair in range(tracers // 2):
        acc = jnp.zeros((SUB, cols), jnp.float32)
        for odd in range(2):
            t = 2 * pair + odd
            rows = [before_ref[t, 1], low_ref[t, 0], low_ref[t, 1], high_ref[t, 0], high_ref[t, 1]]
            for r, x in enumerate(rows + [after_ref[t, 0]]):
                at = HALF * odd + SLOTS * (r + 1)
                acc = jnp.where(lane // SLOTS == at // SLOTS, turn(x, at + NSUB, 1), acc)
        packed_ref[pair] = both_ends(acc)


def pack_tracers(own, rim, after):
    tracers, _, levels, cols = own[0].shape
    rows = pl.BlockSpec((tracers, NSUB, SUB, cols), lambda i: (0, 0, i, 0))
    return pl.pallas_call(
        functools.partial(ignoring, len(after), pack_tracers_kernel),
        grid=(levels // SUB,),
        in_specs=[pl.BlockSpec(memory_space=pl.ANY)] * len(after) + [rows] * 4,
        out_specs=pl.BlockSpec((tracers // 2, SUB, cols), lambda i: (0, i, 0)),
        out_shape=shaped(tracers // 2, levels, cols),
        compiler_params=params(),
    )(*after, *own, *rim)


def ignoring(count, kernel, *refs):
    kernel(*refs[count:])


def call_once(kernel, operands, outs, scratch=(), scalars=(), after=(), limit=VMEM_LIMIT):
    return pl.pallas_call(
        functools.partial(ignoring, len(after), kernel),
        grid=(1,),
        in_specs=[pl.BlockSpec(memory_space=pl.ANY)] * len(after)
        + [smem()] * len(scalars)
        + [whole(x.shape) for x in operands],
        out_specs=[whole(x.shape) for x in outs],
        out_shape=outs,
        scratch_shapes=list(scratch),
        compiler_params=params(limit),
    )(*after, *scalars, *operands)


def pack_ocean_kernel(levels, *refs):
    u_ref, v_ref, t_ref, s_ref, sea_ref, floor_ref, packed_ref, edge_low_ref, edge_high_ref, row_ref = refs
    tile_rows, cols = sea_ref.shape
    lane = lanes_of((levels, cols))
    edge_low_ref[4 * NSUB] = jnp.zeros((levels, cols), jnp.float32)
    edge_high_ref[4 * NSUB] = jnp.zeros((levels, cols), jnp.float32)
    for f, ref in enumerate((u_ref, v_ref, t_ref, s_ref)):
        acc = jnp.zeros((levels, cols), jnp.float32)
        for r in range(tile_rows):
            x = ref[pl.ds(r, levels, stride=tile_rows), :]
            row_ref[f, r] = x
            acc = jnp.where(lane // SLOTS == r, turn(x, SLOTS * r + NSUB, 1), acc)
            if r < NSUB:
                edge_low_ref[NSUB * f + r] = x
            if r >= tile_rows - NSUB:
                edge_high_ref[NSUB * f + r - tile_rows + NSUB] = x
        packed_ref[f] = both_ends(acc)
    depth = jnp.where(sea_ref[...] == 1, floor_ref[...], 0).astype(jnp.float32)
    acc = jnp.zeros((levels, cols), jnp.float32)
    for r in range(tile_rows):
        x = jnp.broadcast_to(depth[r : r + 1], (levels, cols))
        acc = jnp.where(lane // SLOTS == r, turn(x, SLOTS * r + NSUB, 1), acc)
    packed_ref[4] = both_ends(acc)
    edge_low_ref[4 * NSUB, 0:NSUB, :] = depth[0:NSUB]
    edge_high_ref[4 * NSUB, 0:NSUB, :] = depth[tile_rows - NSUB :]


def pack_ocean(flat, sea, levels):
    cols = sea[0].shape[1]
    edge = shaped(4 * NSUB + 1, levels, cols)
    return call_once(
        functools.partial(pack_ocean_kernel, levels),
        [*flat, *sea],
        [shaped(5, levels, cols), edge, edge, shaped(4, sea[0].shape[0], levels, cols)],
        limit=VMEM_MOST,
    )


def with_sides(own, left, right):
    slot = lanes_of(own.shape) % SLOTS
    ends = jnp.where(slot < NSUB, left, right)
    return jnp.where((slot < NSUB) | (slot >= SLOTS - NSUB), ends, own)


def ocean_sides_kernel(place_ref, own_ref, left_ref, right_ref, low_ref, high_ref, up_ref, down_ref, out_ref):
    _, levels, cols = own_ref.shape
    rows = low_ref.shape[0]
    up_ref[0:rows] = low_ref[...]
    down_ref[0:rows] = high_ref[...]
    slot = lanes_of((levels, cols)) % SLOTS
    first, last = place_ref[0] == 0, place_ref[0] == place_ref[1] - 1
    for f in range(5):
        x = with_sides(own_ref[f], left_ref[f], right_ref[f])
        if f == 4:
            x = jnp.where((slot < NSUB) & first, 0.0, x)
            x = jnp.where((slot >= SLOTS - NSUB) & last, 0.0, x)
        out_ref[f] = x
        up_ref[rows + f] = x
        down_ref[rows + f] = x


def ocean_sides(place, own, left, right, low, high):
    edge = shaped(low.shape[0] + 5, *low.shape[1:])
    return call_once(
        ocean_sides_kernel,
        [own, left, right, low, high],
        [edge, edge, shaped(*own.shape)],
        scalars=[place],
    )


def ocean_kernel(blocks, levels, *refs):
    base_ref, own_ref, sea_ref, floor_ref, packed_ref, after_ref, before_ref = refs[:7]
    smix_ref, mixed_ref, send_ref, local_ref, faces_ref, depths_ref, press_ref, total_ref = refs[7:]
    tile_rows, cols = sea_ref.shape
    sub_rows = tile_rows // blocks
    shape = (levels, cols)
    lane = lanes_of(shape)
    first, last = lane == 0, lane == cols - 1
    level = (base_ref[0] + subs_of(shape)).astype(jnp.float32)
    rims = after_ref.shape[0] - 5

    def packed(f):
        after, before = after_ref[rims + f], before_ref[rims + f]
        rim = jnp.where(lane < NSUB * SLOTS, after, jnp.where(lane >= cols - NSUB * SLOTS, before, 0.0))
        return jnp.concatenate([packed_ref[f], rim], axis=1)

    def row_after(x):
        return turn(x, -SLOTS, 1)

    def row_before(x):
        return turn(x, SLOTS, 1)

    up, vp, tp, sp, dp = [packed(f) for f in range(5)]
    wide = jnp.concatenate([level, level], axis=1)
    wet = (wide < dp).astype(jnp.float32)
    heavy = wet * (-0.2 * tp + 0.8 * sp)
    above, total = sums_above(heavy)
    press = above + 0.5 * heavy
    east = up + DT_FLOW * (CORIOLIS * vp - (row_after(press) - press))
    north = vp + DT_FLOW * (-CORIOLIS * up - (turn(press, -1, 1) - press))
    open_n = wet * turn(wet, -1, 1)
    flux_t = open_n * (turn(tp, -1, 1) - tp)
    flux_s = open_n * (turn(sp, -1, 1) - sp)
    total_e, total_n = row_after(total) - total, turn(total, -1, 1) - total
    depth_e, depth_n = jnp.minimum(dp, row_after(dp)), jnp.minimum(dp, turn(dp, -1, 1))

    def window(x, g):
        x = turn(x, -SLOTS * (sub_rows * g - NSUB), 1)[:, 0:cols]
        return jnp.where(lane < HALF, x, turn(x, HALF, 1))

    for g in range(blocks):
        send_ref[g, 13] = window(east, g)
        send_ref[g, 14] = window(north, g)
        send_ref[g, 15, 13:14, :] = window(total_e, g)[0:1]
        send_ref[g, 15, 14:15, :] = window(total_n, g)[0:1]
        send_ref[g, 15, 15:16, :] = jnp.zeros((1, cols), jnp.float32)
        depths_ref[g, 24:25, :] = window(depth_e, g)[0:1]
        depths_ref[g, 25:26, :] = window(depth_n, g)[0:1]
        depths_ref[g, 26:27, :] = window(dp, g)[0:1]

    slot = lanes_of(tp.shape) % SLOTS

    def edges(x, other):
        x = jnp.where(slot == 0, turn(x, -6, 1), other)
        return x[:, 0:cols], x[:, cols:]

    edge_p, edge_w = edges(press, press), edges(wet, wet)
    edge_t, edge_s = edges(tp, flux_t), edges(sp, flux_s)
    edge_total, edge_depth = edges(total, total), edges(dp, dp)

    def edge(pair, r):
        at = r % tile_rows
        return turn(pair[0] if 0 <= r < tile_rows else pair[1], -(SLOTS * at + 1), 1)

    depth = jnp.where(sea_ref[...] == 1, floor_ref[...], 0).astype(jnp.float32)

    def row_of(f, r):
        if r < 0:
            return before_ref[NSUB * f + r + NSUB]
        if r >= tile_rows:
            return after_ref[NSUB * f + r - tile_rows]
        return own_ref[f, r]

    def depth_of(r):
        if r < 0:
            x = before_ref[4 * NSUB, r + NSUB : r + NSUB + 1, :]
        elif r >= tile_rows:
            x = after_ref[4 * NSUB, r - tile_rows : r - tile_rows + 1, :]
        else:
            x = depth[r : r + 1]
        return jnp.broadcast_to(x, shape)

    lo, hi = -NSUB, tile_rows + NSUB
    for r in range(lo, hi):
        heavy = (level < depth_of(r)).astype(jnp.float32) * (-0.2 * row_of(2, r) + 0.8 * row_of(3, r))
        above, total = sums_above(heavy)
        press_ref[r - lo] = above + 0.5 * heavy
        total_ref[r - lo] = total

    def windows(r, before):
        for g in range(blocks):
            j = r - (sub_rows * g - before)
            if 0 <= j < sub_rows + 1 + before:
                yield g, j

    flux_before = [None, None]
    for r in range(lo, hi - 1):
        press, press_e = press_ref[r - lo], press_ref[r - lo + 1]
        total, total_a = total_ref[r - lo], total_ref[r - lo + 1]
        d, d_e = depth_of(r), depth_of(r + 1)
        d_n = jnp.where(last, edge(edge_depth, r), turn(d, -1, 1))
        face_e, face_n = jnp.minimum(d, d_e), jnp.minimum(d, d_n)
        u, v = row_of(0, r), row_of(1, r)
        east = u + DT_FLOW * (CORIOLIS * v - (press_e - press))
        press_n = jnp.where(last, edge(edge_p, r), turn(press, -1, 1))
        north = v + DT_FLOW * (-CORIOLIS * u - (press_n - press))
        total_e = total_a - total
        total_n = jnp.where(last, edge(edge_total, r), turn(total, -1, 1)) - total
        for g, j in windows(r, 2):
            send_ref[g, j] = east
            send_ref[g, 15, j : j + 1, :] = total_e[0:1]
            depths_ref[g, j : j + 1, :] = face_e[0:1]
        for g, j in windows(r, 1):
            send_ref[g, 7 + j] = north
            send_ref[g, 15, 7 + j : 8 + j, :] = total_n[0:1]
            depths_ref[g, 8 + j : 9 + j, :] = face_n[0:1]
            depths_ref[g, 16 + j : 17 + j, :] = d[0:1]
        if 0 <= r < tile_rows:
            local_ref[0, r] = east
            local_ref[1, r] = north
            faces_ref[0, r : r + 1, :] = face_e[0:1]
            faces_ref[1, r : r + 1, :] = face_n[0:1]
            for g in range(blocks):
                send_ref[g, 16, r : r + 1, :] = total_e[0:1]
                send_ref[g, 17, r : r + 1, :] = total_n[0:1]
        if r < -1 or r >= tile_rows:
            continue
        open_e = (level < face_e).astype(jnp.float32)
        open_n = (level < face_n).astype(jnp.float32)
        for i, (f, ends) in enumerate(((2, edge_t), (3, edge_s))):
            x = row_of(f, r)
            flux_e = open_e * (row_of(f, r + 1) - x)
            if r >= 0:
                ending = edge(ends, r)
                flux_n = open_n * (jnp.where(last, ending, turn(x, -1, 1)) - x)
                flux_b = jnp.where(first, ending, turn(flux_n, 1, 1))
                mixed = x + MIXING * ((flux_e - flux_before[i]) + (flux_n - flux_b))
                mixed_ref[i, r] = mixed
                if i == 1:
                    smix_ref[pl.ds(r, levels, stride=tile_rows), :] = mixed
            flux_before[i] = flux_e


def ocean_phase(blocks, levels, base, own, sea, packed, rim_after, rim_before, after):
    tile_rows, cols = sea[0].shape
    outs = [
        shaped(levels * tile_rows, cols),
        shaped(2, tile_rows, levels, cols),
        shaped(blocks, ENTRIES, levels, cols),
        shaped(2, tile_rows, levels, cols),
        shaped(2, tile_rows, cols),
        shaped(blocks, 32, cols),
    ]
    tall = tile_rows + 2 * NSUB
    return call_once(
        functools.partial(ocean_kernel, blocks, levels),
        [own, *sea, packed, rim_after, rim_before],
        outs,
        [pltpu.VMEM((tall, levels, cols), jnp.float32)] * 2,
        [base],
        after,
    )


def velocity_kernel(group_ref, local_ref, faces_ref, received_ref, east_ref, north_ref):
    blocks = received_ref.shape[0]
    _, tile_rows, levels, cols = local_ref.shape
    group = group_ref[0]
    level = (group * levels + subs_of((levels, cols))).astype(jnp.float32)
    for f, out_ref in enumerate((east_ref, north_ref)):
        above = jnp.zeros((tile_rows, cols), jnp.float32)
        for s in range(blocks - 1):
            above = above + jnp.where(s < group, received_ref[s, f], 0.0)
        for r in range(tile_rows):
            x = local_ref[f, r] - DT_FLOW * jnp.broadcast_to(above[r : r + 1], (levels, cols))
            x = jnp.where(level < faces_ref[f, r : r + 1, :], x, 0.0)
            out_ref[pl.ds(r, levels, stride=tile_rows), :] = x


def velocities(group, local, faces, received):
    blocks = received.shape[0]
    _, tile_rows, levels, cols = local.shape
    out = shaped(levels * tile_rows, cols)
    return pl.pallas_call(
        velocity_kernel,
        grid=(1,),
        in_specs=[
            smem(),
            whole(local.shape),
            whole(faces.shape),
            pl.BlockSpec((blocks, 2, levels, cols), lambda i: (0, ENTRIES // 2 - 1, 0, 0)),
        ],
        out_specs=[whole(out.shape)] * 2,
        out_shape=[out] * 2,
        compiler_params=params(),
    )(group, local, faces, received)


def advection_kernel(first_part, parts, level_count, *refs):
    (
        absorb_ref,
        surface_ref,
        depth_ref,
        totals_ref,
        courant_ref,
        low_ref,
        high_ref,
        after_ref,
        before_ref,
        side_ref,
        left_ref,
        right_ref,
        carry_ref,
    ) = refs[:13]
    moved_ref, light_ref, heat_ref, carry_out_ref = refs[-10:-6]
    coef_ref, side_coef_ref, edge_ref, running_ref, above_ref, shift_ref = refs[-6:]
    step = pl.program_id(0)
    tracers, _, _, cols = low_ref.shape
    levels = courant_ref.shape[2]
    sub_rows = surface_ref.shape[0]
    rows = sub_rows + 2
    shape = (levels, cols)
    lane = lanes_of(shape)
    first, last = lane == 0, lane == cols - 1
    first8, last8 = first[0:SUB], last[0:SUB]
    slot = lane % SLOTS

    @pl.when(step == 0)
    def _():
        running_ref[...] = carry_ref[...]
        size = (2 * cols, 2 * cols)
        source, to = subs_of(size) % cols, lanes_of(size)
        hit = ((to < cols) & (source == to + 1)) | ((to >= cols) & (source == to - cols - 1))
        shift_ref[...] = hit.astype(jnp.float32).astype(jnp.bfloat16)

    part = first_part + step
    above = jnp.zeros(above_ref.shape, jnp.float32)
    for s in range(totals_ref.shape[0] - 1):
        above = above + jnp.where(s < part // parts, totals_ref[s, 0], 0.0)
    above_ref[...] = above
    level = (part * levels + subs_of(shape)).astype(jnp.float32)

    def spread(ref, r):
        return jnp.broadcast_to(ref[r : r + 1, :], shape)

    def courant(entry, face):
        x = courant_ref[0, entry] - DT_FLOW * spread(above_ref, entry)
        return COURANT * jnp.tanh(jnp.where(level < spread(depth_ref, face), x, 0.0))

    def coefficients(wet, ce, ce_b, cn, cn_b):
        return (
            wet
            * (
                1.0
                - jnp.maximum(ce, 0.0)
                + jnp.minimum(ce_b, 0.0)
                - jnp.maximum(cn, 0.0)
                + jnp.minimum(cn_b, 0.0)
            ),
            -wet * jnp.minimum(ce, 0.0),
            wet * jnp.maximum(ce_b, 0.0),
            -wet * jnp.minimum(cn, 0.0),
            wet * jnp.maximum(cn_b, 0.0),
        )

    side_e, side_n = courant(13, 24), courant(14, 25)
    wet = (level < spread(depth_ref, 26)).astype(jnp.float32)
    packed_coef = coefficients(wet, side_e, turn(side_e, SLOTS, 1), side_n, turn(side_n, 1, 1))
    for i in range(5):
        side_coef_ref[i] = packed_coef[i]
    ce_b = courant(0, 0)
    for j in range(rows):
        ce, cn = courant(1 + j, 1 + j), courant(7 + j, 8 + j)
        cn_b = jnp.where(first, turn(side_n, -(SLOTS * (j + 1) + 1), 1), turn(cn, 1, 1))
        wet = (level < spread(depth_ref, 16 + j)).astype(jnp.float32)
        for i, x in enumerate(coefficients(wet, ce, ce_b, cn, cn_b)):
            coef_ref[5 * j + i] = x
        ce_b = ce
    for i in range(side_ref.shape[0]):
        x = with_sides(side_ref[i], left_ref[i], right_ref[i])
        edge_ref[i, 0] = jnp.where(slot == 0, turn(x, -6, 1), x)
        x = (
            (side_coef_ref[0] * x + side_coef_ref[1] * turn(x, -SLOTS, 1))
            + (side_coef_ref[2] * turn(x, SLOTS, 1) + side_coef_ref[3] * turn(x, -1, 1))
            + side_coef_ref[4] * turn(x, 1, 1)
        )
        edge_ref[i, 1] = jnp.where(slot == 0, turn(x, -6, 1), x)

    layer = 2.0 / level_count
    zero = jnp.zeros((SUB, cols), jnp.float32)
    for k in range(0, levels, SUB):
        at = slice(k, k + SUB)

        def shifted(tiles):
            high, low = halves(jnp.concatenate(tiles, axis=0))
            return jnp.dot(
                jnp.concatenate([high, low], axis=1),
                shift_ref[...],
                preferred_element_type=jnp.float32,
            )

        def stencil(x, j, edge, beside):
            north = jnp.where(last8, edge, beside[:, :cols])
            south = jnp.where(first8, edge, beside[:, cols:])
            return (
                (coef_ref[5 * j, at] * x[1] + coef_ref[5 * j + 1, at] * x[2])
                + (coef_ref[5 * j + 2, at] * x[0] + coef_ref[5 * j + 3, at] * north)
                + coef_ref[5 * j + 4, at] * south
            )

        def advect(i, sums):
            sums = list(sums)
            fields = []
            for t in range(GROUP):
                t = GROUP * i + t
                rows_of = (before_ref, low_ref, high_ref, after_ref)
                x = [ref[t, n, at] for ref in rows_of for n in range(NSUB)]
                fields.append(x)
            for stage in range(NSUB):
                inner = range(1 + stage, rows + 1 - stage)
                beside = shifted([x[j - stage] for x in fields for j in inner])
                for t, x in enumerate(fields):
                    edges = edge_ref[GROUP // 2 * i + t // 2, stage, at]
                    fresh = []
                    for n, j in enumerate(inner):
                        edge = turn(edges, -(HALF * (t % 2) + SLOTS * j + 1), 1)
                        row = SUB * (len(inner) * t + n)
                        fresh.append(
                            stencil(x[n : n + 3], j - 1, edge, beside[row : row + SUB])
                        )
                    fields[t] = fresh
            for t, x in enumerate(fields):
                for r in range(sub_rows):
                    moved_ref[GROUP * i + t, r, at] = x[r]
                    sums[r] = sums[r] + absorb_ref[GROUP * i + t] * x[r]
            return tuple(sums)

        sums = (zero,) * sub_rows
        for i in range(tracers // GROUP):
            sums = advect(i, sums)
        for r in range(sub_rows):
            optical = layer * (CLEAR_WATER + sums[r])
            above, total = sums_above(optical)
            through = jnp.exp(-(running_ref[r] + above))
            running_ref[r] = running_ref[r] + total
            surface = jnp.broadcast_to(surface_ref[r : r + 1, :], (SUB, cols))
            light_ref[r, at] = surface * through * jnp.exp(-0.5 * optical)
            wet = (level[at] < jnp.broadcast_to(depth_ref[17 + r : 18 + r, :], (SUB, cols))).astype(
                jnp.float32
            )
            heat_ref[0, r, at] = wet * surface * through * (1.0 - jnp.exp(-optical)) / layer
    carry_out_ref[...] = running_ref[...]


def advection(cut, level_count, absorb, surface, depth, received, own, rim, sides, carry, heat, after):
    first_part, count = cut
    tracers, _, _, cols = own[0].shape
    every, _, levels, _ = received.shape
    parts = levels // SUB
    sub_rows = surface.shape[0]
    rows = pl.BlockSpec((tracers, NSUB, SUB, cols), lambda i: (0, 0, i, 0))
    side = pl.BlockSpec((tracers // 2, SUB, cols), lambda i: (0, i, 0))
    operands = [absorb, surface, depth, received, received, *own, *rim, *sides, carry]
    in_specs = [
        smem(),
        whole(surface.shape),
        whole(depth.shape),
        pl.BlockSpec((every, 1, levels, cols), lambda i: (0, 15, 0, 0)),
        pl.BlockSpec(
            (1, ENTRIES, SUB, cols),
            lambda i: ((first_part + i) // parts, 0, (first_part + i) % parts, 0),
        ),
        rows,
        rows,
        rows,
        rows,
        side,
        side,
        side,
        whole(carry.shape),
    ]
    aliases = {}
    if heat is not None:
        aliases = {len(operands): 2}
        operands.append(heat)
    operands += after
    in_specs += [pl.BlockSpec(memory_space=pl.ANY)] * (len(operands) - len(in_specs))
    outs = [
        shaped(tracers, sub_rows, count * SUB, cols),
        shaped(sub_rows, count * SUB, cols),
        shaped(every, sub_rows, levels, cols),
        shaped(*carry.shape),
    ]
    return pl.pallas_call(
        functools.partial(advection_kernel, first_part, parts, level_count),
        grid=(count,),
        in_specs=in_specs,
        out_specs=[
            pl.BlockSpec((tracers, sub_rows, SUB, cols), lambda i: (0, 0, i, 0)),
            pl.BlockSpec((sub_rows, SUB, cols), lambda i: (0, i, 0)),
            pl.BlockSpec(
                (1, sub_rows, SUB, cols),
                lambda i: ((first_part + i) // parts, 0, (first_part + i) % parts, 0),
            ),
            whole(carry.shape),
        ],
        out_shape=outs,
        scratch_shapes=[
            pltpu.VMEM((5 * (sub_rows + 2), SUB, cols), jnp.float32),
            pltpu.VMEM((5, SUB, cols), jnp.float32),
            pltpu.VMEM((tracers // 2, 2, SUB, cols), jnp.float32),
            pltpu.VMEM((sub_rows, SUB, cols), jnp.float32),
            pltpu.VMEM((levels, cols), jnp.float32),
            pltpu.VMEM((2 * cols, 2 * cols), jnp.bfloat16),
        ],
        input_output_aliases=aliases,
        compiler_params=params(),
    )(*operands)


def spread_kernel(matrix_ref, out_ref):
    tracers = matrix_ref.shape[0]
    size = tracers * SUB
    tall = (subs_of((size, tracers)) // SUB == lanes_of((size, tracers))).astype(jnp.float32)
    wide = (lanes_of((tracers, size)) // SUB == subs_of((tracers, size))).astype(jnp.float32)
    exact = functools.partial(
        jnp.dot, precision=lax.Precision.HIGHEST, preferred_element_type=jnp.float32
    )
    same = subs_of((size, size)) % SUB == lanes_of((size, size)) % SUB
    out_ref[...] = jnp.where(same, exact(exact(tall, matrix_ref[...]), wide), 0.0)


def uptake_kernel(first_level, *refs):
    growth_ref, half_ref, dim_ref, matrix_ref, depth_ref, moved_ref, light_ref = refs[:7]
    result_ref, token_ref, uptake_ref = refs[-3:]
    token_ref[...] = jnp.zeros_like(token_ref)
    tracers, sub_rows, levels, cols = moved_ref.shape
    step = pl.program_id(0)
    matrix_high, matrix_low = halves(matrix_ref[...])
    for k in range(0, levels, SUB):
        at = slice(k, k + SUB)
        level = (first_level + step * levels + k + subs_of((SUB, cols))).astype(jnp.float32)
        light = [light_ref[r, at] for r in range(sub_rows)]
        food = [moved_ref[0, r, at] for r in range(sub_rows)]
        both = [light[r] * food[r] for r in range(sub_rows)]

        def uptake(t, _):
            for r in range(sub_rows):
                scale = (half_ref[t] + food[r]) * (light[r] + dim_ref[t])
                value = growth_ref[t] * moved_ref[t, r, at] * (both[r] / scale)
                uptake_ref[pl.ds(t * SUB, SUB), r * cols : (r + 1) * cols] = value
            return _

        lax.fori_loop(0, tracers, uptake, 0, unroll=4)
        amount = uptake_ref[...]
        high, low = halves(amount)
        dot = functools.partial(jnp.dot, preferred_element_type=jnp.float32)
        change = dot(matrix_high, high) + (dot(matrix_high, low) + dot(matrix_low, high))
        for r in range(sub_rows):
            depth = jnp.broadcast_to(depth_ref[17 + r : 18 + r, :], (SUB, cols))
            scale = DT_BIO * (level < depth).astype(jnp.float32)
            for t in range(tracers):
                result_ref[t, pl.ds(sub_rows * k + r, SUB, stride=sub_rows), :] = (
                    moved_ref[t, r, at]
                    + scale * change[SUB * t : SUB * (t + 1), r * cols : (r + 1) * cols]
                )


def uptake(cut, all_rows, scalars, matrix, depth, moved, light, result):
    first_part, count = cut
    tracers, sub_rows, _, cols = moved.shape
    operands = [*scalars, matrix, depth, moved, light]
    in_specs = [smem()] * 3 + [
        whole(matrix.shape),
        whole(depth.shape),
        pl.BlockSpec((tracers, sub_rows, SUB, cols), lambda i: (0, 0, i, 0)),
        pl.BlockSpec((sub_rows, SUB, cols), lambda i: (0, i, 0)),
    ]
    aliases = {}
    if result is not None:
        aliases = {len(operands): 0}
        operands.append(result)
        in_specs.append(pl.BlockSpec(memory_space=pl.ANY))
    return pl.pallas_call(
        functools.partial(uptake_kernel, first_part * SUB),
        grid=(count,),
        in_specs=in_specs,
        out_specs=[
            pl.BlockSpec((tracers, SUB * sub_rows, cols), lambda i: (0, first_part + i, 0)),
            whole((SUB, cols)),
        ],
        out_shape=[shaped(tracers, all_rows, cols), shaped(SUB, cols)],
        scratch_shapes=[pltpu.VMEM((tracers * SUB, sub_rows * cols), jnp.float32)],
        input_output_aliases=aliases,
        compiler_params=params(),
    )(*operands)


def warming_kernel(base_ref, sea_ref, floor_ref, heat_ref, mixed_ref, warm_ref, buoyant_ref):
    blocks, sub_rows, levels, cols = heat_ref.shape
    tile_rows = blocks * sub_rows
    level = (base_ref[0] + subs_of((levels, cols))).astype(jnp.float32)
    depth = jnp.where(sea_ref[...] == 1, floor_ref[...], 0).astype(jnp.float32)
    for r in range(tile_rows):
        at = pl.ds(r, levels, stride=tile_rows)
        warm = mixed_ref[0, r] + WARMING_FACTOR * heat_ref[r // sub_rows, r % sub_rows]
        wet = (level < depth[r : r + 1]).astype(jnp.float32)
        warm_ref[at, :] = warm
        buoyant_ref[at, :] = wet * (0.2 * warm - 0.8 * mixed_ref[1, r])


def warming(base, heat, mixed, sea):
    _, tile_rows, levels, cols = mixed.shape
    outs = [shaped(levels * tile_rows, cols)] * 2
    return call_once(warming_kernel, [*sea, heat, mixed], outs, scalars=[base])


def from_before(x, axis):
    return lax.ppermute(x, axis, [(i, i + 1) for i in range(lax.axis_size(axis) - 1)])


def from_after(x, axis):
    return lax.ppermute(x, axis, [(i + 1, i) for i in range(lax.axis_size(axis) - 1)])


def row_pairs():
    blocks, tiles = lax.axis_size("comp"), lax.axis_size("gx")
    places = [b * tiles + tile for tile in range(tiles) for b in range(blocks)]
    return list(zip(places[:-1], places[1:]))


def from_block_before(x):
    return lax.ppermute(x, ("comp", "gx"), row_pairs())


def from_block_after(x):
    return lax.ppermute(x, ("comp", "gx"), [(later, own) for own, later in row_pairs()])


def from_sides(x):
    if lax.axis_size("gy") == 2:
        other = lax.ppermute(x, "gy", [(0, 1), (1, 0)])
        return other, other
    return from_before(x, "gy"), from_after(x, "gy")


def on_device(
    zonal_flow_speed,
    meridional_flow_speed,
    thermal_anomaly,
    brine_anomaly_values,
    marine_indicator,
    seafloor_layer,
    dissolved_species,
    topmost_sunshine,
    attenuation_coefficient,
    peak_intake_speed,
    feedstock_midpoint_constant,
    photon_midpoint_constant,
    stoichiometry_matrix,
):
    group_index = lax.axis_index("comp")
    blocks = lax.axis_size("comp")
    levels, tile_rows, tile_cols = zonal_flow_speed.shape
    tracer_count, level_count = dissolved_species.shape[:2]
    sub_rows = dissolved_species.shape[4]
    ocean = (zonal_flow_speed, meridional_flow_speed, thermal_anomaly, brine_anomaly_values)
    sea = (marine_indicator, seafloor_layer)
    group = group_index.astype(jnp.int32).reshape(1)
    base = group * levels
    place = jnp.stack([lax.axis_index("gy"), lax.axis_size("gy")]).astype(jnp.int32)

    flat = [x.reshape(levels * tile_rows, tile_cols) for x in ocean]
    q = dissolved_species.reshape(tracer_count, level_count, sub_rows, 1, tile_cols)
    parts = levels // SUB
    every = parts * blocks
    sizes = [every - 5 * every // 8, every // 4, every // 4, every // 8]
    cuts = [(sum(sizes[:i]), size) for i, size in enumerate(sizes)]
    matrix = call_once(
        spread_kernel,
        [stoichiometry_matrix],
        [shaped(SUB * tracer_count, SUB * tracer_count)],
    )[0]
    scalars_of_uptake = (
        peak_intake_speed,
        feedstock_midpoint_constant,
        photon_midpoint_constant,
    )

    def rims(cut, *after):
        low, high = cut_rows(q, cut[0] * SUB, cut[1] * SUB, after)
        own = [x.reshape(tracer_count, NSUB, cut[1] * SUB, tile_cols) for x in (low, high)]
        return own, (from_block_after(own[0]), from_block_before(own[1]))

    def sides(x):
        return (x, *from_sides(x))

    packed, edge_low, edge_high, ocean_rows = pack_ocean(flat, sea, levels)
    cut0, rims0 = rims(cuts[0], packed)
    up, down, packed = ocean_sides(place, packed, *from_sides(packed), edge_low, edge_high)
    after, before = from_after(up, "gx"), from_before(down, "gx")
    cut1, rims1 = rims(cuts[1], after, before)
    smix, mixed, send, local, faces, depths = ocean_phase(
        blocks, levels, base, ocean_rows, sea, packed, after, before, cut1
    )
    received = lax.all_to_all(send, "comp", split_axis=0, concat_axis=0, tiled=True)
    depth = lax.dynamic_index_in_dim(depths, group_index, 0, False)
    east_new, north_new = velocities(group, local, faces, received)
    ahead = [(cut0, rims0), (cut1, rims1), rims(cuts[2], depths)]

    surface = topmost_sunshine.reshape(sub_rows, tile_cols)
    carry = jnp.zeros((sub_rows, SUB, tile_cols), jnp.float32)
    heat, result = None, None
    for i, cut in enumerate(cuts):
        waits = list(ahead[i + 2][0]) if i + 2 < len(cuts) else []
        if i > 0:
            waits.append(token)
        near = sides(pack_tracers(*ahead[i], waits))
        moved, light, heat, carry = advection(
            cut,
            level_count,
            attenuation_coefficient,
            surface,
            depth,
            received,
            *ahead[i],
            near,
            carry,
            heat,
            [],
        )
        if i + 3 < len(cuts):
            ahead.append(rims(cuts[i + 3], carry))
        result, token = uptake(
            cut,
            level_count * sub_rows,
            scalars_of_uptake,
            matrix,
            depth,
            moved,
            light,
            result,
        )
    heat = lax.all_to_all(heat, "comp", split_axis=0, concat_axis=0, tiled=True)
    warmed_result, buoyancy = warming(base, heat, mixed, sea)
    fields = (east_new, north_new, warmed_result, smix, buoyancy)
    return (
        *[x.reshape(zonal_flow_speed.shape) for x in fields],
        result.reshape(dissolved_species.shape),
    )


def solution(mesh):
    return jax.shard_map(
        on_device,
        mesh=mesh,
        in_specs=(
            P("comp", "gx", "gy"),
            P("comp", "gx", "gy"),
            P("comp", "gx", "gy"),
            P("comp", "gx", "gy"),
            P("gx", "gy"),
            P("gx", "gy"),
            P(None, None, "gx", "comp", None, "gy"),
            P("gx", "comp", None, "gy"),
            P(),
            P(),
            P(),
            P(),
            P(),
        ),
        out_specs=(
            P("comp", "gx", "gy"),
            P("comp", "gx", "gy"),
            P("comp", "gx", "gy"),
            P("comp", "gx", "gy"),
            P("comp", "gx", "gy"),
            P(None, None, "gx", "comp", None, "gy"),
        ),
        check_vma=False,
    )
```

```python
import functools

import jax
import jax.numpy as jnp
from jax import lax
from jax.experimental import pallas as pl
from jax.experimental.pallas import tpu as pltpu
from jax.sharding import PartitionSpec as P

NSUB = 2
SLOTS = 4 * NSUB
SUB = 8
GROUP = 24
HALF = 64
ENTRIES = 18

DT_FLOW = 0.1
CORIOLIS = 0.3
MIXING = 0.15
COURANT = 0.24
DT_BIO = 0.5
WARMING_FACTOR = 0.5
CLEAR_WATER = 0.5
VMEM_LIMIT = 16 * 1024 * 1024
VMEM_MOST = 62 * 1024 * 1024


def lanes_of(shape):
    return lax.broadcasted_iota(jnp.int32, shape, len(shape) - 1)


def subs_of(shape):
    return lax.broadcasted_iota(jnp.int32, shape, len(shape) - 2)


def turn(x, by, axis):
    by = by % x.shape[axis]
    return x if by == 0 else pltpu.roll(x, by, axis)


def params(limit=VMEM_LIMIT):
    return pltpu.CompilerParams(vmem_limit_bytes=limit)


def whole(shape):
    return pl.BlockSpec(shape, lambda *_: (0,) * len(shape))


def smem():
    return pl.BlockSpec(memory_space=pltpu.SMEM)


def shaped(*shape):
    return jax.ShapeDtypeStruct(shape, jnp.float32)


def halves(x):
    high = x.astype(jnp.bfloat16)
    return high, (x - high.astype(jnp.float32)).astype(jnp.bfloat16)


def sums_above(x):
    sub = subs_of(x.shape)
    running, total = x, x
    by = 1
    while by < x.shape[0]:
        running = running + jnp.where(sub >= by, turn(running, by, 0), 0.0)
        total = total + turn(total, by, 0)
        by *= 2
    return jnp.where(sub >= 1, turn(running, 1, 0), 0.0), total


def cut_kernel(start, size, q_ref, *refs):
    outs, sems = refs[-3:-1], refs[-1]
    rows = q_ref.shape[2]
    copies = [
        pltpu.make_async_copy(
            q_ref.at[:, pl.ds(start, size), r], outs[r // NSUB].at[:, r % NSUB], sems.at[r]
        )
        for r in range(rows)
    ]
    for copy in copies:
        copy.start()
    for copy in copies:
        copy.wait()


def cut_rows(q, start, size, after):
    tracers, _, rows, _, cols = q.shape
    anywhere = pl.BlockSpec(memory_space=pl.ANY)
    return pl.pallas_call(
        functools.partial(cut_kernel, start, size),
        in_specs=[anywhere] * (1 + len(after)),
        out_specs=[anywhere] * 2,
        out_shape=[shaped(tracers, NSUB, size, 1, cols)] * 2,
        scratch_shapes=[pltpu.SemaphoreType.DMA((rows,))],
        compiler_params=params(),
    )(q, *after)


def both_ends(acc):
    return jnp.where(lanes_of(acc.shape) % SLOTS < SLOTS // 2, acc, turn(acc, SLOTS // 2, 1))


def pack_tracers_kernel(low_ref, high_ref, after_ref, before_ref, packed_ref):
    tracers, _, _, cols = low_ref.shape
    lane = lanes_of((SUB, cols))
    for pair in range(tracers // 2):
        acc = jnp.zeros((SUB, cols), jnp.float32)
        for odd in range(2):
            t = 2 * pair + odd
            rows = [before_ref[t, 1], low_ref[t, 0], low_ref[t, 1], high_ref[t, 0], high_ref[t, 1]]
            for r, x in enumerate(rows + [after_ref[t, 0]]):
                at = HALF * odd + SLOTS * (r + 1)
                acc = jnp.where(lane // SLOTS == at // SLOTS, turn(x, at + NSUB, 1), acc)
        packed_ref[pair] = both_ends(acc)


def pack_tracers(own, rim, after):
    tracers, _, levels, cols = own[0].shape
    rows = pl.BlockSpec((tracers, NSUB, SUB, cols), lambda i: (0, 0, i, 0))
    return pl.pallas_call(
        functools.partial(ignoring, len(after), pack_tracers_kernel),
        grid=(levels // SUB,),
        in_specs=[pl.BlockSpec(memory_space=pl.ANY)] * len(after) + [rows] * 4,
        out_specs=pl.BlockSpec((tracers // 2, SUB, cols), lambda i: (0, i, 0)),
        out_shape=shaped(tracers // 2, levels, cols),
        compiler_params=params(),
    )(*after, *own, *rim)


def ignoring(count, kernel, *refs):
    kernel(*refs[count:])


def call_once(kernel, operands, outs, scratch=(), scalars=(), after=(), limit=VMEM_LIMIT):
    return pl.pallas_call(
        functools.partial(ignoring, len(after), kernel),
        grid=(1,),
        in_specs=[pl.BlockSpec(memory_space=pl.ANY)] * len(after)
        + [smem()] * len(scalars)
        + [whole(x.shape) for x in operands],
        out_specs=[whole(x.shape) for x in outs],
        out_shape=outs,
        scratch_shapes=list(scratch),
        compiler_params=params(limit),
    )(*after, *scalars, *operands)


def pack_ocean_kernel(levels, *refs):
    u_ref, v_ref, t_ref, s_ref, sea_ref, floor_ref, packed_ref, edge_low_ref, edge_high_ref, row_ref = refs
    tile_rows, cols = sea_ref.shape
    lane = lanes_of((levels, cols))
    edge_low_ref[4 * NSUB] = jnp.zeros((levels, cols), jnp.float32)
    edge_high_ref[4 * NSUB] = jnp.zeros((levels, cols), jnp.float32)
    for f, ref in enumerate((u_ref, v_ref, t_ref, s_ref)):
        acc = jnp.zeros((levels, cols), jnp.float32)
        for r in range(tile_rows):
            x = ref[pl.ds(r, levels, stride=tile_rows), :]
            row_ref[f, r] = x
            acc = jnp.where(lane // SLOTS == r, turn(x, SLOTS * r + NSUB, 1), acc)
            if r < NSUB:
                edge_low_ref[NSUB * f + r] = x
            if r >= tile_rows - NSUB:
                edge_high_ref[NSUB * f + r - tile_rows + NSUB] = x
        packed_ref[f] = both_ends(acc)
    depth = jnp.where(sea_ref[...] == 1, floor_ref[...], 0).astype(jnp.float32)
    acc = jnp.zeros((levels, cols), jnp.float32)
    for r in range(tile_rows):
        x = jnp.broadcast_to(depth[r : r + 1], (levels, cols))
        acc = jnp.where(lane // SLOTS == r, turn(x, SLOTS * r + NSUB, 1), acc)
    packed_ref[4] = both_ends(acc)
    edge_low_ref[4 * NSUB, 0:NSUB, :] = depth[0:NSUB]
    edge_high_ref[4 * NSUB, 0:NSUB, :] = depth[tile_rows - NSUB :]


def pack_ocean(flat, sea, levels):
    cols = sea[0].shape[1]
    edge = shaped(4 * NSUB + 1, levels, cols)
    return call_once(
        functools.partial(pack_ocean_kernel, levels),
        [*flat, *sea],
        [shaped(5, levels, cols), edge, edge, shaped(4, sea[0].shape[0], levels, cols)],
        limit=VMEM_MOST,
    )


def with_sides(own, left, right):
    slot = lanes_of(own.shape) % SLOTS
    ends = jnp.where(slot < NSUB, left, right)
    return jnp.where((slot < NSUB) | (slot >= SLOTS - NSUB), ends, own)


def ocean_sides_kernel(own_ref, left_ref, right_ref, low_ref, high_ref, up_ref, down_ref, out_ref):
    _, levels, cols = own_ref.shape
    rows = low_ref.shape[0]
    up_ref[0:rows] = low_ref[...]
    down_ref[0:rows] = high_ref[...]
    slot = lanes_of((levels, cols)) % SLOTS
    place = lax.axis_index("gy")
    first, last = place == 0, place == lax.axis_size("gy") - 1
    for f in range(5):
        x = with_sides(own_ref[f], left_ref[f], right_ref[f])
        if f == 4:
            x = jnp.where((slot < NSUB) & first, 0.0, x)
            x = jnp.where((slot >= SLOTS - NSUB) & last, 0.0, x)
        out_ref[f] = x
        up_ref[rows + f] = x
        down_ref[rows + f] = x


def ocean_sides(own, left, right, low, high):
    edge = shaped(low.shape[0] + 5, *low.shape[1:])
    return call_once(
        ocean_sides_kernel,
        [own, left, right, low, high],
        [edge, edge, shaped(*own.shape)],
    )


def ocean_kernel(blocks, levels, *refs):
    own_ref, sea_ref, floor_ref, packed_ref, after_ref, before_ref = refs[:6]
    smix_ref, mixed_ref, send_ref, local_ref, faces_ref, depths_ref, press_ref, total_ref = refs[6:]
    tile_rows, cols = sea_ref.shape
    sub_rows = tile_rows // blocks
    shape = (levels, cols)
    lane = lanes_of(shape)
    first, last = lane == 0, lane == cols - 1
    base = lax.axis_index("comp") * levels
    level = (base + subs_of(shape)).astype(jnp.float32)
    rims = after_ref.shape[0] - 5

    def packed(f):
        after, before = after_ref[rims + f], before_ref[rims + f]
        rim = jnp.where(lane < NSUB * SLOTS, after, jnp.where(lane >= cols - NSUB * SLOTS, before, 0.0))
        return jnp.concatenate([packed_ref[f], rim], axis=1)

    def row_after(x):
        return turn(x, -SLOTS, 1)

    def row_before(x):
        return turn(x, SLOTS, 1)

    up, vp, tp, sp, dp = [packed(f) for f in range(5)]
    wide = jnp.concatenate([level, level], axis=1)
    wet = (wide < dp).astype(jnp.float32)
    heavy = wet * (-0.2 * tp + 0.8 * sp)
    above, total = sums_above(heavy)
    press = above + 0.5 * heavy
    east = up + DT_FLOW * (CORIOLIS * vp - (row_after(press) - press))
    north = vp + DT_FLOW * (-CORIOLIS * up - (turn(press, -1, 1) - press))
    open_n = wet * turn(wet, -1, 1)
    flux_t = open_n * (turn(tp, -1, 1) - tp)
    flux_s = open_n * (turn(sp, -1, 1) - sp)
    total_e, total_n = row_after(total) - total, turn(total, -1, 1) - total
    depth_e, depth_n = jnp.minimum(dp, row_after(dp)), jnp.minimum(dp, turn(dp, -1, 1))

    def window(x, g):
        x = turn(x, -SLOTS * (sub_rows * g - NSUB), 1)[:, 0:cols]
        return jnp.where(lane < HALF, x, turn(x, HALF, 1))

    for g in range(blocks):
        send_ref[g, 13] = window(east, g)
        send_ref[g, 14] = window(north, g)
        send_ref[g, 15, 13:14, :] = window(total_e, g)[0:1]
        send_ref[g, 15, 14:15, :] = window(total_n, g)[0:1]
        send_ref[g, 15, 15:16, :] = jnp.zeros((1, cols), jnp.float32)
        depths_ref[g, 24:25, :] = window(depth_e, g)[0:1]
        depths_ref[g, 25:26, :] = window(depth_n, g)[0:1]
        depths_ref[g, 26:27, :] = window(dp, g)[0:1]

    slot = lanes_of(tp.shape) % SLOTS

    def edges(x, other):
        x = jnp.where(slot == 0, turn(x, -6, 1), other)
        return x[:, 0:cols], x[:, cols:]

    edge_p, edge_w = edges(press, press), edges(wet, wet)
    edge_t, edge_s = edges(tp, flux_t), edges(sp, flux_s)
    edge_total, edge_depth = edges(total, total), edges(dp, dp)

    def edge(pair, r):
        at = r % tile_rows
        return turn(pair[0] if 0 <= r < tile_rows else pair[1], -(SLOTS * at + 1), 1)

    depth = jnp.where(sea_ref[...] == 1, floor_ref[...], 0).astype(jnp.float32)

    def row_of(f, r):
        if r < 0:
            return before_ref[NSUB * f + r + NSUB]
        if r >= tile_rows:
            return after_ref[NSUB * f + r - tile_rows]
        return own_ref[f, r]

    def depth_of(r):
        if r < 0:
            x = before_ref[4 * NSUB, r + NSUB : r + NSUB + 1, :]
        elif r >= tile_rows:
            x = after_ref[4 * NSUB, r - tile_rows : r - tile_rows + 1, :]
        else:
            x = depth[r : r + 1]
        return jnp.broadcast_to(x, shape)

    lo, hi = -NSUB, tile_rows + NSUB
    for r in range(lo, hi):
        heavy = (level < depth_of(r)).astype(jnp.float32) * (-0.2 * row_of(2, r) + 0.8 * row_of(3, r))
        above, total = sums_above(heavy)
        press_ref[r - lo] = above + 0.5 * heavy
        total_ref[r - lo] = total

    def windows(r, before):
        for g in range(blocks):
            j = r - (sub_rows * g - before)
            if 0 <= j < sub_rows + 1 + before:
                yield g, j

    flux_before = [None, None]
    for r in range(lo, hi - 1):
        press, press_e = press_ref[r - lo], press_ref[r - lo + 1]
        total, total_a = total_ref[r - lo], total_ref[r - lo + 1]
        d, d_e = depth_of(r), depth_of(r + 1)
        d_n = jnp.where(last, edge(edge_depth, r), turn(d, -1, 1))
        face_e, face_n = jnp.minimum(d, d_e), jnp.minimum(d, d_n)
        u, v = row_of(0, r), row_of(1, r)
        east = u + DT_FLOW * (CORIOLIS * v - (press_e - press))
        press_n = jnp.where(last, edge(edge_p, r), turn(press, -1, 1))
        north = v + DT_FLOW * (-CORIOLIS * u - (press_n - press))
        total_e = total_a - total
        total_n = jnp.where(last, edge(edge_total, r), turn(total, -1, 1)) - total
        for g, j in windows(r, 2):
            send_ref[g, j] = east
            send_ref[g, 15, j : j + 1, :] = total_e[0:1]
            depths_ref[g, j : j + 1, :] = face_e[0:1]
        for g, j in windows(r, 1):
            send_ref[g, 7 + j] = north
            send_ref[g, 15, 7 + j : 8 + j, :] = total_n[0:1]
            depths_ref[g, 8 + j : 9 + j, :] = face_n[0:1]
            depths_ref[g, 16 + j : 17 + j, :] = d[0:1]
        if 0 <= r < tile_rows:
            local_ref[0, r] = east
            local_ref[1, r] = north
            faces_ref[0, r : r + 1, :] = face_e[0:1]
            faces_ref[1, r : r + 1, :] = face_n[0:1]
            for g in range(blocks):
                send_ref[g, 16, r : r + 1, :] = total_e[0:1]
                send_ref[g, 17, r : r + 1, :] = total_n[0:1]
        if r < -1 or r >= tile_rows:
            continue
        open_e = (level < face_e).astype(jnp.float32)
        open_n = (level < face_n).astype(jnp.float32)
        for i, (f, ends) in enumerate(((2, edge_t), (3, edge_s))):
            x = row_of(f, r)
            flux_e = open_e * (row_of(f, r + 1) - x)
            if r >= 0:
                ending = edge(ends, r)
                flux_n = open_n * (jnp.where(last, ending, turn(x, -1, 1)) - x)
                flux_b = jnp.where(first, ending, turn(flux_n, 1, 1))
                mixed = x + MIXING * ((flux_e - flux_before[i]) + (flux_n - flux_b))
                mixed_ref[i, r] = mixed
                if i == 1:
                    smix_ref[pl.ds(r, levels, stride=tile_rows), :] = mixed
            flux_before[i] = flux_e


def ocean_phase(blocks, levels, own, sea, packed, rim_after, rim_before, after):
    tile_rows, cols = sea[0].shape
    outs = [
        shaped(levels * tile_rows, cols),
        shaped(2, tile_rows, levels, cols),
        shaped(blocks, ENTRIES, levels, cols),
        shaped(2, tile_rows, levels, cols),
        shaped(2, tile_rows, cols),
        shaped(blocks, 32, cols),
    ]
    tall = tile_rows + 2 * NSUB
    return call_once(
        functools.partial(ocean_kernel, blocks, levels),
        [own, *sea, packed, rim_after, rim_before],
        outs,
        [pltpu.VMEM((tall, levels, cols), jnp.float32)] * 2,
        after=after,
    )


def velocity_kernel(local_ref, faces_ref, received_ref, east_ref, north_ref):
    blocks = received_ref.shape[0]
    _, tile_rows, levels, cols = local_ref.shape
    group = lax.axis_index("comp")
    level = (group * levels + subs_of((levels, cols))).astype(jnp.float32)
    for f, out_ref in enumerate((east_ref, north_ref)):
        above = jnp.zeros((tile_rows, cols), jnp.float32)
        for s in range(blocks - 1):
            above = above + jnp.where(s < group, received_ref[s, f], 0.0)
        for r in range(tile_rows):
            x = local_ref[f, r] - DT_FLOW * jnp.broadcast_to(above[r : r + 1], (levels, cols))
            x = jnp.where(level < faces_ref[f, r : r + 1, :], x, 0.0)
            out_ref[pl.ds(r, levels, stride=tile_rows), :] = x


def velocities(local, faces, received):
    blocks = received.shape[0]
    _, tile_rows, levels, cols = local.shape
    out = shaped(levels * tile_rows, cols)
    return pl.pallas_call(
        velocity_kernel,
        grid=(1,),
        in_specs=[
            whole(local.shape),
            whole(faces.shape),
            pl.BlockSpec((blocks, 2, levels, cols), lambda i: (0, ENTRIES // 2 - 1, 0, 0)),
        ],
        out_specs=[whole(out.shape)] * 2,
        out_shape=[out] * 2,
        compiler_params=params(),
    )(local, faces, received)


def advection_kernel(first_part, parts, level_count, *refs):
    (
        absorb_ref,
        surface_ref,
        depth_ref,
        totals_ref,
        courant_ref,
        low_ref,
        high_ref,
        after_ref,
        before_ref,
        side_ref,
        left_ref,
        right_ref,
    ) = refs[:12]
    moved_ref, light_ref, heat_ref, carry_out_ref = refs[-10:-6]
    coef_ref, side_coef_ref, edge_ref, running_ref, above_ref, shift_ref = refs[-6:]
    depth_ref = depth_ref.at[lax.axis_index("comp")]
    step = pl.program_id(0)
    tracers, _, _, cols = low_ref.shape
    levels = courant_ref.shape[2]
    sub_rows = surface_ref.shape[0]
    rows = sub_rows + 2
    shape = (levels, cols)
    lane = lanes_of(shape)
    first, last = lane == 0, lane == cols - 1
    first8, last8 = first[0:SUB], last[0:SUB]
    slot = lane % SLOTS

    @pl.when(step == 0)
    def _():
        running_ref[...] = refs[12][...] if first_part else jnp.zeros_like(running_ref)
        size = (2 * cols, 2 * cols)
        source, to = subs_of(size) % cols, lanes_of(size)
        hit = ((to < cols) & (source == to + 1)) | ((to >= cols) & (source == to - cols - 1))
        shift_ref[...] = hit.astype(jnp.float32).astype(jnp.bfloat16)

    part = first_part + step
    above = jnp.zeros(above_ref.shape, jnp.float32)
    for s in range(totals_ref.shape[0] - 1):
        above = above + jnp.where(s < part // parts, totals_ref[s, 0], 0.0)
    above_ref[...] = above
    level = (part * levels + subs_of(shape)).astype(jnp.float32)

    def spread(ref, r):
        return jnp.broadcast_to(ref[r : r + 1, :], shape)

    def courant(entry, face):
        x = courant_ref[0, entry] - DT_FLOW * spread(above_ref, entry)
        return COURANT * jnp.tanh(jnp.where(level < spread(depth_ref, face), x, 0.0))

    def coefficients(wet, ce, ce_b, cn, cn_b):
        return (
            wet
            * (
                1.0
                - jnp.maximum(ce, 0.0)
                + jnp.minimum(ce_b, 0.0)
                - jnp.maximum(cn, 0.0)
                + jnp.minimum(cn_b, 0.0)
            ),
            -wet * jnp.minimum(ce, 0.0),
            wet * jnp.maximum(ce_b, 0.0),
            -wet * jnp.minimum(cn, 0.0),
            wet * jnp.maximum(cn_b, 0.0),
        )

    side_e, side_n = courant(13, 24), courant(14, 25)
    wet = (level < spread(depth_ref, 26)).astype(jnp.float32)
    packed_coef = coefficients(wet, side_e, turn(side_e, SLOTS, 1), side_n, turn(side_n, 1, 1))
    for i in range(5):
        side_coef_ref[i] = packed_coef[i]
    ce_b = courant(0, 0)
    for j in range(rows):
        ce, cn = courant(1 + j, 1 + j), courant(7 + j, 8 + j)
        cn_b = jnp.where(first, turn(side_n, -(SLOTS * (j + 1) + 1), 1), turn(cn, 1, 1))
        wet = (level < spread(depth_ref, 16 + j)).astype(jnp.float32)
        for i, x in enumerate(coefficients(wet, ce, ce_b, cn, cn_b)):
            coef_ref[5 * j + i] = x
        ce_b = ce
    for i in range(side_ref.shape[0]):
        x = with_sides(side_ref[i], left_ref[i], right_ref[i])
        edge_ref[i, 0] = jnp.where(slot == 0, turn(x, -6, 1), x)
        x = (
            (side_coef_ref[0] * x + side_coef_ref[1] * turn(x, -SLOTS, 1))
            + (side_coef_ref[2] * turn(x, SLOTS, 1) + side_coef_ref[3] * turn(x, -1, 1))
            + side_coef_ref[4] * turn(x, 1, 1)
        )
        edge_ref[i, 1] = jnp.where(slot == 0, turn(x, -6, 1), x)

    layer = 2.0 / level_count
    zero = jnp.zeros((SUB, cols), jnp.float32)
    for k in range(0, levels, SUB):
        at = slice(k, k + SUB)

        def shifted(tiles):
            high, low = halves(jnp.concatenate(tiles, axis=0))
            return jnp.dot(
                jnp.concatenate([high, low], axis=1),
                shift_ref[...],
                preferred_element_type=jnp.float32,
            )

        def stencil(x, coef, edge, beside):
            north = jnp.where(last8, edge, beside[:, :cols])
            south = jnp.where(first8, edge, beside[:, cols:])
            return (
                (coef[0] * x[1] + coef[1] * x[2])
                + (coef[2] * x[0] + coef[3] * north)
                + coef[4] * south
            )

        def advect(i, sums):
            sums = list(sums)
            fields = []
            for t in range(GROUP):
                t = GROUP * i + t
                rows_of = (before_ref, low_ref, high_ref, after_ref)
                x = [ref[t, n, at] for ref in rows_of for n in range(NSUB)]
                fields.append(x)
            for stage in range(NSUB):
                inner = range(1 + stage, rows + 1 - stage)
                beside = shifted([x[j - stage] for j in inner for x in fields])
                fresh = [[] for _ in fields]
                for n, j in enumerate(inner):
                    coef = [coef_ref[5 * (j - 1) + c, at] for c in range(5)]
                    for t, x in enumerate(fields):
                        edges = edge_ref[GROUP // 2 * i + t // 2, stage, at]
                        edge = turn(edges, -(HALF * (t % 2) + SLOTS * j + 1), 1)
                        row = SUB * (len(fields) * n + t)
                        fresh[t].append(
                            stencil(x[n : n + 3], coef, edge, beside[row : row + SUB])
                        )
                fields = fresh
            for t, x in enumerate(fields):
                for r in range(sub_rows):
                    moved_ref[GROUP * i + t, r, at] = x[r]
                    sums[r] = sums[r] + absorb_ref[GROUP * i + t] * x[r]
            return tuple(sums)

        sums = (zero,) * sub_rows
        for i in range(tracers // GROUP):
            sums = advect(i, sums)
        for r in range(sub_rows):
            optical = layer * (CLEAR_WATER + sums[r])
            above, total = sums_above(optical)
            through = jnp.exp(-(running_ref[r] + above))
            running_ref[r] = running_ref[r] + total
            surface = jnp.broadcast_to(surface_ref[r : r + 1, :], (SUB, cols))
            light_ref[r, at] = surface * through * jnp.exp(-0.5 * optical)
            wet = (level[at] < jnp.broadcast_to(depth_ref[17 + r : 18 + r, :], (SUB, cols))).astype(
                jnp.float32
            )
            heat_ref[0, r, at] = wet * surface * through * (1.0 - jnp.exp(-optical)) / layer
    carry_out_ref[...] = running_ref[...]


def advection(cut, level_count, absorb, surface, depth, received, own, rim, sides, carry, heat, after):
    first_part, count = cut
    tracers, _, _, cols = own[0].shape
    every, _, levels, _ = received.shape
    parts = levels // SUB
    sub_rows = surface.shape[0]
    rows = pl.BlockSpec((tracers, NSUB, SUB, cols), lambda i: (0, 0, i, 0))
    side = pl.BlockSpec((tracers // 2, SUB, cols), lambda i: (0, i, 0))
    operands = [absorb, surface, depth, received, received, *own, *rim, *sides]
    in_specs = [
        smem(),
        whole(surface.shape),
        whole(depth.shape),
        pl.BlockSpec((every, 1, levels, cols), lambda i: (0, 15, 0, 0)),
        pl.BlockSpec(
            (1, ENTRIES, SUB, cols),
            lambda i: ((first_part + i) // parts, 0, (first_part + i) % parts, 0),
        ),
        rows,
        rows,
        rows,
        rows,
        side,
        side,
        side,
    ]
    aliases = {}
    carry_shape = (sub_rows, SUB, cols)
    if carry is not None:
        operands.append(carry)
        in_specs.append(whole(carry_shape))
        aliases = {len(operands): 2}
        operands.append(heat)
    operands += after
    in_specs += [pl.BlockSpec(memory_space=pl.ANY)] * (len(operands) - len(in_specs))
    outs = [
        shaped(tracers, sub_rows, count * SUB, cols),
        shaped(sub_rows, count * SUB, cols),
        shaped(every, sub_rows, levels, cols),
        shaped(*carry_shape),
    ]
    return pl.pallas_call(
        functools.partial(advection_kernel, first_part, parts, level_count),
        grid=(count,),
        in_specs=in_specs,
        out_specs=[
            pl.BlockSpec((tracers, sub_rows, SUB, cols), lambda i: (0, 0, i, 0)),
            pl.BlockSpec((sub_rows, SUB, cols), lambda i: (0, i, 0)),
            pl.BlockSpec(
                (1, sub_rows, SUB, cols),
                lambda i: ((first_part + i) // parts, 0, (first_part + i) % parts, 0),
            ),
            whole(carry_shape),
        ],
        out_shape=outs,
        scratch_shapes=[
            pltpu.VMEM((5 * (sub_rows + 2), SUB, cols), jnp.float32),
            pltpu.VMEM((5, SUB, cols), jnp.float32),
            pltpu.VMEM((tracers // 2, 2, SUB, cols), jnp.float32),
            pltpu.VMEM((sub_rows, SUB, cols), jnp.float32),
            pltpu.VMEM((levels, cols), jnp.float32),
            pltpu.VMEM((2 * cols, 2 * cols), jnp.bfloat16),
        ],
        input_output_aliases=aliases,
        compiler_params=params(),
    )(*operands)


def spread_kernel(matrix_ref, out_ref):
    tracers = matrix_ref.shape[0]
    size = tracers * SUB
    tall = (subs_of((size, tracers)) // SUB == lanes_of((size, tracers))).astype(jnp.float32)
    wide = (lanes_of((tracers, size)) // SUB == subs_of((tracers, size))).astype(jnp.float32)
    exact = functools.partial(
        jnp.dot, precision=lax.Precision.HIGHEST, preferred_element_type=jnp.float32
    )
    same = subs_of((size, size)) % SUB == lanes_of((size, size)) % SUB
    out_ref[...] = jnp.where(same, exact(exact(tall, matrix_ref[...]), wide), 0.0)


def uptake_kernel(first_level, *refs):
    growth_ref, half_ref, dim_ref, matrix_ref, depth_ref, moved_ref, light_ref = refs[:7]
    depth_ref = depth_ref.at[lax.axis_index("comp")]
    result_ref, token_ref, uptake_ref = refs[-3:]
    token_ref[...] = jnp.zeros_like(token_ref)
    tracers, sub_rows, levels, cols = moved_ref.shape
    step = pl.program_id(0)
    matrix_high, matrix_low = halves(matrix_ref[...])
    for k in range(0, levels, SUB):
        at = slice(k, k + SUB)
        level = (first_level + step * levels + k + subs_of((SUB, cols))).astype(jnp.float32)
        light = [light_ref[r, at] for r in range(sub_rows)]
        food = [moved_ref[0, r, at] for r in range(sub_rows)]
        both = [light[r] * food[r] for r in range(sub_rows)]

        def uptake(t, _):
            for r in range(sub_rows):
                scale = (half_ref[t] + food[r]) * (light[r] + dim_ref[t])
                value = growth_ref[t] * moved_ref[t, r, at] * (both[r] / scale)
                uptake_ref[pl.ds(t * SUB, SUB), r * cols : (r + 1) * cols] = value
            return _

        lax.fori_loop(0, tracers, uptake, 0, unroll=4)
        amount = uptake_ref[...]
        high, low = halves(amount)
        dot = functools.partial(jnp.dot, preferred_element_type=jnp.float32)
        change = dot(matrix_high, high) + (dot(matrix_high, low) + dot(matrix_low, high))
        for r in range(sub_rows):
            depth = jnp.broadcast_to(depth_ref[17 + r : 18 + r, :], (SUB, cols))
            scale = DT_BIO * (level < depth).astype(jnp.float32)
            for t in range(tracers):
                result_ref[t, pl.ds(sub_rows * k + r, SUB, stride=sub_rows), :] = (
                    moved_ref[t, r, at]
                    + scale * change[SUB * t : SUB * (t + 1), r * cols : (r + 1) * cols]
                )


def uptake(cut, all_rows, scalars, matrix, depth, moved, light, result):
    first_part, count = cut
    tracers, sub_rows, _, cols = moved.shape
    operands = [*scalars, matrix, depth, moved, light]
    in_specs = [smem()] * 3 + [
        whole(matrix.shape),
        whole(depth.shape),
        pl.BlockSpec((tracers, sub_rows, SUB, cols), lambda i: (0, 0, i, 0)),
        pl.BlockSpec((sub_rows, SUB, cols), lambda i: (0, i, 0)),
    ]
    aliases = {}
    if result is not None:
        aliases = {len(operands): 0}
        operands.append(result)
        in_specs.append(pl.BlockSpec(memory_space=pl.ANY))
    return pl.pallas_call(
        functools.partial(uptake_kernel, first_part * SUB),
        grid=(count,),
        in_specs=in_specs,
        out_specs=[
            pl.BlockSpec((tracers, SUB * sub_rows, cols), lambda i: (0, first_part + i, 0)),
            whole((SUB, cols)),
        ],
        out_shape=[shaped(tracers, all_rows, cols), shaped(SUB, cols)],
        scratch_shapes=[pltpu.VMEM((tracers * SUB, sub_rows * cols), jnp.float32)],
        input_output_aliases=aliases,
        compiler_params=params(),
    )(*operands)


def warming_kernel(sea_ref, floor_ref, heat_ref, mixed_ref, warm_ref, buoyant_ref):
    blocks, sub_rows, levels, cols = heat_ref.shape
    tile_rows = blocks * sub_rows
    base = lax.axis_index("comp") * levels
    level = (base + subs_of((levels, cols))).astype(jnp.float32)
    depth = jnp.where(sea_ref[...] == 1, floor_ref[...], 0).astype(jnp.float32)
    for r in range(tile_rows):
        at = pl.ds(r, levels, stride=tile_rows)
        warm = mixed_ref[0, r] + WARMING_FACTOR * heat_ref[r // sub_rows, r % sub_rows]
        wet = (level < depth[r : r + 1]).astype(jnp.float32)
        warm_ref[at, :] = warm
        buoyant_ref[at, :] = wet * (0.2 * warm - 0.8 * mixed_ref[1, r])


def warming(heat, mixed, sea):
    _, tile_rows, levels, cols = mixed.shape
    outs = [shaped(levels * tile_rows, cols)] * 2
    return call_once(warming_kernel, [*sea, heat, mixed], outs)


def from_before(x, axis):
    return lax.ppermute(x, axis, [(i, i + 1) for i in range(lax.axis_size(axis) - 1)])


def from_after(x, axis):
    return lax.ppermute(x, axis, [(i + 1, i) for i in range(lax.axis_size(axis) - 1)])


def row_pairs():
    blocks, tiles = lax.axis_size("comp"), lax.axis_size("gx")
    places = [b * tiles + tile for tile in range(tiles) for b in range(blocks)]
    return list(zip(places[:-1], places[1:]))


def from_block_before(x):
    return lax.ppermute(x, ("comp", "gx"), row_pairs())


def from_block_after(x):
    return lax.ppermute(x, ("comp", "gx"), [(later, own) for own, later in row_pairs()])


def from_sides(x):
    if lax.axis_size("gy") == 2:
        other = lax.ppermute(x, "gy", [(0, 1), (1, 0)])
        return other, other
    return from_before(x, "gy"), from_after(x, "gy")


def on_device(
    zonal_flow_speed,
    meridional_flow_speed,
    thermal_anomaly,
    brine_anomaly_values,
    marine_indicator,
    seafloor_layer,
    dissolved_species,
    topmost_sunshine,
    attenuation_coefficient,
    peak_intake_speed,
    feedstock_midpoint_constant,
    photon_midpoint_constant,
    stoichiometry_matrix,
):
    blocks = lax.axis_size("comp")
    levels, tile_rows, tile_cols = zonal_flow_speed.shape
    tracer_count, level_count = dissolved_species.shape[:2]
    sub_rows = dissolved_species.shape[4]
    ocean = (zonal_flow_speed, meridional_flow_speed, thermal_anomaly, brine_anomaly_values)
    sea = (marine_indicator, seafloor_layer)
    flat = [x.reshape(levels * tile_rows, tile_cols) for x in ocean]
    q = dissolved_species.reshape(tracer_count, level_count, sub_rows, 1, tile_cols)
    parts = levels // SUB
    every = parts * blocks
    sizes = [every - 5 * every // 8, 3 * every // 8, every // 4]
    cuts = [(sum(sizes[:i]), size) for i, size in enumerate(sizes)]
    matrix = call_once(
        spread_kernel,
        [stoichiometry_matrix],
        [shaped(SUB * tracer_count, SUB * tracer_count)],
    )[0]
    scalars_of_uptake = (
        peak_intake_speed,
        feedstock_midpoint_constant,
        photon_midpoint_constant,
    )

    def rims(cut, *after):
        low, high = cut_rows(q, cut[0] * SUB, cut[1] * SUB, after)
        own = [x.reshape(tracer_count, NSUB, cut[1] * SUB, tile_cols) for x in (low, high)]
        return own, (from_block_after(own[0]), from_block_before(own[1]))

    def sides(x):
        return (x, *from_sides(x))

    packed, edge_low, edge_high, ocean_rows = pack_ocean(flat, sea, levels)
    cut0, rims0 = rims(cuts[0], packed)
    up, down, packed = ocean_sides(packed, *from_sides(packed), edge_low, edge_high)
    after, before = from_after(up, "gx"), from_before(down, "gx")
    cut1, rims1 = rims(cuts[1], after, before)
    smix, mixed, send, local, faces, depths = ocean_phase(
        blocks, levels, ocean_rows, sea, packed, after, before, cut1
    )
    received = lax.all_to_all(send, "comp", split_axis=0, concat_axis=0, tiled=True)
    east_new, north_new = velocities(local, faces, received)
    ahead = [(cut0, rims0), (cut1, rims1), rims(cuts[2], depths)]

    surface = topmost_sunshine.reshape(sub_rows, tile_cols)
    carry, heat, result = None, None, None
    for i, cut in enumerate(cuts):
        waits = list(ahead[i + 2][0]) if i + 2 < len(cuts) else []
        if i > 0:
            waits.append(token)
        near = sides(pack_tracers(*ahead[i], waits))
        moved, light, heat, carry = advection(
            cut,
            level_count,
            attenuation_coefficient,
            surface,
            depths,
            received,
            *ahead[i],
            near,
            carry,
            heat,
            [],
        )
        if i + 3 < len(cuts):
            ahead.append(rims(cuts[i + 3], carry))
        result, token = uptake(
            cut,
            level_count * sub_rows,
            scalars_of_uptake,
            matrix,
            depths,
            moved,
            light,
            result,
        )
    heat = lax.all_to_all(heat, "comp", split_axis=0, concat_axis=0, tiled=True)
    warmed_result, buoyancy = warming(heat, mixed, sea)
    fields = (east_new, north_new, warmed_result, smix, buoyancy)
    return (
        *[x.reshape(zonal_flow_speed.shape) for x in fields],
        result.reshape(dissolved_species.shape),
    )


def solution(mesh):
    return jax.shard_map(
        on_device,
        mesh=mesh,
        in_specs=(
            P("comp", "gx", "gy"),
            P("comp", "gx", "gy"),
            P("comp", "gx", "gy"),
            P("comp", "gx", "gy"),
            P("gx", "gy"),
            P("gx", "gy"),
            P(None, None, "gx", "comp", None, "gy"),
            P("gx", "comp", None, "gy"),
            P(),
            P(),
            P(),
            P(),
            P(),
        ),
        out_specs=(
            P("comp", "gx", "gy"),
            P("comp", "gx", "gy"),
            P("comp", "gx", "gy"),
            P("comp", "gx", "gy"),
            P("comp", "gx", "gy"),
            P(None, None, "gx", "comp", None, "gy"),
        ),
        check_vma=False,
    )
```

```python
import functools

import jax
import jax.numpy as jnp
from jax import lax
from jax.experimental import pallas as pl
from jax.experimental.pallas import tpu as pltpu
from jax.sharding import PartitionSpec as P

NSUB = 2
SLOTS = 4 * NSUB
SUB = 8
GROUP = 24
HALF = 64
ENTRIES = 18

DT_FLOW = 0.1
CORIOLIS = 0.3
MIXING = 0.15
COURANT = 0.24
DT_BIO = 0.5
WARMING_FACTOR = 0.5
CLEAR_WATER = 0.5
VMEM_LIMIT = 16 * 1024 * 1024
VMEM_MOST = 62 * 1024 * 1024


def lanes_of(shape):
    return lax.broadcasted_iota(jnp.int32, shape, len(shape) - 1)


def subs_of(shape):
    return lax.broadcasted_iota(jnp.int32, shape, len(shape) - 2)


def turn(x, by, axis):
    by = by % x.shape[axis]
    return x if by == 0 else pltpu.roll(x, by, axis)


def params(limit=VMEM_LIMIT):
    return pltpu.CompilerParams(vmem_limit_bytes=limit)


def whole(shape):
    return pl.BlockSpec(shape, lambda *_: (0,) * len(shape))


def smem():
    return pl.BlockSpec(memory_space=pltpu.SMEM)


def shaped(*shape):
    return jax.ShapeDtypeStruct(shape, jnp.float32)


def halves(x):
    high = x.astype(jnp.bfloat16)
    return high, (x - high.astype(jnp.float32)).astype(jnp.bfloat16)


def sums_above(x):
    sub = subs_of(x.shape)
    running, total = x, x
    by = 1
    while by < x.shape[0]:
        running = running + jnp.where(sub >= by, turn(running, by, 0), 0.0)
        total = total + turn(total, by, 0)
        by *= 2
    return jnp.where(sub >= 1, turn(running, 1, 0), 0.0), total


def cut_kernel(cuts, q_ref, *refs):
    outs, sems = refs[-2 * len(cuts) - 1 : -1], refs[-1]
    rows = q_ref.shape[2]
    copies = [
        pltpu.make_async_copy(
            q_ref.at[:, pl.ds(start, size), r],
            outs[2 * i + r // NSUB].at[:, r % NSUB],
            sems.at[rows * i + r],
        )
        for i, (start, size) in enumerate(cuts)
        for r in range(rows)
    ]
    for copy in copies:
        copy.start()
    for copy in copies:
        copy.wait()


def cut_rows(q, cuts, after):
    tracers, _, rows, _, cols = q.shape
    anywhere = pl.BlockSpec(memory_space=pl.ANY)
    outs = [shaped(tracers, NSUB, size, 1, cols) for _, size in cuts for _ in range(2)]
    outs = pl.pallas_call(
        functools.partial(cut_kernel, cuts),
        in_specs=[anywhere] * (1 + len(after)),
        out_specs=[anywhere] * len(outs),
        out_shape=outs,
        scratch_shapes=[pltpu.SemaphoreType.DMA((rows * len(cuts),))],
        compiler_params=params(),
    )(q, *after)
    return [x.reshape(tracers, NSUB, x.shape[2], cols) for x in outs]


def hold_kernel(*refs):
    pass


def held_until(arrays, after):
    anywhere = pl.BlockSpec(memory_space=pl.ANY)
    return pl.pallas_call(
        hold_kernel,
        in_specs=[anywhere] * (len(arrays) + len(after)),
        out_specs=[anywhere] * len(arrays),
        out_shape=[shaped(*x.shape) for x in arrays],
        input_output_aliases={i: i for i in range(len(arrays))},
        compiler_params=params(),
    )(*arrays, *after)


def both_ends(acc):
    return jnp.where(lanes_of(acc.shape) % SLOTS < SLOTS // 2, acc, turn(acc, SLOTS // 2, 1))


def pack_tracers_kernel(low_ref, high_ref, after_ref, before_ref, packed_ref):
    tracers, _, _, cols = low_ref.shape
    lane = lanes_of((SUB, cols))
    for pair in range(tracers // 2):
        acc = jnp.zeros((SUB, cols), jnp.float32)
        for odd in range(2):
            t = 2 * pair + odd
            rows = [before_ref[t, 1], low_ref[t, 0], low_ref[t, 1], high_ref[t, 0], high_ref[t, 1]]
            for r, x in enumerate(rows + [after_ref[t, 0]]):
                at = HALF * odd + SLOTS * (r + 1)
                acc = jnp.where(lane // SLOTS == at // SLOTS, turn(x, at + NSUB, 1), acc)
        packed_ref[pair] = both_ends(acc)


def pack_tracers(own, rim, after):
    tracers, _, levels, cols = own[0].shape
    rows = pl.BlockSpec((tracers, NSUB, SUB, cols), lambda i: (0, 0, i, 0))
    return pl.pallas_call(
        functools.partial(ignoring, len(after), pack_tracers_kernel),
        grid=(levels // SUB,),
        in_specs=[pl.BlockSpec(memory_space=pl.ANY)] * len(after) + [rows] * 4,
        out_specs=pl.BlockSpec((tracers // 2, SUB, cols), lambda i: (0, i, 0)),
        out_shape=shaped(tracers // 2, levels, cols),
        compiler_params=params(),
    )(*after, *own, *rim)


def ignoring(count, kernel, *refs):
    kernel(*refs[count:])


def call_once(kernel, operands, outs, scratch=(), scalars=(), after=(), limit=VMEM_LIMIT):
    return pl.pallas_call(
        functools.partial(ignoring, len(after), kernel),
        grid=(1,),
        in_specs=[pl.BlockSpec(memory_space=pl.ANY)] * len(after)
        + [smem()] * len(scalars)
        + [whole(x.shape) for x in operands],
        out_specs=[whole(x.shape) for x in outs],
        out_shape=outs,
        scratch_shapes=list(scratch),
        compiler_params=params(limit),
    )(*after, *scalars, *operands)


def pack_ocean_kernel(levels, *refs):
    u_ref, v_ref, t_ref, s_ref, sea_ref, floor_ref, packed_ref, edges_ref, row_ref = refs
    edge_low_ref, edge_high_ref = edges_ref.at[0], edges_ref.at[1]
    tile_rows, cols = sea_ref.shape
    lane = lanes_of((levels, cols))
    edge_low_ref[4 * NSUB] = jnp.zeros((levels, cols), jnp.float32)
    edge_high_ref[4 * NSUB] = jnp.zeros((levels, cols), jnp.float32)
    for f, ref in enumerate((u_ref, v_ref, t_ref, s_ref)):
        acc = jnp.zeros((levels, cols), jnp.float32)
        for r in range(tile_rows):
            x = ref[pl.ds(r, levels, stride=tile_rows), :]
            row_ref[f, r] = x
            acc = jnp.where(lane // SLOTS == r, turn(x, SLOTS * r + NSUB, 1), acc)
            if r < NSUB:
                edge_low_ref[NSUB * f + r] = x
            if r >= tile_rows - NSUB:
                edge_high_ref[NSUB * f + r - tile_rows + NSUB] = x
        packed_ref[f] = both_ends(acc)
    depth = jnp.where(sea_ref[...] == 1, floor_ref[...], 0).astype(jnp.float32)
    acc = jnp.zeros((levels, cols), jnp.float32)
    for r in range(tile_rows):
        x = jnp.broadcast_to(depth[r : r + 1], (levels, cols))
        acc = jnp.where(lane // SLOTS == r, turn(x, SLOTS * r + NSUB, 1), acc)
    packed_ref[4] = both_ends(acc)
    edge_low_ref[4 * NSUB, 0:NSUB, :] = depth[0:NSUB]
    edge_high_ref[4 * NSUB, 0:NSUB, :] = depth[tile_rows - NSUB :]


def pack_ocean(flat, sea, levels):
    cols = sea[0].shape[1]
    edges = shaped(2, 4 * NSUB + 1, levels, cols)
    return call_once(
        functools.partial(pack_ocean_kernel, levels),
        [*flat, *sea],
        [shaped(5, levels, cols), edges, shaped(4, sea[0].shape[0], levels, cols)],
        limit=VMEM_MOST,
    )


def with_sides(own, left, right):
    slot = lanes_of(own.shape) % SLOTS
    ends = jnp.where(slot < NSUB, left, right)
    return jnp.where((slot < NSUB) | (slot >= SLOTS - NSUB), ends, own)


def ocean_sides_kernel(own_ref, left_ref, right_ref, edges_ref, up_ref, down_ref, out_ref):
    _, levels, cols = own_ref.shape
    rows = edges_ref.shape[1]
    up_ref[0:rows] = edges_ref[0]
    down_ref[0:rows] = edges_ref[1]
    slot = lanes_of((levels, cols)) % SLOTS
    place = lax.axis_index("gy")
    first, last = place == 0, place == lax.axis_size("gy") - 1
    for f in range(5):
        x = with_sides(own_ref[f], left_ref[f], right_ref[f])
        if f == 4:
            x = jnp.where((slot < NSUB) & first, 0.0, x)
            x = jnp.where((slot >= SLOTS - NSUB) & last, 0.0, x)
        out_ref[f] = x
        up_ref[rows + f] = x
        down_ref[rows + f] = x


def ocean_sides(own, left, right, edges):
    edge = shaped(edges.shape[1] + 5, *edges.shape[2:])
    return call_once(
        ocean_sides_kernel,
        [own, left, right, edges],
        [edge, edge, shaped(*own.shape)],
    )


def ocean_kernel(blocks, levels, *refs):
    own_ref, sea_ref, floor_ref, packed_ref, after_ref, before_ref = refs[:6]
    smix_ref, mixed_ref, send_ref, local_ref, faces_ref, depths_ref, press_ref, total_ref = refs[6:]
    tile_rows, cols = sea_ref.shape
    sub_rows = tile_rows // blocks
    shape = (levels, cols)
    lane = lanes_of(shape)
    first, last = lane == 0, lane == cols - 1
    base = lax.axis_index("comp") * levels
    level = (base + subs_of(shape)).astype(jnp.float32)
    rims = after_ref.shape[0] - 5

    def packed(f):
        after, before = after_ref[rims + f], before_ref[rims + f]
        rim = jnp.where(lane < NSUB * SLOTS, after, jnp.where(lane >= cols - NSUB * SLOTS, before, 0.0))
        return jnp.concatenate([packed_ref[f], rim], axis=1)

    def row_after(x):
        return turn(x, -SLOTS, 1)

    def row_before(x):
        return turn(x, SLOTS, 1)

    up, vp, tp, sp, dp = [packed(f) for f in range(5)]
    wide = jnp.concatenate([level, level], axis=1)
    wet = (wide < dp).astype(jnp.float32)
    heavy = wet * (-0.2 * tp + 0.8 * sp)
    above, total = sums_above(heavy)
    press = above + 0.5 * heavy
    east = up + DT_FLOW * (CORIOLIS * vp - (row_after(press) - press))
    north = vp + DT_FLOW * (-CORIOLIS * up - (turn(press, -1, 1) - press))
    open_n = wet * turn(wet, -1, 1)
    flux_t = open_n * (turn(tp, -1, 1) - tp)
    flux_s = open_n * (turn(sp, -1, 1) - sp)
    total_e, total_n = row_after(total) - total, turn(total, -1, 1) - total
    depth_e, depth_n = jnp.minimum(dp, row_after(dp)), jnp.minimum(dp, turn(dp, -1, 1))

    def window(x, g):
        x = turn(x, -SLOTS * (sub_rows * g - NSUB), 1)[:, 0:cols]
        return jnp.where(lane < HALF, x, turn(x, HALF, 1))

    for g in range(blocks):
        send_ref[g, 13] = window(east, g)
        send_ref[g, 14] = window(north, g)
        send_ref[g, 15, 13:14, :] = window(total_e, g)[0:1]
        send_ref[g, 15, 14:15, :] = window(total_n, g)[0:1]
        send_ref[g, 15, 15:16, :] = jnp.zeros((1, cols), jnp.float32)
        depths_ref[g, 24:25, :] = window(depth_e, g)[0:1]
        depths_ref[g, 25:26, :] = window(depth_n, g)[0:1]
        depths_ref[g, 26:27, :] = window(dp, g)[0:1]

    slot = lanes_of(tp.shape) % SLOTS

    def edges(x, other):
        x = jnp.where(slot == 0, turn(x, -6, 1), other)
        return x[:, 0:cols], x[:, cols:]

    edge_p, edge_w = edges(press, press), edges(wet, wet)
    edge_t, edge_s = edges(tp, flux_t), edges(sp, flux_s)
    edge_total, edge_depth = edges(total, total), edges(dp, dp)

    def edge(pair, r):
        at = r % tile_rows
        return turn(pair[0] if 0 <= r < tile_rows else pair[1], -(SLOTS * at + 1), 1)

    depth = jnp.where(sea_ref[...] == 1, floor_ref[...], 0).astype(jnp.float32)

    def row_of(f, r):
        if r < 0:
            return before_ref[NSUB * f + r + NSUB]
        if r >= tile_rows:
            return after_ref[NSUB * f + r - tile_rows]
        return own_ref[f, r]

    def depth_of(r):
        if r < 0:
            x = before_ref[4 * NSUB, r + NSUB : r + NSUB + 1, :]
        elif r >= tile_rows:
            x = after_ref[4 * NSUB, r - tile_rows : r - tile_rows + 1, :]
        else:
            x = depth[r : r + 1]
        return jnp.broadcast_to(x, shape)

    lo, hi = -NSUB, tile_rows + NSUB
    for r in range(lo, hi):
        heavy = (level < depth_of(r)).astype(jnp.float32) * (-0.2 * row_of(2, r) + 0.8 * row_of(3, r))
        above, total = sums_above(heavy)
        press_ref[r - lo] = above + 0.5 * heavy
        total_ref[r - lo] = total

    def windows(r, before):
        for g in range(blocks):
            j = r - (sub_rows * g - before)
            if 0 <= j < sub_rows + 1 + before:
                yield g, j

    flux_before = [None, None]
    for r in range(lo, hi - 1):
        press, press_e = press_ref[r - lo], press_ref[r - lo + 1]
        total, total_a = total_ref[r - lo], total_ref[r - lo + 1]
        d, d_e = depth_of(r), depth_of(r + 1)
        d_n = jnp.where(last, edge(edge_depth, r), turn(d, -1, 1))
        face_e, face_n = jnp.minimum(d, d_e), jnp.minimum(d, d_n)
        u, v = row_of(0, r), row_of(1, r)
        east = u + DT_FLOW * (CORIOLIS * v - (press_e - press))
        press_n = jnp.where(last, edge(edge_p, r), turn(press, -1, 1))
        north = v + DT_FLOW * (-CORIOLIS * u - (press_n - press))
        total_e = total_a - total
        total_n = jnp.where(last, edge(edge_total, r), turn(total, -1, 1)) - total
        for g, j in windows(r, 2):
            send_ref[g, j] = east
            send_ref[g, 15, j : j + 1, :] = total_e[0:1]
            depths_ref[g, j : j + 1, :] = face_e[0:1]
        for g, j in windows(r, 1):
            send_ref[g, 7 + j] = north
            send_ref[g, 15, 7 + j : 8 + j, :] = total_n[0:1]
            depths_ref[g, 8 + j : 9 + j, :] = face_n[0:1]
            depths_ref[g, 16 + j : 17 + j, :] = d[0:1]
        if 0 <= r < tile_rows:
            local_ref[0, r] = east
            local_ref[1, r] = north
            faces_ref[0, r : r + 1, :] = face_e[0:1]
            faces_ref[1, r : r + 1, :] = face_n[0:1]
            for g in range(blocks):
                send_ref[g, 16, r : r + 1, :] = total_e[0:1]
                send_ref[g, 17, r : r + 1, :] = total_n[0:1]
        if r < -1 or r >= tile_rows:
            continue
        open_e = (level < face_e).astype(jnp.float32)
        open_n = (level < face_n).astype(jnp.float32)
        for i, (f, ends) in enumerate(((2, edge_t), (3, edge_s))):
            x = row_of(f, r)
            flux_e = open_e * (row_of(f, r + 1) - x)
            if r >= 0:
                ending = edge(ends, r)
                flux_n = open_n * (jnp.where(last, ending, turn(x, -1, 1)) - x)
                flux_b = jnp.where(first, ending, turn(flux_n, 1, 1))
                mixed = x + MIXING * ((flux_e - flux_before[i]) + (flux_n - flux_b))
                mixed_ref[i, r] = mixed
                if i == 1:
                    smix_ref[pl.ds(r, levels, stride=tile_rows), :] = mixed
            flux_before[i] = flux_e


def ocean_phase(blocks, levels, own, sea, packed, rim_after, rim_before, after):
    tile_rows, cols = sea[0].shape
    outs = [
        shaped(levels * tile_rows, cols),
        shaped(2, tile_rows, levels, cols),
        shaped(blocks, ENTRIES, levels, cols),
        shaped(2, tile_rows, levels, cols),
        shaped(2, tile_rows, cols),
        shaped(blocks, 32, cols),
    ]
    tall = tile_rows + 2 * NSUB
    return call_once(
        functools.partial(ocean_kernel, blocks, levels),
        [own, *sea, packed, rim_after, rim_before],
        outs,
        [pltpu.VMEM((tall, levels, cols), jnp.float32)] * 2,
        after=after,
    )


def velocity_kernel(local_ref, faces_ref, received_ref, east_ref, north_ref):
    blocks = received_ref.shape[0]
    _, tile_rows, levels, cols = local_ref.shape
    group = lax.axis_index("comp")
    level = (group * levels + subs_of((levels, cols))).astype(jnp.float32)
    for f, out_ref in enumerate((east_ref, north_ref)):
        above = jnp.zeros((tile_rows, cols), jnp.float32)
        for s in range(blocks - 1):
            above = above + jnp.where(s < group, received_ref[s, f], 0.0)
        for r in range(tile_rows):
            x = local_ref[f, r] - DT_FLOW * jnp.broadcast_to(above[r : r + 1], (levels, cols))
            x = jnp.where(level < faces_ref[f, r : r + 1, :], x, 0.0)
            out_ref[pl.ds(r, levels, stride=tile_rows), :] = x


def velocities(local, faces, received):
    blocks = received.shape[0]
    _, tile_rows, levels, cols = local.shape
    out = shaped(levels * tile_rows, cols)
    return pl.pallas_call(
        velocity_kernel,
        grid=(1,),
        in_specs=[
            whole(local.shape),
            whole(faces.shape),
            pl.BlockSpec((blocks, 2, levels, cols), lambda i: (0, ENTRIES // 2 - 1, 0, 0)),
        ],
        out_specs=[whole(out.shape)] * 2,
        out_shape=[out] * 2,
        compiler_params=params(),
    )(local, faces, received)


def advection_kernel(first_part, parts, level_count, *refs):
    (
        absorb_ref,
        surface_ref,
        depth_ref,
        totals_ref,
        courant_ref,
        low_ref,
        high_ref,
        after_ref,
        before_ref,
        side_ref,
        left_ref,
        right_ref,
    ) = refs[:12]
    moved_ref, light_ref, heat_ref, carry_out_ref = refs[-10:-6]
    coef_ref, side_coef_ref, edge_ref, running_ref, above_ref, shift_ref = refs[-6:]
    depth_ref = depth_ref.at[lax.axis_index("comp")]
    step = pl.program_id(0)
    tracers, _, _, cols = low_ref.shape
    levels = courant_ref.shape[2]
    sub_rows = surface_ref.shape[0]
    rows = sub_rows + 2
    shape = (levels, cols)
    lane = lanes_of(shape)
    first, last = lane == 0, lane == cols - 1
    first8, last8 = first[0:SUB], last[0:SUB]
    slot = lane % SLOTS

    @pl.when(step == 0)
    def _():
        running_ref[...] = refs[12][...] if first_part else jnp.zeros_like(running_ref)
        size = (2 * cols, 2 * cols)
        source, to = subs_of(size) % cols, lanes_of(size)
        hit = ((to < cols) & (source == to + 1)) | ((to >= cols) & (source == to - cols - 1))
        shift_ref[...] = hit.astype(jnp.float32).astype(jnp.bfloat16)

    part = first_part + step
    above = jnp.zeros(above_ref.shape, jnp.float32)
    for s in range(totals_ref.shape[0] - 1):
        above = above + jnp.where(s < part // parts, totals_ref[s, 0], 0.0)
    above_ref[...] = above
    level = (part * levels + subs_of(shape)).astype(jnp.float32)

    def spread(ref, r):
        return jnp.broadcast_to(ref[r : r + 1, :], shape)

    def courant(entry, face):
        x = courant_ref[0, entry] - DT_FLOW * spread(above_ref, entry)
        return COURANT * jnp.tanh(jnp.where(level < spread(depth_ref, face), x, 0.0))

    def coefficients(wet, ce, ce_b, cn, cn_b):
        return (
            wet
            * (
                1.0
                - jnp.maximum(ce, 0.0)
                + jnp.minimum(ce_b, 0.0)
                - jnp.maximum(cn, 0.0)
                + jnp.minimum(cn_b, 0.0)
            ),
            -wet * jnp.minimum(ce, 0.0),
            wet * jnp.maximum(ce_b, 0.0),
            -wet * jnp.minimum(cn, 0.0),
            wet * jnp.maximum(cn_b, 0.0),
        )

    side_e, side_n = courant(13, 24), courant(14, 25)
    wet = (level < spread(depth_ref, 26)).astype(jnp.float32)
    packed_coef = coefficients(wet, side_e, turn(side_e, SLOTS, 1), side_n, turn(side_n, 1, 1))
    for i in range(5):
        side_coef_ref[i] = packed_coef[i]
    ce_b = courant(0, 0)
    for j in range(rows):
        ce, cn = courant(1 + j, 1 + j), courant(7 + j, 8 + j)
        cn_b = jnp.where(first, turn(side_n, -(SLOTS * (j + 1) + 1), 1), turn(cn, 1, 1))
        wet = (level < spread(depth_ref, 16 + j)).astype(jnp.float32)
        for i, x in enumerate(coefficients(wet, ce, ce_b, cn, cn_b)):
            coef_ref[5 * j + i] = x
        ce_b = ce
    for i in range(side_ref.shape[0]):
        x = with_sides(side_ref[i], left_ref[i], right_ref[i])
        edge_ref[i, 0] = jnp.where(slot == 0, turn(x, -6, 1), x)
        x = (
            (side_coef_ref[0] * x + side_coef_ref[1] * turn(x, -SLOTS, 1))
            + (side_coef_ref[2] * turn(x, SLOTS, 1) + side_coef_ref[3] * turn(x, -1, 1))
            + side_coef_ref[4] * turn(x, 1, 1)
        )
        edge_ref[i, 1] = jnp.where(slot == 0, turn(x, -6, 1), x)

    layer = 2.0 / level_count
    zero = jnp.zeros((SUB, cols), jnp.float32)
    for k in range(0, levels, SUB):
        at = slice(k, k + SUB)

        def shifted(tiles):
            high, low = halves(jnp.concatenate(tiles, axis=0))
            return jnp.dot(
                jnp.concatenate([high, low], axis=1),
                shift_ref[...],
                preferred_element_type=jnp.float32,
            )

        def stencil(x, coef, edge, beside):
            north = jnp.where(last8, edge, beside[:, :cols])
            south = jnp.where(first8, edge, beside[:, cols:])
            return (
                (coef[0] * x[1] + coef[1] * x[2])
                + (coef[2] * x[0] + coef[3] * north)
                + coef[4] * south
            )

        def advect(i, sums):
            sums = list(sums)
            fields = []
            for t in range(GROUP):
                t = GROUP * i + t
                rows_of = (before_ref, low_ref, high_ref, after_ref)
                x = [ref[t, n, at] for ref in rows_of for n in range(NSUB)]
                fields.append(x)
            for stage in range(NSUB):
                inner = range(1 + stage, rows + 1 - stage)
                beside = shifted([x[j - stage] for j in inner for x in fields])
                fresh = [[] for _ in fields]
                for n, j in enumerate(inner):
                    coef = [coef_ref[5 * (j - 1) + c, at] for c in range(5)]
                    for t, x in enumerate(fields):
                        edges = edge_ref[GROUP // 2 * i + t // 2, stage, at]
                        edge = turn(edges, -(HALF * (t % 2) + SLOTS * j + 1), 1)
                        row = SUB * (len(fields) * n + t)
                        fresh[t].append(
                            stencil(x[n : n + 3], coef, edge, beside[row : row + SUB])
                        )
                fields = fresh
            for t, x in enumerate(fields):
                for r in range(sub_rows):
                    moved_ref[GROUP * i + t, r, at] = x[r]
                    sums[r] = sums[r] + absorb_ref[GROUP * i + t] * x[r]
            return tuple(sums)

        sums = (zero,) * sub_rows
        for i in range(tracers // GROUP):
            sums = advect(i, sums)
        for r in range(sub_rows):
            optical = layer * (CLEAR_WATER + sums[r])
            above, total = sums_above(optical)
            through = jnp.exp(-(running_ref[r] + above))
            running_ref[r] = running_ref[r] + total
            surface = jnp.broadcast_to(surface_ref[r : r + 1, :], (SUB, cols))
            light_ref[r, at] = surface * through * jnp.exp(-0.5 * optical)
            wet = (level[at] < jnp.broadcast_to(depth_ref[17 + r : 18 + r, :], (SUB, cols))).astype(
                jnp.float32
            )
            heat_ref[0, r, at] = wet * surface * through * (1.0 - jnp.exp(-optical)) / layer
    carry_out_ref[...] = running_ref[...]


def advection(cut, level_count, absorb, surface, depth, received, own, rim, sides, carry, heat, after):
    first_part, count = cut
    tracers, _, _, cols = own[0].shape
    every, _, levels, _ = received.shape
    parts = levels // SUB
    sub_rows = surface.shape[0]
    rows = pl.BlockSpec((tracers, NSUB, SUB, cols), lambda i: (0, 0, i, 0))
    side = pl.BlockSpec((tracers // 2, SUB, cols), lambda i: (0, i, 0))
    operands = [absorb, surface, depth, received, received, *own, *rim, *sides]
    in_specs = [
        smem(),
        whole(surface.shape),
        whole(depth.shape),
        pl.BlockSpec((every, 1, levels, cols), lambda i: (0, 15, 0, 0)),
        pl.BlockSpec(
            (1, ENTRIES, SUB, cols),
            lambda i: ((first_part + i) // parts, 0, (first_part + i) % parts, 0),
        ),
        rows,
        rows,
        rows,
        rows,
        side,
        side,
        side,
    ]
    aliases = {}
    carry_shape = (sub_rows, SUB, cols)
    if carry is not None:
        operands.append(carry)
        in_specs.append(whole(carry_shape))
        aliases = {len(operands): 2}
        operands.append(heat)
    operands += after
    in_specs += [pl.BlockSpec(memory_space=pl.ANY)] * (len(operands) - len(in_specs))
    outs = [
        shaped(tracers, sub_rows, count * SUB, cols),
        shaped(sub_rows, count * SUB, cols),
        shaped(every, sub_rows, levels, cols),
        shaped(*carry_shape),
    ]
    return pl.pallas_call(
        functools.partial(advection_kernel, first_part, parts, level_count),
        grid=(count,),
        in_specs=in_specs,
        out_specs=[
            pl.BlockSpec((tracers, sub_rows, SUB, cols), lambda i: (0, 0, i, 0)),
            pl.BlockSpec((sub_rows, SUB, cols), lambda i: (0, i, 0)),
            pl.BlockSpec(
                (1, sub_rows, SUB, cols),
                lambda i: ((first_part + i) // parts, 0, (first_part + i) % parts, 0),
            ),
            whole(carry_shape),
        ],
        out_shape=outs,
        scratch_shapes=[
            pltpu.VMEM((5 * (sub_rows + 2), SUB, cols), jnp.float32),
            pltpu.VMEM((5, SUB, cols), jnp.float32),
            pltpu.VMEM((tracers // 2, 2, SUB, cols), jnp.float32),
            pltpu.VMEM((sub_rows, SUB, cols), jnp.float32),
            pltpu.VMEM((levels, cols), jnp.float32),
            pltpu.VMEM((2 * cols, 2 * cols), jnp.bfloat16),
        ],
        input_output_aliases=aliases,
        compiler_params=params(),
    )(*operands)


def spread_kernel(matrix_ref, out_ref):
    tracers = matrix_ref.shape[0]
    size = tracers * SUB
    tall = (subs_of((size, tracers)) // SUB == lanes_of((size, tracers))).astype(jnp.float32)
    wide = (lanes_of((tracers, size)) // SUB == subs_of((tracers, size))).astype(jnp.float32)
    exact = functools.partial(
        jnp.dot, precision=lax.Precision.HIGHEST, preferred_element_type=jnp.float32
    )
    same = subs_of((size, size)) % SUB == lanes_of((size, size)) % SUB
    out_ref[...] = jnp.where(same, exact(exact(tall, matrix_ref[...]), wide), 0.0)


def uptake_kernel(first_level, *refs):
    growth_ref, half_ref, dim_ref, matrix_ref, depth_ref, moved_ref, light_ref = refs[:7]
    depth_ref = depth_ref.at[lax.axis_index("comp")]
    result_ref, token_ref, uptake_ref = refs[-3:]
    token_ref[...] = jnp.zeros_like(token_ref)
    tracers, sub_rows, levels, cols = moved_ref.shape
    step = pl.program_id(0)
    matrix_high, matrix_low = halves(matrix_ref[...])
    for k in range(0, levels, SUB):
        at = slice(k, k + SUB)
        level = (first_level + step * levels + k + subs_of((SUB, cols))).astype(jnp.float32)
        light = [light_ref[r, at] for r in range(sub_rows)]
        food = [moved_ref[0, r, at] for r in range(sub_rows)]
        both = [light[r] * food[r] for r in range(sub_rows)]

        def uptake(t, _):
            for r in range(sub_rows):
                scale = (half_ref[t] + food[r]) * (light[r] + dim_ref[t])
                value = growth_ref[t] * moved_ref[t, r, at] * (both[r] / scale)
                uptake_ref[pl.ds(t * SUB, SUB), r * cols : (r + 1) * cols] = value
            return _

        lax.fori_loop(0, tracers, uptake, 0, unroll=4)
        amount = uptake_ref[...]
        high, low = halves(amount)
        dot = functools.partial(jnp.dot, preferred_element_type=jnp.float32)
        change = dot(matrix_high, high) + (dot(matrix_high, low) + dot(matrix_low, high))
        for r in range(sub_rows):
            depth = jnp.broadcast_to(depth_ref[17 + r : 18 + r, :], (SUB, cols))
            scale = DT_BIO * (level < depth).astype(jnp.float32)
            for t in range(tracers):
                result_ref[t, pl.ds(sub_rows * k + r, SUB, stride=sub_rows), :] = (
                    moved_ref[t, r, at]
                    + scale * change[SUB * t : SUB * (t + 1), r * cols : (r + 1) * cols]
                )


def uptake(cut, all_rows, scalars, matrix, depth, moved, light, result):
    first_part, count = cut
    tracers, sub_rows, _, cols = moved.shape
    operands = [*scalars, matrix, depth, moved, light]
    in_specs = [smem()] * 3 + [
        whole(matrix.shape),
        whole(depth.shape),
        pl.BlockSpec((tracers, sub_rows, SUB, cols), lambda i: (0, 0, i, 0)),
        pl.BlockSpec((sub_rows, SUB, cols), lambda i: (0, i, 0)),
    ]
    aliases = {}
    if result is not None:
        aliases = {len(operands): 0}
        operands.append(result)
        in_specs.append(pl.BlockSpec(memory_space=pl.ANY))
    return pl.pallas_call(
        functools.partial(uptake_kernel, first_part * SUB),
        grid=(count,),
        in_specs=in_specs,
        out_specs=[
            pl.BlockSpec((tracers, SUB * sub_rows, cols), lambda i: (0, first_part + i, 0)),
            whole((SUB, cols)),
        ],
        out_shape=[shaped(tracers, all_rows, cols), shaped(SUB, cols)],
        scratch_shapes=[pltpu.VMEM((tracers * SUB, sub_rows * cols), jnp.float32)],
        input_output_aliases=aliases,
        compiler_params=params(),
    )(*operands)


def warming_kernel(sea_ref, floor_ref, heat_ref, mixed_ref, warm_ref, buoyant_ref):
    blocks, sub_rows, levels, cols = heat_ref.shape
    tile_rows = blocks * sub_rows
    base = lax.axis_index("comp") * levels
    level = (base + subs_of((levels, cols))).astype(jnp.float32)
    depth = jnp.where(sea_ref[...] == 1, floor_ref[...], 0).astype(jnp.float32)
    for r in range(tile_rows):
        at = pl.ds(r, levels, stride=tile_rows)
        warm = mixed_ref[0, r] + WARMING_FACTOR * heat_ref[r // sub_rows, r % sub_rows]
        wet = (level < depth[r : r + 1]).astype(jnp.float32)
        warm_ref[at, :] = warm
        buoyant_ref[at, :] = wet * (0.2 * warm - 0.8 * mixed_ref[1, r])


def warming(heat, mixed, sea):
    _, tile_rows, levels, cols = mixed.shape
    outs = [shaped(levels * tile_rows, cols)] * 2
    return call_once(warming_kernel, [*sea, heat, mixed], outs)


def from_before(x, axis):
    return lax.ppermute(x, axis, [(i, i + 1) for i in range(lax.axis_size(axis) - 1)])


def from_after(x, axis):
    return lax.ppermute(x, axis, [(i + 1, i) for i in range(lax.axis_size(axis) - 1)])


def row_pairs():
    blocks, tiles = lax.axis_size("comp"), lax.axis_size("gx")
    places = [b * tiles + tile for tile in range(tiles) for b in range(blocks)]
    return list(zip(places[:-1], places[1:]))


def from_block_before(x):
    return lax.ppermute(x, ("comp", "gx"), row_pairs())


def from_block_after(x):
    return lax.ppermute(x, ("comp", "gx"), [(later, own) for own, later in row_pairs()])


def from_sides(x):
    if lax.axis_size("gy") == 2:
        other = lax.ppermute(x, "gy", [(0, 1), (1, 0)])
        return other, other
    return from_before(x, "gy"), from_after(x, "gy")


def on_device(
    zonal_flow_speed,
    meridional_flow_speed,
    thermal_anomaly,
    brine_anomaly_values,
    marine_indicator,
    seafloor_layer,
    dissolved_species,
    topmost_sunshine,
    attenuation_coefficient,
    peak_intake_speed,
    feedstock_midpoint_constant,
    photon_midpoint_constant,
    stoichiometry_matrix,
):
    blocks = lax.axis_size("comp")
    levels, tile_rows, tile_cols = zonal_flow_speed.shape
    tracer_count, level_count = dissolved_species.shape[:2]
    sub_rows = dissolved_species.shape[4]
    ocean = (zonal_flow_speed, meridional_flow_speed, thermal_anomaly, brine_anomaly_values)
    sea = (marine_indicator, seafloor_layer)
    flat = [x.reshape(levels * tile_rows, tile_cols) for x in ocean]
    q = dissolved_species.reshape(tracer_count, level_count, sub_rows, 1, tile_cols)
    parts = levels // SUB
    every = parts * blocks
    sizes = [every - 5 * every // 8, 3 * every // 8, every // 4]
    cuts = [(sum(sizes[:i]), size) for i, size in enumerate(sizes)]
    matrix = call_once(
        spread_kernel,
        [stoichiometry_matrix],
        [shaped(SUB * tracer_count, SUB * tracer_count)],
    )[0]
    scalars_of_uptake = (
        peak_intake_speed,
        feedstock_midpoint_constant,
        photon_midpoint_constant,
    )

    def rims(own):
        return own, (from_block_after(own[0]), from_block_before(own[1]))

    def sides(x):
        return (x, *from_sides(x))

    packed, edges, ocean_rows = pack_ocean(flat, sea, levels)
    ranges = [(first * SUB, size * SUB) for first, size in cuts]
    chunks = [rims(cut_rows(q, ranges[:1], [packed]))]
    later = cut_rows(q, ranges[1:], chunks[0][0][:1])
    up, down, packed = ocean_sides(packed, *from_sides(packed), edges)
    after, before = from_after(up, "gx"), from_before(down, "gx")
    smix, mixed, send, local, faces, depths = ocean_phase(
        blocks, levels, ocean_rows, sea, packed, after, before, later[:1]
    )
    received = lax.all_to_all(send, "comp", split_axis=0, concat_axis=0, tiled=True)
    east_new, north_new = velocities(local, faces, received)
    later = held_until(later, [depths])
    chunks += [rims(later[i : i + 2]) for i in range(0, len(later), 2)]

    surface = topmost_sunshine.reshape(sub_rows, tile_cols)
    carry, heat, result = None, None, None
    near = sides(pack_tracers(*chunks[0], later[:1]))
    for i, cut in enumerate(cuts):
        moved, light, heat, carry = advection(
            cut,
            level_count,
            attenuation_coefficient,
            surface,
            depths,
            received,
            *chunks[i],
            near,
            carry,
            heat,
            [] if i == 0 else [token],
        )
        if i + 1 < len(cuts):
            near = sides(pack_tracers(*chunks[i + 1], [carry]))
        result, token = uptake(
            cut,
            level_count * sub_rows,
            scalars_of_uptake,
            matrix,
            depths,
            moved,
            light,
            result,
        )
    heat = lax.all_to_all(heat, "comp", split_axis=0, concat_axis=0, tiled=True)
    warmed_result, buoyancy = warming(heat, mixed, sea)
    fields = (east_new, north_new, warmed_result, smix, buoyancy)
    return (
        *[x.reshape(zonal_flow_speed.shape) for x in fields],
        result.reshape(dissolved_species.shape),
    )


def solution(mesh):
    return jax.shard_map(
        on_device,
        mesh=mesh,
        in_specs=(
            P("comp", "gx", "gy"),
            P("comp", "gx", "gy"),
            P("comp", "gx", "gy"),
            P("comp", "gx", "gy"),
            P("gx", "gy"),
            P("gx", "gy"),
            P(None, None, "gx", "comp", None, "gy"),
            P("gx", "comp", None, "gy"),
            P(),
            P(),
            P(),
            P(),
            P(),
        ),
        out_specs=(
            P("comp", "gx", "gy"),
            P("comp", "gx", "gy"),
            P("comp", "gx", "gy"),
            P("comp", "gx", "gy"),
            P("comp", "gx", "gy"),
            P(None, None, "gx", "comp", None, "gy"),
        ),
        check_vma=False,
    )
```

```python
import functools

import jax
import jax.numpy as jnp
from jax import lax
from jax.experimental import pallas as pl
from jax.experimental.pallas import tpu as pltpu
from jax.sharding import PartitionSpec as P

NSUB = 2
SLOTS = 4 * NSUB
SUB = 8
GROUP = 24
HALF = 64
ENTRIES = 18

DT_FLOW = 0.1
CORIOLIS = 0.3
MIXING = 0.15
COURANT = 0.24
DT_BIO = 0.5
WARMING_FACTOR = 0.5
CLEAR_WATER = 0.5
VMEM_LIMIT = 10 * 1024 * 1024
VMEM_MOST = 62 * 1024 * 1024


def lanes_of(shape):
    return lax.broadcasted_iota(jnp.int32, shape, len(shape) - 1)


def subs_of(shape):
    return lax.broadcasted_iota(jnp.int32, shape, len(shape) - 2)


def turn(x, by, axis):
    by = by % x.shape[axis]
    return x if by == 0 else pltpu.roll(x, by, axis)


def params(limit=VMEM_LIMIT):
    return pltpu.CompilerParams(vmem_limit_bytes=limit)


def whole(shape):
    return pl.BlockSpec(shape, lambda *_: (0,) * len(shape))


def smem():
    return pl.BlockSpec(memory_space=pltpu.SMEM)


def shaped(*shape):
    return jax.ShapeDtypeStruct(shape, jnp.float32)


def halves(x):
    high = x.astype(jnp.bfloat16)
    return high, (x - high.astype(jnp.float32)).astype(jnp.bfloat16)


def sums_above(x):
    sub = subs_of(x.shape)
    running, total = x, x
    by = 1
    while by < x.shape[0]:
        running = running + jnp.where(sub >= by, turn(running, by, 0), 0.0)
        total = total + turn(total, by, 0)
        by *= 2
    return jnp.where(sub >= 1, turn(running, 1, 0), 0.0), total


def cut_kernel(cuts, q_ref, *refs):
    outs, sems = refs[-2 * len(cuts) - 1 : -1], refs[-1]
    rows = q_ref.shape[2]
    copies = [
        pltpu.make_async_copy(
            q_ref.at[:, pl.ds(start, size), r],
            outs[2 * i + r // NSUB].at[:, r % NSUB],
            sems.at[rows * i + r],
        )
        for i, (start, size) in enumerate(cuts)
        for r in range(rows)
    ]
    for copy in copies:
        copy.start()
    for copy in copies:
        copy.wait()


def cut_rows(q, cuts, after):
    tracers, _, rows, _, cols = q.shape
    anywhere = pl.BlockSpec(memory_space=pl.ANY)
    outs = [shaped(tracers, NSUB, size, 1, cols) for _, size in cuts for _ in range(2)]
    outs = pl.pallas_call(
        functools.partial(cut_kernel, cuts),
        in_specs=[anywhere] * (1 + len(after)),
        out_specs=[anywhere] * len(outs),
        out_shape=outs,
        scratch_shapes=[pltpu.SemaphoreType.DMA((rows * len(cuts),))],
        compiler_params=params(),
    )(q, *after)
    return [x.reshape(tracers, NSUB, x.shape[2], cols) for x in outs]


def hold_kernel(*refs):
    pass


def held_until(arrays, after):
    anywhere = pl.BlockSpec(memory_space=pl.ANY)
    return pl.pallas_call(
        hold_kernel,
        in_specs=[anywhere] * (len(arrays) + len(after)),
        out_specs=[anywhere] * len(arrays),
        out_shape=[shaped(*x.shape) for x in arrays],
        input_output_aliases={i: i for i in range(len(arrays))},
        compiler_params=params(),
    )(*arrays, *after)


def both_ends(acc):
    return jnp.where(lanes_of(acc.shape) % SLOTS < SLOTS // 2, acc, turn(acc, SLOTS // 2, 1))


def pack_tracers_kernel(low_ref, high_ref, after_ref, before_ref, packed_ref):
    tracers, _, _, cols = low_ref.shape
    lane = lanes_of((SUB, cols))
    for pair in range(tracers // 2):
        acc = jnp.zeros((SUB, cols), jnp.float32)
        for odd in range(2):
            t = 2 * pair + odd
            rows = [before_ref[t, 1], low_ref[t, 0], low_ref[t, 1], high_ref[t, 0], high_ref[t, 1]]
            for r, x in enumerate(rows + [after_ref[t, 0]]):
                at = HALF * odd + SLOTS * (r + 1)
                acc = jnp.where(lane // SLOTS == at // SLOTS, turn(x, at + NSUB, 1), acc)
        packed_ref[pair] = both_ends(acc)


def pack_tracers(own, rim, after):
    tracers, _, levels, cols = own[0].shape
    rows = pl.BlockSpec((tracers, NSUB, SUB, cols), lambda i: (0, 0, i, 0))
    return pl.pallas_call(
        functools.partial(ignoring, len(after), pack_tracers_kernel),
        grid=(levels // SUB,),
        in_specs=[pl.BlockSpec(memory_space=pl.ANY)] * len(after) + [rows] * 4,
        out_specs=pl.BlockSpec((tracers // 2, SUB, cols), lambda i: (0, i, 0)),
        out_shape=shaped(tracers // 2, levels, cols),
        compiler_params=params(),
    )(*after, *own, *rim)


def ignoring(count, kernel, *refs):
    kernel(*refs[count:])


def call_once(kernel, operands, outs, scratch=(), scalars=(), after=(), limit=VMEM_LIMIT):
    return pl.pallas_call(
        functools.partial(ignoring, len(after), kernel),
        grid=(1,),
        in_specs=[pl.BlockSpec(memory_space=pl.ANY)] * len(after)
        + [smem()] * len(scalars)
        + [whole(x.shape) for x in operands],
        out_specs=[whole(x.shape) for x in outs],
        out_shape=outs,
        scratch_shapes=list(scratch),
        compiler_params=params(limit),
    )(*after, *scalars, *operands)


def pack_ocean_kernel(levels, *refs):
    u_ref, v_ref, t_ref, s_ref, sea_ref, floor_ref, packed_ref, edges_ref, row_ref = refs
    edge_low_ref, edge_high_ref = edges_ref.at[0], edges_ref.at[1]
    tile_rows, cols = sea_ref.shape
    lane = lanes_of((levels, cols))
    edge_low_ref[4 * NSUB] = jnp.zeros((levels, cols), jnp.float32)
    edge_high_ref[4 * NSUB] = jnp.zeros((levels, cols), jnp.float32)
    for f, ref in enumerate((u_ref, v_ref, t_ref, s_ref)):
        acc = jnp.zeros((levels, cols), jnp.float32)
        for r in range(tile_rows):
            x = ref[pl.ds(r, levels, stride=tile_rows), :]
            row_ref[f, r] = x
            acc = jnp.where(lane // SLOTS == r, turn(x, SLOTS * r + NSUB, 1), acc)
            if r < NSUB:
                edge_low_ref[NSUB * f + r] = x
            if r >= tile_rows - NSUB:
                edge_high_ref[NSUB * f + r - tile_rows + NSUB] = x
        packed_ref[f] = both_ends(acc)
    depth = jnp.where(sea_ref[...] == 1, floor_ref[...], 0).astype(jnp.float32)
    acc = jnp.zeros((levels, cols), jnp.float32)
    for r in range(tile_rows):
        x = jnp.broadcast_to(depth[r : r + 1], (levels, cols))
        acc = jnp.where(lane // SLOTS == r, turn(x, SLOTS * r + NSUB, 1), acc)
    packed_ref[4] = both_ends(acc)
    edge_low_ref[4 * NSUB, 0:NSUB, :] = depth[0:NSUB]
    edge_high_ref[4 * NSUB, 0:NSUB, :] = depth[tile_rows - NSUB :]


def pack_ocean(flat, sea, levels):
    cols = sea[0].shape[1]
    edges = shaped(2, 4 * NSUB + 1, levels, cols)
    return call_once(
        functools.partial(pack_ocean_kernel, levels),
        [*flat, *sea],
        [shaped(5, levels, cols), edges, shaped(4, sea[0].shape[0], levels, cols)],
        limit=VMEM_MOST,
    )


def with_sides(own, left, right):
    slot = lanes_of(own.shape) % SLOTS
    ends = jnp.where(slot < NSUB, left, right)
    return jnp.where((slot < NSUB) | (slot >= SLOTS - NSUB), ends, own)


def ocean_sides_kernel(own_ref, left_ref, right_ref, edges_ref, up_ref, down_ref, out_ref):
    _, levels, cols = own_ref.shape
    rows = edges_ref.shape[1]
    up_ref[0:rows] = edges_ref[0]
    down_ref[0:rows] = edges_ref[1]
    slot = lanes_of((levels, cols)) % SLOTS
    place = lax.axis_index("gy")
    first, last = place == 0, place == lax.axis_size("gy") - 1
    for f in range(5):
        x = with_sides(own_ref[f], left_ref[f], right_ref[f])
        if f == 4:
            x = jnp.where((slot < NSUB) & first, 0.0, x)
            x = jnp.where((slot >= SLOTS - NSUB) & last, 0.0, x)
        out_ref[f] = x
        up_ref[rows + f] = x
        down_ref[rows + f] = x


def ocean_sides(own, left, right, edges):
    edge = shaped(edges.shape[1] + 5, *edges.shape[2:])
    return call_once(
        ocean_sides_kernel,
        [own, left, right, edges],
        [edge, edge, shaped(*own.shape)],
    )


def ocean_kernel(blocks, levels, *refs):
    own_ref, sea_ref, floor_ref, packed_ref, after_ref, before_ref = refs[:6]
    smix_ref, mixed_ref, send_ref, local_ref, faces_ref, depths_ref, press_ref, total_ref = refs[6:]
    tile_rows, cols = sea_ref.shape
    sub_rows = tile_rows // blocks
    shape = (levels, cols)
    lane = lanes_of(shape)
    first, last = lane == 0, lane == cols - 1
    base = lax.axis_index("comp") * levels
    level = (base + subs_of(shape)).astype(jnp.float32)
    rims = after_ref.shape[0] - 5

    def packed(f):
        after, before = after_ref[rims + f], before_ref[rims + f]
        rim = jnp.where(lane < NSUB * SLOTS, after, jnp.where(lane >= cols - NSUB * SLOTS, before, 0.0))
        return jnp.concatenate([packed_ref[f], rim], axis=1)

    def row_after(x):
        return turn(x, -SLOTS, 1)

    def row_before(x):
        return turn(x, SLOTS, 1)

    up, vp, tp, sp, dp = [packed(f) for f in range(5)]
    wide = jnp.concatenate([level, level], axis=1)
    wet = (wide < dp).astype(jnp.float32)
    heavy = wet * (-0.2 * tp + 0.8 * sp)
    above, total = sums_above(heavy)
    press = above + 0.5 * heavy
    east = up + DT_FLOW * (CORIOLIS * vp - (row_after(press) - press))
    north = vp + DT_FLOW * (-CORIOLIS * up - (turn(press, -1, 1) - press))
    open_n = wet * turn(wet, -1, 1)
    flux_t = open_n * (turn(tp, -1, 1) - tp)
    flux_s = open_n * (turn(sp, -1, 1) - sp)
    total_e, total_n = row_after(total) - total, turn(total, -1, 1) - total
    depth_e, depth_n = jnp.minimum(dp, row_after(dp)), jnp.minimum(dp, turn(dp, -1, 1))

    def window(x, g):
        x = turn(x, -SLOTS * (sub_rows * g - NSUB), 1)[:, 0:cols]
        return jnp.where(lane < HALF, x, turn(x, HALF, 1))

    for g in range(blocks):
        send_ref[g, 13] = window(east, g)
        send_ref[g, 14] = window(north, g)
        send_ref[g, 15, 13:14, :] = window(total_e, g)[0:1]
        send_ref[g, 15, 14:15, :] = window(total_n, g)[0:1]
        send_ref[g, 15, 15:16, :] = jnp.zeros((1, cols), jnp.float32)
        depths_ref[g, 24:25, :] = window(depth_e, g)[0:1]
        depths_ref[g, 25:26, :] = window(depth_n, g)[0:1]
        depths_ref[g, 26:27, :] = window(dp, g)[0:1]

    slot = lanes_of(tp.shape) % SLOTS

    def edges(x, other):
        x = jnp.where(slot == 0, turn(x, -6, 1), other)
        return x[:, 0:cols], x[:, cols:]

    edge_p, edge_w = edges(press, press), edges(wet, wet)
    edge_t, edge_s = edges(tp, flux_t), edges(sp, flux_s)
    edge_total, edge_depth = edges(total, total), edges(dp, dp)

    def edge(pair, r):
        at = r % tile_rows
        return turn(pair[0] if 0 <= r < tile_rows else pair[1], -(SLOTS * at + 1), 1)

    depth = jnp.where(sea_ref[...] == 1, floor_ref[...], 0).astype(jnp.float32)

    def row_of(f, r):
        if r < 0:
            return before_ref[NSUB * f + r + NSUB]
        if r >= tile_rows:
            return after_ref[NSUB * f + r - tile_rows]
        return own_ref[f, r]

    def depth_of(r):
        if r < 0:
            x = before_ref[4 * NSUB, r + NSUB : r + NSUB + 1, :]
        elif r >= tile_rows:
            x = after_ref[4 * NSUB, r - tile_rows : r - tile_rows + 1, :]
        else:
            x = depth[r : r + 1]
        return jnp.broadcast_to(x, shape)

    lo, hi = -NSUB, tile_rows + NSUB
    for r in range(lo, hi):
        heavy = (level < depth_of(r)).astype(jnp.float32) * (-0.2 * row_of(2, r) + 0.8 * row_of(3, r))
        above, total = sums_above(heavy)
        press_ref[r - lo] = above + 0.5 * heavy
        total_ref[r - lo] = total

    def windows(r, before):
        for g in range(blocks):
            j = r - (sub_rows * g - before)
            if 0 <= j < sub_rows + 1 + before:
                yield g, j

    flux_before = [None, None]
    for r in range(lo, hi - 1):
        press, press_e = press_ref[r - lo], press_ref[r - lo + 1]
        total, total_a = total_ref[r - lo], total_ref[r - lo + 1]
        d, d_e = depth_of(r), depth_of(r + 1)
        d_n = jnp.where(last, edge(edge_depth, r), turn(d, -1, 1))
        face_e, face_n = jnp.minimum(d, d_e), jnp.minimum(d, d_n)
        u, v = row_of(0, r), row_of(1, r)
        east = u + DT_FLOW * (CORIOLIS * v - (press_e - press))
        press_n = jnp.where(last, edge(edge_p, r), turn(press, -1, 1))
        north = v + DT_FLOW * (-CORIOLIS * u - (press_n - press))
        total_e = total_a - total
        total_n = jnp.where(last, edge(edge_total, r), turn(total, -1, 1)) - total
        for g, j in windows(r, 2):
            send_ref[g, j] = east
            send_ref[g, 15, j : j + 1, :] = total_e[0:1]
            depths_ref[g, j : j + 1, :] = face_e[0:1]
        for g, j in windows(r, 1):
            send_ref[g, 7 + j] = north
            send_ref[g, 15, 7 + j : 8 + j, :] = total_n[0:1]
            depths_ref[g, 8 + j : 9 + j, :] = face_n[0:1]
            depths_ref[g, 16 + j : 17 + j, :] = d[0:1]
        if 0 <= r < tile_rows:
            local_ref[0, r] = east
            local_ref[1, r] = north
            faces_ref[0, r : r + 1, :] = face_e[0:1]
            faces_ref[1, r : r + 1, :] = face_n[0:1]
            for g in range(blocks):
                send_ref[g, 16, r : r + 1, :] = total_e[0:1]
                send_ref[g, 17, r : r + 1, :] = total_n[0:1]
        if r < -1 or r >= tile_rows:
            continue
        open_e = (level < face_e).astype(jnp.float32)
        open_n = (level < face_n).astype(jnp.float32)
        for i, (f, ends) in enumerate(((2, edge_t), (3, edge_s))):
            x = row_of(f, r)
            flux_e = open_e * (row_of(f, r + 1) - x)
            if r >= 0:
                ending = edge(ends, r)
                flux_n = open_n * (jnp.where(last, ending, turn(x, -1, 1)) - x)
                flux_b = jnp.where(first, ending, turn(flux_n, 1, 1))
                mixed = x + MIXING * ((flux_e - flux_before[i]) + (flux_n - flux_b))
                mixed_ref[i, r] = mixed
                if i == 1:
                    smix_ref[pl.ds(r, levels, stride=tile_rows), :] = mixed
            flux_before[i] = flux_e


def ocean_phase(blocks, levels, own, sea, packed, rim_after, rim_before, after):
    tile_rows, cols = sea[0].shape
    outs = [
        shaped(levels * tile_rows, cols),
        shaped(2, tile_rows, levels, cols),
        shaped(blocks, ENTRIES, levels, cols),
        shaped(2, tile_rows, levels, cols),
        shaped(2, tile_rows, cols),
        shaped(blocks, 32, cols),
    ]
    tall = tile_rows + 2 * NSUB
    return call_once(
        functools.partial(ocean_kernel, blocks, levels),
        [own, *sea, packed, rim_after, rim_before],
        outs,
        [pltpu.VMEM((tall, levels, cols), jnp.float32)] * 2,
        after=after,
    )


def velocity_kernel(local_ref, faces_ref, received_ref, east_ref, north_ref):
    blocks = received_ref.shape[0]
    _, tile_rows, levels, cols = local_ref.shape
    group = lax.axis_index("comp")
    level = (group * levels + subs_of((levels, cols))).astype(jnp.float32)
    for f, out_ref in enumerate((east_ref, north_ref)):
        above = jnp.zeros((tile_rows, cols), jnp.float32)
        for s in range(blocks - 1):
            above = above + jnp.where(s < group, received_ref[s, f], 0.0)
        for r in range(tile_rows):
            x = local_ref[f, r] - DT_FLOW * jnp.broadcast_to(above[r : r + 1], (levels, cols))
            x = jnp.where(level < faces_ref[f, r : r + 1, :], x, 0.0)
            out_ref[pl.ds(r, levels, stride=tile_rows), :] = x


def velocities(local, faces, received):
    blocks = received.shape[0]
    _, tile_rows, levels, cols = local.shape
    out = shaped(levels * tile_rows, cols)
    return pl.pallas_call(
        velocity_kernel,
        grid=(1,),
        in_specs=[
            whole(local.shape),
            whole(faces.shape),
            pl.BlockSpec((blocks, 2, levels, cols), lambda i: (0, ENTRIES // 2 - 1, 0, 0)),
        ],
        out_specs=[whole(out.shape)] * 2,
        out_shape=[out] * 2,
        compiler_params=params(),
    )(local, faces, received)


def advection_kernel(first_part, parts, level_count, *refs):
    (
        absorb_ref,
        surface_ref,
        depth_ref,
        totals_ref,
        courant_ref,
        low_ref,
        high_ref,
        after_ref,
        before_ref,
        side_ref,
        left_ref,
        right_ref,
    ) = refs[:12]
    moved_ref, light_ref, heat_ref, carry_out_ref = refs[-10:-6]
    coef_ref, side_coef_ref, edge_ref, running_ref, above_ref, shift_ref = refs[-6:]
    depth_ref = depth_ref.at[lax.axis_index("comp")]
    step = pl.program_id(0)
    tracers, _, _, cols = low_ref.shape
    levels = courant_ref.shape[2]
    sub_rows = surface_ref.shape[0]
    rows = sub_rows + 2
    shape = (levels, cols)
    lane = lanes_of(shape)
    first, last = lane == 0, lane == cols - 1
    first8, last8 = first[0:SUB], last[0:SUB]
    slot = lane % SLOTS

    @pl.when(step == 0)
    def _():
        running_ref[...] = refs[12][...] if first_part else jnp.zeros_like(running_ref)
        size = (2 * cols, 2 * cols)
        source, to = subs_of(size) % cols, lanes_of(size)
        hit = ((to < cols) & (source == to + 1)) | ((to >= cols) & (source == to - cols - 1))
        shift_ref[...] = hit.astype(jnp.float32).astype(jnp.bfloat16)

    part = first_part + step
    above = jnp.zeros(above_ref.shape, jnp.float32)
    for s in range(totals_ref.shape[0] - 1):
        above = above + jnp.where(s < part // parts, totals_ref[s, 0], 0.0)
    above_ref[...] = above
    level = (part * levels + subs_of(shape)).astype(jnp.float32)

    def spread(ref, r):
        return jnp.broadcast_to(ref[r : r + 1, :], shape)

    def courant(entry, face):
        x = courant_ref[0, entry] - DT_FLOW * spread(above_ref, entry)
        return COURANT * jnp.tanh(jnp.where(level < spread(depth_ref, face), x, 0.0))

    def coefficients(wet, ce, ce_b, cn, cn_b):
        return (
            wet
            * (
                1.0
                - jnp.maximum(ce, 0.0)
                + jnp.minimum(ce_b, 0.0)
                - jnp.maximum(cn, 0.0)
                + jnp.minimum(cn_b, 0.0)
            ),
            -wet * jnp.minimum(ce, 0.0),
            wet * jnp.maximum(ce_b, 0.0),
            -wet * jnp.minimum(cn, 0.0),
            wet * jnp.maximum(cn_b, 0.0),
        )

    side_e, side_n = courant(13, 24), courant(14, 25)
    wet = (level < spread(depth_ref, 26)).astype(jnp.float32)
    packed_coef = coefficients(wet, side_e, turn(side_e, SLOTS, 1), side_n, turn(side_n, 1, 1))
    for i in range(5):
        side_coef_ref[i] = packed_coef[i]
    ce_b = courant(0, 0)
    for j in range(rows):
        ce, cn = courant(1 + j, 1 + j), courant(7 + j, 8 + j)
        cn_b = jnp.where(first, turn(side_n, -(SLOTS * (j + 1) + 1), 1), turn(cn, 1, 1))
        wet = (level < spread(depth_ref, 16 + j)).astype(jnp.float32)
        for i, x in enumerate(coefficients(wet, ce, ce_b, cn, cn_b)):
            coef_ref[5 * j + i] = x
        ce_b = ce
    for i in range(side_ref.shape[0]):
        x = with_sides(side_ref[i], left_ref[i], right_ref[i])
        edge_ref[i, 0] = jnp.where(slot == 0, turn(x, -6, 1), x)
        x = (
            (side_coef_ref[0] * x + side_coef_ref[1] * turn(x, -SLOTS, 1))
            + (side_coef_ref[2] * turn(x, SLOTS, 1) + side_coef_ref[3] * turn(x, -1, 1))
            + side_coef_ref[4] * turn(x, 1, 1)
        )
        edge_ref[i, 1] = jnp.where(slot == 0, turn(x, -6, 1), x)

    layer = 2.0 / level_count
    zero = jnp.zeros((SUB, cols), jnp.float32)
    for k in range(0, levels, SUB):
        at = slice(k, k + SUB)

        def shifted(tiles):
            high, low = halves(jnp.concatenate(tiles, axis=0))
            return jnp.dot(
                jnp.concatenate([high, low], axis=1),
                shift_ref[...],
                preferred_element_type=jnp.float32,
            )

        def stencil(x, coef, edge, beside):
            north = jnp.where(last8, edge, beside[:, :cols])
            south = jnp.where(first8, edge, beside[:, cols:])
            return (
                (coef[0] * x[1] + coef[1] * x[2])
                + (coef[2] * x[0] + coef[3] * north)
                + coef[4] * south
            )

        def advect(i, sums):
            sums = list(sums)
            fields = []
            for t in range(GROUP):
                t = GROUP * i + t
                rows_of = (before_ref, low_ref, high_ref, after_ref)
                x = [ref[t, n, at] for ref in rows_of for n in range(NSUB)]
                fields.append(x)
            for stage in range(NSUB):
                inner = range(1 + stage, rows + 1 - stage)
                beside = shifted([x[j - stage] for j in inner for x in fields])
                fresh = [[] for _ in fields]
                for n, j in enumerate(inner):
                    coef = [coef_ref[5 * (j - 1) + c, at] for c in range(5)]
                    for t, x in enumerate(fields):
                        edges = edge_ref[GROUP // 2 * i + t // 2, stage, at]
                        edge = turn(edges, -(HALF * (t % 2) + SLOTS * j + 1), 1)
                        row = SUB * (len(fields) * n + t)
                        fresh[t].append(
                            stencil(x[n : n + 3], coef, edge, beside[row : row + SUB])
                        )
                fields = fresh
            for t, x in enumerate(fields):
                for r in range(sub_rows):
                    moved_ref[GROUP * i + t, r, at] = x[r]
                    sums[r] = sums[r] + absorb_ref[GROUP * i + t] * x[r]
            return tuple(sums)

        sums = (zero,) * sub_rows
        for i in range(tracers // GROUP):
            sums = advect(i, sums)
        for r in range(sub_rows):
            optical = layer * (CLEAR_WATER + sums[r])
            above, total = sums_above(optical)
            through = jnp.exp(-(running_ref[r] + above))
            running_ref[r] = running_ref[r] + total
            surface = jnp.broadcast_to(surface_ref[r : r + 1, :], (SUB, cols))
            light_ref[r, at] = surface * through * jnp.exp(-0.5 * optical)
            wet = (level[at] < jnp.broadcast_to(depth_ref[17 + r : 18 + r, :], (SUB, cols))).astype(
                jnp.float32
            )
            heat_ref[0, r, at] = wet * surface * through * (1.0 - jnp.exp(-optical)) / layer
    carry_out_ref[...] = running_ref[...]


def advection(cut, level_count, absorb, surface, depth, received, own, rim, sides, carry, heat, after):
    first_part, count = cut
    tracers, _, _, cols = own[0].shape
    every, _, levels, _ = received.shape
    parts = levels // SUB
    sub_rows = surface.shape[0]
    rows = pl.BlockSpec((tracers, NSUB, SUB, cols), lambda i: (0, 0, i, 0))
    side = pl.BlockSpec((tracers // 2, SUB, cols), lambda i: (0, i, 0))
    operands = [absorb, surface, depth, received, received, *own, *rim, *sides]
    in_specs = [
        smem(),
        whole(surface.shape),
        whole(depth.shape),
        pl.BlockSpec((every, 1, levels, cols), lambda i: (0, 15, 0, 0)),
        pl.BlockSpec(
            (1, ENTRIES, SUB, cols),
            lambda i: ((first_part + i) // parts, 0, (first_part + i) % parts, 0),
        ),
        rows,
        rows,
        rows,
        rows,
        side,
        side,
        side,
    ]
    aliases = {}
    carry_shape = (sub_rows, SUB, cols)
    if carry is not None:
        operands.append(carry)
        in_specs.append(whole(carry_shape))
        aliases = {len(operands): 2}
        operands.append(heat)
    operands += after
    in_specs += [pl.BlockSpec(memory_space=pl.ANY)] * (len(operands) - len(in_specs))
    outs = [
        shaped(tracers, sub_rows, count * SUB, cols),
        shaped(sub_rows, count * SUB, cols),
        shaped(every, sub_rows, levels, cols),
        shaped(*carry_shape),
    ]
    return pl.pallas_call(
        functools.partial(advection_kernel, first_part, parts, level_count),
        grid=(count,),
        in_specs=in_specs,
        out_specs=[
            pl.BlockSpec((tracers, sub_rows, SUB, cols), lambda i: (0, 0, i, 0)),
            pl.BlockSpec((sub_rows, SUB, cols), lambda i: (0, i, 0)),
            pl.BlockSpec(
                (1, sub_rows, SUB, cols),
                lambda i: ((first_part + i) // parts, 0, (first_part + i) % parts, 0),
            ),
            whole(carry_shape),
        ],
        out_shape=outs,
        scratch_shapes=[
            pltpu.VMEM((5 * (sub_rows + 2), SUB, cols), jnp.float32),
            pltpu.VMEM((5, SUB, cols), jnp.float32),
            pltpu.VMEM((tracers // 2, 2, SUB, cols), jnp.float32),
            pltpu.VMEM((sub_rows, SUB, cols), jnp.float32),
            pltpu.VMEM((levels, cols), jnp.float32),
            pltpu.VMEM((2 * cols, 2 * cols), jnp.bfloat16),
        ],
        input_output_aliases=aliases,
        compiler_params=params(),
    )(*operands)


def spread_kernel(matrix_ref, out_ref):
    tracers = matrix_ref.shape[0]
    size = tracers * SUB
    tall = (subs_of((size, tracers)) // SUB == lanes_of((size, tracers))).astype(jnp.float32)
    wide = (lanes_of((tracers, size)) // SUB == subs_of((tracers, size))).astype(jnp.float32)
    exact = functools.partial(
        jnp.dot, precision=lax.Precision.HIGHEST, preferred_element_type=jnp.float32
    )
    same = subs_of((size, size)) % SUB == lanes_of((size, size)) % SUB
    out_ref[...] = jnp.where(same, exact(exact(tall, matrix_ref[...]), wide), 0.0)


def uptake_kernel(first_level, *refs):
    growth_ref, half_ref, dim_ref, matrix_ref, depth_ref, moved_ref, light_ref = refs[:7]
    depth_ref = depth_ref.at[lax.axis_index("comp")]
    result_ref, token_ref, uptake_ref = refs[-3:]
    token_ref[...] = jnp.zeros_like(token_ref)
    tracers, sub_rows, levels, cols = moved_ref.shape
    step = pl.program_id(0)
    matrix_high, matrix_low = halves(matrix_ref[...])
    for k in range(0, levels, SUB):
        at = slice(k, k + SUB)
        level = (first_level + step * levels + k + subs_of((SUB, cols))).astype(jnp.float32)
        light = [light_ref[r, at] for r in range(sub_rows)]
        food = [moved_ref[0, r, at] for r in range(sub_rows)]
        both = [light[r] * food[r] for r in range(sub_rows)]

        def uptake(t, _):
            for r in range(sub_rows):
                scale = (half_ref[t] + food[r]) * (light[r] + dim_ref[t])
                value = growth_ref[t] * moved_ref[t, r, at] * (both[r] / scale)
                uptake_ref[pl.ds(t * SUB, SUB), r * cols : (r + 1) * cols] = value
            return _

        lax.fori_loop(0, tracers, uptake, 0, unroll=4)
        amount = uptake_ref[...]
        high, low = halves(amount)
        dot = functools.partial(jnp.dot, preferred_element_type=jnp.float32)
        change = dot(matrix_high, high) + (dot(matrix_high, low) + dot(matrix_low, high))
        for r in range(sub_rows):
            depth = jnp.broadcast_to(depth_ref[17 + r : 18 + r, :], (SUB, cols))
            scale = DT_BIO * (level < depth).astype(jnp.float32)
            for t in range(tracers):
                result_ref[t, pl.ds(sub_rows * k + r, SUB, stride=sub_rows), :] = (
                    moved_ref[t, r, at]
                    + scale * change[SUB * t : SUB * (t + 1), r * cols : (r + 1) * cols]
                )


def uptake(cut, all_rows, scalars, matrix, depth, moved, light, result):
    first_part, count = cut
    tracers, sub_rows, _, cols = moved.shape
    operands = [*scalars, matrix, depth, moved, light]
    in_specs = [smem()] * 3 + [
        whole(matrix.shape),
        whole(depth.shape),
        pl.BlockSpec((tracers, sub_rows, SUB, cols), lambda i: (0, 0, i, 0)),
        pl.BlockSpec((sub_rows, SUB, cols), lambda i: (0, i, 0)),
    ]
    aliases = {}
    if result is not None:
        aliases = {len(operands): 0}
        operands.append(result)
        in_specs.append(pl.BlockSpec(memory_space=pl.ANY))
    return pl.pallas_call(
        functools.partial(uptake_kernel, first_part * SUB),
        grid=(count,),
        in_specs=in_specs,
        out_specs=[
            pl.BlockSpec((tracers, SUB * sub_rows, cols), lambda i: (0, first_part + i, 0)),
            whole((SUB, cols)),
        ],
        out_shape=[shaped(tracers, all_rows, cols), shaped(SUB, cols)],
        scratch_shapes=[pltpu.VMEM((tracers * SUB, sub_rows * cols), jnp.float32)],
        input_output_aliases=aliases,
        compiler_params=params(),
    )(*operands)


def warming_kernel(sea_ref, floor_ref, heat_ref, mixed_ref, warm_ref, buoyant_ref):
    blocks, sub_rows, levels, cols = heat_ref.shape
    tile_rows = blocks * sub_rows
    base = lax.axis_index("comp") * levels
    level = (base + subs_of((levels, cols))).astype(jnp.float32)
    depth = jnp.where(sea_ref[...] == 1, floor_ref[...], 0).astype(jnp.float32)
    for r in range(tile_rows):
        at = pl.ds(r, levels, stride=tile_rows)
        warm = mixed_ref[0, r] + WARMING_FACTOR * heat_ref[r // sub_rows, r % sub_rows]
        wet = (level < depth[r : r + 1]).astype(jnp.float32)
        warm_ref[at, :] = warm
        buoyant_ref[at, :] = wet * (0.2 * warm - 0.8 * mixed_ref[1, r])


def warming(heat, mixed, sea):
    _, tile_rows, levels, cols = mixed.shape
    outs = [shaped(levels * tile_rows, cols)] * 2
    return call_once(warming_kernel, [*sea, heat, mixed], outs)


def from_before(x, axis):
    return lax.ppermute(x, axis, [(i, i + 1) for i in range(lax.axis_size(axis) - 1)])


def from_after(x, axis):
    return lax.ppermute(x, axis, [(i + 1, i) for i in range(lax.axis_size(axis) - 1)])


def row_pairs():
    blocks, tiles = lax.axis_size("comp"), lax.axis_size("gx")
    places = [b * tiles + tile for tile in range(tiles) for b in range(blocks)]
    return list(zip(places[:-1], places[1:]))


def from_block_before(x):
    return lax.ppermute(x, ("comp", "gx"), row_pairs())


def from_block_after(x):
    return lax.ppermute(x, ("comp", "gx"), [(later, own) for own, later in row_pairs()])


def from_sides(x):
    if lax.axis_size("gy") == 2:
        other = lax.ppermute(x, "gy", [(0, 1), (1, 0)])
        return other, other
    return from_before(x, "gy"), from_after(x, "gy")


def on_device(
    zonal_flow_speed,
    meridional_flow_speed,
    thermal_anomaly,
    brine_anomaly_values,
    marine_indicator,
    seafloor_layer,
    dissolved_species,
    topmost_sunshine,
    attenuation_coefficient,
    peak_intake_speed,
    feedstock_midpoint_constant,
    photon_midpoint_constant,
    stoichiometry_matrix,
):
    blocks = lax.axis_size("comp")
    levels, tile_rows, tile_cols = zonal_flow_speed.shape
    tracer_count, level_count = dissolved_species.shape[:2]
    sub_rows = dissolved_species.shape[4]
    ocean = (zonal_flow_speed, meridional_flow_speed, thermal_anomaly, brine_anomaly_values)
    sea = (marine_indicator, seafloor_layer)
    flat = [x.reshape(levels * tile_rows, tile_cols) for x in ocean]
    q = dissolved_species.reshape(tracer_count, level_count, sub_rows, 1, tile_cols)
    parts = levels // SUB
    every = parts * blocks
    sizes = [every - 5 * every // 8, 3 * every // 8, every // 4]
    cuts = [(sum(sizes[:i]), size) for i, size in enumerate(sizes)]
    matrix = call_once(
        spread_kernel,
        [stoichiometry_matrix],
        [shaped(SUB * tracer_count, SUB * tracer_count)],
    )[0]
    scalars_of_uptake = (
        peak_intake_speed,
        feedstock_midpoint_constant,
        photon_midpoint_constant,
    )

    def rims(own):
        return own, (from_block_after(own[0]), from_block_before(own[1]))

    def sides(x):
        return (x, *from_sides(x))

    packed, edges, ocean_rows = pack_ocean(flat, sea, levels)
    ranges = [(first * SUB, size * SUB) for first, size in cuts]
    chunks = [rims(cut_rows(q, ranges[:1], [packed]))]
    later = cut_rows(q, ranges[1:], chunks[0][0][:1])
    up, down, packed = ocean_sides(packed, *from_sides(packed), edges)
    after, before = from_after(up, "gx"), from_before(down, "gx")
    smix, mixed, send, local, faces, depths = ocean_phase(
        blocks, levels, ocean_rows, sea, packed, after, before, later[:1]
    )
    received = lax.all_to_all(send, "comp", split_axis=0, concat_axis=0, tiled=True)
    east_new, north_new = velocities(local, faces, received)
    later = held_until(later, [received])
    chunks += [rims(later[i : i + 2]) for i in range(0, len(later), 2)]

    surface = topmost_sunshine.reshape(sub_rows, tile_cols)
    carry, heat, result = None, None, None
    near = sides(pack_tracers(*chunks[0], later[:1]))
    for i, cut in enumerate(cuts):
        moved, light, heat, carry = advection(
            cut,
            level_count,
            attenuation_coefficient,
            surface,
            depths,
            received,
            *chunks[i],
            near,
            carry,
            heat,
            [] if i == 0 else [token],
        )
        if i + 1 < len(cuts):
            near = sides(pack_tracers(*chunks[i + 1], [carry]))
        result, token = uptake(
            cut,
            level_count * sub_rows,
            scalars_of_uptake,
            matrix,
            depths,
            moved,
            light,
            result,
        )
    heat = lax.all_to_all(heat, "comp", split_axis=0, concat_axis=0, tiled=True)
    warmed_result, buoyancy = warming(heat, mixed, sea)
    fields = (east_new, north_new, warmed_result, smix, buoyancy)
    return (
        *[x.reshape(zonal_flow_speed.shape) for x in fields],
        result.reshape(dissolved_species.shape),
    )


def solution(mesh):
    return jax.shard_map(
        on_device,
        mesh=mesh,
        in_specs=(
            P("comp", "gx", "gy"),
            P("comp", "gx", "gy"),
            P("comp", "gx", "gy"),
            P("comp", "gx", "gy"),
            P("gx", "gy"),
            P("gx", "gy"),
            P(None, None, "gx", "comp", None, "gy"),
            P("gx", "comp", None, "gy"),
            P(),
            P(),
            P(),
            P(),
            P(),
        ),
        out_specs=(
            P("comp", "gx", "gy"),
            P("comp", "gx", "gy"),
            P("comp", "gx", "gy"),
            P("comp", "gx", "gy"),
            P("comp", "gx", "gy"),
            P(None, None, "gx", "comp", None, "gy"),
        ),
        check_vma=False,
    )
```

```python
import functools

import jax
import jax.numpy as jnp
from jax import lax
from jax.experimental import pallas as pl
from jax.experimental.pallas import tpu as pltpu
from jax.sharding import PartitionSpec as P

NSUB = 2
SLOTS = 4 * NSUB
SUB = 8
GROUP = 24
HALF = 64
ENTRIES = 18

DT_FLOW = 0.1
CORIOLIS = 0.3
MIXING = 0.15
COURANT = 0.24
DT_BIO = 0.5
WARMING_FACTOR = 0.5
CLEAR_WATER = 0.5
VMEM_LIMIT = 10 * 1024 * 1024
VMEM_MOST = 62 * 1024 * 1024


def lanes_of(shape):
    return lax.broadcasted_iota(jnp.int32, shape, len(shape) - 1)


def subs_of(shape):
    return lax.broadcasted_iota(jnp.int32, shape, len(shape) - 2)


def turn(x, by, axis):
    by = by % x.shape[axis]
    return x if by == 0 else pltpu.roll(x, by, axis)


def params(limit=VMEM_LIMIT):
    return pltpu.CompilerParams(vmem_limit_bytes=limit)


def whole(shape):
    return pl.BlockSpec(shape, lambda *_: (0,) * len(shape))


def smem():
    return pl.BlockSpec(memory_space=pltpu.SMEM)


def shaped(*shape):
    return jax.ShapeDtypeStruct(shape, jnp.float32)


def halves(x):
    high = x.astype(jnp.bfloat16)
    return high, (x - high.astype(jnp.float32)).astype(jnp.bfloat16)


def sums_above(x):
    sub = subs_of(x.shape)
    running, total = x, x
    by = 1
    while by < x.shape[0]:
        running = running + jnp.where(sub >= by, turn(running, by, 0), 0.0)
        total = total + turn(total, by, 0)
        by *= 2
    return jnp.where(sub >= 1, turn(running, 1, 0), 0.0), total


def cut_kernel(cuts, q_ref, *refs):
    outs, sems = refs[-2 * len(cuts) - 1 : -1], refs[-1]
    rows = q_ref.shape[2]
    copies = [
        pltpu.make_async_copy(
            q_ref.at[:, pl.ds(start, size), r],
            outs[2 * i + r // NSUB].at[:, r % NSUB],
            sems.at[rows * i + r],
        )
        for i, (start, size) in enumerate(cuts)
        for r in range(rows)
    ]
    for copy in copies:
        copy.start()
    for copy in copies:
        copy.wait()


def cut_rows(q, cuts, after):
    tracers, _, rows, _, cols = q.shape
    anywhere = pl.BlockSpec(memory_space=pl.ANY)
    outs = [shaped(tracers, NSUB, size, 1, cols) for _, size in cuts for _ in range(2)]
    outs = pl.pallas_call(
        functools.partial(cut_kernel, cuts),
        in_specs=[anywhere] * (1 + len(after)),
        out_specs=[anywhere] * len(outs),
        out_shape=outs,
        scratch_shapes=[pltpu.SemaphoreType.DMA((rows * len(cuts),))],
        compiler_params=params(),
    )(q, *after)
    return [x.reshape(tracers, NSUB, x.shape[2], cols) for x in outs]


def hold_kernel(*refs):
    refs[-1][...] = jnp.zeros_like(refs[-1])


def held_until(arrays, after):
    anywhere = pl.BlockSpec(memory_space=pl.ANY)
    token = shaped(SUB, arrays[0].shape[-1])
    outs = pl.pallas_call(
        hold_kernel,
        in_specs=[anywhere] * (len(arrays) + len(after)),
        out_specs=[anywhere] * len(arrays) + [pl.BlockSpec(memory_space=pltpu.VMEM)],
        out_shape=[shaped(*x.shape) for x in arrays] + [token],
        input_output_aliases={i: i for i in range(len(arrays))},
        compiler_params=params(),
    )(*arrays, *after)
    return outs[:-1], outs[-1]


def both_ends(acc):
    return jnp.where(lanes_of(acc.shape) % SLOTS < SLOTS // 2, acc, turn(acc, SLOTS // 2, 1))


def pack_tracers_kernel(low_ref, high_ref, after_ref, before_ref, packed_ref):
    tracers, _, _, cols = low_ref.shape
    lane = lanes_of((SUB, cols))
    for pair in range(tracers // 2):
        acc = jnp.zeros((SUB, cols), jnp.float32)
        for odd in range(2):
            t = 2 * pair + odd
            rows = [before_ref[t, 1], low_ref[t, 0], low_ref[t, 1], high_ref[t, 0], high_ref[t, 1]]
            for r, x in enumerate(rows + [after_ref[t, 0]]):
                at = HALF * odd + SLOTS * (r + 1)
                acc = jnp.where(lane // SLOTS == at // SLOTS, turn(x, at + NSUB, 1), acc)
        packed_ref[pair] = both_ends(acc)


def pack_tracers(own, rim, after):
    tracers, _, levels, cols = own[0].shape
    rows = pl.BlockSpec((tracers, NSUB, SUB, cols), lambda i: (0, 0, i, 0))
    return pl.pallas_call(
        functools.partial(ignoring, len(after), pack_tracers_kernel),
        grid=(levels // SUB,),
        in_specs=[pl.BlockSpec(memory_space=pl.ANY)] * len(after) + [rows] * 4,
        out_specs=pl.BlockSpec((tracers // 2, SUB, cols), lambda i: (0, i, 0)),
        out_shape=shaped(tracers // 2, levels, cols),
        compiler_params=params(),
    )(*after, *own, *rim)


def ignoring(count, kernel, *refs):
    kernel(*refs[count:])


def call_once(kernel, operands, outs, scratch=(), scalars=(), after=(), limit=VMEM_LIMIT):
    return pl.pallas_call(
        functools.partial(ignoring, len(after), kernel),
        grid=(1,),
        in_specs=[pl.BlockSpec(memory_space=pl.ANY)] * len(after)
        + [smem()] * len(scalars)
        + [whole(x.shape) for x in operands],
        out_specs=[whole(x.shape) for x in outs],
        out_shape=outs,
        scratch_shapes=list(scratch),
        compiler_params=params(limit),
    )(*after, *scalars, *operands)


def pack_ocean_kernel(levels, *refs):
    u_ref, v_ref, t_ref, s_ref, sea_ref, floor_ref, packed_ref, edges_ref, row_ref = refs
    edge_low_ref, edge_high_ref = edges_ref.at[0], edges_ref.at[1]
    tile_rows, cols = sea_ref.shape
    lane = lanes_of((levels, cols))
    edge_low_ref[4 * NSUB] = jnp.zeros((levels, cols), jnp.float32)
    edge_high_ref[4 * NSUB] = jnp.zeros((levels, cols), jnp.float32)
    for f, ref in enumerate((u_ref, v_ref, t_ref, s_ref)):
        acc = jnp.zeros((levels, cols), jnp.float32)
        for r in range(tile_rows):
            x = ref[pl.ds(r, levels, stride=tile_rows), :]
            row_ref[f, r] = x
            acc = jnp.where(lane // SLOTS == r, turn(x, SLOTS * r + NSUB, 1), acc)
            if r < NSUB:
                edge_low_ref[NSUB * f + r] = x
            if r >= tile_rows - NSUB:
                edge_high_ref[NSUB * f + r - tile_rows + NSUB] = x
        packed_ref[f] = both_ends(acc)
    depth = jnp.where(sea_ref[...] == 1, floor_ref[...], 0).astype(jnp.float32)
    acc = jnp.zeros((levels, cols), jnp.float32)
    for r in range(tile_rows):
        x = jnp.broadcast_to(depth[r : r + 1], (levels, cols))
        acc = jnp.where(lane // SLOTS == r, turn(x, SLOTS * r + NSUB, 1), acc)
    packed_ref[4] = both_ends(acc)
    edge_low_ref[4 * NSUB, 0:NSUB, :] = depth[0:NSUB]
    edge_high_ref[4 * NSUB, 0:NSUB, :] = depth[tile_rows - NSUB :]


def pack_ocean(flat, sea, levels):
    cols = sea[0].shape[1]
    edges = shaped(2, 4 * NSUB + 1, levels, cols)
    return call_once(
        functools.partial(pack_ocean_kernel, levels),
        [*flat, *sea],
        [shaped(5, levels, cols), edges, shaped(4, sea[0].shape[0], levels, cols)],
        limit=VMEM_MOST,
    )


def with_sides(own, left, right):
    slot = lanes_of(own.shape) % SLOTS
    ends = jnp.where(slot < NSUB, left, right)
    return jnp.where((slot < NSUB) | (slot >= SLOTS - NSUB), ends, own)


def ocean_sides_kernel(own_ref, left_ref, right_ref, edges_ref, up_ref, down_ref, out_ref):
    _, levels, cols = own_ref.shape
    rows = edges_ref.shape[1]
    up_ref[0:rows] = edges_ref[0]
    down_ref[0:rows] = edges_ref[1]
    slot = lanes_of((levels, cols)) % SLOTS
    place = lax.axis_index("gy")
    first, last = place == 0, place == lax.axis_size("gy") - 1
    for f in range(5):
        x = with_sides(own_ref[f], left_ref[f], right_ref[f])
        if f == 4:
            x = jnp.where((slot < NSUB) & first, 0.0, x)
            x = jnp.where((slot >= SLOTS - NSUB) & last, 0.0, x)
        out_ref[f] = x
        up_ref[rows + f] = x
        down_ref[rows + f] = x


def ocean_sides(own, left, right, edges):
    edge = shaped(edges.shape[1] + 5, *edges.shape[2:])
    return call_once(
        ocean_sides_kernel,
        [own, left, right, edges],
        [edge, edge, shaped(*own.shape)],
    )


def ocean_kernel(blocks, levels, *refs):
    own_ref, sea_ref, floor_ref, packed_ref, after_ref, before_ref = refs[:6]
    smix_ref, mixed_ref, send_ref, local_ref, faces_ref, depths_ref, press_ref, total_ref = refs[6:]
    tile_rows, cols = sea_ref.shape
    sub_rows = tile_rows // blocks
    shape = (levels, cols)
    lane = lanes_of(shape)
    first, last = lane == 0, lane == cols - 1
    base = lax.axis_index("comp") * levels
    level = (base + subs_of(shape)).astype(jnp.float32)
    rims = after_ref.shape[0] - 5

    def packed(f):
        after, before = after_ref[rims + f], before_ref[rims + f]
        rim = jnp.where(lane < NSUB * SLOTS, after, jnp.where(lane >= cols - NSUB * SLOTS, before, 0.0))
        return jnp.concatenate([packed_ref[f], rim], axis=1)

    def row_after(x):
        return turn(x, -SLOTS, 1)

    def row_before(x):
        return turn(x, SLOTS, 1)

    up, vp, tp, sp, dp = [packed(f) for f in range(5)]
    wide = jnp.concatenate([level, level], axis=1)
    wet = (wide < dp).astype(jnp.float32)
    heavy = wet * (-0.2 * tp + 0.8 * sp)
    above, total = sums_above(heavy)
    press = above + 0.5 * heavy
    east = up + DT_FLOW * (CORIOLIS * vp - (row_after(press) - press))
    north = vp + DT_FLOW * (-CORIOLIS * up - (turn(press, -1, 1) - press))
    open_n = wet * turn(wet, -1, 1)
    flux_t = open_n * (turn(tp, -1, 1) - tp)
    flux_s = open_n * (turn(sp, -1, 1) - sp)
    total_e, total_n = row_after(total) - total, turn(total, -1, 1) - total
    depth_e, depth_n = jnp.minimum(dp, row_after(dp)), jnp.minimum(dp, turn(dp, -1, 1))

    def window(x, g):
        x = turn(x, -SLOTS * (sub_rows * g - NSUB), 1)[:, 0:cols]
        return jnp.where(lane < HALF, x, turn(x, HALF, 1))

    for g in range(blocks):
        send_ref[g, 13] = window(east, g)
        send_ref[g, 14] = window(north, g)
        send_ref[g, 15, 13:14, :] = window(total_e, g)[0:1]
        send_ref[g, 15, 14:15, :] = window(total_n, g)[0:1]
        send_ref[g, 15, 15:16, :] = jnp.zeros((1, cols), jnp.float32)
        depths_ref[g, 24:25, :] = window(depth_e, g)[0:1]
        depths_ref[g, 25:26, :] = window(depth_n, g)[0:1]
        depths_ref[g, 26:27, :] = window(dp, g)[0:1]

    slot = lanes_of(tp.shape) % SLOTS

    def edges(x, other):
        x = jnp.where(slot == 0, turn(x, -6, 1), other)
        return x[:, 0:cols], x[:, cols:]

    edge_p, edge_w = edges(press, press), edges(wet, wet)
    edge_t, edge_s = edges(tp, flux_t), edges(sp, flux_s)
    edge_total, edge_depth = edges(total, total), edges(dp, dp)

    def edge(pair, r):
        at = r % tile_rows
        return turn(pair[0] if 0 <= r < tile_rows else pair[1], -(SLOTS * at + 1), 1)

    depth = jnp.where(sea_ref[...] == 1, floor_ref[...], 0).astype(jnp.float32)

    def row_of(f, r):
        if r < 0:
            return before_ref[NSUB * f + r + NSUB]
        if r >= tile_rows:
            return after_ref[NSUB * f + r - tile_rows]
        return own_ref[f, r]

    def depth_of(r):
        if r < 0:
            x = before_ref[4 * NSUB, r + NSUB : r + NSUB + 1, :]
        elif r >= tile_rows:
            x = after_ref[4 * NSUB, r - tile_rows : r - tile_rows + 1, :]
        else:
            x = depth[r : r + 1]
        return jnp.broadcast_to(x, shape)

    lo, hi = -NSUB, tile_rows + NSUB
    for r in range(lo, hi):
        heavy = (level < depth_of(r)).astype(jnp.float32) * (-0.2 * row_of(2, r) + 0.8 * row_of(3, r))
        above, total = sums_above(heavy)
        press_ref[r - lo] = above + 0.5 * heavy
        total_ref[r - lo] = total

    def windows(r, before):
        for g in range(blocks):
            j = r - (sub_rows * g - before)
            if 0 <= j < sub_rows + 1 + before:
                yield g, j

    flux_before = [None, None]
    for r in range(lo, hi - 1):
        press, press_e = press_ref[r - lo], press_ref[r - lo + 1]
        total, total_a = total_ref[r - lo], total_ref[r - lo + 1]
        d, d_e = depth_of(r), depth_of(r + 1)
        d_n = jnp.where(last, edge(edge_depth, r), turn(d, -1, 1))
        face_e, face_n = jnp.minimum(d, d_e), jnp.minimum(d, d_n)
        u, v = row_of(0, r), row_of(1, r)
        east = u + DT_FLOW * (CORIOLIS * v - (press_e - press))
        press_n = jnp.where(last, edge(edge_p, r), turn(press, -1, 1))
        north = v + DT_FLOW * (-CORIOLIS * u - (press_n - press))
        total_e = total_a - total
        total_n = jnp.where(last, edge(edge_total, r), turn(total, -1, 1)) - total
        for g, j in windows(r, 2):
            send_ref[g, j] = east
            send_ref[g, 15, j : j + 1, :] = total_e[0:1]
            depths_ref[g, j : j + 1, :] = face_e[0:1]
        for g, j in windows(r, 1):
            send_ref[g, 7 + j] = north
            send_ref[g, 15, 7 + j : 8 + j, :] = total_n[0:1]
            depths_ref[g, 8 + j : 9 + j, :] = face_n[0:1]
            depths_ref[g, 16 + j : 17 + j, :] = d[0:1]
        if 0 <= r < tile_rows:
            local_ref[0, r] = east
            local_ref[1, r] = north
            faces_ref[0, r : r + 1, :] = face_e[0:1]
            faces_ref[1, r : r + 1, :] = face_n[0:1]
            for g in range(blocks):
                send_ref[g, 16, r : r + 1, :] = total_e[0:1]
                send_ref[g, 17, r : r + 1, :] = total_n[0:1]
        if r < -1 or r >= tile_rows:
            continue
        open_e = (level < face_e).astype(jnp.float32)
        open_n = (level < face_n).astype(jnp.float32)
        for i, (f, ends) in enumerate(((2, edge_t), (3, edge_s))):
            x = row_of(f, r)
            flux_e = open_e * (row_of(f, r + 1) - x)
            if r >= 0:
                ending = edge(ends, r)
                flux_n = open_n * (jnp.where(last, ending, turn(x, -1, 1)) - x)
                flux_b = jnp.where(first, ending, turn(flux_n, 1, 1))
                mixed = x + MIXING * ((flux_e - flux_before[i]) + (flux_n - flux_b))
                mixed_ref[i, r] = mixed
                if i == 1:
                    smix_ref[pl.ds(r, levels, stride=tile_rows), :] = mixed
            flux_before[i] = flux_e


def ocean_phase(blocks, levels, own, sea, packed, rim_after, rim_before, after):
    tile_rows, cols = sea[0].shape
    outs = [
        shaped(levels * tile_rows, cols),
        shaped(2, tile_rows, levels, cols),
        shaped(blocks, ENTRIES, levels, cols),
        shaped(2, tile_rows, levels, cols),
        shaped(2, tile_rows, cols),
        shaped(blocks, 32, cols),
    ]
    tall = tile_rows + 2 * NSUB
    return call_once(
        functools.partial(ocean_kernel, blocks, levels),
        [own, *sea, packed, rim_after, rim_before],
        outs,
        [pltpu.VMEM((tall, levels, cols), jnp.float32)] * 2,
        after=after,
    )


def velocity_kernel(local_ref, faces_ref, received_ref, east_ref, north_ref):
    blocks = received_ref.shape[0]
    _, tile_rows, levels, cols = local_ref.shape
    group = lax.axis_index("comp")
    level = (group * levels + subs_of((levels, cols))).astype(jnp.float32)
    for f, out_ref in enumerate((east_ref, north_ref)):
        above = jnp.zeros((tile_rows, cols), jnp.float32)
        for s in range(blocks - 1):
            above = above + jnp.where(s < group, received_ref[s, f], 0.0)
        for r in range(tile_rows):
            x = local_ref[f, r] - DT_FLOW * jnp.broadcast_to(above[r : r + 1], (levels, cols))
            x = jnp.where(level < faces_ref[f, r : r + 1, :], x, 0.0)
            out_ref[pl.ds(r, levels, stride=tile_rows), :] = x


def velocities(local, faces, received):
    blocks = received.shape[0]
    _, tile_rows, levels, cols = local.shape
    out = shaped(levels * tile_rows, cols)
    return pl.pallas_call(
        velocity_kernel,
        grid=(1,),
        in_specs=[
            whole(local.shape),
            whole(faces.shape),
            pl.BlockSpec((blocks, 2, levels, cols), lambda i: (0, ENTRIES // 2 - 1, 0, 0)),
        ],
        out_specs=[whole(out.shape)] * 2,
        out_shape=[out] * 2,
        compiler_params=params(),
    )(local, faces, received)


def advection_kernel(first_part, parts, level_count, *refs):
    (
        absorb_ref,
        surface_ref,
        depth_ref,
        totals_ref,
        courant_ref,
        low_ref,
        high_ref,
        after_ref,
        before_ref,
        side_ref,
        left_ref,
        right_ref,
    ) = refs[:12]
    moved_ref, light_ref, heat_ref, carry_out_ref = refs[-10:-6]
    coef_ref, side_coef_ref, edge_ref, running_ref, above_ref, shift_ref = refs[-6:]
    depth_ref = depth_ref.at[lax.axis_index("comp")]
    step = pl.program_id(0)
    tracers, _, _, cols = low_ref.shape
    levels = courant_ref.shape[2]
    sub_rows = surface_ref.shape[0]
    rows = sub_rows + 2
    shape = (levels, cols)
    lane = lanes_of(shape)
    first, last = lane == 0, lane == cols - 1
    first8, last8 = first[0:SUB], last[0:SUB]
    slot = lane % SLOTS

    @pl.when(step == 0)
    def _():
        running_ref[...] = refs[12][...] if first_part else jnp.zeros_like(running_ref)
        size = (2 * cols, 2 * cols)
        source, to = subs_of(size) % cols, lanes_of(size)
        hit = ((to < cols) & (source == to + 1)) | ((to >= cols) & (source == to - cols - 1))
        shift_ref[...] = hit.astype(jnp.float32).astype(jnp.bfloat16)

    part = first_part + step
    above = jnp.zeros(above_ref.shape, jnp.float32)
    for s in range(totals_ref.shape[0] - 1):
        above = above + jnp.where(s < part // parts, totals_ref[s, 0], 0.0)
    above_ref[...] = above
    level = (part * levels + subs_of(shape)).astype(jnp.float32)

    def spread(ref, r):
        return jnp.broadcast_to(ref[r : r + 1, :], shape)

    def courant(entry, face):
        x = courant_ref[0, entry] - DT_FLOW * spread(above_ref, entry)
        return COURANT * jnp.tanh(jnp.where(level < spread(depth_ref, face), x, 0.0))

    def coefficients(wet, ce, ce_b, cn, cn_b):
        return (
            wet
            * (
                1.0
                - jnp.maximum(ce, 0.0)
                + jnp.minimum(ce_b, 0.0)
                - jnp.maximum(cn, 0.0)
                + jnp.minimum(cn_b, 0.0)
            ),
            -wet * jnp.minimum(ce, 0.0),
            wet * jnp.maximum(ce_b, 0.0),
            -wet * jnp.minimum(cn, 0.0),
            wet * jnp.maximum(cn_b, 0.0),
        )

    side_e, side_n = courant(13, 24), courant(14, 25)
    wet = (level < spread(depth_ref, 26)).astype(jnp.float32)
    packed_coef = coefficients(wet, side_e, turn(side_e, SLOTS, 1), side_n, turn(side_n, 1, 1))
    for i in range(5):
        side_coef_ref[i] = packed_coef[i]
    ce_b = courant(0, 0)
    for j in range(rows):
        ce, cn = courant(1 + j, 1 + j), courant(7 + j, 8 + j)
        cn_b = jnp.where(first, turn(side_n, -(SLOTS * (j + 1) + 1), 1), turn(cn, 1, 1))
        wet = (level < spread(depth_ref, 16 + j)).astype(jnp.float32)
        for i, x in enumerate(coefficients(wet, ce, ce_b, cn, cn_b)):
            coef_ref[5 * j + i] = x
        ce_b = ce
    for i in range(side_ref.shape[0]):
        x = with_sides(side_ref[i], left_ref[i], right_ref[i])
        edge_ref[i, 0] = jnp.where(slot == 0, turn(x, -6, 1), x)
        x = (
            (side_coef_ref[0] * x + side_coef_ref[1] * turn(x, -SLOTS, 1))
            + (side_coef_ref[2] * turn(x, SLOTS, 1) + side_coef_ref[3] * turn(x, -1, 1))
            + side_coef_ref[4] * turn(x, 1, 1)
        )
        edge_ref[i, 1] = jnp.where(slot == 0, turn(x, -6, 1), x)

    layer = 2.0 / level_count
    zero = jnp.zeros((SUB, cols), jnp.float32)
    for k in range(0, levels, SUB):
        at = slice(k, k + SUB)

        def shifted(tiles):
            high, low = halves(jnp.concatenate(tiles, axis=0))
            return jnp.dot(
                jnp.concatenate([high, low], axis=1),
                shift_ref[...],
                preferred_element_type=jnp.float32,
            )

        def stencil(x, coef, edge, beside):
            north = jnp.where(last8, edge, beside[:, :cols])
            south = jnp.where(first8, edge, beside[:, cols:])
            return (
                (coef[0] * x[1] + coef[1] * x[2])
                + (coef[2] * x[0] + coef[3] * north)
                + coef[4] * south
            )

        def advect(i, sums):
            sums = list(sums)
            fields = []
            for t in range(GROUP):
                t = GROUP * i + t
                rows_of = (before_ref, low_ref, high_ref, after_ref)
                x = [ref[t, n, at] for ref in rows_of for n in range(NSUB)]
                fields.append(x)
            for stage in range(NSUB):
                inner = range(1 + stage, rows + 1 - stage)
                beside = shifted([x[j - stage] for j in inner for x in fields])
                fresh = [[] for _ in fields]
                for n, j in enumerate(inner):
                    coef = [coef_ref[5 * (j - 1) + c, at] for c in range(5)]
                    for t, x in enumerate(fields):
                        edges = edge_ref[GROUP // 2 * i + t // 2, stage, at]
                        edge = turn(edges, -(HALF * (t % 2) + SLOTS * j + 1), 1)
                        row = SUB * (len(fields) * n + t)
                        fresh[t].append(
                            stencil(x[n : n + 3], coef, edge, beside[row : row + SUB])
                        )
                fields = fresh
            for t, x in enumerate(fields):
                for r in range(sub_rows):
                    moved_ref[GROUP * i + t, r, at] = x[r]
                    sums[r] = sums[r] + absorb_ref[GROUP * i + t] * x[r]
            return tuple(sums)

        sums = (zero,) * sub_rows
        for i in range(tracers // GROUP):
            sums = advect(i, sums)
        for r in range(sub_rows):
            optical = layer * (CLEAR_WATER + sums[r])
            above, total = sums_above(optical)
            through = jnp.exp(-(running_ref[r] + above))
            running_ref[r] = running_ref[r] + total
            surface = jnp.broadcast_to(surface_ref[r : r + 1, :], (SUB, cols))
            light_ref[r, at] = surface * through * jnp.exp(-0.5 * optical)
            wet = (level[at] < jnp.broadcast_to(depth_ref[17 + r : 18 + r, :], (SUB, cols))).astype(
                jnp.float32
            )
            heat_ref[0, r, at] = wet * surface * through * (1.0 - jnp.exp(-optical)) / layer
    carry_out_ref[...] = running_ref[...]


def advection(cut, level_count, absorb, surface, depth, received, own, rim, sides, carry, heat, after):
    first_part, count = cut
    tracers, _, _, cols = own[0].shape
    every, _, levels, _ = received.shape
    parts = levels // SUB
    sub_rows = surface.shape[0]
    rows = pl.BlockSpec((tracers, NSUB, SUB, cols), lambda i: (0, 0, i, 0))
    side = pl.BlockSpec((tracers // 2, SUB, cols), lambda i: (0, i, 0))
    operands = [absorb, surface, depth, received, received, *own, *rim, *sides]
    in_specs = [
        smem(),
        whole(surface.shape),
        whole(depth.shape),
        pl.BlockSpec((every, 1, levels, cols), lambda i: (0, 15, 0, 0)),
        pl.BlockSpec(
            (1, ENTRIES, SUB, cols),
            lambda i: ((first_part + i) // parts, 0, (first_part + i) % parts, 0),
        ),
        rows,
        rows,
        rows,
        rows,
        side,
        side,
        side,
    ]
    aliases = {}
    carry_shape = (sub_rows, SUB, cols)
    if carry is not None:
        operands.append(carry)
        in_specs.append(whole(carry_shape))
        aliases = {len(operands): 2}
        operands.append(heat)
    operands += after
    in_specs += [pl.BlockSpec(memory_space=pl.ANY)] * (len(operands) - len(in_specs))
    outs = [
        shaped(tracers, sub_rows, count * SUB, cols),
        shaped(sub_rows, count * SUB, cols),
        shaped(every, sub_rows, levels, cols),
        shaped(*carry_shape),
    ]
    return pl.pallas_call(
        functools.partial(advection_kernel, first_part, parts, level_count),
        grid=(count,),
        in_specs=in_specs,
        out_specs=[
            pl.BlockSpec((tracers, sub_rows, SUB, cols), lambda i: (0, 0, i, 0)),
            pl.BlockSpec((sub_rows, SUB, cols), lambda i: (0, i, 0)),
            pl.BlockSpec(
                (1, sub_rows, SUB, cols),
                lambda i: ((first_part + i) // parts, 0, (first_part + i) % parts, 0),
            ),
            whole(carry_shape),
        ],
        out_shape=outs,
        scratch_shapes=[
            pltpu.VMEM((5 * (sub_rows + 2), SUB, cols), jnp.float32),
            pltpu.VMEM((5, SUB, cols), jnp.float32),
            pltpu.VMEM((tracers // 2, 2, SUB, cols), jnp.float32),
            pltpu.VMEM((sub_rows, SUB, cols), jnp.float32),
            pltpu.VMEM((levels, cols), jnp.float32),
            pltpu.VMEM((2 * cols, 2 * cols), jnp.bfloat16),
        ],
        input_output_aliases=aliases,
        compiler_params=params(),
    )(*operands)


def spread_kernel(matrix_ref, out_ref):
    tracers = matrix_ref.shape[0]
    size = tracers * SUB
    tall = (subs_of((size, tracers)) // SUB == lanes_of((size, tracers))).astype(jnp.float32)
    wide = (lanes_of((tracers, size)) // SUB == subs_of((tracers, size))).astype(jnp.float32)
    exact = functools.partial(
        jnp.dot, precision=lax.Precision.HIGHEST, preferred_element_type=jnp.float32
    )
    same = subs_of((size, size)) % SUB == lanes_of((size, size)) % SUB
    out_ref[...] = jnp.where(same, exact(exact(tall, matrix_ref[...]), wide), 0.0)


def uptake_kernel(first_level, *refs):
    growth_ref, half_ref, dim_ref, matrix_ref, depth_ref, moved_ref, light_ref = refs[:7]
    depth_ref = depth_ref.at[lax.axis_index("comp")]
    result_ref, token_ref, uptake_ref = refs[-3:]
    token_ref[...] = jnp.zeros_like(token_ref)
    tracers, sub_rows, levels, cols = moved_ref.shape
    step = pl.program_id(0)
    matrix_high, matrix_low = halves(matrix_ref[...])
    for k in range(0, levels, SUB):
        at = slice(k, k + SUB)
        level = (first_level + step * levels + k + subs_of((SUB, cols))).astype(jnp.float32)
        light = [light_ref[r, at] for r in range(sub_rows)]
        food = [moved_ref[0, r, at] for r in range(sub_rows)]
        both = [light[r] * food[r] for r in range(sub_rows)]

        def uptake(t, _):
            for r in range(sub_rows):
                scale = (half_ref[t] + food[r]) * (light[r] + dim_ref[t])
                value = growth_ref[t] * moved_ref[t, r, at] * (both[r] / scale)
                uptake_ref[pl.ds(t * SUB, SUB), r * cols : (r + 1) * cols] = value
            return _

        lax.fori_loop(0, tracers, uptake, 0, unroll=4)
        amount = uptake_ref[...]
        high, low = halves(amount)
        dot = functools.partial(jnp.dot, preferred_element_type=jnp.float32)
        change = dot(matrix_high, high) + (dot(matrix_high, low) + dot(matrix_low, high))
        for r in range(sub_rows):
            depth = jnp.broadcast_to(depth_ref[17 + r : 18 + r, :], (SUB, cols))
            scale = DT_BIO * (level < depth).astype(jnp.float32)
            for t in range(tracers):
                result_ref[t, pl.ds(sub_rows * k + r, SUB, stride=sub_rows), :] = (
                    moved_ref[t, r, at]
                    + scale * change[SUB * t : SUB * (t + 1), r * cols : (r + 1) * cols]
                )


def uptake(cut, all_rows, scalars, matrix, depth, moved, light, result):
    first_part, count = cut
    tracers, sub_rows, _, cols = moved.shape
    operands = [*scalars, matrix, depth, moved, light]
    in_specs = [smem()] * 3 + [
        whole(matrix.shape),
        whole(depth.shape),
        pl.BlockSpec((tracers, sub_rows, SUB, cols), lambda i: (0, 0, i, 0)),
        pl.BlockSpec((sub_rows, SUB, cols), lambda i: (0, i, 0)),
    ]
    aliases = {}
    if result is not None:
        aliases = {len(operands): 0}
        operands.append(result)
        in_specs.append(pl.BlockSpec(memory_space=pl.ANY))
    return pl.pallas_call(
        functools.partial(uptake_kernel, first_part * SUB),
        grid=(count,),
        in_specs=in_specs,
        out_specs=[
            pl.BlockSpec((tracers, SUB * sub_rows, cols), lambda i: (0, first_part + i, 0)),
            whole((SUB, cols)),
        ],
        out_shape=[shaped(tracers, all_rows, cols), shaped(SUB, cols)],
        scratch_shapes=[pltpu.VMEM((tracers * SUB, sub_rows * cols), jnp.float32)],
        input_output_aliases=aliases,
        compiler_params=params(),
    )(*operands)


def warming_kernel(sea_ref, floor_ref, heat_ref, mixed_ref, warm_ref, buoyant_ref):
    blocks, sub_rows, levels, cols = heat_ref.shape
    tile_rows = blocks * sub_rows
    base = lax.axis_index("comp") * levels
    level = (base + subs_of((levels, cols))).astype(jnp.float32)
    depth = jnp.where(sea_ref[...] == 1, floor_ref[...], 0).astype(jnp.float32)
    for r in range(tile_rows):
        at = pl.ds(r, levels, stride=tile_rows)
        warm = mixed_ref[0, r] + WARMING_FACTOR * heat_ref[r // sub_rows, r % sub_rows]
        wet = (level < depth[r : r + 1]).astype(jnp.float32)
        warm_ref[at, :] = warm
        buoyant_ref[at, :] = wet * (0.2 * warm - 0.8 * mixed_ref[1, r])


def warming(heat, mixed, sea):
    _, tile_rows, levels, cols = mixed.shape
    outs = [shaped(levels * tile_rows, cols)] * 2
    return call_once(warming_kernel, [*sea, heat, mixed], outs)


def from_before(x, axis):
    return lax.ppermute(x, axis, [(i, i + 1) for i in range(lax.axis_size(axis) - 1)])


def from_after(x, axis):
    return lax.ppermute(x, axis, [(i + 1, i) for i in range(lax.axis_size(axis) - 1)])


def row_pairs():
    blocks, tiles = lax.axis_size("comp"), lax.axis_size("gx")
    places = [b * tiles + tile for tile in range(tiles) for b in range(blocks)]
    return list(zip(places[:-1], places[1:]))


def from_block_before(x):
    return lax.ppermute(x, ("comp", "gx"), row_pairs())


def from_block_after(x):
    return lax.ppermute(x, ("comp", "gx"), [(later, own) for own, later in row_pairs()])


def from_sides(x):
    if lax.axis_size("gy") == 2:
        other = lax.ppermute(x, "gy", [(0, 1), (1, 0)])
        return other, other
    return from_before(x, "gy"), from_after(x, "gy")


def on_device(
    zonal_flow_speed,
    meridional_flow_speed,
    thermal_anomaly,
    brine_anomaly_values,
    marine_indicator,
    seafloor_layer,
    dissolved_species,
    topmost_sunshine,
    attenuation_coefficient,
    peak_intake_speed,
    feedstock_midpoint_constant,
    photon_midpoint_constant,
    stoichiometry_matrix,
):
    blocks = lax.axis_size("comp")
    levels, tile_rows, tile_cols = zonal_flow_speed.shape
    tracer_count, level_count = dissolved_species.shape[:2]
    sub_rows = dissolved_species.shape[4]
    ocean = (zonal_flow_speed, meridional_flow_speed, thermal_anomaly, brine_anomaly_values)
    sea = (marine_indicator, seafloor_layer)
    flat = [x.reshape(levels * tile_rows, tile_cols) for x in ocean]
    q = dissolved_species.reshape(tracer_count, level_count, sub_rows, 1, tile_cols)
    parts = levels // SUB
    every = parts * blocks
    sizes = [every - 5 * every // 8, 3 * every // 8, every // 4]
    cuts = [(sum(sizes[:i]), size) for i, size in enumerate(sizes)]
    matrix = call_once(
        spread_kernel,
        [stoichiometry_matrix],
        [shaped(SUB * tracer_count, SUB * tracer_count)],
    )[0]
    scalars_of_uptake = (
        peak_intake_speed,
        feedstock_midpoint_constant,
        photon_midpoint_constant,
    )

    def rims(own):
        return own, (from_block_after(own[0]), from_block_before(own[1]))

    def sides(x):
        return (x, *from_sides(x))

    packed, edges, ocean_rows = pack_ocean(flat, sea, levels)
    ranges = [(first * SUB, size * SUB) for first, size in cuts]
    chunks = [rims(cut_rows(q, ranges[:1], [packed]))]
    later = cut_rows(q, ranges[1:], chunks[0][0][:1])
    up, down, packed = ocean_sides(packed, *from_sides(packed), edges)
    after, before = from_after(up, "gx"), from_before(down, "gx")
    rim, arrived = held_until(chunks[0][1], later[:1])
    chunks = [(chunks[0][0], rim)]
    smix, mixed, send, local, faces, depths = ocean_phase(
        blocks, levels, ocean_rows, sea, packed, after, before, [arrived]
    )
    received = lax.all_to_all(send, "comp", split_axis=0, concat_axis=0, tiled=True)
    east_new, north_new = velocities(local, faces, received)
    later, _ = held_until(later, [received])
    chunks += [rims(later[i : i + 2]) for i in range(0, len(later), 2)]

    surface = topmost_sunshine.reshape(sub_rows, tile_cols)
    carry, heat, result = None, None, None
    near = sides(pack_tracers(*chunks[0], []))
    for i, cut in enumerate(cuts):
        moved, light, heat, carry = advection(
            cut,
            level_count,
            attenuation_coefficient,
            surface,
            depths,
            received,
            *chunks[i],
            near,
            carry,
            heat,
            [] if i == 0 else [token],
        )
        if i + 1 < len(cuts):
            near = sides(pack_tracers(*chunks[i + 1], [carry]))
        result, token = uptake(
            cut,
            level_count * sub_rows,
            scalars_of_uptake,
            matrix,
            depths,
            moved,
            light,
            result,
        )
    heat = lax.all_to_all(heat, "comp", split_axis=0, concat_axis=0, tiled=True)
    warmed_result, buoyancy = warming(heat, mixed, sea)
    fields = (east_new, north_new, warmed_result, smix, buoyancy)
    return (
        *[x.reshape(zonal_flow_speed.shape) for x in fields],
        result.reshape(dissolved_species.shape),
    )


def solution(mesh):
    return jax.shard_map(
        on_device,
        mesh=mesh,
        in_specs=(
            P("comp", "gx", "gy"),
            P("comp", "gx", "gy"),
            P("comp", "gx", "gy"),
            P("comp", "gx", "gy"),
            P("gx", "gy"),
            P("gx", "gy"),
            P(None, None, "gx", "comp", None, "gy"),
            P("gx", "comp", None, "gy"),
            P(),
            P(),
            P(),
            P(),
            P(),
        ),
        out_specs=(
            P("comp", "gx", "gy"),
            P("comp", "gx", "gy"),
            P("comp", "gx", "gy"),
            P("comp", "gx", "gy"),
            P("comp", "gx", "gy"),
            P(None, None, "gx", "comp", None, "gy"),
        ),
        check_vma=False,
    )
```

```python
import functools

import jax
import jax.numpy as jnp
from jax import lax
from jax.experimental import pallas as pl
from jax.experimental.pallas import tpu as pltpu
from jax.sharding import PartitionSpec as P

NSUB = 2
SLOTS = 4 * NSUB
SUB = 8
GROUP = 24
HALF = 64
ENTRIES = 18

DT_FLOW = 0.1
CORIOLIS = 0.3
MIXING = 0.15
COURANT = 0.24
DT_BIO = 0.5
WARMING_FACTOR = 0.5
CLEAR_WATER = 0.5
VMEM_LIMIT = 10 * 1024 * 1024
VMEM_MOST = 62 * 1024 * 1024


def lanes_of(shape):
    return lax.broadcasted_iota(jnp.int32, shape, len(shape) - 1)


def subs_of(shape):
    return lax.broadcasted_iota(jnp.int32, shape, len(shape) - 2)


def turn(x, by, axis):
    by = by % x.shape[axis]
    return x if by == 0 else pltpu.roll(x, by, axis)


def params(limit=VMEM_LIMIT):
    return pltpu.CompilerParams(vmem_limit_bytes=limit)


def whole(shape):
    return pl.BlockSpec(shape, lambda *_: (0,) * len(shape))


def smem():
    return pl.BlockSpec(memory_space=pltpu.SMEM)


def shaped(*shape):
    return jax.ShapeDtypeStruct(shape, jnp.float32)


def halves(x):
    high = x.astype(jnp.bfloat16)
    return high, (x - high.astype(jnp.float32)).astype(jnp.bfloat16)


def sums_above(x):
    sub = subs_of(x.shape)
    running, total = x, x
    by = 1
    while by < x.shape[0]:
        running = running + jnp.where(sub >= by, turn(running, by, 0), 0.0)
        total = total + turn(total, by, 0)
        by *= 2
    return jnp.where(sub >= 1, turn(running, 1, 0), 0.0), total


def cut_kernel(cuts, q_ref, *refs):
    outs, sems = refs[-2 * len(cuts) - 1 : -1], refs[-1]
    rows = q_ref.shape[2]
    copies = [
        pltpu.make_async_copy(
            q_ref.at[:, pl.ds(start, size), r],
            outs[2 * i + r // NSUB].at[:, r % NSUB],
            sems.at[rows * i + r],
        )
        for i, (start, size) in enumerate(cuts)
        for r in range(rows)
    ]
    for copy in copies:
        copy.start()
    for copy in copies:
        copy.wait()


def cut_rows(q, cuts, after):
    tracers, _, rows, _, cols = q.shape
    anywhere = pl.BlockSpec(memory_space=pl.ANY)
    outs = [shaped(tracers, NSUB, size, 1, cols) for _, size in cuts for _ in range(2)]
    outs = pl.pallas_call(
        functools.partial(cut_kernel, cuts),
        in_specs=[anywhere] * (1 + len(after)),
        out_specs=[anywhere] * len(outs),
        out_shape=outs,
        scratch_shapes=[pltpu.SemaphoreType.DMA((rows * len(cuts),))],
        compiler_params=params(),
    )(q, *after)
    return [x.reshape(tracers, NSUB, x.shape[2], cols) for x in outs]


def hold_kernel(*refs):
    refs[-1][...] = jnp.zeros_like(refs[-1])


def held_until(arrays, after):
    anywhere = pl.BlockSpec(memory_space=pl.ANY)
    token = shaped(SUB, arrays[0].shape[-1])
    outs = pl.pallas_call(
        hold_kernel,
        in_specs=[anywhere] * (len(arrays) + len(after)),
        out_specs=[anywhere] * len(arrays) + [pl.BlockSpec(memory_space=pltpu.VMEM)],
        out_shape=[shaped(*x.shape) for x in arrays] + [token],
        input_output_aliases={i: i for i in range(len(arrays))},
        compiler_params=params(),
    )(*arrays, *after)
    return outs[:-1], outs[-1]


def both_ends(acc):
    return jnp.where(lanes_of(acc.shape) % SLOTS < SLOTS // 2, acc, turn(acc, SLOTS // 2, 1))


def pack_tracers_kernel(low_ref, high_ref, after_ref, before_ref, packed_ref):
    tracers, _, _, cols = low_ref.shape
    lane = lanes_of((SUB, cols))
    for pair in range(tracers // 2):
        acc = jnp.zeros((SUB, cols), jnp.float32)
        for odd in range(2):
            t = 2 * pair + odd
            rows = [before_ref[t, 1], low_ref[t, 0], low_ref[t, 1], high_ref[t, 0], high_ref[t, 1]]
            for r, x in enumerate(rows + [after_ref[t, 0]]):
                at = HALF * odd + SLOTS * (r + 1)
                acc = jnp.where(lane // SLOTS == at // SLOTS, turn(x, at + NSUB, 1), acc)
        packed_ref[pair] = both_ends(acc)


def pack_tracers(own, rim, after):
    tracers, _, levels, cols = own[0].shape
    rows = pl.BlockSpec((tracers, NSUB, SUB, cols), lambda i: (0, 0, i, 0))
    return pl.pallas_call(
        functools.partial(ignoring, len(after), pack_tracers_kernel),
        grid=(levels // SUB,),
        in_specs=[pl.BlockSpec(memory_space=pl.ANY)] * len(after) + [rows] * 4,
        out_specs=pl.BlockSpec((tracers // 2, SUB, cols), lambda i: (0, i, 0)),
        out_shape=shaped(tracers // 2, levels, cols),
        compiler_params=params(),
    )(*after, *own, *rim)


def ignoring(count, kernel, *refs):
    kernel(*refs[count:])


def call_once(kernel, operands, outs, scratch=(), scalars=(), after=(), limit=VMEM_LIMIT):
    return pl.pallas_call(
        functools.partial(ignoring, len(after), kernel),
        grid=(1,),
        in_specs=[pl.BlockSpec(memory_space=pl.ANY)] * len(after)
        + [smem()] * len(scalars)
        + [whole(x.shape) for x in operands],
        out_specs=[whole(x.shape) for x in outs],
        out_shape=outs,
        scratch_shapes=list(scratch),
        compiler_params=params(limit),
    )(*after, *scalars, *operands)


def pack_ocean_kernel(levels, *refs):
    u_ref, v_ref, t_ref, s_ref, sea_ref, floor_ref, packed_ref, edges_ref, row_ref = refs
    edge_low_ref, edge_high_ref = edges_ref.at[0], edges_ref.at[1]
    tile_rows, cols = sea_ref.shape
    lane = lanes_of((levels, cols))
    edge_low_ref[4 * NSUB] = jnp.zeros((levels, cols), jnp.float32)
    edge_high_ref[4 * NSUB] = jnp.zeros((levels, cols), jnp.float32)
    for f, ref in enumerate((u_ref, v_ref, t_ref, s_ref)):
        acc = jnp.zeros((levels, cols), jnp.float32)
        for r in range(tile_rows):
            x = ref[pl.ds(r, levels, stride=tile_rows), :]
            row_ref[f, r] = x
            acc = jnp.where(lane // SLOTS == r, turn(x, SLOTS * r + NSUB, 1), acc)
            if r < NSUB:
                edge_low_ref[NSUB * f + r] = x
            if r >= tile_rows - NSUB:
                edge_high_ref[NSUB * f + r - tile_rows + NSUB] = x
        packed_ref[f] = both_ends(acc)
    depth = jnp.where(sea_ref[...] == 1, floor_ref[...], 0).astype(jnp.float32)
    acc = jnp.zeros((levels, cols), jnp.float32)
    for r in range(tile_rows):
        x = jnp.broadcast_to(depth[r : r + 1], (levels, cols))
        acc = jnp.where(lane // SLOTS == r, turn(x, SLOTS * r + NSUB, 1), acc)
    packed_ref[4] = both_ends(acc)
    edge_low_ref[4 * NSUB, 0:NSUB, :] = depth[0:NSUB]
    edge_high_ref[4 * NSUB, 0:NSUB, :] = depth[tile_rows - NSUB :]


def pack_ocean(flat, sea, levels):
    cols = sea[0].shape[1]
    edges = shaped(2, 4 * NSUB + 1, levels, cols)
    return call_once(
        functools.partial(pack_ocean_kernel, levels),
        [*flat, *sea],
        [shaped(5, levels, cols), edges, shaped(4, sea[0].shape[0], levels, cols)],
        limit=VMEM_MOST,
    )


def with_sides(own, left, right):
    slot = lanes_of(own.shape) % SLOTS
    ends = jnp.where(slot < NSUB, left, right)
    return jnp.where((slot < NSUB) | (slot >= SLOTS - NSUB), ends, own)


def ocean_sides_kernel(own_ref, left_ref, right_ref, edges_ref, up_ref, down_ref, out_ref):
    _, levels, cols = own_ref.shape
    rows = edges_ref.shape[1]
    up_ref[0:rows] = edges_ref[0]
    down_ref[0:rows] = edges_ref[1]
    slot = lanes_of((levels, cols)) % SLOTS
    place = lax.axis_index("gy")
    first, last = place == 0, place == lax.axis_size("gy") - 1
    for f in range(5):
        x = with_sides(own_ref[f], left_ref[f], right_ref[f])
        if f == 4:
            x = jnp.where((slot < NSUB) & first, 0.0, x)
            x = jnp.where((slot >= SLOTS - NSUB) & last, 0.0, x)
        out_ref[f] = x
        up_ref[rows + f] = x
        down_ref[rows + f] = x


def ocean_sides(own, left, right, edges):
    edge = shaped(edges.shape[1] + 5, *edges.shape[2:])
    return call_once(
        ocean_sides_kernel,
        [own, left, right, edges],
        [edge, edge, shaped(*own.shape)],
    )


def ocean_kernel(blocks, levels, *refs):
    own_ref, sea_ref, floor_ref, packed_ref, after_ref, before_ref = refs[:6]
    smix_ref, mixed_ref, send_ref, local_ref, faces_ref, depths_ref, press_ref, total_ref = refs[6:]
    tile_rows, cols = sea_ref.shape
    sub_rows = tile_rows // blocks
    shape = (levels, cols)
    lane = lanes_of(shape)
    first, last = lane == 0, lane == cols - 1
    base = lax.axis_index("comp") * levels
    level = (base + subs_of(shape)).astype(jnp.float32)
    rims = after_ref.shape[0] - 5

    def packed(f):
        after, before = after_ref[rims + f], before_ref[rims + f]
        rim = jnp.where(lane < NSUB * SLOTS, after, jnp.where(lane >= cols - NSUB * SLOTS, before, 0.0))
        return jnp.concatenate([packed_ref[f], rim], axis=1)

    def row_after(x):
        return turn(x, -SLOTS, 1)

    def row_before(x):
        return turn(x, SLOTS, 1)

    up, vp, tp, sp, dp = [packed(f) for f in range(5)]
    wide = jnp.concatenate([level, level], axis=1)
    wet = (wide < dp).astype(jnp.float32)
    heavy = wet * (-0.2 * tp + 0.8 * sp)
    above, total = sums_above(heavy)
    press = above + 0.5 * heavy
    east = up + DT_FLOW * (CORIOLIS * vp - (row_after(press) - press))
    north = vp + DT_FLOW * (-CORIOLIS * up - (turn(press, -1, 1) - press))
    open_n = wet * turn(wet, -1, 1)
    flux_t = open_n * (turn(tp, -1, 1) - tp)
    flux_s = open_n * (turn(sp, -1, 1) - sp)
    total_e, total_n = row_after(total) - total, turn(total, -1, 1) - total
    depth_e, depth_n = jnp.minimum(dp, row_after(dp)), jnp.minimum(dp, turn(dp, -1, 1))

    def window(x, g):
        x = turn(x, -SLOTS * (sub_rows * g - NSUB), 1)[:, 0:cols]
        return jnp.where(lane < HALF, x, turn(x, HALF, 1))

    for g in range(blocks):
        send_ref[g, 13] = window(east, g)
        send_ref[g, 14] = window(north, g)
        send_ref[g, 15, 13:14, :] = window(total_e, g)[0:1]
        send_ref[g, 15, 14:15, :] = window(total_n, g)[0:1]
        send_ref[g, 15, 15:16, :] = jnp.zeros((1, cols), jnp.float32)
        depths_ref[g, 24:25, :] = window(depth_e, g)[0:1]
        depths_ref[g, 25:26, :] = window(depth_n, g)[0:1]
        depths_ref[g, 26:27, :] = window(dp, g)[0:1]

    slot = lanes_of(tp.shape) % SLOTS

    def edges(x, other):
        x = jnp.where(slot == 0, turn(x, -6, 1), other)
        return x[:, 0:cols], x[:, cols:]

    edge_p, edge_w = edges(press, press), edges(wet, wet)
    edge_t, edge_s = edges(tp, flux_t), edges(sp, flux_s)
    edge_total, edge_depth = edges(total, total), edges(dp, dp)

    def edge(pair, r):
        at = r % tile_rows
        return turn(pair[0] if 0 <= r < tile_rows else pair[1], -(SLOTS * at + 1), 1)

    depth = jnp.where(sea_ref[...] == 1, floor_ref[...], 0).astype(jnp.float32)

    def row_of(f, r):
        if r < 0:
            return before_ref[NSUB * f + r + NSUB]
        if r >= tile_rows:
            return after_ref[NSUB * f + r - tile_rows]
        return own_ref[f, r]

    def depth_of(r):
        if r < 0:
            x = before_ref[4 * NSUB, r + NSUB : r + NSUB + 1, :]
        elif r >= tile_rows:
            x = after_ref[4 * NSUB, r - tile_rows : r - tile_rows + 1, :]
        else:
            x = depth[r : r + 1]
        return jnp.broadcast_to(x, shape)

    lo, hi = -NSUB, tile_rows + NSUB
    for r in range(lo, hi):
        heavy = (level < depth_of(r)).astype(jnp.float32) * (-0.2 * row_of(2, r) + 0.8 * row_of(3, r))
        above, total = sums_above(heavy)
        press_ref[r - lo] = above + 0.5 * heavy
        total_ref[r - lo] = total

    def windows(r, before):
        for g in range(blocks):
            j = r - (sub_rows * g - before)
            if 0 <= j < sub_rows + 1 + before:
                yield g, j

    flux_before = [None, None]
    for r in range(lo, hi - 1):
        press, press_e = press_ref[r - lo], press_ref[r - lo + 1]
        total, total_a = total_ref[r - lo], total_ref[r - lo + 1]
        d, d_e = depth_of(r), depth_of(r + 1)
        d_n = jnp.where(last, edge(edge_depth, r), turn(d, -1, 1))
        face_e, face_n = jnp.minimum(d, d_e), jnp.minimum(d, d_n)
        u, v = row_of(0, r), row_of(1, r)
        east = u + DT_FLOW * (CORIOLIS * v - (press_e - press))
        press_n = jnp.where(last, edge(edge_p, r), turn(press, -1, 1))
        north = v + DT_FLOW * (-CORIOLIS * u - (press_n - press))
        total_e = total_a - total
        total_n = jnp.where(last, edge(edge_total, r), turn(total, -1, 1)) - total
        for g, j in windows(r, 2):
            send_ref[g, j] = east
            send_ref[g, 15, j : j + 1, :] = total_e[0:1]
            depths_ref[g, j : j + 1, :] = face_e[0:1]
        for g, j in windows(r, 1):
            send_ref[g, 7 + j] = north
            send_ref[g, 15, 7 + j : 8 + j, :] = total_n[0:1]
            depths_ref[g, 8 + j : 9 + j, :] = face_n[0:1]
            depths_ref[g, 16 + j : 17 + j, :] = d[0:1]
        if 0 <= r < tile_rows:
            local_ref[0, r] = east
            local_ref[1, r] = north
            faces_ref[0, r : r + 1, :] = face_e[0:1]
            faces_ref[1, r : r + 1, :] = face_n[0:1]
            for g in range(blocks):
                send_ref[g, 16, r : r + 1, :] = total_e[0:1]
                send_ref[g, 17, r : r + 1, :] = total_n[0:1]
        if r < -1 or r >= tile_rows:
            continue
        open_e = (level < face_e).astype(jnp.float32)
        open_n = (level < face_n).astype(jnp.float32)
        for i, (f, ends) in enumerate(((2, edge_t), (3, edge_s))):
            x = row_of(f, r)
            flux_e = open_e * (row_of(f, r + 1) - x)
            if r >= 0:
                ending = edge(ends, r)
                flux_n = open_n * (jnp.where(last, ending, turn(x, -1, 1)) - x)
                flux_b = jnp.where(first, ending, turn(flux_n, 1, 1))
                mixed = x + MIXING * ((flux_e - flux_before[i]) + (flux_n - flux_b))
                mixed_ref[i, r] = mixed
                if i == 1:
                    smix_ref[pl.ds(r, levels, stride=tile_rows), :] = mixed
            flux_before[i] = flux_e


def ocean_phase(blocks, levels, own, sea, packed, rim_after, rim_before, after):
    tile_rows, cols = sea[0].shape
    outs = [
        shaped(levels * tile_rows, cols),
        shaped(2, tile_rows, levels, cols),
        shaped(blocks, ENTRIES, levels, cols),
        shaped(2, tile_rows, levels, cols),
        shaped(2, tile_rows, cols),
        shaped(blocks, 32, cols),
    ]
    tall = tile_rows + 2 * NSUB
    return call_once(
        functools.partial(ocean_kernel, blocks, levels),
        [own, *sea, packed, rim_after, rim_before],
        outs,
        [pltpu.VMEM((tall, levels, cols), jnp.float32)] * 2,
        after=after,
    )


def velocity_kernel(local_ref, faces_ref, received_ref, east_ref, north_ref):
    blocks = received_ref.shape[0]
    _, tile_rows, levels, cols = local_ref.shape
    group = lax.axis_index("comp")
    level = (group * levels + subs_of((levels, cols))).astype(jnp.float32)
    for f, out_ref in enumerate((east_ref, north_ref)):
        above = jnp.zeros((tile_rows, cols), jnp.float32)
        for s in range(blocks - 1):
            above = above + jnp.where(s < group, received_ref[s, f], 0.0)
        for r in range(tile_rows):
            x = local_ref[f, r] - DT_FLOW * jnp.broadcast_to(above[r : r + 1], (levels, cols))
            x = jnp.where(level < faces_ref[f, r : r + 1, :], x, 0.0)
            out_ref[pl.ds(r, levels, stride=tile_rows), :] = x


def velocities(local, faces, received):
    blocks = received.shape[0]
    _, tile_rows, levels, cols = local.shape
    out = shaped(levels * tile_rows, cols)
    return pl.pallas_call(
        velocity_kernel,
        grid=(1,),
        in_specs=[
            whole(local.shape),
            whole(faces.shape),
            pl.BlockSpec((blocks, 2, levels, cols), lambda i: (0, ENTRIES // 2 - 1, 0, 0)),
        ],
        out_specs=[whole(out.shape)] * 2,
        out_shape=[out] * 2,
        compiler_params=params(),
    )(local, faces, received)


def advection_kernel(first_part, parts, level_count, *refs):
    (
        absorb_ref,
        surface_ref,
        depth_ref,
        totals_ref,
        courant_ref,
        low_ref,
        high_ref,
        after_ref,
        before_ref,
        side_ref,
        left_ref,
        right_ref,
    ) = refs[:12]
    moved_ref, light_ref, heat_ref, carry_out_ref = refs[-10:-6]
    coef_ref, side_coef_ref, edge_ref, running_ref, above_ref, shift_ref = refs[-6:]
    depth_ref = depth_ref.at[lax.axis_index("comp")]
    step = pl.program_id(0)
    tracers, _, _, cols = low_ref.shape
    levels = courant_ref.shape[2]
    sub_rows = surface_ref.shape[0]
    rows = sub_rows + 2
    shape = (levels, cols)
    lane = lanes_of(shape)
    first, last = lane == 0, lane == cols - 1
    first8, last8 = first[0:SUB], last[0:SUB]
    slot = lane % SLOTS

    @pl.when(step == 0)
    def _():
        running_ref[...] = refs[12][...] if first_part else jnp.zeros_like(running_ref)
        size = (2 * cols, 2 * cols)
        source, to = subs_of(size) % cols, lanes_of(size)
        hit = ((to < cols) & (source == to + 1)) | ((to >= cols) & (source == to - cols - 1))
        shift_ref[...] = hit.astype(jnp.float32).astype(jnp.bfloat16)

    part = first_part + step
    above = jnp.zeros(above_ref.shape, jnp.float32)
    for s in range(totals_ref.shape[0] - 1):
        above = above + jnp.where(s < part // parts, totals_ref[s, 0], 0.0)
    above_ref[...] = above
    level = (part * levels + subs_of(shape)).astype(jnp.float32)

    def spread(ref, r):
        return jnp.broadcast_to(ref[r : r + 1, :], shape)

    def courant(entry, face):
        x = courant_ref[0, entry] - DT_FLOW * spread(above_ref, entry)
        return COURANT * jnp.tanh(jnp.where(level < spread(depth_ref, face), x, 0.0))

    def coefficients(wet, ce, ce_b, cn, cn_b):
        return (
            wet
            * (
                1.0
                - jnp.maximum(ce, 0.0)
                + jnp.minimum(ce_b, 0.0)
                - jnp.maximum(cn, 0.0)
                + jnp.minimum(cn_b, 0.0)
            ),
            -wet * jnp.minimum(ce, 0.0),
            wet * jnp.maximum(ce_b, 0.0),
            -wet * jnp.minimum(cn, 0.0),
            wet * jnp.maximum(cn_b, 0.0),
        )

    side_e, side_n = courant(13, 24), courant(14, 25)
    wet = (level < spread(depth_ref, 26)).astype(jnp.float32)
    packed_coef = coefficients(wet, side_e, turn(side_e, SLOTS, 1), side_n, turn(side_n, 1, 1))
    for i in range(5):
        side_coef_ref[i] = packed_coef[i]
    ce_b = courant(0, 0)
    for j in range(rows):
        ce, cn = courant(1 + j, 1 + j), courant(7 + j, 8 + j)
        cn_b = jnp.where(first, turn(side_n, -(SLOTS * (j + 1) + 1), 1), turn(cn, 1, 1))
        wet = (level < spread(depth_ref, 16 + j)).astype(jnp.float32)
        for i, x in enumerate(coefficients(wet, ce, ce_b, cn, cn_b)):
            coef_ref[5 * j + i] = x
        ce_b = ce
    for i in range(side_ref.shape[0]):
        x = with_sides(side_ref[i], left_ref[i], right_ref[i])
        edge_ref[i, 0] = jnp.where(slot == 0, turn(x, -6, 1), x)
        x = (
            (side_coef_ref[0] * x + side_coef_ref[1] * turn(x, -SLOTS, 1))
            + (side_coef_ref[2] * turn(x, SLOTS, 1) + side_coef_ref[3] * turn(x, -1, 1))
            + side_coef_ref[4] * turn(x, 1, 1)
        )
        edge_ref[i, 1] = jnp.where(slot == 0, turn(x, -6, 1), x)

    layer = 2.0 / level_count
    zero = jnp.zeros((SUB, cols), jnp.float32)
    for k in range(0, levels, SUB):
        at = slice(k, k + SUB)

        def shifted(tiles):
            high, low = halves(jnp.concatenate(tiles, axis=0))
            return jnp.dot(
                jnp.concatenate([high, low], axis=1),
                shift_ref[...],
                preferred_element_type=jnp.float32,
            )

        def stencil(x, coef, edge, beside):
            north = jnp.where(last8, edge, beside[:, :cols])
            south = jnp.where(first8, edge, beside[:, cols:])
            return (
                (coef[0] * x[1] + coef[1] * x[2])
                + (coef[2] * x[0] + coef[3] * north)
                + coef[4] * south
            )

        def advect(i, sums):
            sums = list(sums)
            fields = []
            for t in range(GROUP):
                t = GROUP * i + t
                rows_of = (before_ref, low_ref, high_ref, after_ref)
                x = [ref[t, n, at] for ref in rows_of for n in range(NSUB)]
                fields.append(x)
            for stage in range(NSUB):
                inner = range(1 + stage, rows + 1 - stage)
                beside = shifted([x[j - stage] for j in inner for x in fields])
                fresh = [[] for _ in fields]
                for n, j in enumerate(inner):
                    coef = [coef_ref[5 * (j - 1) + c, at] for c in range(5)]
                    for t, x in enumerate(fields):
                        edges = edge_ref[GROUP // 2 * i + t // 2, stage, at]
                        edge = turn(edges, -(HALF * (t % 2) + SLOTS * j + 1), 1)
                        row = SUB * (len(fields) * n + t)
                        fresh[t].append(
                            stencil(x[n : n + 3], coef, edge, beside[row : row + SUB])
                        )
                fields = fresh
            for t, x in enumerate(fields):
                for r in range(sub_rows):
                    moved_ref[GROUP * i + t, r, at] = x[r]
                    sums[r] = sums[r] + absorb_ref[GROUP * i + t] * x[r]
            return tuple(sums)

        sums = (zero,) * sub_rows
        for i in range(tracers // GROUP):
            sums = advect(i, sums)
        for r in range(sub_rows):
            optical = layer * (CLEAR_WATER + sums[r])
            above, total = sums_above(optical)
            through = jnp.exp(-(running_ref[r] + above))
            running_ref[r] = running_ref[r] + total
            surface = jnp.broadcast_to(surface_ref[r : r + 1, :], (SUB, cols))
            light_ref[r, at] = surface * through * jnp.exp(-0.5 * optical)
            wet = (level[at] < jnp.broadcast_to(depth_ref[17 + r : 18 + r, :], (SUB, cols))).astype(
                jnp.float32
            )
            heat_ref[0, r, at] = wet * surface * through * (1.0 - jnp.exp(-optical)) / layer
    carry_out_ref[...] = running_ref[...]


def advection(cut, level_count, absorb, surface, depth, received, own, rim, sides, carry, heat, after):
    first_part, count = cut
    tracers, _, _, cols = own[0].shape
    every, _, levels, _ = received.shape
    parts = levels // SUB
    sub_rows = surface.shape[0]
    rows = pl.BlockSpec((tracers, NSUB, SUB, cols), lambda i: (0, 0, i, 0))
    side = pl.BlockSpec((tracers // 2, SUB, cols), lambda i: (0, i, 0))
    operands = [absorb, surface, depth, received, received, *own, *rim, *sides]
    in_specs = [
        smem(),
        whole(surface.shape),
        whole(depth.shape),
        pl.BlockSpec((every, 1, levels, cols), lambda i: (0, 15, 0, 0)),
        pl.BlockSpec(
            (1, ENTRIES, SUB, cols),
            lambda i: ((first_part + i) // parts, 0, (first_part + i) % parts, 0),
        ),
        rows,
        rows,
        rows,
        rows,
        side,
        side,
        side,
    ]
    aliases = {}
    carry_shape = (sub_rows, SUB, cols)
    if carry is not None:
        operands.append(carry)
        in_specs.append(whole(carry_shape))
        aliases = {len(operands): 2}
        operands.append(heat)
    operands += after
    in_specs += [pl.BlockSpec(memory_space=pl.ANY)] * (len(operands) - len(in_specs))
    outs = [
        shaped(tracers, sub_rows, count * SUB, cols),
        shaped(sub_rows, count * SUB, cols),
        shaped(every, sub_rows, levels, cols),
        shaped(*carry_shape),
    ]
    return pl.pallas_call(
        functools.partial(advection_kernel, first_part, parts, level_count),
        grid=(count,),
        in_specs=in_specs,
        out_specs=[
            pl.BlockSpec((tracers, sub_rows, SUB, cols), lambda i: (0, 0, i, 0)),
            pl.BlockSpec((sub_rows, SUB, cols), lambda i: (0, i, 0)),
            pl.BlockSpec(
                (1, sub_rows, SUB, cols),
                lambda i: ((first_part + i) // parts, 0, (first_part + i) % parts, 0),
            ),
            whole(carry_shape),
        ],
        out_shape=outs,
        scratch_shapes=[
            pltpu.VMEM((5 * (sub_rows + 2), SUB, cols), jnp.float32),
            pltpu.VMEM((5, SUB, cols), jnp.float32),
            pltpu.VMEM((tracers // 2, 2, SUB, cols), jnp.float32),
            pltpu.VMEM((sub_rows, SUB, cols), jnp.float32),
            pltpu.VMEM((levels, cols), jnp.float32),
            pltpu.VMEM((2 * cols, 2 * cols), jnp.bfloat16),
        ],
        input_output_aliases=aliases,
        compiler_params=params(),
    )(*operands)


def spread_kernel(matrix_ref, out_ref):
    tracers = matrix_ref.shape[0]
    size = tracers * SUB
    tall = (subs_of((size, tracers)) // SUB == lanes_of((size, tracers))).astype(jnp.float32)
    wide = (lanes_of((tracers, size)) // SUB == subs_of((tracers, size))).astype(jnp.float32)
    exact = functools.partial(
        jnp.dot, precision=lax.Precision.HIGHEST, preferred_element_type=jnp.float32
    )
    same = subs_of((size, size)) % SUB == lanes_of((size, size)) % SUB
    out_ref[...] = jnp.where(same, exact(exact(tall, matrix_ref[...]), wide), 0.0)


def uptake_kernel(first_level, *refs):
    growth_ref, half_ref, dim_ref, matrix_ref, depth_ref, moved_ref, light_ref = refs[:7]
    depth_ref = depth_ref.at[lax.axis_index("comp")]
    result_ref, token_ref, uptake_ref = refs[-3:]
    token_ref[...] = jnp.zeros_like(token_ref)
    tracers, sub_rows, levels, cols = moved_ref.shape
    step = pl.program_id(0)
    matrix_high, matrix_low = halves(matrix_ref[...])
    for k in range(0, levels, SUB):
        at = slice(k, k + SUB)
        level = (first_level + step * levels + k + subs_of((SUB, cols))).astype(jnp.float32)
        light = [light_ref[r, at] for r in range(sub_rows)]
        food = [moved_ref[0, r, at] for r in range(sub_rows)]
        both = [light[r] * food[r] for r in range(sub_rows)]

        def uptake(t, _):
            for r in range(sub_rows):
                scale = (half_ref[t] + food[r]) * (light[r] + dim_ref[t])
                value = growth_ref[t] * moved_ref[t, r, at] * (both[r] / scale)
                uptake_ref[pl.ds(t * SUB, SUB), r * cols : (r + 1) * cols] = value
            return _

        lax.fori_loop(0, tracers, uptake, 0, unroll=4)
        amount = uptake_ref[...]
        high, low = halves(amount)
        dot = functools.partial(jnp.dot, preferred_element_type=jnp.float32)
        change = dot(matrix_high, high) + (dot(matrix_high, low) + dot(matrix_low, high))
        for r in range(sub_rows):
            depth = jnp.broadcast_to(depth_ref[17 + r : 18 + r, :], (SUB, cols))
            scale = DT_BIO * (level < depth).astype(jnp.float32)
            for t in range(tracers):
                result_ref[t, pl.ds(sub_rows * k + r, SUB, stride=sub_rows), :] = (
                    moved_ref[t, r, at]
                    + scale * change[SUB * t : SUB * (t + 1), r * cols : (r + 1) * cols]
                )


def uptake(cut, all_rows, scalars, matrix, depth, moved, light, result):
    first_part, count = cut
    tracers, sub_rows, _, cols = moved.shape
    operands = [*scalars, matrix, depth, moved, light]
    in_specs = [smem()] * 3 + [
        whole(matrix.shape),
        whole(depth.shape),
        pl.BlockSpec((tracers, sub_rows, SUB, cols), lambda i: (0, 0, i, 0)),
        pl.BlockSpec((sub_rows, SUB, cols), lambda i: (0, i, 0)),
    ]
    aliases = {}
    if result is not None:
        aliases = {len(operands): 0}
        operands.append(result)
        in_specs.append(pl.BlockSpec(memory_space=pl.ANY))
    return pl.pallas_call(
        functools.partial(uptake_kernel, first_part * SUB),
        grid=(count,),
        in_specs=in_specs,
        out_specs=[
            pl.BlockSpec((tracers, SUB * sub_rows, cols), lambda i: (0, first_part + i, 0)),
            whole((SUB, cols)),
        ],
        out_shape=[shaped(tracers, all_rows, cols), shaped(SUB, cols)],
        scratch_shapes=[pltpu.VMEM((tracers * SUB, sub_rows * cols), jnp.float32)],
        input_output_aliases=aliases,
        compiler_params=params(),
    )(*operands)


def warming_kernel(sea_ref, floor_ref, heat_ref, mixed_ref, warm_ref, buoyant_ref):
    blocks, sub_rows, levels, cols = heat_ref.shape
    tile_rows = blocks * sub_rows
    base = lax.axis_index("comp") * levels
    level = (base + subs_of((levels, cols))).astype(jnp.float32)
    depth = jnp.where(sea_ref[...] == 1, floor_ref[...], 0).astype(jnp.float32)
    for r in range(tile_rows):
        at = pl.ds(r, levels, stride=tile_rows)
        warm = mixed_ref[0, r] + WARMING_FACTOR * heat_ref[r // sub_rows, r % sub_rows]
        wet = (level < depth[r : r + 1]).astype(jnp.float32)
        warm_ref[at, :] = warm
        buoyant_ref[at, :] = wet * (0.2 * warm - 0.8 * mixed_ref[1, r])


def warming(heat, mixed, sea):
    _, tile_rows, levels, cols = mixed.shape
    outs = [shaped(levels * tile_rows, cols)] * 2
    return call_once(warming_kernel, [*sea, heat, mixed], outs)


def from_before(x, axis):
    return lax.ppermute(x, axis, [(i, i + 1) for i in range(lax.axis_size(axis) - 1)])


def from_after(x, axis):
    return lax.ppermute(x, axis, [(i + 1, i) for i in range(lax.axis_size(axis) - 1)])


def row_pairs():
    blocks, tiles = lax.axis_size("comp"), lax.axis_size("gx")
    places = [b * tiles + tile for tile in range(tiles) for b in range(blocks)]
    return list(zip(places[:-1], places[1:]))


def from_block_before(x):
    return lax.ppermute(x, ("comp", "gx"), row_pairs())


def from_block_after(x):
    return lax.ppermute(x, ("comp", "gx"), [(later, own) for own, later in row_pairs()])


def from_sides(x):
    if lax.axis_size("gy") == 2:
        other = lax.ppermute(x, "gy", [(0, 1), (1, 0)])
        return other, other
    return from_before(x, "gy"), from_after(x, "gy")


def on_device(
    zonal_flow_speed,
    meridional_flow_speed,
    thermal_anomaly,
    brine_anomaly_values,
    marine_indicator,
    seafloor_layer,
    dissolved_species,
    topmost_sunshine,
    attenuation_coefficient,
    peak_intake_speed,
    feedstock_midpoint_constant,
    photon_midpoint_constant,
    stoichiometry_matrix,
):
    blocks = lax.axis_size("comp")
    levels, tile_rows, tile_cols = zonal_flow_speed.shape
    tracer_count, level_count = dissolved_species.shape[:2]
    sub_rows = dissolved_species.shape[4]
    ocean = (zonal_flow_speed, meridional_flow_speed, thermal_anomaly, brine_anomaly_values)
    sea = (marine_indicator, seafloor_layer)
    flat = [x.reshape(levels * tile_rows, tile_cols) for x in ocean]
    q = dissolved_species.reshape(tracer_count, level_count, sub_rows, 1, tile_cols)
    parts = levels // SUB
    every = parts * blocks
    sizes = [every - 3 * every // 4, every // 2, every // 4]
    cuts = [(sum(sizes[:i]), size) for i, size in enumerate(sizes)]
    matrix = call_once(
        spread_kernel,
        [stoichiometry_matrix],
        [shaped(SUB * tracer_count, SUB * tracer_count)],
    )[0]
    scalars_of_uptake = (
        peak_intake_speed,
        feedstock_midpoint_constant,
        photon_midpoint_constant,
    )

    def rims(own):
        return own, (from_block_after(own[0]), from_block_before(own[1]))

    def sides(x):
        return (x, *from_sides(x))

    packed, edges, ocean_rows = pack_ocean(flat, sea, levels)
    ranges = [(first * SUB, size * SUB) for first, size in cuts]
    chunks = [rims(cut_rows(q, ranges[:1], [packed]))]
    later = cut_rows(q, ranges[1:], chunks[0][0][:1])
    up, down, packed = ocean_sides(packed, *from_sides(packed), edges)
    after, before = from_after(up, "gx"), from_before(down, "gx")
    rim, arrived = held_until(chunks[0][1], later[:1])
    chunks = [(chunks[0][0], rim)]
    smix, mixed, send, local, faces, depths = ocean_phase(
        blocks, levels, ocean_rows, sea, packed, after, before, [arrived]
    )
    received = lax.all_to_all(send, "comp", split_axis=0, concat_axis=0, tiled=True)
    east_new, north_new = velocities(local, faces, received)
    held, _ = held_until(later[:2], [received])
    chunks.append(rims(held))

    surface = topmost_sunshine.reshape(sub_rows, tile_cols)
    carry, heat, result = None, None, None
    near = sides(pack_tracers(*chunks[0], []))
    for i, cut in enumerate(cuts):
        moved, light, heat, carry = advection(
            cut,
            level_count,
            attenuation_coefficient,
            surface,
            depths,
            received,
            *chunks[i],
            near,
            carry,
            heat,
            [] if i == 0 else [token],
        )
        if i == 0:
            held, _ = held_until(later[2:], [carry])
            chunks.append(rims(held))
        if i + 1 < len(cuts):
            near = sides(pack_tracers(*chunks[i + 1], [carry]))
        result, token = uptake(
            cut,
            level_count * sub_rows,
            scalars_of_uptake,
            matrix,
            depths,
            moved,
            light,
            result,
        )
    heat = lax.all_to_all(heat, "comp", split_axis=0, concat_axis=0, tiled=True)
    warmed_result, buoyancy = warming(heat, mixed, sea)
    fields = (east_new, north_new, warmed_result, smix, buoyancy)
    return (
        *[x.reshape(zonal_flow_speed.shape) for x in fields],
        result.reshape(dissolved_species.shape),
    )


def solution(mesh):
    return jax.shard_map(
        on_device,
        mesh=mesh,
        in_specs=(
            P("comp", "gx", "gy"),
            P("comp", "gx", "gy"),
            P("comp", "gx", "gy"),
            P("comp", "gx", "gy"),
            P("gx", "gy"),
            P("gx", "gy"),
            P(None, None, "gx", "comp", None, "gy"),
            P("gx", "comp", None, "gy"),
            P(),
            P(),
            P(),
            P(),
            P(),
        ),
        out_specs=(
            P("comp", "gx", "gy"),
            P("comp", "gx", "gy"),
            P("comp", "gx", "gy"),
            P("comp", "gx", "gy"),
            P("comp", "gx", "gy"),
            P(None, None, "gx", "comp", None, "gy"),
        ),
        check_vma=False,
    )
```

```python
import functools

import jax
import jax.numpy as jnp
from jax import lax
from jax.experimental import pallas as pl
from jax.experimental.pallas import tpu as pltpu
from jax.sharding import PartitionSpec as P

NSUB = 2
SLOTS = 4 * NSUB
SUB = 8
GROUP = 24
HALF = 64
ENTRIES = 18

DT_FLOW = 0.1
CORIOLIS = 0.3
MIXING = 0.15
COURANT = 0.24
DT_BIO = 0.5
WARMING_FACTOR = 0.5
CLEAR_WATER = 0.5
VMEM_LIMIT = 16 * 1024 * 1024
COVER = pl.CostEstimate(flops=0, bytes_accessed=200_000_000, transcendentals=0)
VMEM_MOST = 62 * 1024 * 1024


def lanes_of(shape):
    return lax.broadcasted_iota(jnp.int32, shape, len(shape) - 1)


def subs_of(shape):
    return lax.broadcasted_iota(jnp.int32, shape, len(shape) - 2)


def turn(x, by, axis):
    by = by % x.shape[axis]
    return x if by == 0 else pltpu.roll(x, by, axis)


def params(limit=VMEM_LIMIT):
    return pltpu.CompilerParams(vmem_limit_bytes=limit)


def whole(shape):
    return pl.BlockSpec(shape, lambda *_: (0,) * len(shape))


def smem():
    return pl.BlockSpec(memory_space=pltpu.SMEM)


def shaped(*shape):
    return jax.ShapeDtypeStruct(shape, jnp.float32)


def halves(x):
    high = x.astype(jnp.bfloat16)
    return high, (x - high.astype(jnp.float32)).astype(jnp.bfloat16)


def sums_above(x):
    sub = subs_of(x.shape)
    running, total = x, x
    by = 1
    while by < x.shape[0]:
        running = running + jnp.where(sub >= by, turn(running, by, 0), 0.0)
        total = total + turn(total, by, 0)
        by *= 2
    return jnp.where(sub >= 1, turn(running, 1, 0), 0.0), total


def cut_kernel(cuts, q_ref, *refs):
    outs, sems = refs[-2 * len(cuts) - 1 : -1], refs[-1]
    rows = q_ref.shape[2]
    copies = [
        pltpu.make_async_copy(
            q_ref.at[:, pl.ds(start, size), r],
            outs[2 * i + r // NSUB].at[:, r % NSUB],
            sems.at[rows * i + r],
        )
        for i, (start, size) in enumerate(cuts)
        for r in range(rows)
    ]
    for copy in copies:
        copy.start()
    for copy in copies:
        copy.wait()


def cut_rows(q, cuts, after):
    tracers, _, rows, _, cols = q.shape
    anywhere = pl.BlockSpec(memory_space=pl.ANY)
    outs = [shaped(tracers, NSUB, size, 1, cols) for _, size in cuts for _ in range(2)]
    outs = pl.pallas_call(
        functools.partial(cut_kernel, cuts),
        in_specs=[anywhere] * (1 + len(after)),
        out_specs=[anywhere] * len(outs),
        out_shape=outs,
        scratch_shapes=[pltpu.SemaphoreType.DMA((rows * len(cuts),))],
        compiler_params=params(),
    )(q, *after)
    return [x.reshape(tracers, NSUB, x.shape[2], cols) for x in outs]


def hold_kernel(*refs):
    pass


def held_until(arrays, after):
    anywhere = pl.BlockSpec(memory_space=pl.ANY)
    return pl.pallas_call(
        hold_kernel,
        in_specs=[anywhere] * (len(arrays) + len(after)),
        out_specs=[anywhere] * len(arrays),
        out_shape=[shaped(*x.shape) for x in arrays],
        input_output_aliases={i: i for i in range(len(arrays))},
        compiler_params=params(),
    )(*arrays, *after)


def both_ends(acc):
    return jnp.where(lanes_of(acc.shape) % SLOTS < SLOTS // 2, acc, turn(acc, SLOTS // 2, 1))


def pack_tracers_kernel(low_ref, high_ref, after_ref, before_ref, packed_ref):
    tracers, _, _, cols = low_ref.shape
    lane = lanes_of((SUB, cols))
    for pair in range(tracers // 2):
        acc = jnp.zeros((SUB, cols), jnp.float32)
        for odd in range(2):
            t = 2 * pair + odd
            rows = [before_ref[t, 1], low_ref[t, 0], low_ref[t, 1], high_ref[t, 0], high_ref[t, 1]]
            for r, x in enumerate(rows + [after_ref[t, 0]]):
                at = HALF * odd + SLOTS * (r + 1)
                acc = jnp.where(lane // SLOTS == at // SLOTS, turn(x, at + NSUB, 1), acc)
        packed_ref[pair] = both_ends(acc)


def pack_tracers(own, rim, after, cost=None):
    tracers, _, levels, cols = own[0].shape
    rows = pl.BlockSpec((tracers, NSUB, SUB, cols), lambda i: (0, 0, i, 0))
    return pl.pallas_call(
        functools.partial(ignoring, len(after), pack_tracers_kernel),
        grid=(levels // SUB,),
        in_specs=[pl.BlockSpec(memory_space=pl.ANY)] * len(after) + [rows] * 4,
        out_specs=pl.BlockSpec((tracers // 2, SUB, cols), lambda i: (0, i, 0)),
        out_shape=shaped(tracers // 2, levels, cols),
        compiler_params=params(),
        cost_estimate=cost,
    )(*after, *own, *rim)


def ignoring(count, kernel, *refs):
    kernel(*refs[count:])


def call_once(kernel, operands, outs, scratch=(), scalars=(), after=(), limit=VMEM_LIMIT):
    return pl.pallas_call(
        functools.partial(ignoring, len(after), kernel),
        grid=(1,),
        in_specs=[pl.BlockSpec(memory_space=pl.ANY)] * len(after)
        + [smem()] * len(scalars)
        + [whole(x.shape) for x in operands],
        out_specs=[whole(x.shape) for x in outs],
        out_shape=outs,
        scratch_shapes=list(scratch),
        compiler_params=params(limit),
    )(*after, *scalars, *operands)


def pack_ocean_kernel(levels, *refs):
    u_ref, v_ref, t_ref, s_ref, sea_ref, floor_ref, packed_ref, edges_ref, row_ref = refs
    edge_low_ref, edge_high_ref = edges_ref.at[0], edges_ref.at[1]
    tile_rows, cols = sea_ref.shape
    lane = lanes_of((levels, cols))
    edge_low_ref[4 * NSUB] = jnp.zeros((levels, cols), jnp.float32)
    edge_high_ref[4 * NSUB] = jnp.zeros((levels, cols), jnp.float32)
    for f, ref in enumerate((u_ref, v_ref, t_ref, s_ref)):
        acc = jnp.zeros((levels, cols), jnp.float32)
        for r in range(tile_rows):
            x = ref[pl.ds(r, levels, stride=tile_rows), :]
            row_ref[f, r] = x
            acc = jnp.where(lane // SLOTS == r, turn(x, SLOTS * r + NSUB, 1), acc)
            if r < NSUB:
                edge_low_ref[NSUB * f + r] = x
            if r >= tile_rows - NSUB:
                edge_high_ref[NSUB * f + r - tile_rows + NSUB] = x
        packed_ref[f] = both_ends(acc)
    depth = jnp.where(sea_ref[...] == 1, floor_ref[...], 0).astype(jnp.float32)
    acc = jnp.zeros((levels, cols), jnp.float32)
    for r in range(tile_rows):
        x = jnp.broadcast_to(depth[r : r + 1], (levels, cols))
        acc = jnp.where(lane // SLOTS == r, turn(x, SLOTS * r + NSUB, 1), acc)
    packed_ref[4] = both_ends(acc)
    edge_low_ref[4 * NSUB, 0:NSUB, :] = depth[0:NSUB]
    edge_high_ref[4 * NSUB, 0:NSUB, :] = depth[tile_rows - NSUB :]


def pack_ocean(flat, sea, levels):
    cols = sea[0].shape[1]
    edges = shaped(2, 4 * NSUB + 1, levels, cols)
    return call_once(
        functools.partial(pack_ocean_kernel, levels),
        [*flat, *sea],
        [shaped(5, levels, cols), edges, shaped(4, sea[0].shape[0], levels, cols)],
        limit=VMEM_MOST,
    )


def with_sides(own, left, right):
    slot = lanes_of(own.shape) % SLOTS
    ends = jnp.where(slot < NSUB, left, right)
    return jnp.where((slot < NSUB) | (slot >= SLOTS - NSUB), ends, own)


def ocean_sides_kernel(own_ref, left_ref, right_ref, edges_ref, up_ref, down_ref, out_ref):
    _, levels, cols = own_ref.shape
    rows = edges_ref.shape[1]
    up_ref[0:rows] = edges_ref[0]
    down_ref[0:rows] = edges_ref[1]
    slot = lanes_of((levels, cols)) % SLOTS
    place = lax.axis_index("gy")
    first, last = place == 0, place == lax.axis_size("gy") - 1
    for f in range(5):
        x = with_sides(own_ref[f], left_ref[f], right_ref[f])
        if f == 4:
            x = jnp.where((slot < NSUB) & first, 0.0, x)
            x = jnp.where((slot >= SLOTS - NSUB) & last, 0.0, x)
        out_ref[f] = x
        up_ref[rows + f] = x
        down_ref[rows + f] = x


def ocean_sides(own, left, right, edges):
    edge = shaped(edges.shape[1] + 5, *edges.shape[2:])
    return call_once(
        ocean_sides_kernel,
        [own, left, right, edges],
        [edge, edge, shaped(*own.shape)],
    )


def ocean_kernel(blocks, levels, *refs):
    own_ref, sea_ref, floor_ref, packed_ref, after_ref, before_ref = refs[:6]
    smix_ref, mixed_ref, send_ref, local_ref, faces_ref, depths_ref, press_ref, total_ref = refs[6:]
    tile_rows, cols = sea_ref.shape
    sub_rows = tile_rows // blocks
    shape = (levels, cols)
    lane = lanes_of(shape)
    first, last = lane == 0, lane == cols - 1
    base = lax.axis_index("comp") * levels
    level = (base + subs_of(shape)).astype(jnp.float32)
    rims = after_ref.shape[0] - 5

    def packed(f):
        after, before = after_ref[rims + f], before_ref[rims + f]
        rim = jnp.where(lane < NSUB * SLOTS, after, jnp.where(lane >= cols - NSUB * SLOTS, before, 0.0))
        return jnp.concatenate([packed_ref[f], rim], axis=1)

    def row_after(x):
        return turn(x, -SLOTS, 1)

    def row_before(x):
        return turn(x, SLOTS, 1)

    up, vp, tp, sp, dp = [packed(f) for f in range(5)]
    wide = jnp.concatenate([level, level], axis=1)
    wet = (wide < dp).astype(jnp.float32)
    heavy = wet * (-0.2 * tp + 0.8 * sp)
    above, total = sums_above(heavy)
    press = above + 0.5 * heavy
    east = up + DT_FLOW * (CORIOLIS * vp - (row_after(press) - press))
    north = vp + DT_FLOW * (-CORIOLIS * up - (turn(press, -1, 1) - press))
    open_n = wet * turn(wet, -1, 1)
    flux_t = open_n * (turn(tp, -1, 1) - tp)
    flux_s = open_n * (turn(sp, -1, 1) - sp)
    total_e, total_n = row_after(total) - total, turn(total, -1, 1) - total
    depth_e, depth_n = jnp.minimum(dp, row_after(dp)), jnp.minimum(dp, turn(dp, -1, 1))

    def window(x, g):
        x = turn(x, -SLOTS * (sub_rows * g - NSUB), 1)[:, 0:cols]
        return jnp.where(lane < HALF, x, turn(x, HALF, 1))

    for g in range(blocks):
        send_ref[g, 13] = window(east, g)
        send_ref[g, 14] = window(north, g)
        send_ref[g, 15, 13:14, :] = window(total_e, g)[0:1]
        send_ref[g, 15, 14:15, :] = window(total_n, g)[0:1]
        send_ref[g, 15, 15:16, :] = jnp.zeros((1, cols), jnp.float32)
        depths_ref[g, 24:25, :] = window(depth_e, g)[0:1]
        depths_ref[g, 25:26, :] = window(depth_n, g)[0:1]
        depths_ref[g, 26:27, :] = window(dp, g)[0:1]

    slot = lanes_of(tp.shape) % SLOTS

    def edges(x, other):
        x = jnp.where(slot == 0, turn(x, -6, 1), other)
        return x[:, 0:cols], x[:, cols:]

    edge_p, edge_w = edges(press, press), edges(wet, wet)
    edge_t, edge_s = edges(tp, flux_t), edges(sp, flux_s)
    edge_total, edge_depth = edges(total, total), edges(dp, dp)

    def edge(pair, r):
        at = r % tile_rows
        return turn(pair[0] if 0 <= r < tile_rows else pair[1], -(SLOTS * at + 1), 1)

    depth = jnp.where(sea_ref[...] == 1, floor_ref[...], 0).astype(jnp.float32)

    def row_of(f, r):
        if r < 0:
            return before_ref[NSUB * f + r + NSUB]
        if r >= tile_rows:
            return after_ref[NSUB * f + r - tile_rows]
        return own_ref[f, r]

    def depth_of(r):
        if r < 0:
            x = before_ref[4 * NSUB, r + NSUB : r + NSUB + 1, :]
        elif r >= tile_rows:
            x = after_ref[4 * NSUB, r - tile_rows : r - tile_rows + 1, :]
        else:
            x = depth[r : r + 1]
        return jnp.broadcast_to(x, shape)

    lo, hi = -NSUB, tile_rows + NSUB
    for r in range(lo, hi):
        heavy = (level < depth_of(r)).astype(jnp.float32) * (-0.2 * row_of(2, r) + 0.8 * row_of(3, r))
        above, total = sums_above(heavy)
        press_ref[r - lo] = above + 0.5 * heavy
        total_ref[r - lo] = total

    def windows(r, before):
        for g in range(blocks):
            j = r - (sub_rows * g - before)
            if 0 <= j < sub_rows + 1 + before:
                yield g, j

    flux_before = [None, None]
    for r in range(lo, hi - 1):
        press, press_e = press_ref[r - lo], press_ref[r - lo + 1]
        total, total_a = total_ref[r - lo], total_ref[r - lo + 1]
        d, d_e = depth_of(r), depth_of(r + 1)
        d_n = jnp.where(last, edge(edge_depth, r), turn(d, -1, 1))
        face_e, face_n = jnp.minimum(d, d_e), jnp.minimum(d, d_n)
        u, v = row_of(0, r), row_of(1, r)
        east = u + DT_FLOW * (CORIOLIS * v - (press_e - press))
        press_n = jnp.where(last, edge(edge_p, r), turn(press, -1, 1))
        north = v + DT_FLOW * (-CORIOLIS * u - (press_n - press))
        total_e = total_a - total
        total_n = jnp.where(last, edge(edge_total, r), turn(total, -1, 1)) - total
        for g, j in windows(r, 2):
            send_ref[g, j] = east
            send_ref[g, 15, j : j + 1, :] = total_e[0:1]
            depths_ref[g, j : j + 1, :] = face_e[0:1]
        for g, j in windows(r, 1):
            send_ref[g, 7 + j] = north
            send_ref[g, 15, 7 + j : 8 + j, :] = total_n[0:1]
            depths_ref[g, 8 + j : 9 + j, :] = face_n[0:1]
            depths_ref[g, 16 + j : 17 + j, :] = d[0:1]
        if 0 <= r < tile_rows:
            local_ref[0, r] = east
            local_ref[1, r] = north
            faces_ref[0, r : r + 1, :] = face_e[0:1]
            faces_ref[1, r : r + 1, :] = face_n[0:1]
            for g in range(blocks):
                send_ref[g, 16, r : r + 1, :] = total_e[0:1]
                send_ref[g, 17, r : r + 1, :] = total_n[0:1]
        if r < -1 or r >= tile_rows:
            continue
        open_e = (level < face_e).astype(jnp.float32)
        open_n = (level < face_n).astype(jnp.float32)
        for i, (f, ends) in enumerate(((2, edge_t), (3, edge_s))):
            x = row_of(f, r)
            flux_e = open_e * (row_of(f, r + 1) - x)
            if r >= 0:
                ending = edge(ends, r)
                flux_n = open_n * (jnp.where(last, ending, turn(x, -1, 1)) - x)
                flux_b = jnp.where(first, ending, turn(flux_n, 1, 1))
                mixed = x + MIXING * ((flux_e - flux_before[i]) + (flux_n - flux_b))
                mixed_ref[i, r] = mixed
                if i == 1:
                    smix_ref[pl.ds(r, levels, stride=tile_rows), :] = mixed
            flux_before[i] = flux_e


def ocean_phase(blocks, levels, own, sea, packed, rim_after, rim_before, after):
    tile_rows, cols = sea[0].shape
    outs = [
        shaped(levels * tile_rows, cols),
        shaped(2, tile_rows, levels, cols),
        shaped(blocks, ENTRIES, levels, cols),
        shaped(2, tile_rows, levels, cols),
        shaped(2, tile_rows, cols),
        shaped(blocks, 32, cols),
    ]
    tall = tile_rows + 2 * NSUB
    return call_once(
        functools.partial(ocean_kernel, blocks, levels),
        [own, *sea, packed, rim_after, rim_before],
        outs,
        [pltpu.VMEM((tall, levels, cols), jnp.float32)] * 2,
        after=after,
    )


def velocity_kernel(local_ref, faces_ref, received_ref, east_ref, north_ref):
    blocks = received_ref.shape[0]
    _, tile_rows, levels, cols = local_ref.shape
    group = lax.axis_index("comp")
    level = (group * levels + subs_of((levels, cols))).astype(jnp.float32)
    for f, out_ref in enumerate((east_ref, north_ref)):
        above = jnp.zeros((tile_rows, cols), jnp.float32)
        for s in range(blocks - 1):
            above = above + jnp.where(s < group, received_ref[s, f], 0.0)
        for r in range(tile_rows):
            x = local_ref[f, r] - DT_FLOW * jnp.broadcast_to(above[r : r + 1], (levels, cols))
            x = jnp.where(level < faces_ref[f, r : r + 1, :], x, 0.0)
            out_ref[pl.ds(r, levels, stride=tile_rows), :] = x


def velocities(local, faces, received):
    blocks = received.shape[0]
    _, tile_rows, levels, cols = local.shape
    out = shaped(levels * tile_rows, cols)
    return pl.pallas_call(
        velocity_kernel,
        grid=(1,),
        in_specs=[
            whole(local.shape),
            whole(faces.shape),
            pl.BlockSpec((blocks, 2, levels, cols), lambda i: (0, ENTRIES // 2 - 1, 0, 0)),
        ],
        out_specs=[whole(out.shape)] * 2,
        out_shape=[out] * 2,
        compiler_params=params(),
    )(local, faces, received)


def advection_kernel(first_part, parts, level_count, *refs):
    (
        absorb_ref,
        surface_ref,
        depth_ref,
        totals_ref,
        courant_ref,
        low_ref,
        high_ref,
        after_ref,
        before_ref,
        side_ref,
        left_ref,
        right_ref,
    ) = refs[:12]
    moved_ref, light_ref, heat_ref, carry_out_ref = refs[-10:-6]
    coef_ref, side_coef_ref, edge_ref, running_ref, above_ref, shift_ref = refs[-6:]
    depth_ref = depth_ref.at[lax.axis_index("comp")]
    step = pl.program_id(0)
    tracers, _, _, cols = low_ref.shape
    levels = courant_ref.shape[2]
    sub_rows = surface_ref.shape[0]
    rows = sub_rows + 2
    shape = (levels, cols)
    lane = lanes_of(shape)
    first, last = lane == 0, lane == cols - 1
    first8, last8 = first[0:SUB], last[0:SUB]
    slot = lane % SLOTS

    @pl.when(step == 0)
    def _():
        running_ref[...] = refs[12][...] if first_part else jnp.zeros_like(running_ref)
        size = (2 * cols, 2 * cols)
        source, to = subs_of(size) % cols, lanes_of(size)
        hit = ((to < cols) & (source == to + 1)) | ((to >= cols) & (source == to - cols - 1))
        shift_ref[...] = hit.astype(jnp.float32).astype(jnp.bfloat16)

    part = first_part + step
    above = jnp.zeros(above_ref.shape, jnp.float32)
    for s in range(totals_ref.shape[0] - 1):
        above = above + jnp.where(s < part // parts, totals_ref[s, 0], 0.0)
    above_ref[...] = above
    level = (part * levels + subs_of(shape)).astype(jnp.float32)

    def spread(ref, r):
        return jnp.broadcast_to(ref[r : r + 1, :], shape)

    def courant(entry, face):
        x = courant_ref[0, entry] - DT_FLOW * spread(above_ref, entry)
        return COURANT * jnp.tanh(jnp.where(level < spread(depth_ref, face), x, 0.0))

    def coefficients(wet, ce, ce_b, cn, cn_b):
        return (
            wet
            * (
                1.0
                - jnp.maximum(ce, 0.0)
                + jnp.minimum(ce_b, 0.0)
                - jnp.maximum(cn, 0.0)
                + jnp.minimum(cn_b, 0.0)
            ),
            -wet * jnp.minimum(ce, 0.0),
            wet * jnp.maximum(ce_b, 0.0),
            -wet * jnp.minimum(cn, 0.0),
            wet * jnp.maximum(cn_b, 0.0),
        )

    side_e, side_n = courant(13, 24), courant(14, 25)
    wet = (level < spread(depth_ref, 26)).astype(jnp.float32)
    packed_coef = coefficients(wet, side_e, turn(side_e, SLOTS, 1), side_n, turn(side_n, 1, 1))
    for i in range(5):
        side_coef_ref[i] = packed_coef[i]
    ce_b = courant(0, 0)
    for j in range(rows):
        ce, cn = courant(1 + j, 1 + j), courant(7 + j, 8 + j)
        cn_b = jnp.where(first, turn(side_n, -(SLOTS * (j + 1) + 1), 1), turn(cn, 1, 1))
        wet = (level < spread(depth_ref, 16 + j)).astype(jnp.float32)
        for i, x in enumerate(coefficients(wet, ce, ce_b, cn, cn_b)):
            coef_ref[5 * j + i] = x
        ce_b = ce
    for i in range(side_ref.shape[0]):
        x = with_sides(side_ref[i], left_ref[i], right_ref[i])
        edge_ref[i, 0] = jnp.where(slot == 0, turn(x, -6, 1), x)
        x = (
            (side_coef_ref[0] * x + side_coef_ref[1] * turn(x, -SLOTS, 1))
            + (side_coef_ref[2] * turn(x, SLOTS, 1) + side_coef_ref[3] * turn(x, -1, 1))
            + side_coef_ref[4] * turn(x, 1, 1)
        )
        edge_ref[i, 1] = jnp.where(slot == 0, turn(x, -6, 1), x)

    layer = 2.0 / level_count
    zero = jnp.zeros((SUB, cols), jnp.float32)
    for k in range(0, levels, SUB):
        at = slice(k, k + SUB)

        def shifted(tiles):
            high, low = halves(jnp.concatenate(tiles, axis=0))
            return jnp.dot(
                jnp.concatenate([high, low], axis=1),
                shift_ref[...],
                preferred_element_type=jnp.float32,
            )

        def stencil(x, coef, edge, beside):
            north = jnp.where(last8, edge, beside[:, :cols])
            south = jnp.where(first8, edge, beside[:, cols:])
            return (
                (coef[0] * x[1] + coef[1] * x[2])
                + (coef[2] * x[0] + coef[3] * north)
                + coef[4] * south
            )

        def advect(i, sums):
            sums = list(sums)
            fields = []
            for t in range(GROUP):
                t = GROUP * i + t
                rows_of = (before_ref, low_ref, high_ref, after_ref)
                x = [ref[t, n, at] for ref in rows_of for n in range(NSUB)]
                fields.append(x)
            for stage in range(NSUB):
                inner = range(1 + stage, rows + 1 - stage)
                beside = shifted([x[j - stage] for j in inner for x in fields])
                fresh = [[] for _ in fields]
                for n, j in enumerate(inner):
                    coef = [coef_ref[5 * (j - 1) + c, at] for c in range(5)]
                    for t, x in enumerate(fields):
                        edges = edge_ref[GROUP // 2 * i + t // 2, stage, at]
                        edge = turn(edges, -(HALF * (t % 2) + SLOTS * j + 1), 1)
                        row = SUB * (len(fields) * n + t)
                        fresh[t].append(
                            stencil(x[n : n + 3], coef, edge, beside[row : row + SUB])
                        )
                fields = fresh
            for t, x in enumerate(fields):
                for r in range(sub_rows):
                    moved_ref[GROUP * i + t, r, at] = x[r]
                    sums[r] = sums[r] + absorb_ref[GROUP * i + t] * x[r]
            return tuple(sums)

        sums = (zero,) * sub_rows
        for i in range(tracers // GROUP):
            sums = advect(i, sums)
        for r in range(sub_rows):
            optical = layer * (CLEAR_WATER + sums[r])
            above, total = sums_above(optical)
            through = jnp.exp(-(running_ref[r] + above))
            running_ref[r] = running_ref[r] + total
            surface = jnp.broadcast_to(surface_ref[r : r + 1, :], (SUB, cols))
            light_ref[r, at] = surface * through * jnp.exp(-0.5 * optical)
            wet = (level[at] < jnp.broadcast_to(depth_ref[17 + r : 18 + r, :], (SUB, cols))).astype(
                jnp.float32
            )
            heat_ref[0, r, at] = wet * surface * through * (1.0 - jnp.exp(-optical)) / layer
    carry_out_ref[...] = running_ref[...]


def advection(cut, level_count, absorb, surface, depth, received, own, rim, sides, carry, heat, after):
    first_part, count = cut
    tracers, _, _, cols = own[0].shape
    every, _, levels, _ = received.shape
    parts = levels // SUB
    sub_rows = surface.shape[0]
    rows = pl.BlockSpec((tracers, NSUB, SUB, cols), lambda i: (0, 0, i, 0))
    side = pl.BlockSpec((tracers // 2, SUB, cols), lambda i: (0, i, 0))
    operands = [absorb, surface, depth, received, received, *own, *rim, *sides]
    in_specs = [
        smem(),
        whole(surface.shape),
        whole(depth.shape),
        pl.BlockSpec((every, 1, levels, cols), lambda i: (0, 15, 0, 0)),
        pl.BlockSpec(
            (1, ENTRIES, SUB, cols),
            lambda i: ((first_part + i) // parts, 0, (first_part + i) % parts, 0),
        ),
        rows,
        rows,
        rows,
        rows,
        side,
        side,
        side,
    ]
    aliases = {}
    carry_shape = (sub_rows, SUB, cols)
    if carry is not None:
        operands.append(carry)
        in_specs.append(whole(carry_shape))
        aliases = {len(operands): 2}
        operands.append(heat)
    operands += after
    in_specs += [pl.BlockSpec(memory_space=pl.ANY)] * (len(operands) - len(in_specs))
    outs = [
        shaped(tracers, sub_rows, count * SUB, cols),
        shaped(sub_rows, count * SUB, cols),
        shaped(every, sub_rows, levels, cols),
        shaped(*carry_shape),
    ]
    return pl.pallas_call(
        functools.partial(advection_kernel, first_part, parts, level_count),
        grid=(count,),
        in_specs=in_specs,
        out_specs=[
            pl.BlockSpec((tracers, sub_rows, SUB, cols), lambda i: (0, 0, i, 0)),
            pl.BlockSpec((sub_rows, SUB, cols), lambda i: (0, i, 0)),
            pl.BlockSpec(
                (1, sub_rows, SUB, cols),
                lambda i: ((first_part + i) // parts, 0, (first_part + i) % parts, 0),
            ),
            whole(carry_shape),
        ],
        out_shape=outs,
        scratch_shapes=[
            pltpu.VMEM((5 * (sub_rows + 2), SUB, cols), jnp.float32),
            pltpu.VMEM((5, SUB, cols), jnp.float32),
            pltpu.VMEM((tracers // 2, 2, SUB, cols), jnp.float32),
            pltpu.VMEM((sub_rows, SUB, cols), jnp.float32),
            pltpu.VMEM((levels, cols), jnp.float32),
            pltpu.VMEM((2 * cols, 2 * cols), jnp.bfloat16),
        ],
        input_output_aliases=aliases,
        compiler_params=params(),
    )(*operands)


def spread_kernel(matrix_ref, out_ref):
    tracers = matrix_ref.shape[0]
    size = tracers * SUB
    tall = (subs_of((size, tracers)) // SUB == lanes_of((size, tracers))).astype(jnp.float32)
    wide = (lanes_of((tracers, size)) // SUB == subs_of((tracers, size))).astype(jnp.float32)
    exact = functools.partial(
        jnp.dot, precision=lax.Precision.HIGHEST, preferred_element_type=jnp.float32
    )
    same = subs_of((size, size)) % SUB == lanes_of((size, size)) % SUB
    out_ref[...] = jnp.where(same, exact(exact(tall, matrix_ref[...]), wide), 0.0)


def uptake_kernel(first_level, *refs):
    growth_ref, half_ref, dim_ref, matrix_ref, depth_ref, moved_ref, light_ref = refs[:7]
    depth_ref = depth_ref.at[lax.axis_index("comp")]
    result_ref, token_ref, uptake_ref = refs[-3:]
    token_ref[...] = jnp.zeros_like(token_ref)
    tracers, sub_rows, levels, cols = moved_ref.shape
    step = pl.program_id(0)
    matrix_high, matrix_low = halves(matrix_ref[...])
    for k in range(0, levels, SUB):
        at = slice(k, k + SUB)
        level = (first_level + step * levels + k + subs_of((SUB, cols))).astype(jnp.float32)
        light = [light_ref[r, at] for r in range(sub_rows)]
        food = [moved_ref[0, r, at] for r in range(sub_rows)]
        both = [light[r] * food[r] for r in range(sub_rows)]

        def uptake(t, _):
            for r in range(sub_rows):
                scale = (half_ref[t] + food[r]) * (light[r] + dim_ref[t])
                value = growth_ref[t] * moved_ref[t, r, at] * (both[r] / scale)
                uptake_ref[pl.ds(t * SUB, SUB), r * cols : (r + 1) * cols] = value
            return _

        lax.fori_loop(0, tracers, uptake, 0, unroll=4)
        amount = uptake_ref[...]
        high, low = halves(amount)
        dot = functools.partial(jnp.dot, preferred_element_type=jnp.float32)
        change = dot(matrix_high, high) + (dot(matrix_high, low) + dot(matrix_low, high))
        for r in range(sub_rows):
            depth = jnp.broadcast_to(depth_ref[17 + r : 18 + r, :], (SUB, cols))
            scale = DT_BIO * (level < depth).astype(jnp.float32)
            for t in range(tracers):
                result_ref[t, pl.ds(sub_rows * k + r, SUB, stride=sub_rows), :] = (
                    moved_ref[t, r, at]
                    + scale * change[SUB * t : SUB * (t + 1), r * cols : (r + 1) * cols]
                )


def uptake(cut, all_rows, scalars, matrix, depth, moved, light, result):
    first_part, count = cut
    tracers, sub_rows, _, cols = moved.shape
    operands = [*scalars, matrix, depth, moved, light]
    in_specs = [smem()] * 3 + [
        whole(matrix.shape),
        whole(depth.shape),
        pl.BlockSpec((tracers, sub_rows, SUB, cols), lambda i: (0, 0, i, 0)),
        pl.BlockSpec((sub_rows, SUB, cols), lambda i: (0, i, 0)),
    ]
    aliases = {}
    if result is not None:
        aliases = {len(operands): 0}
        operands.append(result)
        in_specs.append(pl.BlockSpec(memory_space=pl.ANY))
    return pl.pallas_call(
        functools.partial(uptake_kernel, first_part * SUB),
        grid=(count,),
        in_specs=in_specs,
        out_specs=[
            pl.BlockSpec((tracers, SUB * sub_rows, cols), lambda i: (0, first_part + i, 0)),
            whole((SUB, cols)),
        ],
        out_shape=[shaped(tracers, all_rows, cols), shaped(SUB, cols)],
        scratch_shapes=[pltpu.VMEM((tracers * SUB, sub_rows * cols), jnp.float32)],
        input_output_aliases=aliases,
        compiler_params=params(),
    )(*operands)


def warming_kernel(sea_ref, floor_ref, heat_ref, mixed_ref, warm_ref, buoyant_ref):
    blocks, sub_rows, levels, cols = heat_ref.shape
    tile_rows = blocks * sub_rows
    base = lax.axis_index("comp") * levels
    level = (base + subs_of((levels, cols))).astype(jnp.float32)
    depth = jnp.where(sea_ref[...] == 1, floor_ref[...], 0).astype(jnp.float32)
    for r in range(tile_rows):
        at = pl.ds(r, levels, stride=tile_rows)
        warm = mixed_ref[0, r] + WARMING_FACTOR * heat_ref[r // sub_rows, r % sub_rows]
        wet = (level < depth[r : r + 1]).astype(jnp.float32)
        warm_ref[at, :] = warm
        buoyant_ref[at, :] = wet * (0.2 * warm - 0.8 * mixed_ref[1, r])


def warming(heat, mixed, sea):
    _, tile_rows, levels, cols = mixed.shape
    outs = [shaped(levels * tile_rows, cols)] * 2
    return call_once(warming_kernel, [*sea, heat, mixed], outs)


def from_before(x, axis):
    return lax.ppermute(x, axis, [(i, i + 1) for i in range(lax.axis_size(axis) - 1)])


def from_after(x, axis):
    return lax.ppermute(x, axis, [(i + 1, i) for i in range(lax.axis_size(axis) - 1)])


def row_pairs():
    blocks, tiles = lax.axis_size("comp"), lax.axis_size("gx")
    places = [b * tiles + tile for tile in range(tiles) for b in range(blocks)]
    return list(zip(places[:-1], places[1:]))


def from_block_before(x):
    return lax.ppermute(x, ("comp", "gx"), row_pairs())


def from_block_after(x):
    return lax.ppermute(x, ("comp", "gx"), [(later, own) for own, later in row_pairs()])


def from_sides(x):
    if lax.axis_size("gy") == 2:
        other = lax.ppermute(x, "gy", [(0, 1), (1, 0)])
        return other, other
    return from_before(x, "gy"), from_after(x, "gy")


def on_device(
    zonal_flow_speed,
    meridional_flow_speed,
    thermal_anomaly,
    brine_anomaly_values,
    marine_indicator,
    seafloor_layer,
    dissolved_species,
    topmost_sunshine,
    attenuation_coefficient,
    peak_intake_speed,
    feedstock_midpoint_constant,
    photon_midpoint_constant,
    stoichiometry_matrix,
):
    blocks = lax.axis_size("comp")
    levels, tile_rows, tile_cols = zonal_flow_speed.shape
    tracer_count, level_count = dissolved_species.shape[:2]
    sub_rows = dissolved_species.shape[4]
    ocean = (zonal_flow_speed, meridional_flow_speed, thermal_anomaly, brine_anomaly_values)
    sea = (marine_indicator, seafloor_layer)
    flat = [x.reshape(levels * tile_rows, tile_cols) for x in ocean]
    q = dissolved_species.reshape(tracer_count, level_count, sub_rows, 1, tile_cols)
    parts = levels // SUB
    every = parts * blocks
    sizes = [every - 5 * every // 8, 3 * every // 8, every // 4]
    cuts = [(sum(sizes[:i]), size) for i, size in enumerate(sizes)]
    matrix = call_once(
        spread_kernel,
        [stoichiometry_matrix],
        [shaped(SUB * tracer_count, SUB * tracer_count)],
    )[0]
    scalars_of_uptake = (
        peak_intake_speed,
        feedstock_midpoint_constant,
        photon_midpoint_constant,
    )

    def rims(own):
        return own, (from_block_after(own[0]), from_block_before(own[1]))

    def sides(x):
        return (x, *from_sides(x))

    packed, edges, ocean_rows = pack_ocean(flat, sea, levels)
    ranges = [(first * SUB, size * SUB) for first, size in cuts]
    chunks = [rims(cut_rows(q, ranges[:1], [packed]))]
    later = cut_rows(q, ranges[1:], chunks[0][0][:1])
    up, down, packed = ocean_sides(packed, *from_sides(packed), edges)
    after, before = from_after(up, "gx"), from_before(down, "gx")
    smix, mixed, send, local, faces, depths = ocean_phase(
        blocks, levels, ocean_rows, sea, packed, after, before, later[:1]
    )
    received = lax.all_to_all(send, "comp", split_axis=0, concat_axis=0, tiled=True)
    east_new, north_new = velocities(local, faces, received)
    own = pack_tracers(*chunks[0], [depths], COVER)
    chunks.append(rims(held_until(later[:2], [own])))

    surface = topmost_sunshine.reshape(sub_rows, tile_cols)
    carry, heat, result = None, None, None
    near = sides(own)
    for i, cut in enumerate(cuts):
        moved, light, heat, carry = advection(
            cut,
            level_count,
            attenuation_coefficient,
            surface,
            depths,
            received,
            *chunks[i],
            near,
            carry,
            heat,
            [] if i == 0 else [token],
        )
        if i == 0:
            chunks.append(rims(held_until(later[2:], [carry])))
        if i + 1 < len(cuts):
            near = sides(pack_tracers(*chunks[i + 1], [carry]))
        result, token = uptake(
            cut,
            level_count * sub_rows,
            scalars_of_uptake,
            matrix,
            depths,
            moved,
            light,
            result,
        )
    heat = lax.all_to_all(heat, "comp", split_axis=0, concat_axis=0, tiled=True)
    warmed_result, buoyancy = warming(heat, mixed, sea)
    fields = (east_new, north_new, warmed_result, smix, buoyancy)
    return (
        *[x.reshape(zonal_flow_speed.shape) for x in fields],
        result.reshape(dissolved_species.shape),
    )


def solution(mesh):
    return jax.shard_map(
        on_device,
        mesh=mesh,
        in_specs=(
            P("comp", "gx", "gy"),
            P("comp", "gx", "gy"),
            P("comp", "gx", "gy"),
            P("comp", "gx", "gy"),
            P("gx", "gy"),
            P("gx", "gy"),
            P(None, None, "gx", "comp", None, "gy"),
            P("gx", "comp", None, "gy"),
            P(),
            P(),
            P(),
            P(),
            P(),
        ),
        out_specs=(
            P("comp", "gx", "gy"),
            P("comp", "gx", "gy"),
            P("comp", "gx", "gy"),
            P("comp", "gx", "gy"),
            P("comp", "gx", "gy"),
            P(None, None, "gx", "comp", None, "gy"),
        ),
        check_vma=False,
    )
```

```python
import functools

import jax
import jax.numpy as jnp
from jax import lax
from jax.experimental import pallas as pl
from jax.experimental.pallas import tpu as pltpu
from jax.sharding import PartitionSpec as P

NSUB = 2
SLOTS = 4 * NSUB
SUB = 8
GROUP = 24
HALF = 64
ENTRIES = 18

DT_FLOW = 0.1
CORIOLIS = 0.3
MIXING = 0.15
COURANT = 0.24
DT_BIO = 0.5
WARMING_FACTOR = 0.5
CLEAR_WATER = 0.5
VMEM_LIMIT = 10 * 1024 * 1024
COVER = pl.CostEstimate(flops=0, bytes_accessed=200_000_000, transcendentals=0)
VMEM_MOST = 62 * 1024 * 1024


def lanes_of(shape):
    return lax.broadcasted_iota(jnp.int32, shape, len(shape) - 1)


def subs_of(shape):
    return lax.broadcasted_iota(jnp.int32, shape, len(shape) - 2)


def turn(x, by, axis):
    by = by % x.shape[axis]
    return x if by == 0 else pltpu.roll(x, by, axis)


def params(limit=VMEM_LIMIT):
    return pltpu.CompilerParams(vmem_limit_bytes=limit)


def whole(shape):
    return pl.BlockSpec(shape, lambda *_: (0,) * len(shape))


def smem():
    return pl.BlockSpec(memory_space=pltpu.SMEM)


def shaped(*shape):
    return jax.ShapeDtypeStruct(shape, jnp.float32)


def halves(x):
    high = x.astype(jnp.bfloat16)
    return high, (x - high.astype(jnp.float32)).astype(jnp.bfloat16)


def sums_above(x):
    sub = subs_of(x.shape)
    running, total = x, x
    by = 1
    while by < x.shape[0]:
        running = running + jnp.where(sub >= by, turn(running, by, 0), 0.0)
        total = total + turn(total, by, 0)
        by *= 2
    return jnp.where(sub >= 1, turn(running, 1, 0), 0.0), total


def cut_kernel(cuts, q_ref, *refs):
    outs, sems = refs[-2 * len(cuts) - 1 : -1], refs[-1]
    rows = q_ref.shape[2]
    copies = [
        pltpu.make_async_copy(
            q_ref.at[:, pl.ds(start, size), r],
            outs[2 * i + r // NSUB].at[:, r % NSUB],
            sems.at[rows * i + r],
        )
        for i, (start, size) in enumerate(cuts)
        for r in range(rows)
    ]
    for copy in copies:
        copy.start()
    for copy in copies:
        copy.wait()


def cut_rows(q, cuts, after):
    tracers, _, rows, _, cols = q.shape
    anywhere = pl.BlockSpec(memory_space=pl.ANY)
    outs = [shaped(tracers, NSUB, size, 1, cols) for _, size in cuts for _ in range(2)]
    outs = pl.pallas_call(
        functools.partial(cut_kernel, cuts),
        in_specs=[anywhere] * (1 + len(after)),
        out_specs=[anywhere] * len(outs),
        out_shape=outs,
        scratch_shapes=[pltpu.SemaphoreType.DMA((rows * len(cuts),))],
        compiler_params=params(),
    )(q, *after)
    return [x.reshape(tracers, NSUB, x.shape[2], cols) for x in outs]


def hold_kernel(*refs):
    pass


def held_until(arrays, after):
    anywhere = pl.BlockSpec(memory_space=pl.ANY)
    return pl.pallas_call(
        hold_kernel,
        in_specs=[anywhere] * (len(arrays) + len(after)),
        out_specs=[anywhere] * len(arrays),
        out_shape=[shaped(*x.shape) for x in arrays],
        input_output_aliases={i: i for i in range(len(arrays))},
        compiler_params=params(),
    )(*arrays, *after)


def both_ends(acc):
    return jnp.where(lanes_of(acc.shape) % SLOTS < SLOTS // 2, acc, turn(acc, SLOTS // 2, 1))


def pack_tracers_kernel(low_ref, high_ref, after_ref, before_ref, packed_ref):
    tracers, _, _, cols = low_ref.shape
    lane = lanes_of((SUB, cols))
    for pair in range(tracers // 2):
        acc = jnp.zeros((SUB, cols), jnp.float32)
        for odd in range(2):
            t = 2 * pair + odd
            rows = [before_ref[t, 1], low_ref[t, 0], low_ref[t, 1], high_ref[t, 0], high_ref[t, 1]]
            for r, x in enumerate(rows + [after_ref[t, 0]]):
                at = HALF * odd + SLOTS * (r + 1)
                acc = jnp.where(lane // SLOTS == at // SLOTS, turn(x, at + NSUB, 1), acc)
        packed_ref[pair] = both_ends(acc)


def pack_tracers(own, rim, after, cost=None):
    tracers, _, levels, cols = own[0].shape
    rows = pl.BlockSpec((tracers, NSUB, SUB, cols), lambda i: (0, 0, i, 0))
    return pl.pallas_call(
        functools.partial(ignoring, len(after), pack_tracers_kernel),
        grid=(levels // SUB,),
        in_specs=[pl.BlockSpec(memory_space=pl.ANY)] * len(after) + [rows] * 4,
        out_specs=pl.BlockSpec((tracers // 2, SUB, cols), lambda i: (0, i, 0)),
        out_shape=shaped(tracers // 2, levels, cols),
        compiler_params=params(),
        cost_estimate=cost,
    )(*after, *own, *rim)


def ignoring(count, kernel, *refs):
    kernel(*refs[count:])


def call_once(kernel, operands, outs, scratch=(), scalars=(), after=(), limit=VMEM_LIMIT):
    return pl.pallas_call(
        functools.partial(ignoring, len(after), kernel),
        grid=(1,),
        in_specs=[pl.BlockSpec(memory_space=pl.ANY)] * len(after)
        + [smem()] * len(scalars)
        + [whole(x.shape) for x in operands],
        out_specs=[whole(x.shape) for x in outs],
        out_shape=outs,
        scratch_shapes=list(scratch),
        compiler_params=params(limit),
    )(*after, *scalars, *operands)


def pack_ocean_kernel(levels, *refs):
    u_ref, v_ref, t_ref, s_ref, sea_ref, floor_ref, packed_ref, edges_ref, row_ref = refs
    edge_low_ref, edge_high_ref = edges_ref.at[0], edges_ref.at[1]
    tile_rows, cols = sea_ref.shape
    lane = lanes_of((levels, cols))
    edge_low_ref[4 * NSUB] = jnp.zeros((levels, cols), jnp.float32)
    edge_high_ref[4 * NSUB] = jnp.zeros((levels, cols), jnp.float32)
    for f, ref in enumerate((u_ref, v_ref, t_ref, s_ref)):
        acc = jnp.zeros((levels, cols), jnp.float32)
        for r in range(tile_rows):
            x = ref[pl.ds(r, levels, stride=tile_rows), :]
            row_ref[f, r] = x
            acc = jnp.where(lane // SLOTS == r, turn(x, SLOTS * r + NSUB, 1), acc)
            if r < NSUB:
                edge_low_ref[NSUB * f + r] = x
            if r >= tile_rows - NSUB:
                edge_high_ref[NSUB * f + r - tile_rows + NSUB] = x
        packed_ref[f] = both_ends(acc)
    depth = jnp.where(sea_ref[...] == 1, floor_ref[...], 0).astype(jnp.float32)
    acc = jnp.zeros((levels, cols), jnp.float32)
    for r in range(tile_rows):
        x = jnp.broadcast_to(depth[r : r + 1], (levels, cols))
        acc = jnp.where(lane // SLOTS == r, turn(x, SLOTS * r + NSUB, 1), acc)
    packed_ref[4] = both_ends(acc)
    edge_low_ref[4 * NSUB, 0:NSUB, :] = depth[0:NSUB]
    edge_high_ref[4 * NSUB, 0:NSUB, :] = depth[tile_rows - NSUB :]


def pack_ocean(flat, sea, levels):
    cols = sea[0].shape[1]
    edges = shaped(2, 4 * NSUB + 1, levels, cols)
    return call_once(
        functools.partial(pack_ocean_kernel, levels),
        [*flat, *sea],
        [shaped(5, levels, cols), edges, shaped(4, sea[0].shape[0], levels, cols)],
        limit=VMEM_MOST,
    )


def with_sides(own, left, right):
    slot = lanes_of(own.shape) % SLOTS
    ends = jnp.where(slot < NSUB, left, right)
    return jnp.where((slot < NSUB) | (slot >= SLOTS - NSUB), ends, own)


def ocean_sides_kernel(own_ref, left_ref, right_ref, edges_ref, up_ref, down_ref, out_ref):
    _, levels, cols = own_ref.shape
    rows = edges_ref.shape[1]
    up_ref[0:rows] = edges_ref[0]
    down_ref[0:rows] = edges_ref[1]
    slot = lanes_of((levels, cols)) % SLOTS
    place = lax.axis_index("gy")
    first, last = place == 0, place == lax.axis_size("gy") - 1
    for f in range(5):
        x = with_sides(own_ref[f], left_ref[f], right_ref[f])
        if f == 4:
            x = jnp.where((slot < NSUB) & first, 0.0, x)
            x = jnp.where((slot >= SLOTS - NSUB) & last, 0.0, x)
        out_ref[f] = x
        up_ref[rows + f] = x
        down_ref[rows + f] = x


def ocean_sides(own, left, right, edges):
    edge = shaped(edges.shape[1] + 5, *edges.shape[2:])
    return call_once(
        ocean_sides_kernel,
        [own, left, right, edges],
        [edge, edge, shaped(*own.shape)],
    )


def ocean_kernel(blocks, levels, *refs):
    own_ref, sea_ref, floor_ref, packed_ref, after_ref, before_ref = refs[:6]
    smix_ref, mixed_ref, send_ref, local_ref, faces_ref, depths_ref, press_ref, total_ref = refs[6:]
    tile_rows, cols = sea_ref.shape
    sub_rows = tile_rows // blocks
    shape = (levels, cols)
    lane = lanes_of(shape)
    first, last = lane == 0, lane == cols - 1
    base = lax.axis_index("comp") * levels
    level = (base + subs_of(shape)).astype(jnp.float32)
    rims = after_ref.shape[0] - 5

    def packed(f):
        after, before = after_ref[rims + f], before_ref[rims + f]
        rim = jnp.where(lane < NSUB * SLOTS, after, jnp.where(lane >= cols - NSUB * SLOTS, before, 0.0))
        return jnp.concatenate([packed_ref[f], rim], axis=1)

    def row_after(x):
        return turn(x, -SLOTS, 1)

    def row_before(x):
        return turn(x, SLOTS, 1)

    up, vp, tp, sp, dp = [packed(f) for f in range(5)]
    wide = jnp.concatenate([level, level], axis=1)
    wet = (wide < dp).astype(jnp.float32)
    heavy = wet * (-0.2 * tp + 0.8 * sp)
    above, total = sums_above(heavy)
    press = above + 0.5 * heavy
    east = up + DT_FLOW * (CORIOLIS * vp - (row_after(press) - press))
    north = vp + DT_FLOW * (-CORIOLIS * up - (turn(press, -1, 1) - press))
    open_n = wet * turn(wet, -1, 1)
    flux_t = open_n * (turn(tp, -1, 1) - tp)
    flux_s = open_n * (turn(sp, -1, 1) - sp)
    total_e, total_n = row_after(total) - total, turn(total, -1, 1) - total
    depth_e, depth_n = jnp.minimum(dp, row_after(dp)), jnp.minimum(dp, turn(dp, -1, 1))

    def window(x, g):
        x = turn(x, -SLOTS * (sub_rows * g - NSUB), 1)[:, 0:cols]
        return jnp.where(lane < HALF, x, turn(x, HALF, 1))

    for g in range(blocks):
        send_ref[g, 13] = window(east, g)
        send_ref[g, 14] = window(north, g)
        send_ref[g, 15, 13:14, :] = window(total_e, g)[0:1]
        send_ref[g, 15, 14:15, :] = window(total_n, g)[0:1]
        send_ref[g, 15, 15:16, :] = jnp.zeros((1, cols), jnp.float32)
        depths_ref[g, 24:25, :] = window(depth_e, g)[0:1]
        depths_ref[g, 25:26, :] = window(depth_n, g)[0:1]
        depths_ref[g, 26:27, :] = window(dp, g)[0:1]

    slot = lanes_of(tp.shape) % SLOTS

    def edges(x, other):
        x = jnp.where(slot == 0, turn(x, -6, 1), other)
        return x[:, 0:cols], x[:, cols:]

    edge_p, edge_w = edges(press, press), edges(wet, wet)
    edge_t, edge_s = edges(tp, flux_t), edges(sp, flux_s)
    edge_total, edge_depth = edges(total, total), edges(dp, dp)

    def edge(pair, r):
        at = r % tile_rows
        return turn(pair[0] if 0 <= r < tile_rows else pair[1], -(SLOTS * at + 1), 1)

    depth = jnp.where(sea_ref[...] == 1, floor_ref[...], 0).astype(jnp.float32)

    def row_of(f, r):
        if r < 0:
            return before_ref[NSUB * f + r + NSUB]
        if r >= tile_rows:
            return after_ref[NSUB * f + r - tile_rows]
        return own_ref[f, r]

    def depth_of(r):
        if r < 0:
            x = before_ref[4 * NSUB, r + NSUB : r + NSUB + 1, :]
        elif r >= tile_rows:
            x = after_ref[4 * NSUB, r - tile_rows : r - tile_rows + 1, :]
        else:
            x = depth[r : r + 1]
        return jnp.broadcast_to(x, shape)

    lo, hi = -NSUB, tile_rows + NSUB
    for r in range(lo, hi):
        heavy = (level < depth_of(r)).astype(jnp.float32) * (-0.2 * row_of(2, r) + 0.8 * row_of(3, r))
        above, total = sums_above(heavy)
        press_ref[r - lo] = above + 0.5 * heavy
        total_ref[r - lo] = total

    def windows(r, before):
        for g in range(blocks):
            j = r - (sub_rows * g - before)
            if 0 <= j < sub_rows + 1 + before:
                yield g, j

    flux_before = [None, None]
    for r in range(lo, hi - 1):
        press, press_e = press_ref[r - lo], press_ref[r - lo + 1]
        total, total_a = total_ref[r - lo], total_ref[r - lo + 1]
        d, d_e = depth_of(r), depth_of(r + 1)
        d_n = jnp.where(last, edge(edge_depth, r), turn(d, -1, 1))
        face_e, face_n = jnp.minimum(d, d_e), jnp.minimum(d, d_n)
        u, v = row_of(0, r), row_of(1, r)
        east = u + DT_FLOW * (CORIOLIS * v - (press_e - press))
        press_n = jnp.where(last, edge(edge_p, r), turn(press, -1, 1))
        north = v + DT_FLOW * (-CORIOLIS * u - (press_n - press))
        total_e = total_a - total
        total_n = jnp.where(last, edge(edge_total, r), turn(total, -1, 1)) - total
        for g, j in windows(r, 2):
            send_ref[g, j] = east
            send_ref[g, 15, j : j + 1, :] = total_e[0:1]
            depths_ref[g, j : j + 1, :] = face_e[0:1]
        for g, j in windows(r, 1):
            send_ref[g, 7 + j] = north
            send_ref[g, 15, 7 + j : 8 + j, :] = total_n[0:1]
            depths_ref[g, 8 + j : 9 + j, :] = face_n[0:1]
            depths_ref[g, 16 + j : 17 + j, :] = d[0:1]
        if 0 <= r < tile_rows:
            local_ref[0, r] = east
            local_ref[1, r] = north
            faces_ref[0, r : r + 1, :] = face_e[0:1]
            faces_ref[1, r : r + 1, :] = face_n[0:1]
            for g in range(blocks):
                send_ref[g, 16, r : r + 1, :] = total_e[0:1]
                send_ref[g, 17, r : r + 1, :] = total_n[0:1]
        if r < -1 or r >= tile_rows:
            continue
        open_e = (level < face_e).astype(jnp.float32)
        open_n = (level < face_n).astype(jnp.float32)
        for i, (f, ends) in enumerate(((2, edge_t), (3, edge_s))):
            x = row_of(f, r)
            flux_e = open_e * (row_of(f, r + 1) - x)
            if r >= 0:
                ending = edge(ends, r)
                flux_n = open_n * (jnp.where(last, ending, turn(x, -1, 1)) - x)
                flux_b = jnp.where(first, ending, turn(flux_n, 1, 1))
                mixed = x + MIXING * ((flux_e - flux_before[i]) + (flux_n - flux_b))
                mixed_ref[i, r] = mixed
                if i == 1:
                    smix_ref[pl.ds(r, levels, stride=tile_rows), :] = mixed
            flux_before[i] = flux_e


def ocean_phase(blocks, levels, own, sea, packed, rim_after, rim_before, after):
    tile_rows, cols = sea[0].shape
    outs = [
        shaped(levels * tile_rows, cols),
        shaped(2, tile_rows, levels, cols),
        shaped(blocks, ENTRIES, levels, cols),
        shaped(2, tile_rows, levels, cols),
        shaped(2, tile_rows, cols),
        shaped(blocks, 32, cols),
    ]
    tall = tile_rows + 2 * NSUB
    return call_once(
        functools.partial(ocean_kernel, blocks, levels),
        [own, *sea, packed, rim_after, rim_before],
        outs,
        [pltpu.VMEM((tall, levels, cols), jnp.float32)] * 2,
        after=after,
    )


def velocity_kernel(local_ref, faces_ref, received_ref, east_ref, north_ref):
    blocks = received_ref.shape[0]
    _, tile_rows, levels, cols = local_ref.shape
    group = lax.axis_index("comp")
    level = (group * levels + subs_of((levels, cols))).astype(jnp.float32)
    for f, out_ref in enumerate((east_ref, north_ref)):
        above = jnp.zeros((tile_rows, cols), jnp.float32)
        for s in range(blocks - 1):
            above = above + jnp.where(s < group, received_ref[s, f], 0.0)
        for r in range(tile_rows):
            x = local_ref[f, r] - DT_FLOW * jnp.broadcast_to(above[r : r + 1], (levels, cols))
            x = jnp.where(level < faces_ref[f, r : r + 1, :], x, 0.0)
            out_ref[pl.ds(r, levels, stride=tile_rows), :] = x


def velocities(local, faces, received):
    blocks = received.shape[0]
    _, tile_rows, levels, cols = local.shape
    out = shaped(levels * tile_rows, cols)
    return pl.pallas_call(
        velocity_kernel,
        grid=(1,),
        in_specs=[
            whole(local.shape),
            whole(faces.shape),
            pl.BlockSpec((blocks, 2, levels, cols), lambda i: (0, ENTRIES // 2 - 1, 0, 0)),
        ],
        out_specs=[whole(out.shape)] * 2,
        out_shape=[out] * 2,
        compiler_params=params(),
    )(local, faces, received)


def advection_kernel(first_part, parts, level_count, *refs):
    (
        absorb_ref,
        surface_ref,
        depth_ref,
        totals_ref,
        courant_ref,
        low_ref,
        high_ref,
        after_ref,
        before_ref,
        side_ref,
        left_ref,
        right_ref,
    ) = refs[:12]
    moved_ref, light_ref, heat_ref, carry_out_ref = refs[-10:-6]
    coef_ref, side_coef_ref, edge_ref, running_ref, above_ref, shift_ref = refs[-6:]
    depth_ref = depth_ref.at[lax.axis_index("comp")]
    step = pl.program_id(0)
    tracers, _, _, cols = low_ref.shape
    levels = courant_ref.shape[2]
    sub_rows = surface_ref.shape[0]
    rows = sub_rows + 2
    shape = (levels, cols)
    lane = lanes_of(shape)
    first, last = lane == 0, lane == cols - 1
    first8, last8 = first[0:SUB], last[0:SUB]
    slot = lane % SLOTS

    @pl.when(step == 0)
    def _():
        running_ref[...] = refs[12][...] if first_part else jnp.zeros_like(running_ref)
        size = (2 * cols, 2 * cols)
        source, to = subs_of(size) % cols, lanes_of(size)
        hit = ((to < cols) & (source == to + 1)) | ((to >= cols) & (source == to - cols - 1))
        shift_ref[...] = hit.astype(jnp.float32).astype(jnp.bfloat16)

    part = first_part + step
    above = jnp.zeros(above_ref.shape, jnp.float32)
    for s in range(totals_ref.shape[0] - 1):
        above = above + jnp.where(s < part // parts, totals_ref[s, 0], 0.0)
    above_ref[...] = above
    level = (part * levels + subs_of(shape)).astype(jnp.float32)

    def spread(ref, r):
        return jnp.broadcast_to(ref[r : r + 1, :], shape)

    def courant(entry, face):
        x = courant_ref[0, entry] - DT_FLOW * spread(above_ref, entry)
        return COURANT * jnp.tanh(jnp.where(level < spread(depth_ref, face), x, 0.0))

    def coefficients(wet, ce, ce_b, cn, cn_b):
        return (
            wet
            * (
                1.0
                - jnp.maximum(ce, 0.0)
                + jnp.minimum(ce_b, 0.0)
                - jnp.maximum(cn, 0.0)
                + jnp.minimum(cn_b, 0.0)
            ),
            -wet * jnp.minimum(ce, 0.0),
            wet * jnp.maximum(ce_b, 0.0),
            -wet * jnp.minimum(cn, 0.0),
            wet * jnp.maximum(cn_b, 0.0),
        )

    side_e, side_n = courant(13, 24), courant(14, 25)
    wet = (level < spread(depth_ref, 26)).astype(jnp.float32)
    packed_coef = coefficients(wet, side_e, turn(side_e, SLOTS, 1), side_n, turn(side_n, 1, 1))
    for i in range(5):
        side_coef_ref[i] = packed_coef[i]
    ce_b = courant(0, 0)
    for j in range(rows):
        ce, cn = courant(1 + j, 1 + j), courant(7 + j, 8 + j)
        cn_b = jnp.where(first, turn(side_n, -(SLOTS * (j + 1) + 1), 1), turn(cn, 1, 1))
        wet = (level < spread(depth_ref, 16 + j)).astype(jnp.float32)
        for i, x in enumerate(coefficients(wet, ce, ce_b, cn, cn_b)):
            coef_ref[5 * j + i] = x
        ce_b = ce
    for i in range(side_ref.shape[0]):
        x = with_sides(side_ref[i], left_ref[i], right_ref[i])
        edge_ref[i, 0] = jnp.where(slot == 0, turn(x, -6, 1), x)
        x = (
            (side_coef_ref[0] * x + side_coef_ref[1] * turn(x, -SLOTS, 1))
            + (side_coef_ref[2] * turn(x, SLOTS, 1) + side_coef_ref[3] * turn(x, -1, 1))
            + side_coef_ref[4] * turn(x, 1, 1)
        )
        edge_ref[i, 1] = jnp.where(slot == 0, turn(x, -6, 1), x)

    layer = 2.0 / level_count
    zero = jnp.zeros((SUB, cols), jnp.float32)
    for k in range(0, levels, SUB):
        at = slice(k, k + SUB)

        def shifted(tiles):
            high, low = halves(jnp.concatenate(tiles, axis=0))
            return jnp.dot(
                jnp.concatenate([high, low], axis=1),
                shift_ref[...],
                preferred_element_type=jnp.float32,
            )

        def stencil(x, coef, edge, beside):
            north = jnp.where(last8, edge, beside[:, :cols])
            south = jnp.where(first8, edge, beside[:, cols:])
            return (
                (coef[0] * x[1] + coef[1] * x[2])
                + (coef[2] * x[0] + coef[3] * north)
                + coef[4] * south
            )

        def advect(i, sums):
            sums = list(sums)
            fields = []
            for t in range(GROUP):
                t = GROUP * i + t
                rows_of = (before_ref, low_ref, high_ref, after_ref)
                x = [ref[t, n, at] for ref in rows_of for n in range(NSUB)]
                fields.append(x)
            for stage in range(NSUB):
                inner = range(1 + stage, rows + 1 - stage)
                beside = shifted([x[j - stage] for j in inner for x in fields])
                fresh = [[] for _ in fields]
                for n, j in enumerate(inner):
                    coef = [coef_ref[5 * (j - 1) + c, at] for c in range(5)]
                    for t, x in enumerate(fields):
                        edges = edge_ref[GROUP // 2 * i + t // 2, stage, at]
                        edge = turn(edges, -(HALF * (t % 2) + SLOTS * j + 1), 1)
                        row = SUB * (len(fields) * n + t)
                        fresh[t].append(
                            stencil(x[n : n + 3], coef, edge, beside[row : row + SUB])
                        )
                fields = fresh
            for t, x in enumerate(fields):
                for r in range(sub_rows):
                    moved_ref[GROUP * i + t, r, at] = x[r]
                    sums[r] = sums[r] + absorb_ref[GROUP * i + t] * x[r]
            return tuple(sums)

        sums = (zero,) * sub_rows
        for i in range(tracers // GROUP):
            sums = advect(i, sums)
        for r in range(sub_rows):
            optical = layer * (CLEAR_WATER + sums[r])
            above, total = sums_above(optical)
            through = jnp.exp(-(running_ref[r] + above))
            running_ref[r] = running_ref[r] + total
            surface = jnp.broadcast_to(surface_ref[r : r + 1, :], (SUB, cols))
            light_ref[r, at] = surface * through * jnp.exp(-0.5 * optical)
            wet = (level[at] < jnp.broadcast_to(depth_ref[17 + r : 18 + r, :], (SUB, cols))).astype(
                jnp.float32
            )
            heat_ref[0, r, at] = wet * surface * through * (1.0 - jnp.exp(-optical)) / layer
    carry_out_ref[...] = running_ref[...]


def advection(cut, level_count, absorb, surface, depth, received, own, rim, sides, carry, heat, after):
    first_part, count = cut
    tracers, _, _, cols = own[0].shape
    every, _, levels, _ = received.shape
    parts = levels // SUB
    sub_rows = surface.shape[0]
    rows = pl.BlockSpec((tracers, NSUB, SUB, cols), lambda i: (0, 0, i, 0))
    side = pl.BlockSpec((tracers // 2, SUB, cols), lambda i: (0, i, 0))
    operands = [absorb, surface, depth, received, received, *own, *rim, *sides]
    in_specs = [
        smem(),
        whole(surface.shape),
        whole(depth.shape),
        pl.BlockSpec((every, 1, levels, cols), lambda i: (0, 15, 0, 0)),
        pl.BlockSpec(
            (1, ENTRIES, SUB, cols),
            lambda i: ((first_part + i) // parts, 0, (first_part + i) % parts, 0),
        ),
        rows,
        rows,
        rows,
        rows,
        side,
        side,
        side,
    ]
    aliases = {}
    carry_shape = (sub_rows, SUB, cols)
    if carry is not None:
        operands.append(carry)
        in_specs.append(whole(carry_shape))
        aliases = {len(operands): 2}
        operands.append(heat)
    operands += after
    in_specs += [pl.BlockSpec(memory_space=pl.ANY)] * (len(operands) - len(in_specs))
    outs = [
        shaped(tracers, sub_rows, count * SUB, cols),
        shaped(sub_rows, count * SUB, cols),
        shaped(every, sub_rows, levels, cols),
        shaped(*carry_shape),
    ]
    return pl.pallas_call(
        functools.partial(advection_kernel, first_part, parts, level_count),
        grid=(count,),
        in_specs=in_specs,
        out_specs=[
            pl.BlockSpec((tracers, sub_rows, SUB, cols), lambda i: (0, 0, i, 0)),
            pl.BlockSpec((sub_rows, SUB, cols), lambda i: (0, i, 0)),
            pl.BlockSpec(
                (1, sub_rows, SUB, cols),
                lambda i: ((first_part + i) // parts, 0, (first_part + i) % parts, 0),
            ),
            whole(carry_shape),
        ],
        out_shape=outs,
        scratch_shapes=[
            pltpu.VMEM((5 * (sub_rows + 2), SUB, cols), jnp.float32),
            pltpu.VMEM((5, SUB, cols), jnp.float32),
            pltpu.VMEM((tracers // 2, 2, SUB, cols), jnp.float32),
            pltpu.VMEM((sub_rows, SUB, cols), jnp.float32),
            pltpu.VMEM((levels, cols), jnp.float32),
            pltpu.VMEM((2 * cols, 2 * cols), jnp.bfloat16),
        ],
        input_output_aliases=aliases,
        compiler_params=params(),
    )(*operands)


def spread_kernel(matrix_ref, out_ref):
    tracers = matrix_ref.shape[0]
    size = tracers * SUB
    tall = (subs_of((size, tracers)) // SUB == lanes_of((size, tracers))).astype(jnp.float32)
    wide = (lanes_of((tracers, size)) // SUB == subs_of((tracers, size))).astype(jnp.float32)
    exact = functools.partial(
        jnp.dot, precision=lax.Precision.HIGHEST, preferred_element_type=jnp.float32
    )
    same = subs_of((size, size)) % SUB == lanes_of((size, size)) % SUB
    out_ref[...] = jnp.where(same, exact(exact(tall, matrix_ref[...]), wide), 0.0)


def uptake_kernel(first_level, *refs):
    growth_ref, half_ref, dim_ref, matrix_ref, depth_ref, moved_ref, light_ref = refs[:7]
    depth_ref = depth_ref.at[lax.axis_index("comp")]
    result_ref, token_ref, uptake_ref = refs[-3:]
    token_ref[...] = jnp.zeros_like(token_ref)
    tracers, sub_rows, levels, cols = moved_ref.shape
    step = pl.program_id(0)
    matrix_high, matrix_low = halves(matrix_ref[...])
    for k in range(0, levels, SUB):
        at = slice(k, k + SUB)
        level = (first_level + step * levels + k + subs_of((SUB, cols))).astype(jnp.float32)
        light = [light_ref[r, at] for r in range(sub_rows)]
        food = [moved_ref[0, r, at] for r in range(sub_rows)]
        both = [light[r] * food[r] for r in range(sub_rows)]

        def uptake(t, _):
            for r in range(sub_rows):
                scale = (half_ref[t] + food[r]) * (light[r] + dim_ref[t])
                value = growth_ref[t] * moved_ref[t, r, at] * (both[r] / scale)
                uptake_ref[pl.ds(t * SUB, SUB), r * cols : (r + 1) * cols] = value
            return _

        lax.fori_loop(0, tracers, uptake, 0, unroll=4)
        amount = uptake_ref[...]
        high, low = halves(amount)
        dot = functools.partial(jnp.dot, preferred_element_type=jnp.float32)
        change = dot(matrix_high, high) + (dot(matrix_high, low) + dot(matrix_low, high))
        for r in range(sub_rows):
            depth = jnp.broadcast_to(depth_ref[17 + r : 18 + r, :], (SUB, cols))
            scale = DT_BIO * (level < depth).astype(jnp.float32)
            for t in range(tracers):
                result_ref[t, pl.ds(sub_rows * k + r, SUB, stride=sub_rows), :] = (
                    moved_ref[t, r, at]
                    + scale * change[SUB * t : SUB * (t + 1), r * cols : (r + 1) * cols]
                )


def uptake(cut, all_rows, scalars, matrix, depth, moved, light, result):
    first_part, count = cut
    tracers, sub_rows, _, cols = moved.shape
    operands = [*scalars, matrix, depth, moved, light]
    in_specs = [smem()] * 3 + [
        whole(matrix.shape),
        whole(depth.shape),
        pl.BlockSpec((tracers, sub_rows, SUB, cols), lambda i: (0, 0, i, 0)),
        pl.BlockSpec((sub_rows, SUB, cols), lambda i: (0, i, 0)),
    ]
    aliases = {}
    if result is not None:
        aliases = {len(operands): 0}
        operands.append(result)
        in_specs.append(pl.BlockSpec(memory_space=pl.ANY))
    return pl.pallas_call(
        functools.partial(uptake_kernel, first_part * SUB),
        grid=(count,),
        in_specs=in_specs,
        out_specs=[
            pl.BlockSpec((tracers, SUB * sub_rows, cols), lambda i: (0, first_part + i, 0)),
            whole((SUB, cols)),
        ],
        out_shape=[shaped(tracers, all_rows, cols), shaped(SUB, cols)],
        scratch_shapes=[pltpu.VMEM((tracers * SUB, sub_rows * cols), jnp.float32)],
        input_output_aliases=aliases,
        compiler_params=params(),
    )(*operands)


def warming_kernel(sea_ref, floor_ref, heat_ref, mixed_ref, warm_ref, buoyant_ref):
    blocks, sub_rows, levels, cols = heat_ref.shape
    tile_rows = blocks * sub_rows
    base = lax.axis_index("comp") * levels
    level = (base + subs_of((levels, cols))).astype(jnp.float32)
    depth = jnp.where(sea_ref[...] == 1, floor_ref[...], 0).astype(jnp.float32)
    for r in range(tile_rows):
        at = pl.ds(r, levels, stride=tile_rows)
        warm = mixed_ref[0, r] + WARMING_FACTOR * heat_ref[r // sub_rows, r % sub_rows]
        wet = (level < depth[r : r + 1]).astype(jnp.float32)
        warm_ref[at, :] = warm
        buoyant_ref[at, :] = wet * (0.2 * warm - 0.8 * mixed_ref[1, r])


def warming(heat, mixed, sea):
    _, tile_rows, levels, cols = mixed.shape
    outs = [shaped(levels * tile_rows, cols)] * 2
    return call_once(warming_kernel, [*sea, heat, mixed], outs)


def from_before(x, axis):
    return lax.ppermute(x, axis, [(i, i + 1) for i in range(lax.axis_size(axis) - 1)])


def from_after(x, axis):
    return lax.ppermute(x, axis, [(i + 1, i) for i in range(lax.axis_size(axis) - 1)])


def row_pairs():
    blocks, tiles = lax.axis_size("comp"), lax.axis_size("gx")
    places = [b * tiles + tile for tile in range(tiles) for b in range(blocks)]
    return list(zip(places[:-1], places[1:]))


def from_block_before(x):
    return lax.ppermute(x, ("comp", "gx"), row_pairs())


def from_block_after(x):
    return lax.ppermute(x, ("comp", "gx"), [(later, own) for own, later in row_pairs()])


def from_sides(x):
    if lax.axis_size("gy") == 2:
        other = lax.ppermute(x, "gy", [(0, 1), (1, 0)])
        return other, other
    return from_before(x, "gy"), from_after(x, "gy")


def on_device(
    zonal_flow_speed,
    meridional_flow_speed,
    thermal_anomaly,
    brine_anomaly_values,
    marine_indicator,
    seafloor_layer,
    dissolved_species,
    topmost_sunshine,
    attenuation_coefficient,
    peak_intake_speed,
    feedstock_midpoint_constant,
    photon_midpoint_constant,
    stoichiometry_matrix,
):
    blocks = lax.axis_size("comp")
    levels, tile_rows, tile_cols = zonal_flow_speed.shape
    tracer_count, level_count = dissolved_species.shape[:2]
    sub_rows = dissolved_species.shape[4]
    ocean = (zonal_flow_speed, meridional_flow_speed, thermal_anomaly, brine_anomaly_values)
    sea = (marine_indicator, seafloor_layer)
    flat = [x.reshape(levels * tile_rows, tile_cols) for x in ocean]
    q = dissolved_species.reshape(tracer_count, level_count, sub_rows, 1, tile_cols)
    parts = levels // SUB
    every = parts * blocks
    sizes = [every - 5 * every // 8, 3 * every // 8, every // 4]
    cuts = [(sum(sizes[:i]), size) for i, size in enumerate(sizes)]
    matrix = call_once(
        spread_kernel,
        [stoichiometry_matrix],
        [shaped(SUB * tracer_count, SUB * tracer_count)],
    )[0]
    scalars_of_uptake = (
        peak_intake_speed,
        feedstock_midpoint_constant,
        photon_midpoint_constant,
    )

    def rims(own):
        return own, (from_block_after(own[0]), from_block_before(own[1]))

    def sides(x):
        return (x, *from_sides(x))

    packed, edges, ocean_rows = pack_ocean(flat, sea, levels)
    ranges = [(first * SUB, size * SUB) for first, size in cuts]
    chunks = [rims(cut_rows(q, ranges[:1], [packed]))]
    later = cut_rows(q, ranges[1:], chunks[0][0][:1])
    up, down, packed = ocean_sides(packed, *from_sides(packed), edges)
    after, before = from_after(up, "gx"), from_before(down, "gx")
    smix, mixed, send, local, faces, depths = ocean_phase(
        blocks, levels, ocean_rows, sea, packed, after, before, later[:1]
    )
    received = lax.all_to_all(send, "comp", split_axis=0, concat_axis=0, tiled=True)
    east_new, north_new = velocities(local, faces, received)
    own = pack_tracers(*chunks[0], [depths], COVER)
    chunks.append(rims(held_until(later[:2], [own])))

    surface = topmost_sunshine.reshape(sub_rows, tile_cols)
    carry, heat, result = None, None, None
    near = sides(own)
    for i, cut in enumerate(cuts):
        moved, light, heat, carry = advection(
            cut,
            level_count,
            attenuation_coefficient,
            surface,
            depths,
            received,
            *chunks[i],
            near,
            carry,
            heat,
            [] if i == 0 else [token],
        )
        if i > 0 and i + 1 < len(cuts):
            near = sides(pack_tracers(*chunks[i + 1], [carry]))
        result, token = uptake(
            cut,
            level_count * sub_rows,
            scalars_of_uptake,
            matrix,
            depths,
            moved,
            light,
            result,
        )
        if i == 0:
            chunks.append(rims(held_until(later[2:], [token])))
            near = sides(pack_tracers(*chunks[1], [token]))
    heat = lax.all_to_all(heat, "comp", split_axis=0, concat_axis=0, tiled=True)
    warmed_result, buoyancy = warming(heat, mixed, sea)
    fields = (east_new, north_new, warmed_result, smix, buoyancy)
    return (
        *[x.reshape(zonal_flow_speed.shape) for x in fields],
        result.reshape(dissolved_species.shape),
    )


def solution(mesh):
    return jax.shard_map(
        on_device,
        mesh=mesh,
        in_specs=(
            P("comp", "gx", "gy"),
            P("comp", "gx", "gy"),
            P("comp", "gx", "gy"),
            P("comp", "gx", "gy"),
            P("gx", "gy"),
            P("gx", "gy"),
            P(None, None, "gx", "comp", None, "gy"),
            P("gx", "comp", None, "gy"),
            P(),
            P(),
            P(),
            P(),
            P(),
        ),
        out_specs=(
            P("comp", "gx", "gy"),
            P("comp", "gx", "gy"),
            P("comp", "gx", "gy"),
            P("comp", "gx", "gy"),
            P("comp", "gx", "gy"),
            P(None, None, "gx", "comp", None, "gy"),
        ),
        check_vma=False,
    )
```

```python
import functools

import jax
import jax.numpy as jnp
from jax import lax
from jax.experimental import pallas as pl
from jax.experimental.pallas import tpu as pltpu
from jax.sharding import PartitionSpec as P

NSUB = 2
SLOTS = 4 * NSUB
SUB = 8
GROUP = 24
HALF = 64
ENTRIES = 18

DT_FLOW = 0.1
CORIOLIS = 0.3
MIXING = 0.15
COURANT = 0.24
DT_BIO = 0.5
WARMING_FACTOR = 0.5
CLEAR_WATER = 0.5
VMEM_LIMIT = 10 * 1024 * 1024
COVER = pl.CostEstimate(flops=0, bytes_accessed=200_000_000, transcendentals=0)
VMEM_MOST = 62 * 1024 * 1024


def lanes_of(shape):
    return lax.broadcasted_iota(jnp.int32, shape, len(shape) - 1)


def subs_of(shape):
    return lax.broadcasted_iota(jnp.int32, shape, len(shape) - 2)


def turn(x, by, axis):
    by = by % x.shape[axis]
    return x if by == 0 else pltpu.roll(x, by, axis)


def params(limit=VMEM_LIMIT):
    return pltpu.CompilerParams(vmem_limit_bytes=limit)


def whole(shape):
    return pl.BlockSpec(shape, lambda *_: (0,) * len(shape))


def smem():
    return pl.BlockSpec(memory_space=pltpu.SMEM)


def shaped(*shape):
    return jax.ShapeDtypeStruct(shape, jnp.float32)


def halves(x):
    high = x.astype(jnp.bfloat16)
    return high, (x - high.astype(jnp.float32)).astype(jnp.bfloat16)


def sums_above(x):
    sub = subs_of(x.shape)
    running, total = x, x
    by = 1
    while by < x.shape[0]:
        running = running + jnp.where(sub >= by, turn(running, by, 0), 0.0)
        total = total + turn(total, by, 0)
        by *= 2
    return jnp.where(sub >= 1, turn(running, 1, 0), 0.0), total


def cut_kernel(cuts, q_ref, *refs):
    outs, sems = refs[-2 * len(cuts) - 1 : -1], refs[-1]
    rows = q_ref.shape[2]
    copies = [
        pltpu.make_async_copy(
            q_ref.at[:, pl.ds(start, size), r],
            outs[2 * i + r // NSUB].at[:, r % NSUB],
            sems.at[rows * i + r],
        )
        for i, (start, size) in enumerate(cuts)
        for r in range(rows)
    ]
    for copy in copies:
        copy.start()
    for copy in copies:
        copy.wait()


def cut_rows(q, cuts, after):
    tracers, _, rows, _, cols = q.shape
    anywhere = pl.BlockSpec(memory_space=pl.ANY)
    outs = [shaped(tracers, NSUB, size, 1, cols) for _, size in cuts for _ in range(2)]
    outs = pl.pallas_call(
        functools.partial(cut_kernel, cuts),
        in_specs=[anywhere] * (1 + len(after)),
        out_specs=[anywhere] * len(outs),
        out_shape=outs,
        scratch_shapes=[pltpu.SemaphoreType.DMA((rows * len(cuts),))],
        compiler_params=params(),
    )(q, *after)
    return [x.reshape(tracers, NSUB, x.shape[2], cols) for x in outs]


def hold_kernel(*refs):
    pass


def held_until(arrays, after):
    anywhere = pl.BlockSpec(memory_space=pl.ANY)
    return pl.pallas_call(
        hold_kernel,
        in_specs=[anywhere] * (len(arrays) + len(after)),
        out_specs=[anywhere] * len(arrays),
        out_shape=[shaped(*x.shape) for x in arrays],
        input_output_aliases={i: i for i in range(len(arrays))},
        compiler_params=params(),
    )(*arrays, *after)


def both_ends(acc):
    return jnp.where(lanes_of(acc.shape) % SLOTS < SLOTS // 2, acc, turn(acc, SLOTS // 2, 1))


def pack_tracers_kernel(low_ref, high_ref, after_ref, before_ref, packed_ref):
    tracers, _, _, cols = low_ref.shape
    lane = lanes_of((SUB, cols))
    for pair in range(tracers // 2):
        acc = jnp.zeros((SUB, cols), jnp.float32)
        for odd in range(2):
            t = 2 * pair + odd
            rows = [before_ref[t, 1], low_ref[t, 0], low_ref[t, 1], high_ref[t, 0], high_ref[t, 1]]
            for r, x in enumerate(rows + [after_ref[t, 0]]):
                at = HALF * odd + SLOTS * (r + 1)
                acc = jnp.where(lane // SLOTS == at // SLOTS, turn(x, at + NSUB, 1), acc)
        packed_ref[pair] = both_ends(acc)


def pack_tracers(own, rim, after):
    tracers, _, levels, cols = own[0].shape
    rows = pl.BlockSpec((tracers, NSUB, SUB, cols), lambda i: (0, 0, i, 0))
    return pl.pallas_call(
        functools.partial(ignoring, len(after), pack_tracers_kernel),
        grid=(levels // SUB,),
        in_specs=[pl.BlockSpec(memory_space=pl.ANY)] * len(after) + [rows] * 4,
        out_specs=pl.BlockSpec((tracers // 2, SUB, cols), lambda i: (0, i, 0)),
        out_shape=shaped(tracers // 2, levels, cols),
        compiler_params=params(),
    )(*after, *own, *rim)


def ignoring(count, kernel, *refs):
    kernel(*refs[count:])


def call_once(kernel, operands, outs, scratch=(), scalars=(), after=(), limit=VMEM_LIMIT, cost=None):
    return pl.pallas_call(
        functools.partial(ignoring, len(after), kernel),
        grid=(1,),
        in_specs=[pl.BlockSpec(memory_space=pl.ANY)] * len(after)
        + [smem()] * len(scalars)
        + [whole(x.shape) for x in operands],
        out_specs=[whole(x.shape) for x in outs],
        out_shape=outs,
        scratch_shapes=list(scratch),
        compiler_params=params(limit),
        cost_estimate=cost,
    )(*after, *scalars, *operands)


def pack_ocean_kernel(levels, *refs):
    u_ref, v_ref, t_ref, s_ref, sea_ref, floor_ref, packed_ref, edges_ref, row_ref = refs
    edge_low_ref, edge_high_ref = edges_ref.at[0], edges_ref.at[1]
    tile_rows, cols = sea_ref.shape
    lane = lanes_of((levels, cols))
    edge_low_ref[4 * NSUB] = jnp.zeros((levels, cols), jnp.float32)
    edge_high_ref[4 * NSUB] = jnp.zeros((levels, cols), jnp.float32)
    for f, ref in enumerate((u_ref, v_ref, t_ref, s_ref)):
        acc = jnp.zeros((levels, cols), jnp.float32)
        for r in range(tile_rows):
            x = ref[pl.ds(r, levels, stride=tile_rows), :]
            row_ref[f, r] = x
            acc = jnp.where(lane // SLOTS == r, turn(x, SLOTS * r + NSUB, 1), acc)
            if r < NSUB:
                edge_low_ref[NSUB * f + r] = x
            if r >= tile_rows - NSUB:
                edge_high_ref[NSUB * f + r - tile_rows + NSUB] = x
        packed_ref[f] = both_ends(acc)
    depth = jnp.where(sea_ref[...] == 1, floor_ref[...], 0).astype(jnp.float32)
    acc = jnp.zeros((levels, cols), jnp.float32)
    for r in range(tile_rows):
        x = jnp.broadcast_to(depth[r : r + 1], (levels, cols))
        acc = jnp.where(lane // SLOTS == r, turn(x, SLOTS * r + NSUB, 1), acc)
    packed_ref[4] = both_ends(acc)
    edge_low_ref[4 * NSUB, 0:NSUB, :] = depth[0:NSUB]
    edge_high_ref[4 * NSUB, 0:NSUB, :] = depth[tile_rows - NSUB :]


def pack_ocean(flat, sea, levels):
    cols = sea[0].shape[1]
    edges = shaped(2, 4 * NSUB + 1, levels, cols)
    return call_once(
        functools.partial(pack_ocean_kernel, levels),
        [*flat, *sea],
        [shaped(5, levels, cols), edges, shaped(4, sea[0].shape[0], levels, cols)],
        limit=VMEM_MOST,
    )


def with_sides(own, left, right):
    slot = lanes_of(own.shape) % SLOTS
    ends = jnp.where(slot < NSUB, left, right)
    return jnp.where((slot < NSUB) | (slot >= SLOTS - NSUB), ends, own)


def ocean_sides_kernel(own_ref, left_ref, right_ref, edges_ref, up_ref, down_ref, out_ref):
    _, levels, cols = own_ref.shape
    rows = edges_ref.shape[1]
    up_ref[0:rows] = edges_ref[0]
    down_ref[0:rows] = edges_ref[1]
    slot = lanes_of((levels, cols)) % SLOTS
    place = lax.axis_index("gy")
    first, last = place == 0, place == lax.axis_size("gy") - 1
    for f in range(5):
        x = with_sides(own_ref[f], left_ref[f], right_ref[f])
        if f == 4:
            x = jnp.where((slot < NSUB) & first, 0.0, x)
            x = jnp.where((slot >= SLOTS - NSUB) & last, 0.0, x)
        out_ref[f] = x
        up_ref[rows + f] = x
        down_ref[rows + f] = x


def ocean_sides(own, left, right, edges):
    edge = shaped(edges.shape[1] + 5, *edges.shape[2:])
    return call_once(
        ocean_sides_kernel,
        [own, left, right, edges],
        [edge, edge, shaped(*own.shape)],
    )


def ocean_kernel(blocks, levels, *refs):
    own_ref, sea_ref, floor_ref, packed_ref, after_ref, before_ref = refs[:6]
    smix_ref, mixed_ref, send_ref, local_ref, faces_ref, depths_ref, press_ref, total_ref = refs[6:]
    tile_rows, cols = sea_ref.shape
    sub_rows = tile_rows // blocks
    shape = (levels, cols)
    lane = lanes_of(shape)
    first, last = lane == 0, lane == cols - 1
    base = lax.axis_index("comp") * levels
    level = (base + subs_of(shape)).astype(jnp.float32)
    rims = after_ref.shape[0] - 5

    def packed(f):
        after, before = after_ref[rims + f], before_ref[rims + f]
        rim = jnp.where(lane < NSUB * SLOTS, after, jnp.where(lane >= cols - NSUB * SLOTS, before, 0.0))
        return jnp.concatenate([packed_ref[f], rim], axis=1)

    def row_after(x):
        return turn(x, -SLOTS, 1)

    def row_before(x):
        return turn(x, SLOTS, 1)

    up, vp, tp, sp, dp = [packed(f) for f in range(5)]
    wide = jnp.concatenate([level, level], axis=1)
    wet = (wide < dp).astype(jnp.float32)
    heavy = wet * (-0.2 * tp + 0.8 * sp)
    above, total = sums_above(heavy)
    press = above + 0.5 * heavy
    east = up + DT_FLOW * (CORIOLIS * vp - (row_after(press) - press))
    north = vp + DT_FLOW * (-CORIOLIS * up - (turn(press, -1, 1) - press))
    open_n = wet * turn(wet, -1, 1)
    flux_t = open_n * (turn(tp, -1, 1) - tp)
    flux_s = open_n * (turn(sp, -1, 1) - sp)
    total_e, total_n = row_after(total) - total, turn(total, -1, 1) - total
    depth_e, depth_n = jnp.minimum(dp, row_after(dp)), jnp.minimum(dp, turn(dp, -1, 1))

    def window(x, g):
        x = turn(x, -SLOTS * (sub_rows * g - NSUB), 1)[:, 0:cols]
        return jnp.where(lane < HALF, x, turn(x, HALF, 1))

    for g in range(blocks):
        send_ref[g, 13] = window(east, g)
        send_ref[g, 14] = window(north, g)
        send_ref[g, 15, 13:14, :] = window(total_e, g)[0:1]
        send_ref[g, 15, 14:15, :] = window(total_n, g)[0:1]
        send_ref[g, 15, 15:16, :] = jnp.zeros((1, cols), jnp.float32)
        depths_ref[g, 24:25, :] = window(depth_e, g)[0:1]
        depths_ref[g, 25:26, :] = window(depth_n, g)[0:1]
        depths_ref[g, 26:27, :] = window(dp, g)[0:1]

    slot = lanes_of(tp.shape) % SLOTS

    def edges(x, other):
        x = jnp.where(slot == 0, turn(x, -6, 1), other)
        return x[:, 0:cols], x[:, cols:]

    edge_p, edge_w = edges(press, press), edges(wet, wet)
    edge_t, edge_s = edges(tp, flux_t), edges(sp, flux_s)
    edge_total, edge_depth = edges(total, total), edges(dp, dp)

    def edge(pair, r):
        at = r % tile_rows
        return turn(pair[0] if 0 <= r < tile_rows else pair[1], -(SLOTS * at + 1), 1)

    depth = jnp.where(sea_ref[...] == 1, floor_ref[...], 0).astype(jnp.float32)

    def row_of(f, r):
        if r < 0:
            return before_ref[NSUB * f + r + NSUB]
        if r >= tile_rows:
            return after_ref[NSUB * f + r - tile_rows]
        return own_ref[f, r]

    def depth_of(r):
        if r < 0:
            x = before_ref[4 * NSUB, r + NSUB : r + NSUB + 1, :]
        elif r >= tile_rows:
            x = after_ref[4 * NSUB, r - tile_rows : r - tile_rows + 1, :]
        else:
            x = depth[r : r + 1]
        return jnp.broadcast_to(x, shape)

    lo, hi = -NSUB, tile_rows + NSUB
    for r in range(lo, hi):
        heavy = (level < depth_of(r)).astype(jnp.float32) * (-0.2 * row_of(2, r) + 0.8 * row_of(3, r))
        above, total = sums_above(heavy)
        press_ref[r - lo] = above + 0.5 * heavy
        total_ref[r - lo] = total

    def windows(r, before):
        for g in range(blocks):
            j = r - (sub_rows * g - before)
            if 0 <= j < sub_rows + 1 + before:
                yield g, j

    flux_before = [None, None]
    for r in range(lo, hi - 1):
        press, press_e = press_ref[r - lo], press_ref[r - lo + 1]
        total, total_a = total_ref[r - lo], total_ref[r - lo + 1]
        d, d_e = depth_of(r), depth_of(r + 1)
        d_n = jnp.where(last, edge(edge_depth, r), turn(d, -1, 1))
        face_e, face_n = jnp.minimum(d, d_e), jnp.minimum(d, d_n)
        u, v = row_of(0, r), row_of(1, r)
        east = u + DT_FLOW * (CORIOLIS * v - (press_e - press))
        press_n = jnp.where(last, edge(edge_p, r), turn(press, -1, 1))
        north = v + DT_FLOW * (-CORIOLIS * u - (press_n - press))
        total_e = total_a - total
        total_n = jnp.where(last, edge(edge_total, r), turn(total, -1, 1)) - total
        for g, j in windows(r, 2):
            send_ref[g, j] = east
            send_ref[g, 15, j : j + 1, :] = total_e[0:1]
            depths_ref[g, j : j + 1, :] = face_e[0:1]
        for g, j in windows(r, 1):
            send_ref[g, 7 + j] = north
            send_ref[g, 15, 7 + j : 8 + j, :] = total_n[0:1]
            depths_ref[g, 8 + j : 9 + j, :] = face_n[0:1]
            depths_ref[g, 16 + j : 17 + j, :] = d[0:1]
        if 0 <= r < tile_rows:
            local_ref[0, r] = east
            local_ref[1, r] = north
            faces_ref[0, r : r + 1, :] = face_e[0:1]
            faces_ref[1, r : r + 1, :] = face_n[0:1]
            for g in range(blocks):
                send_ref[g, 16, r : r + 1, :] = total_e[0:1]
                send_ref[g, 17, r : r + 1, :] = total_n[0:1]
        if r < -1 or r >= tile_rows:
            continue
        open_e = (level < face_e).astype(jnp.float32)
        open_n = (level < face_n).astype(jnp.float32)
        for i, (f, ends) in enumerate(((2, edge_t), (3, edge_s))):
            x = row_of(f, r)
            flux_e = open_e * (row_of(f, r + 1) - x)
            if r >= 0:
                ending = edge(ends, r)
                flux_n = open_n * (jnp.where(last, ending, turn(x, -1, 1)) - x)
                flux_b = jnp.where(first, ending, turn(flux_n, 1, 1))
                mixed = x + MIXING * ((flux_e - flux_before[i]) + (flux_n - flux_b))
                mixed_ref[i, r] = mixed
                if i == 1:
                    smix_ref[pl.ds(r, levels, stride=tile_rows), :] = mixed
            flux_before[i] = flux_e


def ocean_phase(blocks, levels, own, sea, packed, rim_after, rim_before, after):
    tile_rows, cols = sea[0].shape
    outs = [
        shaped(levels * tile_rows, cols),
        shaped(2, tile_rows, levels, cols),
        shaped(blocks, ENTRIES, levels, cols),
        shaped(2, tile_rows, levels, cols),
        shaped(2, tile_rows, cols),
        shaped(blocks, 32, cols),
    ]
    tall = tile_rows + 2 * NSUB
    return call_once(
        functools.partial(ocean_kernel, blocks, levels),
        [own, *sea, packed, rim_after, rim_before],
        outs,
        [pltpu.VMEM((tall, levels, cols), jnp.float32)] * 2,
        after=after,
    )


def velocity_kernel(local_ref, faces_ref, received_ref, east_ref, north_ref):
    blocks = received_ref.shape[0]
    _, tile_rows, levels, cols = local_ref.shape
    group = lax.axis_index("comp")
    level = (group * levels + subs_of((levels, cols))).astype(jnp.float32)
    for f, out_ref in enumerate((east_ref, north_ref)):
        above = jnp.zeros((tile_rows, cols), jnp.float32)
        for s in range(blocks - 1):
            above = above + jnp.where(s < group, received_ref[s, f], 0.0)
        for r in range(tile_rows):
            x = local_ref[f, r] - DT_FLOW * jnp.broadcast_to(above[r : r + 1], (levels, cols))
            x = jnp.where(level < faces_ref[f, r : r + 1, :], x, 0.0)
            out_ref[pl.ds(r, levels, stride=tile_rows), :] = x


def velocities(local, faces, received):
    blocks = received.shape[0]
    _, tile_rows, levels, cols = local.shape
    out = shaped(levels * tile_rows, cols)
    return pl.pallas_call(
        velocity_kernel,
        grid=(1,),
        in_specs=[
            whole(local.shape),
            whole(faces.shape),
            pl.BlockSpec((blocks, 2, levels, cols), lambda i: (0, ENTRIES // 2 - 1, 0, 0)),
        ],
        out_specs=[whole(out.shape)] * 2,
        out_shape=[out] * 2,
        compiler_params=params(),
    )(local, faces, received)


def advection_kernel(first_part, parts, level_count, *refs):
    (
        absorb_ref,
        surface_ref,
        depth_ref,
        totals_ref,
        courant_ref,
        low_ref,
        high_ref,
        after_ref,
        before_ref,
        side_ref,
        left_ref,
        right_ref,
    ) = refs[:12]
    moved_ref, light_ref, heat_ref, carry_out_ref = refs[-10:-6]
    coef_ref, side_coef_ref, edge_ref, running_ref, above_ref, shift_ref = refs[-6:]
    depth_ref = depth_ref.at[lax.axis_index("comp")]
    step = pl.program_id(0)
    tracers, _, _, cols = low_ref.shape
    levels = courant_ref.shape[2]
    sub_rows = surface_ref.shape[0]
    rows = sub_rows + 2
    shape = (levels, cols)
    lane = lanes_of(shape)
    first, last = lane == 0, lane == cols - 1
    first8, last8 = first[0:SUB], last[0:SUB]
    slot = lane % SLOTS

    @pl.when(step == 0)
    def _():
        running_ref[...] = refs[12][...] if first_part else jnp.zeros_like(running_ref)
        size = (2 * cols, 2 * cols)
        source, to = subs_of(size) % cols, lanes_of(size)
        hit = ((to < cols) & (source == to + 1)) | ((to >= cols) & (source == to - cols - 1))
        shift_ref[...] = hit.astype(jnp.float32).astype(jnp.bfloat16)

    part = first_part + step
    above = jnp.zeros(above_ref.shape, jnp.float32)
    for s in range(totals_ref.shape[0] - 1):
        above = above + jnp.where(s < part // parts, totals_ref[s, 0], 0.0)
    above_ref[...] = above
    level = (part * levels + subs_of(shape)).astype(jnp.float32)

    def spread(ref, r):
        return jnp.broadcast_to(ref[r : r + 1, :], shape)

    def courant(entry, face):
        x = courant_ref[0, entry] - DT_FLOW * spread(above_ref, entry)
        return COURANT * jnp.tanh(jnp.where(level < spread(depth_ref, face), x, 0.0))

    def coefficients(wet, ce, ce_b, cn, cn_b):
        return (
            wet
            * (
                1.0
                - jnp.maximum(ce, 0.0)
                + jnp.minimum(ce_b, 0.0)
                - jnp.maximum(cn, 0.0)
                + jnp.minimum(cn_b, 0.0)
            ),
            -wet * jnp.minimum(ce, 0.0),
            wet * jnp.maximum(ce_b, 0.0),
            -wet * jnp.minimum(cn, 0.0),
            wet * jnp.maximum(cn_b, 0.0),
        )

    side_e, side_n = courant(13, 24), courant(14, 25)
    wet = (level < spread(depth_ref, 26)).astype(jnp.float32)
    packed_coef = coefficients(wet, side_e, turn(side_e, SLOTS, 1), side_n, turn(side_n, 1, 1))
    for i in range(5):
        side_coef_ref[i] = packed_coef[i]
    ce_b = courant(0, 0)
    for j in range(rows):
        ce, cn = courant(1 + j, 1 + j), courant(7 + j, 8 + j)
        cn_b = jnp.where(first, turn(side_n, -(SLOTS * (j + 1) + 1), 1), turn(cn, 1, 1))
        wet = (level < spread(depth_ref, 16 + j)).astype(jnp.float32)
        for i, x in enumerate(coefficients(wet, ce, ce_b, cn, cn_b)):
            coef_ref[5 * j + i] = x
        ce_b = ce
    for i in range(side_ref.shape[0]):
        x = with_sides(side_ref[i], left_ref[i], right_ref[i])
        edge_ref[i, 0] = jnp.where(slot == 0, turn(x, -6, 1), x)
        x = (
            (side_coef_ref[0] * x + side_coef_ref[1] * turn(x, -SLOTS, 1))
            + (side_coef_ref[2] * turn(x, SLOTS, 1) + side_coef_ref[3] * turn(x, -1, 1))
            + side_coef_ref[4] * turn(x, 1, 1)
        )
        edge_ref[i, 1] = jnp.where(slot == 0, turn(x, -6, 1), x)

    layer = 2.0 / level_count
    zero = jnp.zeros((SUB, cols), jnp.float32)
    for k in range(0, levels, SUB):
        at = slice(k, k + SUB)

        def shifted(tiles):
            high, low = halves(jnp.concatenate(tiles, axis=0))
            return jnp.dot(
                jnp.concatenate([high, low], axis=1),
                shift_ref[...],
                preferred_element_type=jnp.float32,
            )

        def stencil(x, coef, edge, beside):
            north = jnp.where(last8, edge, beside[:, :cols])
            south = jnp.where(first8, edge, beside[:, cols:])
            return (
                (coef[0] * x[1] + coef[1] * x[2])
                + (coef[2] * x[0] + coef[3] * north)
                + coef[4] * south
            )

        def advect(i, sums):
            sums = list(sums)
            fields = []
            for t in range(GROUP):
                t = GROUP * i + t
                rows_of = (before_ref, low_ref, high_ref, after_ref)
                x = [ref[t, n, at] for ref in rows_of for n in range(NSUB)]
                fields.append(x)
            for stage in range(NSUB):
                inner = range(1 + stage, rows + 1 - stage)
                beside = shifted([x[j - stage] for j in inner for x in fields])
                fresh = [[] for _ in fields]
                for n, j in enumerate(inner):
                    coef = [coef_ref[5 * (j - 1) + c, at] for c in range(5)]
                    for t, x in enumerate(fields):
                        edges = edge_ref[GROUP // 2 * i + t // 2, stage, at]
                        edge = turn(edges, -(HALF * (t % 2) + SLOTS * j + 1), 1)
                        row = SUB * (len(fields) * n + t)
                        fresh[t].append(
                            stencil(x[n : n + 3], coef, edge, beside[row : row + SUB])
                        )
                fields = fresh
            for t, x in enumerate(fields):
                for r in range(sub_rows):
                    moved_ref[GROUP * i + t, r, at] = x[r]
                    sums[r] = sums[r] + absorb_ref[GROUP * i + t] * x[r]
            return tuple(sums)

        sums = (zero,) * sub_rows
        for i in range(tracers // GROUP):
            sums = advect(i, sums)
        for r in range(sub_rows):
            optical = layer * (CLEAR_WATER + sums[r])
            above, total = sums_above(optical)
            through = jnp.exp(-(running_ref[r] + above))
            running_ref[r] = running_ref[r] + total
            surface = jnp.broadcast_to(surface_ref[r : r + 1, :], (SUB, cols))
            light_ref[r, at] = surface * through * jnp.exp(-0.5 * optical)
            wet = (level[at] < jnp.broadcast_to(depth_ref[17 + r : 18 + r, :], (SUB, cols))).astype(
                jnp.float32
            )
            heat_ref[0, r, at] = wet * surface * through * (1.0 - jnp.exp(-optical)) / layer
    carry_out_ref[...] = running_ref[...]


def advection(cut, level_count, absorb, surface, depth, received, own, rim, sides, carry, heat, after):
    first_part, count = cut
    tracers, _, _, cols = own[0].shape
    every, _, levels, _ = received.shape
    parts = levels // SUB
    sub_rows = surface.shape[0]
    rows = pl.BlockSpec((tracers, NSUB, SUB, cols), lambda i: (0, 0, i, 0))
    side = pl.BlockSpec((tracers // 2, SUB, cols), lambda i: (0, i, 0))
    operands = [absorb, surface, depth, received, received, *own, *rim, *sides]
    in_specs = [
        smem(),
        whole(surface.shape),
        whole(depth.shape),
        pl.BlockSpec((every, 1, levels, cols), lambda i: (0, 15, 0, 0)),
        pl.BlockSpec(
            (1, ENTRIES, SUB, cols),
            lambda i: ((first_part + i) // parts, 0, (first_part + i) % parts, 0),
        ),
        rows,
        rows,
        rows,
        rows,
        side,
        side,
        side,
    ]
    aliases = {}
    carry_shape = (sub_rows, SUB, cols)
    if carry is not None:
        operands.append(carry)
        in_specs.append(whole(carry_shape))
        aliases = {len(operands): 2}
        operands.append(heat)
    operands += after
    in_specs += [pl.BlockSpec(memory_space=pl.ANY)] * (len(operands) - len(in_specs))
    outs = [
        shaped(tracers, sub_rows, count * SUB, cols),
        shaped(sub_rows, count * SUB, cols),
        shaped(every, sub_rows, levels, cols),
        shaped(*carry_shape),
    ]
    return pl.pallas_call(
        functools.partial(advection_kernel, first_part, parts, level_count),
        grid=(count,),
        in_specs=in_specs,
        out_specs=[
            pl.BlockSpec((tracers, sub_rows, SUB, cols), lambda i: (0, 0, i, 0)),
            pl.BlockSpec((sub_rows, SUB, cols), lambda i: (0, i, 0)),
            pl.BlockSpec(
                (1, sub_rows, SUB, cols),
                lambda i: ((first_part + i) // parts, 0, (first_part + i) % parts, 0),
            ),
            whole(carry_shape),
        ],
        out_shape=outs,
        scratch_shapes=[
            pltpu.VMEM((5 * (sub_rows + 2), SUB, cols), jnp.float32),
            pltpu.VMEM((5, SUB, cols), jnp.float32),
            pltpu.VMEM((tracers // 2, 2, SUB, cols), jnp.float32),
            pltpu.VMEM((sub_rows, SUB, cols), jnp.float32),
            pltpu.VMEM((levels, cols), jnp.float32),
            pltpu.VMEM((2 * cols, 2 * cols), jnp.bfloat16),
        ],
        input_output_aliases=aliases,
        compiler_params=params(),
    )(*operands)


def spread_kernel(matrix_ref, out_ref):
    tracers = matrix_ref.shape[0]
    size = tracers * SUB
    tall = (subs_of((size, tracers)) // SUB == lanes_of((size, tracers))).astype(jnp.float32)
    wide = (lanes_of((tracers, size)) // SUB == subs_of((tracers, size))).astype(jnp.float32)
    exact = functools.partial(
        jnp.dot, precision=lax.Precision.HIGHEST, preferred_element_type=jnp.float32
    )
    same = subs_of((size, size)) % SUB == lanes_of((size, size)) % SUB
    out_ref[...] = jnp.where(same, exact(exact(tall, matrix_ref[...]), wide), 0.0)


def uptake_kernel(first_level, *refs):
    growth_ref, half_ref, dim_ref, matrix_ref, depth_ref, moved_ref, light_ref = refs[:7]
    depth_ref = depth_ref.at[lax.axis_index("comp")]
    result_ref, token_ref, uptake_ref = refs[-3:]
    token_ref[...] = jnp.zeros_like(token_ref)
    tracers, sub_rows, levels, cols = moved_ref.shape
    step = pl.program_id(0)
    matrix_high, matrix_low = halves(matrix_ref[...])
    for k in range(0, levels, SUB):
        at = slice(k, k + SUB)
        level = (first_level + step * levels + k + subs_of((SUB, cols))).astype(jnp.float32)
        light = [light_ref[r, at] for r in range(sub_rows)]
        food = [moved_ref[0, r, at] for r in range(sub_rows)]
        both = [light[r] * food[r] for r in range(sub_rows)]

        def uptake(t, _):
            for r in range(sub_rows):
                scale = (half_ref[t] + food[r]) * (light[r] + dim_ref[t])
                value = growth_ref[t] * moved_ref[t, r, at] * (both[r] / scale)
                uptake_ref[pl.ds(t * SUB, SUB), r * cols : (r + 1) * cols] = value
            return _

        lax.fori_loop(0, tracers, uptake, 0, unroll=4)
        amount = uptake_ref[...]
        high, low = halves(amount)
        dot = functools.partial(jnp.dot, preferred_element_type=jnp.float32)
        change = dot(matrix_high, high) + (dot(matrix_high, low) + dot(matrix_low, high))
        for r in range(sub_rows):
            depth = jnp.broadcast_to(depth_ref[17 + r : 18 + r, :], (SUB, cols))
            scale = DT_BIO * (level < depth).astype(jnp.float32)
            for t in range(tracers):
                result_ref[t, pl.ds(sub_rows * k + r, SUB, stride=sub_rows), :] = (
                    moved_ref[t, r, at]
                    + scale * change[SUB * t : SUB * (t + 1), r * cols : (r + 1) * cols]
                )


def uptake(cut, all_rows, scalars, matrix, depth, moved, light, result):
    first_part, count = cut
    tracers, sub_rows, _, cols = moved.shape
    operands = [*scalars, matrix, depth, moved, light]
    in_specs = [smem()] * 3 + [
        whole(matrix.shape),
        whole(depth.shape),
        pl.BlockSpec((tracers, sub_rows, SUB, cols), lambda i: (0, 0, i, 0)),
        pl.BlockSpec((sub_rows, SUB, cols), lambda i: (0, i, 0)),
    ]
    aliases = {}
    if result is not None:
        aliases = {len(operands): 0}
        operands.append(result)
        in_specs.append(pl.BlockSpec(memory_space=pl.ANY))
    return pl.pallas_call(
        functools.partial(uptake_kernel, first_part * SUB),
        grid=(count,),
        in_specs=in_specs,
        out_specs=[
            pl.BlockSpec((tracers, SUB * sub_rows, cols), lambda i: (0, first_part + i, 0)),
            whole((SUB, cols)),
        ],
        out_shape=[shaped(tracers, all_rows, cols), shaped(SUB, cols)],
        scratch_shapes=[pltpu.VMEM((tracers * SUB, sub_rows * cols), jnp.float32)],
        input_output_aliases=aliases,
        compiler_params=params(),
    )(*operands)


def warming_kernel(sea_ref, floor_ref, heat_ref, mixed_ref, warm_ref, buoyant_ref):
    blocks, sub_rows, levels, cols = heat_ref.shape
    tile_rows = blocks * sub_rows
    base = lax.axis_index("comp") * levels
    level = (base + subs_of((levels, cols))).astype(jnp.float32)
    depth = jnp.where(sea_ref[...] == 1, floor_ref[...], 0).astype(jnp.float32)
    for r in range(tile_rows):
        at = pl.ds(r, levels, stride=tile_rows)
        warm = mixed_ref[0, r] + WARMING_FACTOR * heat_ref[r // sub_rows, r % sub_rows]
        wet = (level < depth[r : r + 1]).astype(jnp.float32)
        warm_ref[at, :] = warm
        buoyant_ref[at, :] = wet * (0.2 * warm - 0.8 * mixed_ref[1, r])


def warming(heat, mixed, sea):
    _, tile_rows, levels, cols = mixed.shape
    outs = [shaped(levels * tile_rows, cols)] * 2
    return call_once(warming_kernel, [*sea, heat, mixed], outs)


def from_before(x, axis):
    return lax.ppermute(x, axis, [(i, i + 1) for i in range(lax.axis_size(axis) - 1)])


def from_after(x, axis):
    return lax.ppermute(x, axis, [(i + 1, i) for i in range(lax.axis_size(axis) - 1)])


def row_pairs():
    blocks, tiles = lax.axis_size("comp"), lax.axis_size("gx")
    places = [b * tiles + tile for tile in range(tiles) for b in range(blocks)]
    return list(zip(places[:-1], places[1:]))


def from_block_before(x):
    return lax.ppermute(x, ("comp", "gx"), row_pairs())


def from_block_after(x):
    return lax.ppermute(x, ("comp", "gx"), [(later, own) for own, later in row_pairs()])


def from_sides(x):
    if lax.axis_size("gy") == 2:
        other = lax.ppermute(x, "gy", [(0, 1), (1, 0)])
        return other, other
    return from_before(x, "gy"), from_after(x, "gy")


def on_device(
    zonal_flow_speed,
    meridional_flow_speed,
    thermal_anomaly,
    brine_anomaly_values,
    marine_indicator,
    seafloor_layer,
    dissolved_species,
    topmost_sunshine,
    attenuation_coefficient,
    peak_intake_speed,
    feedstock_midpoint_constant,
    photon_midpoint_constant,
    stoichiometry_matrix,
):
    blocks = lax.axis_size("comp")
    levels, tile_rows, tile_cols = zonal_flow_speed.shape
    tracer_count, level_count = dissolved_species.shape[:2]
    sub_rows = dissolved_species.shape[4]
    ocean = (zonal_flow_speed, meridional_flow_speed, thermal_anomaly, brine_anomaly_values)
    sea = (marine_indicator, seafloor_layer)
    flat = [x.reshape(levels * tile_rows, tile_cols) for x in ocean]
    q = dissolved_species.reshape(tracer_count, level_count, sub_rows, 1, tile_cols)
    parts = levels // SUB
    every = parts * blocks
    sizes = [every - 5 * every // 8, every // 4, every // 4, every // 8]
    cuts = [(sum(sizes[:i]), size) for i, size in enumerate(sizes)]
    scalars_of_uptake = (
        peak_intake_speed,
        feedstock_midpoint_constant,
        photon_midpoint_constant,
    )

    def rims(own):
        return own, (from_block_after(own[0]), from_block_before(own[1]))

    def sides(x):
        return (x, *from_sides(x))

    packed, edges, ocean_rows = pack_ocean(flat, sea, levels)
    ranges = [(first * SUB, size * SUB) for first, size in cuts]
    chunks = [rims(cut_rows(q, ranges[:1], [packed]))]
    later = cut_rows(q, ranges[1:], chunks[0][0][:1])
    up, down, packed = ocean_sides(packed, *from_sides(packed), edges)
    after, before = from_after(up, "gx"), from_before(down, "gx")
    smix, mixed, send, local, faces, depths = ocean_phase(
        blocks, levels, ocean_rows, sea, packed, after, before, later[:1]
    )
    received = lax.all_to_all(send, "comp", split_axis=0, concat_axis=0, tiled=True)
    east_new, north_new = velocities(local, faces, received)
    matrix = call_once(
        spread_kernel,
        [stoichiometry_matrix],
        [shaped(SUB * tracer_count, SUB * tracer_count)],
        after=[depths],
        cost=COVER,
    )[0]
    chunks.append(rims(held_until(later[:2], [matrix])))
    own = pack_tracers(*chunks[0], [matrix])

    surface = topmost_sunshine.reshape(sub_rows, tile_cols)
    carry, heat, result = None, None, None
    near = sides(own)
    for i, cut in enumerate(cuts):
        moved, light, heat, carry = advection(
            cut,
            level_count,
            attenuation_coefficient,
            surface,
            depths,
            received,
            *chunks[i],
            near,
            carry,
            heat,
            [] if i == 0 else [token],
        )
        if i > 0 and i + 1 < len(cuts):
            near = sides(pack_tracers(*chunks[i + 1], [carry]))
        result, token = uptake(
            cut,
            level_count * sub_rows,
            scalars_of_uptake,
            matrix,
            depths,
            moved,
            light,
            result,
        )
        if i + 2 < len(cuts):
            at = 2 * (i + 1)
            chunks.append(rims(held_until(later[at : at + 2], [token])))
        if i == 0:
            near = sides(pack_tracers(*chunks[1], [token]))
    heat = lax.all_to_all(heat, "comp", split_axis=0, concat_axis=0, tiled=True)
    warmed_result, buoyancy = warming(heat, mixed, sea)
    fields = (east_new, north_new, warmed_result, smix, buoyancy)
    return (
        *[x.reshape(zonal_flow_speed.shape) for x in fields],
        result.reshape(dissolved_species.shape),
    )


def solution(mesh):
    return jax.shard_map(
        on_device,
        mesh=mesh,
        in_specs=(
            P("comp", "gx", "gy"),
            P("comp", "gx", "gy"),
            P("comp", "gx", "gy"),
            P("comp", "gx", "gy"),
            P("gx", "gy"),
            P("gx", "gy"),
            P(None, None, "gx", "comp", None, "gy"),
            P("gx", "comp", None, "gy"),
            P(),
            P(),
            P(),
            P(),
            P(),
        ),
        out_specs=(
            P("comp", "gx", "gy"),
            P("comp", "gx", "gy"),
            P("comp", "gx", "gy"),
            P("comp", "gx", "gy"),
            P("comp", "gx", "gy"),
            P(None, None, "gx", "comp", None, "gy"),
        ),
        check_vma=False,
    )
```

```python
import functools

import jax
import jax.numpy as jnp
from jax import lax
from jax.experimental import pallas as pl
from jax.experimental.pallas import tpu as pltpu
from jax.sharding import PartitionSpec as P

NSUB = 2
SLOTS = 4 * NSUB
SUB = 8
GROUP = 24
HALF = 64
ENTRIES = 18

DT_FLOW = 0.1
CORIOLIS = 0.3
MIXING = 0.15
COURANT = 0.24
DT_BIO = 0.5
WARMING_FACTOR = 0.5
CLEAR_WATER = 0.5
VMEM_LIMIT = 10 * 1024 * 1024
COVER = pl.CostEstimate(flops=0, bytes_accessed=200_000_000, transcendentals=0)
VMEM_MOST = 62 * 1024 * 1024


def lanes_of(shape):
    return lax.broadcasted_iota(jnp.int32, shape, len(shape) - 1)


def subs_of(shape):
    return lax.broadcasted_iota(jnp.int32, shape, len(shape) - 2)


def turn(x, by, axis):
    by = by % x.shape[axis]
    return x if by == 0 else pltpu.roll(x, by, axis)


def params(limit=VMEM_LIMIT):
    return pltpu.CompilerParams(vmem_limit_bytes=limit)


def whole(shape):
    return pl.BlockSpec(shape, lambda *_: (0,) * len(shape))


def smem():
    return pl.BlockSpec(memory_space=pltpu.SMEM)


def shaped(*shape):
    return jax.ShapeDtypeStruct(shape, jnp.float32)


def halves(x):
    high = x.astype(jnp.bfloat16)
    return high, (x - high.astype(jnp.float32)).astype(jnp.bfloat16)


def sums_above(x):
    sub = subs_of(x.shape)
    running, total = x, x
    by = 1
    while by < x.shape[0]:
        running = running + jnp.where(sub >= by, turn(running, by, 0), 0.0)
        total = total + turn(total, by, 0)
        by *= 2
    return jnp.where(sub >= 1, turn(running, 1, 0), 0.0), total


def cut_kernel(cuts, q_ref, *refs):
    outs, sems = refs[-2 * len(cuts) - 1 : -1], refs[-1]
    rows = q_ref.shape[2]
    copies = [
        pltpu.make_async_copy(
            q_ref.at[:, pl.ds(start, size), r],
            outs[2 * i + r // NSUB].at[:, r % NSUB],
            sems.at[rows * i + r],
        )
        for i, (start, size) in enumerate(cuts)
        for r in range(rows)
    ]
    for copy in copies:
        copy.start()
    for copy in copies:
        copy.wait()


def cut_rows(q, cuts, after):
    tracers, _, rows, _, cols = q.shape
    anywhere = pl.BlockSpec(memory_space=pl.ANY)
    outs = [shaped(tracers, NSUB, size, 1, cols) for _, size in cuts for _ in range(2)]
    outs = pl.pallas_call(
        functools.partial(cut_kernel, cuts),
        in_specs=[anywhere] * (1 + len(after)),
        out_specs=[anywhere] * len(outs),
        out_shape=outs,
        scratch_shapes=[pltpu.SemaphoreType.DMA((rows * len(cuts),))],
        compiler_params=params(),
    )(q, *after)
    return [x.reshape(tracers, NSUB, x.shape[2], cols) for x in outs]


def hold_kernel(*refs):
    pass


def held_until(arrays, after):
    anywhere = pl.BlockSpec(memory_space=pl.ANY)
    return pl.pallas_call(
        hold_kernel,
        in_specs=[anywhere] * (len(arrays) + len(after)),
        out_specs=[anywhere] * len(arrays),
        out_shape=[shaped(*x.shape) for x in arrays],
        input_output_aliases={i: i for i in range(len(arrays))},
        compiler_params=params(),
    )(*arrays, *after)


def both_ends(acc):
    return jnp.where(lanes_of(acc.shape) % SLOTS < SLOTS // 2, acc, turn(acc, SLOTS // 2, 1))


def pack_tracers_kernel(low_ref, high_ref, after_ref, before_ref, packed_ref):
    tracers, _, levels, cols = low_ref.shape
    lane = lanes_of((SUB, cols))
    for pair in range(tracers // 2):
        for k in range(0, levels, SUB):
            near = slice(k, k + SUB)
            acc = jnp.zeros((SUB, cols), jnp.float32)
            for odd in range(2):
                t = 2 * pair + odd
                rows = [(before_ref, 1), (low_ref, 0), (low_ref, 1), (high_ref, 0), (high_ref, 1)]
                for r, (ref, n) in enumerate(rows + [(after_ref, 0)]):
                    at = HALF * odd + SLOTS * (r + 1)
                    x = turn(ref[t, n, near], at + NSUB, 1)
                    acc = jnp.where(lane // SLOTS == at // SLOTS, x, acc)
            packed_ref[pair, near] = both_ends(acc)


def pack_tracers(own, rim, after):
    tracers, _, levels, cols = own[0].shape
    group = 4 if tracers % 4 == 0 else 2
    rows = pl.BlockSpec((group, NSUB, levels, cols), lambda i: (i, 0, 0, 0))
    return pl.pallas_call(
        functools.partial(ignoring, len(after), pack_tracers_kernel),
        grid=(tracers // group,),
        in_specs=[pl.BlockSpec(memory_space=pl.ANY)] * len(after) + [rows] * 4,
        out_specs=pl.BlockSpec((group // 2, levels, cols), lambda i: (i, 0, 0)),
        out_shape=shaped(tracers // 2, levels, cols),
        compiler_params=params(),
    )(*after, *own, *rim)


def ignoring(count, kernel, *refs):
    kernel(*refs[count:])


def call_once(kernel, operands, outs, scratch=(), scalars=(), after=(), limit=VMEM_LIMIT, cost=None):
    return pl.pallas_call(
        functools.partial(ignoring, len(after), kernel),
        grid=(1,),
        in_specs=[pl.BlockSpec(memory_space=pl.ANY)] * len(after)
        + [smem()] * len(scalars)
        + [whole(x.shape) for x in operands],
        out_specs=[whole(x.shape) for x in outs],
        out_shape=outs,
        scratch_shapes=list(scratch),
        compiler_params=params(limit),
        cost_estimate=cost,
    )(*after, *scalars, *operands)


def pack_ocean_kernel(levels, *refs):
    u_ref, v_ref, t_ref, s_ref, sea_ref, floor_ref, packed_ref, edges_ref, row_ref = refs
    edge_low_ref, edge_high_ref = edges_ref.at[0], edges_ref.at[1]
    tile_rows, cols = sea_ref.shape
    lane = lanes_of((levels, cols))
    edge_low_ref[4 * NSUB] = jnp.zeros((levels, cols), jnp.float32)
    edge_high_ref[4 * NSUB] = jnp.zeros((levels, cols), jnp.float32)
    for f, ref in enumerate((u_ref, v_ref, t_ref, s_ref)):
        acc = jnp.zeros((levels, cols), jnp.float32)
        for r in range(tile_rows):
            x = ref[pl.ds(r, levels, stride=tile_rows), :]
            row_ref[f, r] = x
            acc = jnp.where(lane // SLOTS == r, turn(x, SLOTS * r + NSUB, 1), acc)
            if r < NSUB:
                edge_low_ref[NSUB * f + r] = x
            if r >= tile_rows - NSUB:
                edge_high_ref[NSUB * f + r - tile_rows + NSUB] = x
        packed_ref[f] = both_ends(acc)
    depth = jnp.where(sea_ref[...] == 1, floor_ref[...], 0).astype(jnp.float32)
    acc = jnp.zeros((levels, cols), jnp.float32)
    for r in range(tile_rows):
        x = jnp.broadcast_to(depth[r : r + 1], (levels, cols))
        acc = jnp.where(lane // SLOTS == r, turn(x, SLOTS * r + NSUB, 1), acc)
    packed_ref[4] = both_ends(acc)
    edge_low_ref[4 * NSUB, 0:NSUB, :] = depth[0:NSUB]
    edge_high_ref[4 * NSUB, 0:NSUB, :] = depth[tile_rows - NSUB :]


def pack_ocean(flat, sea, levels):
    cols = sea[0].shape[1]
    edges = shaped(2, 4 * NSUB + 1, levels, cols)
    return call_once(
        functools.partial(pack_ocean_kernel, levels),
        [*flat, *sea],
        [shaped(5, levels, cols), edges, shaped(4, sea[0].shape[0], levels, cols)],
        limit=VMEM_MOST,
    )


def with_sides(own, left, right):
    slot = lanes_of(own.shape) % SLOTS
    ends = jnp.where(slot < NSUB, left, right)
    return jnp.where((slot < NSUB) | (slot >= SLOTS - NSUB), ends, own)


def ocean_sides_kernel(own_ref, left_ref, right_ref, edges_ref, up_ref, down_ref, out_ref):
    _, levels, cols = own_ref.shape
    rows = edges_ref.shape[1]
    up_ref[0:rows] = edges_ref[0]
    down_ref[0:rows] = edges_ref[1]
    slot = lanes_of((levels, cols)) % SLOTS
    place = lax.axis_index("gy")
    first, last = place == 0, place == lax.axis_size("gy") - 1
    for f in range(5):
        x = with_sides(own_ref[f], left_ref[f], right_ref[f])
        if f == 4:
            x = jnp.where((slot < NSUB) & first, 0.0, x)
            x = jnp.where((slot >= SLOTS - NSUB) & last, 0.0, x)
        out_ref[f] = x
        up_ref[rows + f] = x
        down_ref[rows + f] = x


def ocean_sides(own, left, right, edges):
    edge = shaped(edges.shape[1] + 5, *edges.shape[2:])
    return call_once(
        ocean_sides_kernel,
        [own, left, right, edges],
        [edge, edge, shaped(*own.shape)],
    )


def ocean_kernel(blocks, levels, *refs):
    own_ref, sea_ref, floor_ref, packed_ref, after_ref, before_ref = refs[:6]
    smix_ref, mixed_ref, send_ref, local_ref, faces_ref, depths_ref, press_ref, total_ref = refs[6:]
    tile_rows, cols = sea_ref.shape
    sub_rows = tile_rows // blocks
    shape = (levels, cols)
    lane = lanes_of(shape)
    first, last = lane == 0, lane == cols - 1
    base = lax.axis_index("comp") * levels
    level = (base + subs_of(shape)).astype(jnp.float32)
    rims = after_ref.shape[0] - 5

    def packed(f):
        after, before = after_ref[rims + f], before_ref[rims + f]
        rim = jnp.where(lane < NSUB * SLOTS, after, jnp.where(lane >= cols - NSUB * SLOTS, before, 0.0))
        return jnp.concatenate([packed_ref[f], rim], axis=1)

    def row_after(x):
        return turn(x, -SLOTS, 1)

    def row_before(x):
        return turn(x, SLOTS, 1)

    up, vp, tp, sp, dp = [packed(f) for f in range(5)]
    wide = jnp.concatenate([level, level], axis=1)
    wet = (wide < dp).astype(jnp.float32)
    heavy = wet * (-0.2 * tp + 0.8 * sp)
    above, total = sums_above(heavy)
    press = above + 0.5 * heavy
    east = up + DT_FLOW * (CORIOLIS * vp - (row_after(press) - press))
    north = vp + DT_FLOW * (-CORIOLIS * up - (turn(press, -1, 1) - press))
    open_n = wet * turn(wet, -1, 1)
    flux_t = open_n * (turn(tp, -1, 1) - tp)
    flux_s = open_n * (turn(sp, -1, 1) - sp)
    total_e, total_n = row_after(total) - total, turn(total, -1, 1) - total
    depth_e, depth_n = jnp.minimum(dp, row_after(dp)), jnp.minimum(dp, turn(dp, -1, 1))

    def window(x, g):
        x = turn(x, -SLOTS * (sub_rows * g - NSUB), 1)[:, 0:cols]
        return jnp.where(lane < HALF, x, turn(x, HALF, 1))

    for g in range(blocks):
        send_ref[g, 13] = window(east, g)
        send_ref[g, 14] = window(north, g)
        send_ref[g, 15, 13:14, :] = window(total_e, g)[0:1]
        send_ref[g, 15, 14:15, :] = window(total_n, g)[0:1]
        send_ref[g, 15, 15:16, :] = jnp.zeros((1, cols), jnp.float32)
        depths_ref[g, 24:25, :] = window(depth_e, g)[0:1]
        depths_ref[g, 25:26, :] = window(depth_n, g)[0:1]
        depths_ref[g, 26:27, :] = window(dp, g)[0:1]

    slot = lanes_of(tp.shape) % SLOTS

    def edges(x, other):
        x = jnp.where(slot == 0, turn(x, -6, 1), other)
        return x[:, 0:cols], x[:, cols:]

    edge_p, edge_w = edges(press, press), edges(wet, wet)
    edge_t, edge_s = edges(tp, flux_t), edges(sp, flux_s)
    edge_total, edge_depth = edges(total, total), edges(dp, dp)

    def edge(pair, r):
        at = r % tile_rows
        return turn(pair[0] if 0 <= r < tile_rows else pair[1], -(SLOTS * at + 1), 1)

    depth = jnp.where(sea_ref[...] == 1, floor_ref[...], 0).astype(jnp.float32)

    def row_of(f, r):
        if r < 0:
            return before_ref[NSUB * f + r + NSUB]
        if r >= tile_rows:
            return after_ref[NSUB * f + r - tile_rows]
        return own_ref[f, r]

    def depth_of(r):
        if r < 0:
            x = before_ref[4 * NSUB, r + NSUB : r + NSUB + 1, :]
        elif r >= tile_rows:
            x = after_ref[4 * NSUB, r - tile_rows : r - tile_rows + 1, :]
        else:
            x = depth[r : r + 1]
        return jnp.broadcast_to(x, shape)

    lo, hi = -NSUB, tile_rows + NSUB
    for r in range(lo, hi):
        heavy = (level < depth_of(r)).astype(jnp.float32) * (-0.2 * row_of(2, r) + 0.8 * row_of(3, r))
        above, total = sums_above(heavy)
        press_ref[r - lo] = above + 0.5 * heavy
        total_ref[r - lo] = total

    def windows(r, before):
        for g in range(blocks):
            j = r - (sub_rows * g - before)
            if 0 <= j < sub_rows + 1 + before:
                yield g, j

    flux_before = [None, None]
    for r in range(lo, hi - 1):
        press, press_e = press_ref[r - lo], press_ref[r - lo + 1]
        total, total_a = total_ref[r - lo], total_ref[r - lo + 1]
        d, d_e = depth_of(r), depth_of(r + 1)
        d_n = jnp.where(last, edge(edge_depth, r), turn(d, -1, 1))
        face_e, face_n = jnp.minimum(d, d_e), jnp.minimum(d, d_n)
        u, v = row_of(0, r), row_of(1, r)
        east = u + DT_FLOW * (CORIOLIS * v - (press_e - press))
        press_n = jnp.where(last, edge(edge_p, r), turn(press, -1, 1))
        north = v + DT_FLOW * (-CORIOLIS * u - (press_n - press))
        total_e = total_a - total
        total_n = jnp.where(last, edge(edge_total, r), turn(total, -1, 1)) - total
        for g, j in windows(r, 2):
            send_ref[g, j] = east
            send_ref[g, 15, j : j + 1, :] = total_e[0:1]
            depths_ref[g, j : j + 1, :] = face_e[0:1]
        for g, j in windows(r, 1):
            send_ref[g, 7 + j] = north
            send_ref[g, 15, 7 + j : 8 + j, :] = total_n[0:1]
            depths_ref[g, 8 + j : 9 + j, :] = face_n[0:1]
            depths_ref[g, 16 + j : 17 + j, :] = d[0:1]
        if 0 <= r < tile_rows:
            local_ref[0, r] = east
            local_ref[1, r] = north
            faces_ref[0, r : r + 1, :] = face_e[0:1]
            faces_ref[1, r : r + 1, :] = face_n[0:1]
            for g in range(blocks):
                send_ref[g, 16, r : r + 1, :] = total_e[0:1]
                send_ref[g, 17, r : r + 1, :] = total_n[0:1]
        if r < -1 or r >= tile_rows:
            continue
        open_e = (level < face_e).astype(jnp.float32)
        open_n = (level < face_n).astype(jnp.float32)
        for i, (f, ends) in enumerate(((2, edge_t), (3, edge_s))):
            x = row_of(f, r)
            flux_e = open_e * (row_of(f, r + 1) - x)
            if r >= 0:
                ending = edge(ends, r)
                flux_n = open_n * (jnp.where(last, ending, turn(x, -1, 1)) - x)
                flux_b = jnp.where(first, ending, turn(flux_n, 1, 1))
                mixed = x + MIXING * ((flux_e - flux_before[i]) + (flux_n - flux_b))
                mixed_ref[i, r] = mixed
                if i == 1:
                    smix_ref[pl.ds(r, levels, stride=tile_rows), :] = mixed
            flux_before[i] = flux_e


def ocean_phase(blocks, levels, own, sea, packed, rim_after, rim_before, after):
    tile_rows, cols = sea[0].shape
    outs = [
        shaped(levels * tile_rows, cols),
        shaped(2, tile_rows, levels, cols),
        shaped(blocks, ENTRIES, levels, cols),
        shaped(2, tile_rows, levels, cols),
        shaped(2, tile_rows, cols),
        shaped(blocks, 32, cols),
    ]
    tall = tile_rows + 2 * NSUB
    return call_once(
        functools.partial(ocean_kernel, blocks, levels),
        [own, *sea, packed, rim_after, rim_before],
        outs,
        [pltpu.VMEM((tall, levels, cols), jnp.float32)] * 2,
        after=after,
    )


def velocity_kernel(local_ref, faces_ref, received_ref, east_ref, north_ref, token_ref):
    blocks = received_ref.shape[0]
    _, tile_rows, levels, cols = local_ref.shape
    token_ref[...] = jnp.zeros_like(token_ref)
    group = lax.axis_index("comp")
    level = (group * levels + subs_of((levels, cols))).astype(jnp.float32)
    for f, out_ref in enumerate((east_ref, north_ref)):
        above = jnp.zeros((tile_rows, cols), jnp.float32)
        for s in range(blocks - 1):
            above = above + jnp.where(s < group, received_ref[s, f], 0.0)
        for r in range(tile_rows):
            x = local_ref[f, r] - DT_FLOW * jnp.broadcast_to(above[r : r + 1], (levels, cols))
            x = jnp.where(level < faces_ref[f, r : r + 1, :], x, 0.0)
            out_ref[pl.ds(r, levels, stride=tile_rows), :] = x


def velocities(local, faces, received):
    blocks = received.shape[0]
    _, tile_rows, levels, cols = local.shape
    out = shaped(levels * tile_rows, cols)
    return pl.pallas_call(
        velocity_kernel,
        grid=(1,),
        in_specs=[
            whole(local.shape),
            whole(faces.shape),
            pl.BlockSpec((blocks, 2, levels, cols), lambda i: (0, ENTRIES // 2 - 1, 0, 0)),
        ],
        out_specs=[whole(out.shape)] * 2 + [whole((SUB, cols))],
        out_shape=[out] * 2 + [shaped(SUB, cols)],
        compiler_params=params(),
    )(local, faces, received)


def advection_kernel(first_part, parts, level_count, *refs):
    (
        absorb_ref,
        surface_ref,
        depth_ref,
        totals_ref,
        courant_ref,
        low_ref,
        high_ref,
        after_ref,
        before_ref,
        side_ref,
        left_ref,
        right_ref,
    ) = refs[:12]
    moved_ref, light_ref, heat_ref, carry_out_ref = refs[-10:-6]
    coef_ref, side_coef_ref, edge_ref, running_ref, above_ref, shift_ref = refs[-6:]
    depth_ref = depth_ref.at[lax.axis_index("comp")]
    step = pl.program_id(0)
    tracers, _, _, cols = low_ref.shape
    levels = courant_ref.shape[2]
    sub_rows = surface_ref.shape[0]
    rows = sub_rows + 2
    shape = (levels, cols)
    lane = lanes_of(shape)
    first, last = lane == 0, lane == cols - 1
    first8, last8 = first[0:SUB], last[0:SUB]
    slot = lane % SLOTS

    @pl.when(step == 0)
    def _():
        running_ref[...] = refs[12][...] if first_part else jnp.zeros_like(running_ref)
        size = (2 * cols, 2 * cols)
        source, to = subs_of(size) % cols, lanes_of(size)
        hit = ((to < cols) & (source == to + 1)) | ((to >= cols) & (source == to - cols - 1))
        shift_ref[...] = hit.astype(jnp.float32).astype(jnp.bfloat16)

    part = first_part + step
    above = jnp.zeros(above_ref.shape, jnp.float32)
    for s in range(totals_ref.shape[0] - 1):
        above = above + jnp.where(s < part // parts, totals_ref[s, 0], 0.0)
    above_ref[...] = above
    level = (part * levels + subs_of(shape)).astype(jnp.float32)

    def spread(ref, r):
        return jnp.broadcast_to(ref[r : r + 1, :], shape)

    def courant(entry, face):
        x = courant_ref[0, entry] - DT_FLOW * spread(above_ref, entry)
        return COURANT * jnp.tanh(jnp.where(level < spread(depth_ref, face), x, 0.0))

    def coefficients(wet, ce, ce_b, cn, cn_b):
        return (
            wet
            * (
                1.0
                - jnp.maximum(ce, 0.0)
                + jnp.minimum(ce_b, 0.0)
                - jnp.maximum(cn, 0.0)
                + jnp.minimum(cn_b, 0.0)
            ),
            -wet * jnp.minimum(ce, 0.0),
            wet * jnp.maximum(ce_b, 0.0),
            -wet * jnp.minimum(cn, 0.0),
            wet * jnp.maximum(cn_b, 0.0),
        )

    side_e, side_n = courant(13, 24), courant(14, 25)
    wet = (level < spread(depth_ref, 26)).astype(jnp.float32)
    packed_coef = coefficients(wet, side_e, turn(side_e, SLOTS, 1), side_n, turn(side_n, 1, 1))
    for i in range(5):
        side_coef_ref[i] = packed_coef[i]
    ce_b = courant(0, 0)
    for j in range(rows):
        ce, cn = courant(1 + j, 1 + j), courant(7 + j, 8 + j)
        cn_b = jnp.where(first, turn(side_n, -(SLOTS * (j + 1) + 1), 1), turn(cn, 1, 1))
        wet = (level < spread(depth_ref, 16 + j)).astype(jnp.float32)
        for i, x in enumerate(coefficients(wet, ce, ce_b, cn, cn_b)):
            coef_ref[5 * j + i] = x
        ce_b = ce
    for i in range(side_ref.shape[0]):
        x = with_sides(side_ref[i], left_ref[i], right_ref[i])
        edge_ref[i, 0] = jnp.where(slot == 0, turn(x, -6, 1), x)
        x = (
            (side_coef_ref[0] * x + side_coef_ref[1] * turn(x, -SLOTS, 1))
            + (side_coef_ref[2] * turn(x, SLOTS, 1) + side_coef_ref[3] * turn(x, -1, 1))
            + side_coef_ref[4] * turn(x, 1, 1)
        )
        edge_ref[i, 1] = jnp.where(slot == 0, turn(x, -6, 1), x)

    layer = 2.0 / level_count
    zero = jnp.zeros((SUB, cols), jnp.float32)
    for k in range(0, levels, SUB):
        at = slice(k, k + SUB)

        def shifted(tiles):
            high, low = halves(jnp.concatenate(tiles, axis=0))
            return jnp.dot(
                jnp.concatenate([high, low], axis=1),
                shift_ref[...],
                preferred_element_type=jnp.float32,
            )

        def stencil(x, coef, edge, beside):
            north = jnp.where(last8, edge, beside[:, :cols])
            south = jnp.where(first8, edge, beside[:, cols:])
            return (
                (coef[0] * x[1] + coef[1] * x[2])
                + (coef[2] * x[0] + coef[3] * north)
                + coef[4] * south
            )

        def advect(i, sums):
            sums = list(sums)
            fields = []
            for t in range(GROUP):
                t = GROUP * i + t
                rows_of = (before_ref, low_ref, high_ref, after_ref)
                x = [ref[t, n, at] for ref in rows_of for n in range(NSUB)]
                fields.append(x)
            for stage in range(NSUB):
                inner = range(1 + stage, rows + 1 - stage)
                beside = shifted([x[j - stage] for j in inner for x in fields])
                fresh = [[] for _ in fields]
                for n, j in enumerate(inner):
                    coef = [coef_ref[5 * (j - 1) + c, at] for c in range(5)]
                    for t, x in enumerate(fields):
                        edges = edge_ref[GROUP // 2 * i + t // 2, stage, at]
                        edge = turn(edges, -(HALF * (t % 2) + SLOTS * j + 1), 1)
                        row = SUB * (len(fields) * n + t)
                        fresh[t].append(
                            stencil(x[n : n + 3], coef, edge, beside[row : row + SUB])
                        )
                fields = fresh
            for t, x in enumerate(fields):
                for r in range(sub_rows):
                    moved_ref[GROUP * i + t, r, at] = x[r]
                    sums[r] = sums[r] + absorb_ref[GROUP * i + t] * x[r]
            return tuple(sums)

        sums = (zero,) * sub_rows
        for i in range(tracers // GROUP):
            sums = advect(i, sums)
        for r in range(sub_rows):
            optical = layer * (CLEAR_WATER + sums[r])
            above, total = sums_above(optical)
            through = jnp.exp(-(running_ref[r] + above))
            running_ref[r] = running_ref[r] + total
            surface = jnp.broadcast_to(surface_ref[r : r + 1, :], (SUB, cols))
            light_ref[r, at] = surface * through * jnp.exp(-0.5 * optical)
            wet = (level[at] < jnp.broadcast_to(depth_ref[17 + r : 18 + r, :], (SUB, cols))).astype(
                jnp.float32
            )
            heat_ref[0, r, at] = wet * surface * through * (1.0 - jnp.exp(-optical)) / layer
    carry_out_ref[...] = running_ref[...]


def advection(cut, level_count, absorb, surface, depth, received, own, rim, sides, carry, heat, after):
    first_part, count = cut
    tracers, _, _, cols = own[0].shape
    every, _, levels, _ = received.shape
    parts = levels // SUB
    sub_rows = surface.shape[0]
    rows = pl.BlockSpec((tracers, NSUB, SUB, cols), lambda i: (0, 0, i, 0))
    side = pl.BlockSpec((tracers // 2, SUB, cols), lambda i: (0, i, 0))
    operands = [absorb, surface, depth, received, received, *own, *rim, *sides]
    in_specs = [
        smem(),
        whole(surface.shape),
        whole(depth.shape),
        pl.BlockSpec((every, 1, levels, cols), lambda i: (0, 15, 0, 0)),
        pl.BlockSpec(
            (1, ENTRIES, SUB, cols),
            lambda i: ((first_part + i) // parts, 0, (first_part + i) % parts, 0),
        ),
        rows,
        rows,
        rows,
        rows,
        side,
        side,
        side,
    ]
    aliases = {}
    carry_shape = (sub_rows, SUB, cols)
    if carry is not None:
        operands.append(carry)
        in_specs.append(whole(carry_shape))
        aliases = {len(operands): 2}
        operands.append(heat)
    operands += after
    in_specs += [pl.BlockSpec(memory_space=pl.ANY)] * (len(operands) - len(in_specs))
    outs = [
        shaped(tracers, sub_rows, count * SUB, cols),
        shaped(sub_rows, count * SUB, cols),
        shaped(every, sub_rows, levels, cols),
        shaped(*carry_shape),
    ]
    return pl.pallas_call(
        functools.partial(advection_kernel, first_part, parts, level_count),
        grid=(count,),
        in_specs=in_specs,
        out_specs=[
            pl.BlockSpec((tracers, sub_rows, SUB, cols), lambda i: (0, 0, i, 0)),
            pl.BlockSpec((sub_rows, SUB, cols), lambda i: (0, i, 0)),
            pl.BlockSpec(
                (1, sub_rows, SUB, cols),
                lambda i: ((first_part + i) // parts, 0, (first_part + i) % parts, 0),
            ),
            whole(carry_shape),
        ],
        out_shape=outs,
        scratch_shapes=[
            pltpu.VMEM((5 * (sub_rows + 2), SUB, cols), jnp.float32),
            pltpu.VMEM((5, SUB, cols), jnp.float32),
            pltpu.VMEM((tracers // 2, 2, SUB, cols), jnp.float32),
            pltpu.VMEM((sub_rows, SUB, cols), jnp.float32),
            pltpu.VMEM((levels, cols), jnp.float32),
            pltpu.VMEM((2 * cols, 2 * cols), jnp.bfloat16),
        ],
        input_output_aliases=aliases,
        compiler_params=params(),
    )(*operands)


def spread_kernel(matrix_ref, out_ref):
    tracers = matrix_ref.shape[0]
    size = tracers * SUB
    tall = (subs_of((size, tracers)) // SUB == lanes_of((size, tracers))).astype(jnp.float32)
    wide = (lanes_of((tracers, size)) // SUB == subs_of((tracers, size))).astype(jnp.float32)
    exact = functools.partial(
        jnp.dot, precision=lax.Precision.HIGHEST, preferred_element_type=jnp.float32
    )
    same = subs_of((size, size)) % SUB == lanes_of((size, size)) % SUB
    out_ref[...] = jnp.where(same, exact(exact(tall, matrix_ref[...]), wide), 0.0)


def uptake_kernel(first_level, *refs):
    growth_ref, half_ref, dim_ref, matrix_ref, depth_ref, moved_ref, light_ref = refs[:7]
    depth_ref = depth_ref.at[lax.axis_index("comp")]
    result_ref, token_ref, uptake_ref = refs[-3:]
    token_ref[...] = jnp.zeros_like(token_ref)
    tracers, sub_rows, levels, cols = moved_ref.shape
    step = pl.program_id(0)
    matrix_high, matrix_low = halves(matrix_ref[...])
    for k in range(0, levels, SUB):
        at = slice(k, k + SUB)
        level = (first_level + step * levels + k + subs_of((SUB, cols))).astype(jnp.float32)
        light = [light_ref[r, at] for r in range(sub_rows)]
        food = [moved_ref[0, r, at] for r in range(sub_rows)]
        both = [light[r] * food[r] for r in range(sub_rows)]

        def uptake(t, _):
            for r in range(sub_rows):
                scale = (half_ref[t] + food[r]) * (light[r] + dim_ref[t])
                value = growth_ref[t] * moved_ref[t, r, at] * (both[r] / scale)
                uptake_ref[pl.ds(t * SUB, SUB), r * cols : (r + 1) * cols] = value
            return _

        lax.fori_loop(0, tracers, uptake, 0, unroll=4)
        amount = uptake_ref[...]
        high, low = halves(amount)
        dot = functools.partial(jnp.dot, preferred_element_type=jnp.float32)
        change = dot(matrix_high, high) + (dot(matrix_high, low) + dot(matrix_low, high))
        for r in range(sub_rows):
            depth = jnp.broadcast_to(depth_ref[17 + r : 18 + r, :], (SUB, cols))
            scale = DT_BIO * (level < depth).astype(jnp.float32)
            for t in range(tracers):
                result_ref[t, pl.ds(sub_rows * k + r, SUB, stride=sub_rows), :] = (
                    moved_ref[t, r, at]
                    + scale * change[SUB * t : SUB * (t + 1), r * cols : (r + 1) * cols]
                )


def uptake(cut, all_rows, scalars, matrix, depth, moved, light, result):
    first_part, count = cut
    tracers, sub_rows, _, cols = moved.shape
    operands = [*scalars, matrix, depth, moved, light]
    in_specs = [smem()] * 3 + [
        whole(matrix.shape),
        whole(depth.shape),
        pl.BlockSpec((tracers, sub_rows, SUB, cols), lambda i: (0, 0, i, 0)),
        pl.BlockSpec((sub_rows, SUB, cols), lambda i: (0, i, 0)),
    ]
    aliases = {}
    if result is not None:
        aliases = {len(operands): 0}
        operands.append(result)
        in_specs.append(pl.BlockSpec(memory_space=pl.ANY))
    return pl.pallas_call(
        functools.partial(uptake_kernel, first_part * SUB),
        grid=(count,),
        in_specs=in_specs,
        out_specs=[
            pl.BlockSpec((tracers, SUB * sub_rows, cols), lambda i: (0, first_part + i, 0)),
            whole((SUB, cols)),
        ],
        out_shape=[shaped(tracers, all_rows, cols), shaped(SUB, cols)],
        scratch_shapes=[pltpu.VMEM((tracers * SUB, sub_rows * cols), jnp.float32)],
        input_output_aliases=aliases,
        compiler_params=params(),
    )(*operands)


def warming_kernel(sea_ref, floor_ref, heat_ref, mixed_ref, warm_ref, buoyant_ref):
    blocks, sub_rows, levels, cols = heat_ref.shape
    tile_rows = blocks * sub_rows
    base = lax.axis_index("comp") * levels
    level = (base + subs_of((levels, cols))).astype(jnp.float32)
    depth = jnp.where(sea_ref[...] == 1, floor_ref[...], 0).astype(jnp.float32)
    for r in range(tile_rows):
        at = pl.ds(r, levels, stride=tile_rows)
        warm = mixed_ref[0, r] + WARMING_FACTOR * heat_ref[r // sub_rows, r % sub_rows]
        wet = (level < depth[r : r + 1]).astype(jnp.float32)
        warm_ref[at, :] = warm
        buoyant_ref[at, :] = wet * (0.2 * warm - 0.8 * mixed_ref[1, r])


def warming(heat, mixed, sea):
    _, tile_rows, levels, cols = mixed.shape
    outs = [shaped(levels * tile_rows, cols)] * 2
    return call_once(warming_kernel, [*sea, heat, mixed], outs)


def from_before(x, axis):
    return lax.ppermute(x, axis, [(i, i + 1) for i in range(lax.axis_size(axis) - 1)])


def from_after(x, axis):
    return lax.ppermute(x, axis, [(i + 1, i) for i in range(lax.axis_size(axis) - 1)])


def row_pairs():
    blocks, tiles = lax.axis_size("comp"), lax.axis_size("gx")
    places = [b * tiles + tile for tile in range(tiles) for b in range(blocks)]
    return list(zip(places[:-1], places[1:]))


def from_block_before(x):
    return lax.ppermute(x, ("comp", "gx"), row_pairs())


def from_block_after(x):
    return lax.ppermute(x, ("comp", "gx"), [(later, own) for own, later in row_pairs()])


def from_sides(x):
    if lax.axis_size("gy") == 2:
        other = lax.ppermute(x, "gy", [(0, 1), (1, 0)])
        return other, other
    return from_before(x, "gy"), from_after(x, "gy")


def on_device(
    zonal_flow_speed,
    meridional_flow_speed,
    thermal_anomaly,
    brine_anomaly_values,
    marine_indicator,
    seafloor_layer,
    dissolved_species,
    topmost_sunshine,
    attenuation_coefficient,
    peak_intake_speed,
    feedstock_midpoint_constant,
    photon_midpoint_constant,
    stoichiometry_matrix,
):
    blocks = lax.axis_size("comp")
    levels, tile_rows, tile_cols = zonal_flow_speed.shape
    tracer_count, level_count = dissolved_species.shape[:2]
    sub_rows = dissolved_species.shape[4]
    ocean = (zonal_flow_speed, meridional_flow_speed, thermal_anomaly, brine_anomaly_values)
    sea = (marine_indicator, seafloor_layer)
    flat = [x.reshape(levels * tile_rows, tile_cols) for x in ocean]
    q = dissolved_species.reshape(tracer_count, level_count, sub_rows, 1, tile_cols)
    parts = levels // SUB
    every = parts * blocks
    sizes = [every - 5 * every // 8, 3 * every // 8, every // 4]
    cuts = [(sum(sizes[:i]), size) for i, size in enumerate(sizes)]
    scalars_of_uptake = (
        peak_intake_speed,
        feedstock_midpoint_constant,
        photon_midpoint_constant,
    )

    def rims(own):
        return own, (from_block_after(own[0]), from_block_before(own[1]))

    def sides(x):
        return (x, *from_sides(x))

    packed, edges, ocean_rows = pack_ocean(flat, sea, levels)
    ranges = [(first * SUB, size * SUB) for first, size in cuts]
    chunks = [rims(cut_rows(q, ranges[:1], [packed]))]
    later = cut_rows(q, ranges[1:], chunks[0][0][:1])
    up, down, packed = ocean_sides(packed, *from_sides(packed), edges)
    after, before = from_after(up, "gx"), from_before(down, "gx")
    smix, mixed, send, local, faces, depths = ocean_phase(
        blocks, levels, ocean_rows, sea, packed, after, before, later[:1]
    )
    received = lax.all_to_all(send, "comp", split_axis=0, concat_axis=0, tiled=True)
    east_new, north_new, finished = velocities(local, faces, received)
    matrix = call_once(
        spread_kernel,
        [stoichiometry_matrix],
        [shaped(SUB * tracer_count, SUB * tracer_count)],
        after=[depths],
        cost=COVER,
    )[0]
    chunks.append(rims(held_until(later[:2], [matrix])))
    own = pack_tracers(*chunks[0], [matrix])

    surface = topmost_sunshine.reshape(sub_rows, tile_cols)
    carry, heat, result = None, None, None
    near = sides(own)
    for i, cut in enumerate(cuts):
        moved, light, heat, carry = advection(
            cut,
            level_count,
            attenuation_coefficient,
            surface,
            depths,
            received,
            *chunks[i],
            near,
            carry,
            heat,
            [] if i == 0 else [token],
        )
        if i > 0 and i + 1 < len(cuts):
            near = sides(pack_tracers(*chunks[i + 1], [carry]))
        result, token = uptake(
            cut,
            level_count * sub_rows,
            scalars_of_uptake,
            matrix,
            depths,
            moved,
            light,
            result,
        )
        if i + 2 < len(cuts):
            at = 2 * (i + 1)
            chunks.append(rims(held_until(later[at : at + 2], [token])))
        if i == 0:
            near = sides(pack_tracers(*chunks[1], [token, finished]))
    heat = lax.all_to_all(heat, "comp", split_axis=0, concat_axis=0, tiled=True)
    warmed_result, buoyancy = warming(heat, mixed, sea)
    fields = (east_new, north_new, warmed_result, smix, buoyancy)
    return (
        *[x.reshape(zonal_flow_speed.shape) for x in fields],
        result.reshape(dissolved_species.shape),
    )


def solution(mesh):
    return jax.shard_map(
        on_device,
        mesh=mesh,
        in_specs=(
            P("comp", "gx", "gy"),
            P("comp", "gx", "gy"),
            P("comp", "gx", "gy"),
            P("comp", "gx", "gy"),
            P("gx", "gy"),
            P("gx", "gy"),
            P(None, None, "gx", "comp", None, "gy"),
            P("gx", "comp", None, "gy"),
            P(),
            P(),
            P(),
            P(),
            P(),
        ),
        out_specs=(
            P("comp", "gx", "gy"),
            P("comp", "gx", "gy"),
            P("comp", "gx", "gy"),
            P("comp", "gx", "gy"),
            P("comp", "gx", "gy"),
            P(None, None, "gx", "comp", None, "gy"),
        ),
        check_vma=False,
    )
```

```python
import functools

import jax
import jax.numpy as jnp
from jax import lax
from jax.experimental import pallas as pl
from jax.experimental.pallas import tpu as pltpu
from jax.sharding import PartitionSpec as P

NSUB = 2
SLOTS = 4 * NSUB
SUB = 8
GROUP = 24
HALF = 64
ENTRIES = 18

DT_FLOW = 0.1
CORIOLIS = 0.3
MIXING = 0.15
COURANT = 0.24
DT_BIO = 0.5
WARMING_FACTOR = 0.5
CLEAR_WATER = 0.5
VMEM_LIMIT = 10 * 1024 * 1024
COVER = pl.CostEstimate(flops=0, bytes_accessed=200_000_000, transcendentals=0)
VMEM_MOST = 62 * 1024 * 1024


def lanes_of(shape):
    return lax.broadcasted_iota(jnp.int32, shape, len(shape) - 1)


def subs_of(shape):
    return lax.broadcasted_iota(jnp.int32, shape, len(shape) - 2)


def turn(x, by, axis):
    by = by % x.shape[axis]
    return x if by == 0 else pltpu.roll(x, by, axis)


def params(limit=VMEM_LIMIT):
    return pltpu.CompilerParams(vmem_limit_bytes=limit)


def whole(shape):
    return pl.BlockSpec(shape, lambda *_: (0,) * len(shape))


def smem():
    return pl.BlockSpec(memory_space=pltpu.SMEM)


def shaped(*shape):
    return jax.ShapeDtypeStruct(shape, jnp.float32)


def halves(x):
    high = x.astype(jnp.bfloat16)
    return high, (x - high.astype(jnp.float32)).astype(jnp.bfloat16)


def sums_above(x):
    sub = subs_of(x.shape)
    running, total = x, x
    by = 1
    while by < x.shape[0]:
        running = running + jnp.where(sub >= by, turn(running, by, 0), 0.0)
        total = total + turn(total, by, 0)
        by *= 2
    return jnp.where(sub >= 1, turn(running, 1, 0), 0.0), total


def cut_kernel(cuts, q_ref, *refs):
    outs, sems = refs[-2 * len(cuts) - 1 : -1], refs[-1]
    rows = q_ref.shape[2]
    copies = [
        pltpu.make_async_copy(
            q_ref.at[:, pl.ds(start, size), r],
            outs[2 * i + r // NSUB].at[:, r % NSUB],
            sems.at[rows * i + r],
        )
        for i, (start, size) in enumerate(cuts)
        for r in range(rows)
    ]
    for copy in copies:
        copy.start()
    for copy in copies:
        copy.wait()


def cut_rows(q, cuts, after):
    tracers, _, rows, _, cols = q.shape
    anywhere = pl.BlockSpec(memory_space=pl.ANY)
    outs = [shaped(tracers, NSUB, size, 1, cols) for _, size in cuts for _ in range(2)]
    outs = pl.pallas_call(
        functools.partial(cut_kernel, cuts),
        in_specs=[anywhere] * (1 + len(after)),
        out_specs=[anywhere] * len(outs),
        out_shape=outs,
        scratch_shapes=[pltpu.SemaphoreType.DMA((rows * len(cuts),))],
        compiler_params=params(),
    )(q, *after)
    return [x.reshape(tracers, NSUB, x.shape[2], cols) for x in outs]


def hold_kernel(*refs):
    pass


def held_until(arrays, after):
    anywhere = pl.BlockSpec(memory_space=pl.ANY)
    return pl.pallas_call(
        hold_kernel,
        in_specs=[anywhere] * (len(arrays) + len(after)),
        out_specs=[anywhere] * len(arrays),
        out_shape=[shaped(*x.shape) for x in arrays],
        input_output_aliases={i: i for i in range(len(arrays))},
        compiler_params=params(),
    )(*arrays, *after)


def both_ends(acc):
    return jnp.where(lanes_of(acc.shape) % SLOTS < SLOTS // 2, acc, turn(acc, SLOTS // 2, 1))


def pack_tracers_kernel(low_ref, high_ref, after_ref, before_ref, packed_ref):
    tracers, _, _, cols = low_ref.shape
    lane = lanes_of((SUB, cols))
    for pair in range(tracers // 2):
        acc = jnp.zeros((SUB, cols), jnp.float32)
        for odd in range(2):
            t = 2 * pair + odd
            rows = [before_ref[t, 1], low_ref[t, 0], low_ref[t, 1], high_ref[t, 0], high_ref[t, 1]]
            for r, x in enumerate(rows + [after_ref[t, 0]]):
                at = HALF * odd + SLOTS * (r + 1)
                acc = jnp.where(lane // SLOTS == at // SLOTS, turn(x, at + NSUB, 1), acc)
        packed_ref[pair] = both_ends(acc)


def pack_tracers(own, rim, after):
    tracers, _, levels, cols = own[0].shape
    rows = pl.BlockSpec((tracers, NSUB, SUB, cols), lambda i: (0, 0, i, 0))
    return pl.pallas_call(
        functools.partial(ignoring, len(after), pack_tracers_kernel),
        grid=(levels // SUB,),
        in_specs=[pl.BlockSpec(memory_space=pl.ANY)] * len(after) + [rows] * 4,
        out_specs=pl.BlockSpec((tracers // 2, SUB, cols), lambda i: (0, i, 0)),
        out_shape=shaped(tracers // 2, levels, cols),
        compiler_params=params(),
    )(*after, *own, *rim)


def ignoring(count, kernel, *refs):
    kernel(*refs[count:])


def call_once(kernel, operands, outs, scratch=(), scalars=(), after=(), limit=VMEM_LIMIT, cost=None):
    return pl.pallas_call(
        functools.partial(ignoring, len(after), kernel),
        grid=(1,),
        in_specs=[pl.BlockSpec(memory_space=pl.ANY)] * len(after)
        + [smem()] * len(scalars)
        + [whole(x.shape) for x in operands],
        out_specs=[whole(x.shape) for x in outs],
        out_shape=outs,
        scratch_shapes=list(scratch),
        compiler_params=params(limit),
        cost_estimate=cost,
    )(*after, *scalars, *operands)


def pack_ocean_kernel(levels, *refs):
    u_ref, v_ref, t_ref, s_ref, sea_ref, floor_ref, packed_ref, edges_ref, row_ref = refs
    edge_low_ref, edge_high_ref = edges_ref.at[0], edges_ref.at[1]
    tile_rows, cols = sea_ref.shape
    lane = lanes_of((levels, cols))
    edge_low_ref[4 * NSUB] = jnp.zeros((levels, cols), jnp.float32)
    edge_high_ref[4 * NSUB] = jnp.zeros((levels, cols), jnp.float32)
    for f, ref in enumerate((u_ref, v_ref, t_ref, s_ref)):
        acc = jnp.zeros((levels, cols), jnp.float32)
        for r in range(tile_rows):
            x = ref[pl.ds(r, levels, stride=tile_rows), :]
            row_ref[f, r] = x
            acc = jnp.where(lane // SLOTS == r, turn(x, SLOTS * r + NSUB, 1), acc)
            if r < NSUB:
                edge_low_ref[NSUB * f + r] = x
            if r >= tile_rows - NSUB:
                edge_high_ref[NSUB * f + r - tile_rows + NSUB] = x
        packed_ref[f] = both_ends(acc)
    depth = jnp.where(sea_ref[...] == 1, floor_ref[...], 0).astype(jnp.float32)
    acc = jnp.zeros((levels, cols), jnp.float32)
    for r in range(tile_rows):
        x = jnp.broadcast_to(depth[r : r + 1], (levels, cols))
        acc = jnp.where(lane // SLOTS == r, turn(x, SLOTS * r + NSUB, 1), acc)
    packed_ref[4] = both_ends(acc)
    edge_low_ref[4 * NSUB, 0:NSUB, :] = depth[0:NSUB]
    edge_high_ref[4 * NSUB, 0:NSUB, :] = depth[tile_rows - NSUB :]


def pack_ocean(flat, sea, levels):
    cols = sea[0].shape[1]
    edges = shaped(2, 4 * NSUB + 1, levels, cols)
    return call_once(
        functools.partial(pack_ocean_kernel, levels),
        [*flat, *sea],
        [shaped(5, levels, cols), edges, shaped(4, sea[0].shape[0], levels, cols)],
        limit=VMEM_MOST,
    )


def with_sides(own, left, right):
    slot = lanes_of(own.shape) % SLOTS
    ends = jnp.where(slot < NSUB, left, right)
    return jnp.where((slot < NSUB) | (slot >= SLOTS - NSUB), ends, own)


def ocean_sides_kernel(own_ref, left_ref, right_ref, edges_ref, up_ref, down_ref, out_ref):
    _, levels, cols = own_ref.shape
    rows = edges_ref.shape[1]
    up_ref[0:rows] = edges_ref[0]
    down_ref[0:rows] = edges_ref[1]
    slot = lanes_of((levels, cols)) % SLOTS
    place = lax.axis_index("gy")
    first, last = place == 0, place == lax.axis_size("gy") - 1
    for f in range(5):
        x = with_sides(own_ref[f], left_ref[f], right_ref[f])
        if f == 4:
            x = jnp.where((slot < NSUB) & first, 0.0, x)
            x = jnp.where((slot >= SLOTS - NSUB) & last, 0.0, x)
        out_ref[f] = x
        up_ref[rows + f] = x
        down_ref[rows + f] = x


def ocean_sides(own, left, right, edges):
    edge = shaped(edges.shape[1] + 5, *edges.shape[2:])
    return call_once(
        ocean_sides_kernel,
        [own, left, right, edges],
        [edge, edge, shaped(*own.shape)],
    )


def ocean_kernel(blocks, levels, *refs):
    own_ref, sea_ref, floor_ref, packed_ref, after_ref, before_ref = refs[:6]
    smix_ref, mixed_ref, send_ref, local_ref, faces_ref, depths_ref, press_ref, total_ref = refs[6:]
    tile_rows, cols = sea_ref.shape
    sub_rows = tile_rows // blocks
    shape = (levels, cols)
    lane = lanes_of(shape)
    first, last = lane == 0, lane == cols - 1
    base = lax.axis_index("comp") * levels
    level = (base + subs_of(shape)).astype(jnp.float32)
    rims = after_ref.shape[0] - 5

    def packed(f):
        after, before = after_ref[rims + f], before_ref[rims + f]
        rim = jnp.where(lane < NSUB * SLOTS, after, jnp.where(lane >= cols - NSUB * SLOTS, before, 0.0))
        return jnp.concatenate([packed_ref[f], rim], axis=1)

    def row_after(x):
        return turn(x, -SLOTS, 1)

    def row_before(x):
        return turn(x, SLOTS, 1)

    up, vp, tp, sp, dp = [packed(f) for f in range(5)]
    wide = jnp.concatenate([level, level], axis=1)
    wet = (wide < dp).astype(jnp.float32)
    heavy = wet * (-0.2 * tp + 0.8 * sp)
    above, total = sums_above(heavy)
    press = above + 0.5 * heavy
    east = up + DT_FLOW * (CORIOLIS * vp - (row_after(press) - press))
    north = vp + DT_FLOW * (-CORIOLIS * up - (turn(press, -1, 1) - press))
    open_n = wet * turn(wet, -1, 1)
    flux_t = open_n * (turn(tp, -1, 1) - tp)
    flux_s = open_n * (turn(sp, -1, 1) - sp)
    total_e, total_n = row_after(total) - total, turn(total, -1, 1) - total
    depth_e, depth_n = jnp.minimum(dp, row_after(dp)), jnp.minimum(dp, turn(dp, -1, 1))

    def window(x, g):
        x = turn(x, -SLOTS * (sub_rows * g - NSUB), 1)[:, 0:cols]
        return jnp.where(lane < HALF, x, turn(x, HALF, 1))

    for g in range(blocks):
        send_ref[g, 13] = window(east, g)
        send_ref[g, 14] = window(north, g)
        send_ref[g, 15, 13:14, :] = window(total_e, g)[0:1]
        send_ref[g, 15, 14:15, :] = window(total_n, g)[0:1]
        send_ref[g, 15, 15:16, :] = jnp.zeros((1, cols), jnp.float32)
        depths_ref[g, 24:25, :] = window(depth_e, g)[0:1]
        depths_ref[g, 25:26, :] = window(depth_n, g)[0:1]
        depths_ref[g, 26:27, :] = window(dp, g)[0:1]

    slot = lanes_of(tp.shape) % SLOTS

    def edges(x, other):
        x = jnp.where(slot == 0, turn(x, -6, 1), other)
        return x[:, 0:cols], x[:, cols:]

    edge_p, edge_w = edges(press, press), edges(wet, wet)
    edge_t, edge_s = edges(tp, flux_t), edges(sp, flux_s)
    edge_total, edge_depth = edges(total, total), edges(dp, dp)

    def edge(pair, r):
        at = r % tile_rows
        return turn(pair[0] if 0 <= r < tile_rows else pair[1], -(SLOTS * at + 1), 1)

    depth = jnp.where(sea_ref[...] == 1, floor_ref[...], 0).astype(jnp.float32)

    def row_of(f, r):
        if r < 0:
            return before_ref[NSUB * f + r + NSUB]
        if r >= tile_rows:
            return after_ref[NSUB * f + r - tile_rows]
        return own_ref[f, r]

    def depth_of(r):
        if r < 0:
            x = before_ref[4 * NSUB, r + NSUB : r + NSUB + 1, :]
        elif r >= tile_rows:
            x = after_ref[4 * NSUB, r - tile_rows : r - tile_rows + 1, :]
        else:
            x = depth[r : r + 1]
        return jnp.broadcast_to(x, shape)

    lo, hi = -NSUB, tile_rows + NSUB
    for r in range(lo, hi):
        heavy = (level < depth_of(r)).astype(jnp.float32) * (-0.2 * row_of(2, r) + 0.8 * row_of(3, r))
        above, total = sums_above(heavy)
        press_ref[r - lo] = above + 0.5 * heavy
        total_ref[r - lo] = total

    def windows(r, before):
        for g in range(blocks):
            j = r - (sub_rows * g - before)
            if 0 <= j < sub_rows + 1 + before:
                yield g, j

    flux_before = [None, None]
    for r in range(lo, hi - 1):
        press, press_e = press_ref[r - lo], press_ref[r - lo + 1]
        total, total_a = total_ref[r - lo], total_ref[r - lo + 1]
        d, d_e = depth_of(r), depth_of(r + 1)
        d_n = jnp.where(last, edge(edge_depth, r), turn(d, -1, 1))
        face_e, face_n = jnp.minimum(d, d_e), jnp.minimum(d, d_n)
        u, v = row_of(0, r), row_of(1, r)
        east = u + DT_FLOW * (CORIOLIS * v - (press_e - press))
        press_n = jnp.where(last, edge(edge_p, r), turn(press, -1, 1))
        north = v + DT_FLOW * (-CORIOLIS * u - (press_n - press))
        total_e = total_a - total
        total_n = jnp.where(last, edge(edge_total, r), turn(total, -1, 1)) - total
        for g, j in windows(r, 2):
            send_ref[g, j] = east
            send_ref[g, 15, j : j + 1, :] = total_e[0:1]
            depths_ref[g, j : j + 1, :] = face_e[0:1]
        for g, j in windows(r, 1):
            send_ref[g, 7 + j] = north
            send_ref[g, 15, 7 + j : 8 + j, :] = total_n[0:1]
            depths_ref[g, 8 + j : 9 + j, :] = face_n[0:1]
            depths_ref[g, 16 + j : 17 + j, :] = d[0:1]
        if 0 <= r < tile_rows:
            local_ref[0, r] = east
            local_ref[1, r] = north
            faces_ref[0, r : r + 1, :] = face_e[0:1]
            faces_ref[1, r : r + 1, :] = face_n[0:1]
            for g in range(blocks):
                send_ref[g, 16, r : r + 1, :] = total_e[0:1]
                send_ref[g, 17, r : r + 1, :] = total_n[0:1]
        if r < -1 or r >= tile_rows:
            continue
        open_e = (level < face_e).astype(jnp.float32)
        open_n = (level < face_n).astype(jnp.float32)
        for i, (f, ends) in enumerate(((2, edge_t), (3, edge_s))):
            x = row_of(f, r)
            flux_e = open_e * (row_of(f, r + 1) - x)
            if r >= 0:
                ending = edge(ends, r)
                flux_n = open_n * (jnp.where(last, ending, turn(x, -1, 1)) - x)
                flux_b = jnp.where(first, ending, turn(flux_n, 1, 1))
                mixed = x + MIXING * ((flux_e - flux_before[i]) + (flux_n - flux_b))
                mixed_ref[i, r] = mixed
                if i == 1:
                    smix_ref[pl.ds(r, levels, stride=tile_rows), :] = mixed
            flux_before[i] = flux_e


def ocean_phase(blocks, levels, own, sea, packed, rim_after, rim_before, after):
    tile_rows, cols = sea[0].shape
    outs = [
        shaped(levels * tile_rows, cols),
        shaped(2, tile_rows, levels, cols),
        shaped(blocks, ENTRIES, levels, cols),
        shaped(2, tile_rows, levels, cols),
        shaped(2, tile_rows, cols),
        shaped(blocks, 32, cols),
    ]
    tall = tile_rows + 2 * NSUB
    return call_once(
        functools.partial(ocean_kernel, blocks, levels),
        [own, *sea, packed, rim_after, rim_before],
        outs,
        [pltpu.VMEM((tall, levels, cols), jnp.float32)] * 2,
        after=after,
    )


def velocity_kernel(local_ref, faces_ref, received_ref, east_ref, north_ref, token_ref):
    blocks = received_ref.shape[0]
    _, tile_rows, levels, cols = local_ref.shape
    token_ref[...] = jnp.zeros_like(token_ref)
    group = lax.axis_index("comp")
    level = (group * levels + subs_of((levels, cols))).astype(jnp.float32)
    for f, out_ref in enumerate((east_ref, north_ref)):
        above = jnp.zeros((tile_rows, cols), jnp.float32)
        for s in range(blocks - 1):
            above = above + jnp.where(s < group, received_ref[s, f], 0.0)
        for r in range(tile_rows):
            x = local_ref[f, r] - DT_FLOW * jnp.broadcast_to(above[r : r + 1], (levels, cols))
            x = jnp.where(level < faces_ref[f, r : r + 1, :], x, 0.0)
            out_ref[pl.ds(r, levels, stride=tile_rows), :] = x


def velocities(local, faces, received):
    blocks = received.shape[0]
    _, tile_rows, levels, cols = local.shape
    out = shaped(levels * tile_rows, cols)
    return pl.pallas_call(
        velocity_kernel,
        grid=(1,),
        in_specs=[
            whole(local.shape),
            whole(faces.shape),
            pl.BlockSpec((blocks, 2, levels, cols), lambda i: (0, ENTRIES // 2 - 1, 0, 0)),
        ],
        out_specs=[whole(out.shape)] * 2 + [whole((SUB, cols))],
        out_shape=[out] * 2 + [shaped(SUB, cols)],
        compiler_params=params(),
    )(local, faces, received)


def advection_kernel(first_part, parts, level_count, *refs):
    (
        absorb_ref,
        surface_ref,
        depth_ref,
        totals_ref,
        courant_ref,
        low_ref,
        high_ref,
        after_ref,
        before_ref,
        side_ref,
        left_ref,
        right_ref,
    ) = refs[:12]
    moved_ref, light_ref, heat_ref, carry_out_ref = refs[-10:-6]
    coef_ref, side_coef_ref, edge_ref, running_ref, above_ref, shift_ref = refs[-6:]
    depth_ref = depth_ref.at[lax.axis_index("comp")]
    step = pl.program_id(0)
    tracers, _, _, cols = low_ref.shape
    levels = courant_ref.shape[2]
    sub_rows = surface_ref.shape[0]
    rows = sub_rows + 2
    shape = (levels, cols)
    lane = lanes_of(shape)
    first, last = lane == 0, lane == cols - 1
    first8, last8 = first[0:SUB], last[0:SUB]
    slot = lane % SLOTS

    @pl.when(step == 0)
    def _():
        running_ref[...] = refs[12][...] if first_part else jnp.zeros_like(running_ref)
        size = (2 * cols, 2 * cols)
        source, to = subs_of(size) % cols, lanes_of(size)
        hit = ((to < cols) & (source == to + 1)) | ((to >= cols) & (source == to - cols - 1))
        shift_ref[...] = hit.astype(jnp.float32).astype(jnp.bfloat16)

    part = first_part + step
    above = jnp.zeros(above_ref.shape, jnp.float32)
    for s in range(totals_ref.shape[0] - 1):
        above = above + jnp.where(s < part // parts, totals_ref[s, 0], 0.0)
    above_ref[...] = above
    level = (part * levels + subs_of(shape)).astype(jnp.float32)

    def spread(ref, r):
        return jnp.broadcast_to(ref[r : r + 1, :], shape)

    def courant(entry, face):
        x = courant_ref[0, entry] - DT_FLOW * spread(above_ref, entry)
        return COURANT * jnp.tanh(jnp.where(level < spread(depth_ref, face), x, 0.0))

    def coefficients(wet, ce, ce_b, cn, cn_b):
        return (
            wet
            * (
                1.0
                - jnp.maximum(ce, 0.0)
                + jnp.minimum(ce_b, 0.0)
                - jnp.maximum(cn, 0.0)
                + jnp.minimum(cn_b, 0.0)
            ),
            -wet * jnp.minimum(ce, 0.0),
            wet * jnp.maximum(ce_b, 0.0),
            -wet * jnp.minimum(cn, 0.0),
            wet * jnp.maximum(cn_b, 0.0),
        )

    side_e, side_n = courant(13, 24), courant(14, 25)
    wet = (level < spread(depth_ref, 26)).astype(jnp.float32)
    packed_coef = coefficients(wet, side_e, turn(side_e, SLOTS, 1), side_n, turn(side_n, 1, 1))
    for i in range(5):
        side_coef_ref[i] = packed_coef[i]
    ce_b = courant(0, 0)
    for j in range(rows):
        ce, cn = courant(1 + j, 1 + j), courant(7 + j, 8 + j)
        cn_b = jnp.where(first, turn(side_n, -(SLOTS * (j + 1) + 1), 1), turn(cn, 1, 1))
        wet = (level < spread(depth_ref, 16 + j)).astype(jnp.float32)
        for i, x in enumerate(coefficients(wet, ce, ce_b, cn, cn_b)):
            coef_ref[5 * j + i] = x
        ce_b = ce
    for i in range(side_ref.shape[0]):
        x = with_sides(side_ref[i], left_ref[i], right_ref[i])
        edge_ref[i, 0] = jnp.where(slot == 0, turn(x, -6, 1), x)
        x = (
            (side_coef_ref[0] * x + side_coef_ref[1] * turn(x, -SLOTS, 1))
            + (side_coef_ref[2] * turn(x, SLOTS, 1) + side_coef_ref[3] * turn(x, -1, 1))
            + side_coef_ref[4] * turn(x, 1, 1)
        )
        edge_ref[i, 1] = jnp.where(slot == 0, turn(x, -6, 1), x)

    layer = 2.0 / level_count
    zero = jnp.zeros((SUB, cols), jnp.float32)
    for k in range(0, levels, SUB):
        at = slice(k, k + SUB)

        def shifted(tiles):
            high, low = halves(jnp.concatenate(tiles, axis=0))
            return jnp.dot(
                jnp.concatenate([high, low], axis=1),
                shift_ref[...],
                preferred_element_type=jnp.float32,
            )

        def stencil(x, coef, edge, beside):
            north = jnp.where(last8, edge, beside[:, :cols])
            south = jnp.where(first8, edge, beside[:, cols:])
            return (
                (coef[0] * x[1] + coef[1] * x[2])
                + (coef[2] * x[0] + coef[3] * north)
                + coef[4] * south
            )

        def advect(i, sums):
            sums = list(sums)
            fields = []
            for t in range(GROUP):
                t = GROUP * i + t
                rows_of = (before_ref, low_ref, high_ref, after_ref)
                x = [ref[t, n, at] for ref in rows_of for n in range(NSUB)]
                fields.append(x)
            for stage in range(NSUB):
                inner = range(1 + stage, rows + 1 - stage)
                beside = shifted([x[j - stage] for j in inner for x in fields])
                fresh = [[] for _ in fields]
                for n, j in enumerate(inner):
                    coef = [coef_ref[5 * (j - 1) + c, at] for c in range(5)]
                    for t, x in enumerate(fields):
                        edges = edge_ref[GROUP // 2 * i + t // 2, stage, at]
                        edge = turn(edges, -(HALF * (t % 2) + SLOTS * j + 1), 1)
                        row = SUB * (len(fields) * n + t)
                        fresh[t].append(
                            stencil(x[n : n + 3], coef, edge, beside[row : row + SUB])
                        )
                fields = fresh
            for t, x in enumerate(fields):
                for r in range(sub_rows):
                    moved_ref[GROUP * i + t, r, at] = x[r]
                    sums[r] = sums[r] + absorb_ref[GROUP * i + t] * x[r]
            return tuple(sums)

        sums = (zero,) * sub_rows
        for i in range(tracers // GROUP):
            sums = advect(i, sums)
        for r in range(sub_rows):
            optical = layer * (CLEAR_WATER + sums[r])
            above, total = sums_above(optical)
            through = jnp.exp(-(running_ref[r] + above))
            running_ref[r] = running_ref[r] + total
            surface = jnp.broadcast_to(surface_ref[r : r + 1, :], (SUB, cols))
            light_ref[r, at] = surface * through * jnp.exp(-0.5 * optical)
            wet = (level[at] < jnp.broadcast_to(depth_ref[17 + r : 18 + r, :], (SUB, cols))).astype(
                jnp.float32
            )
            heat_ref[0, r, at] = wet * surface * through * (1.0 - jnp.exp(-optical)) / layer
    carry_out_ref[...] = running_ref[...]


def advection(cut, level_count, absorb, surface, depth, received, own, rim, sides, carry, heat, after):
    first_part, count = cut
    tracers, _, _, cols = own[0].shape
    every, _, levels, _ = received.shape
    parts = levels // SUB
    sub_rows = surface.shape[0]
    rows = pl.BlockSpec((tracers, NSUB, SUB, cols), lambda i: (0, 0, i, 0))
    side = pl.BlockSpec((tracers // 2, SUB, cols), lambda i: (0, i, 0))
    operands = [absorb, surface, depth, received, received, *own, *rim, *sides]
    in_specs = [
        smem(),
        whole(surface.shape),
        whole(depth.shape),
        pl.BlockSpec((every, 1, levels, cols), lambda i: (0, 15, 0, 0)),
        pl.BlockSpec(
            (1, ENTRIES, SUB, cols),
            lambda i: ((first_part + i) // parts, 0, (first_part + i) % parts, 0),
        ),
        rows,
        rows,
        rows,
        rows,
        side,
        side,
        side,
    ]
    aliases = {}
    carry_shape = (sub_rows, SUB, cols)
    if carry is not None:
        operands.append(carry)
        in_specs.append(whole(carry_shape))
        aliases = {len(operands): 2}
        operands.append(heat)
    operands += after
    in_specs += [pl.BlockSpec(memory_space=pl.ANY)] * (len(operands) - len(in_specs))
    outs = [
        shaped(tracers, sub_rows, count * SUB, cols),
        shaped(sub_rows, count * SUB, cols),
        shaped(every, sub_rows, levels, cols),
        shaped(*carry_shape),
    ]
    return pl.pallas_call(
        functools.partial(advection_kernel, first_part, parts, level_count),
        grid=(count,),
        in_specs=in_specs,
        out_specs=[
            pl.BlockSpec((tracers, sub_rows, SUB, cols), lambda i: (0, 0, i, 0)),
            pl.BlockSpec((sub_rows, SUB, cols), lambda i: (0, i, 0)),
            pl.BlockSpec(
                (1, sub_rows, SUB, cols),
                lambda i: ((first_part + i) // parts, 0, (first_part + i) % parts, 0),
            ),
            whole(carry_shape),
        ],
        out_shape=outs,
        scratch_shapes=[
            pltpu.VMEM((5 * (sub_rows + 2), SUB, cols), jnp.float32),
            pltpu.VMEM((5, SUB, cols), jnp.float32),
            pltpu.VMEM((tracers // 2, 2, SUB, cols), jnp.float32),
            pltpu.VMEM((sub_rows, SUB, cols), jnp.float32),
            pltpu.VMEM((levels, cols), jnp.float32),
            pltpu.VMEM((2 * cols, 2 * cols), jnp.bfloat16),
        ],
        input_output_aliases=aliases,
        compiler_params=params(),
    )(*operands)


def spread_kernel(matrix_ref, out_ref):
    tracers = matrix_ref.shape[0]
    size = tracers * SUB
    tall = (subs_of((size, tracers)) // SUB == lanes_of((size, tracers))).astype(jnp.float32)
    wide = (lanes_of((tracers, size)) // SUB == subs_of((tracers, size))).astype(jnp.float32)
    exact = functools.partial(
        jnp.dot, precision=lax.Precision.HIGHEST, preferred_element_type=jnp.float32
    )
    same = subs_of((size, size)) % SUB == lanes_of((size, size)) % SUB
    out_ref[...] = jnp.where(same, exact(exact(tall, matrix_ref[...]), wide), 0.0)


def uptake_kernel(first_level, *refs):
    growth_ref, half_ref, dim_ref, matrix_ref, depth_ref, moved_ref, light_ref = refs[:7]
    depth_ref = depth_ref.at[lax.axis_index("comp")]
    result_ref, token_ref, uptake_ref = refs[-3:]
    token_ref[...] = jnp.zeros_like(token_ref)
    tracers, sub_rows, levels, cols = moved_ref.shape
    step = pl.program_id(0)
    matrix_high, matrix_low = halves(matrix_ref[...])
    for k in range(0, levels, SUB):
        at = slice(k, k + SUB)
        level = (first_level + step * levels + k + subs_of((SUB, cols))).astype(jnp.float32)
        light = [light_ref[r, at] for r in range(sub_rows)]
        food = [moved_ref[0, r, at] for r in range(sub_rows)]
        both = [light[r] * food[r] for r in range(sub_rows)]

        def uptake(t, _):
            for r in range(sub_rows):
                scale = (half_ref[t] + food[r]) * (light[r] + dim_ref[t])
                value = growth_ref[t] * moved_ref[t, r, at] * (both[r] / scale)
                uptake_ref[pl.ds(t * SUB, SUB), r * cols : (r + 1) * cols] = value
            return _

        lax.fori_loop(0, tracers, uptake, 0, unroll=4)
        amount = uptake_ref[...]
        high, low = halves(amount)
        dot = functools.partial(jnp.dot, preferred_element_type=jnp.float32)
        change = dot(matrix_high, high) + (dot(matrix_high, low) + dot(matrix_low, high))
        for r in range(sub_rows):
            depth = jnp.broadcast_to(depth_ref[17 + r : 18 + r, :], (SUB, cols))
            scale = DT_BIO * (level < depth).astype(jnp.float32)
            for t in range(tracers):
                result_ref[t, pl.ds(sub_rows * k + r, SUB, stride=sub_rows), :] = (
                    moved_ref[t, r, at]
                    + scale * change[SUB * t : SUB * (t + 1), r * cols : (r + 1) * cols]
                )


def uptake(cut, all_rows, scalars, matrix, depth, moved, light, result):
    first_part, count = cut
    tracers, sub_rows, _, cols = moved.shape
    operands = [*scalars, matrix, depth, moved, light]
    in_specs = [smem()] * 3 + [
        whole(matrix.shape),
        whole(depth.shape),
        pl.BlockSpec((tracers, sub_rows, SUB, cols), lambda i: (0, 0, i, 0)),
        pl.BlockSpec((sub_rows, SUB, cols), lambda i: (0, i, 0)),
    ]
    aliases = {}
    if result is not None:
        aliases = {len(operands): 0}
        operands.append(result)
        in_specs.append(pl.BlockSpec(memory_space=pl.ANY))
    return pl.pallas_call(
        functools.partial(uptake_kernel, first_part * SUB),
        grid=(count,),
        in_specs=in_specs,
        out_specs=[
            pl.BlockSpec((tracers, SUB * sub_rows, cols), lambda i: (0, first_part + i, 0)),
            whole((SUB, cols)),
        ],
        out_shape=[shaped(tracers, all_rows, cols), shaped(SUB, cols)],
        scratch_shapes=[pltpu.VMEM((tracers * SUB, sub_rows * cols), jnp.float32)],
        input_output_aliases=aliases,
        compiler_params=params(),
    )(*operands)


def warming_kernel(sea_ref, floor_ref, heat_ref, mixed_ref, warm_ref, buoyant_ref):
    blocks, sub_rows, levels, cols = heat_ref.shape
    tile_rows = blocks * sub_rows
    base = lax.axis_index("comp") * levels
    level = (base + subs_of((levels, cols))).astype(jnp.float32)
    depth = jnp.where(sea_ref[...] == 1, floor_ref[...], 0).astype(jnp.float32)
    for r in range(tile_rows):
        at = pl.ds(r, levels, stride=tile_rows)
        warm = mixed_ref[0, r] + WARMING_FACTOR * heat_ref[r // sub_rows, r % sub_rows]
        wet = (level < depth[r : r + 1]).astype(jnp.float32)
        warm_ref[at, :] = warm
        buoyant_ref[at, :] = wet * (0.2 * warm - 0.8 * mixed_ref[1, r])


def warming(heat, mixed, sea):
    _, tile_rows, levels, cols = mixed.shape
    outs = [shaped(levels * tile_rows, cols)] * 2
    return call_once(warming_kernel, [*sea, heat, mixed], outs)


def from_before(x, axis):
    return lax.ppermute(x, axis, [(i, i + 1) for i in range(lax.axis_size(axis) - 1)])


def from_after(x, axis):
    return lax.ppermute(x, axis, [(i + 1, i) for i in range(lax.axis_size(axis) - 1)])


def row_pairs():
    blocks, tiles = lax.axis_size("comp"), lax.axis_size("gx")
    places = [b * tiles + tile for tile in range(tiles) for b in range(blocks)]
    return list(zip(places[:-1], places[1:]))


def from_block_before(x):
    return lax.ppermute(x, ("comp", "gx"), row_pairs())


def from_block_after(x):
    return lax.ppermute(x, ("comp", "gx"), [(later, own) for own, later in row_pairs()])


def from_sides(x):
    if lax.axis_size("gy") == 2:
        other = lax.ppermute(x, "gy", [(0, 1), (1, 0)])
        return other, other
    return from_before(x, "gy"), from_after(x, "gy")


def on_device(
    zonal_flow_speed,
    meridional_flow_speed,
    thermal_anomaly,
    brine_anomaly_values,
    marine_indicator,
    seafloor_layer,
    dissolved_species,
    topmost_sunshine,
    attenuation_coefficient,
    peak_intake_speed,
    feedstock_midpoint_constant,
    photon_midpoint_constant,
    stoichiometry_matrix,
):
    blocks = lax.axis_size("comp")
    levels, tile_rows, tile_cols = zonal_flow_speed.shape
    tracer_count, level_count = dissolved_species.shape[:2]
    sub_rows = dissolved_species.shape[4]
    ocean = (zonal_flow_speed, meridional_flow_speed, thermal_anomaly, brine_anomaly_values)
    sea = (marine_indicator, seafloor_layer)
    flat = [x.reshape(levels * tile_rows, tile_cols) for x in ocean]
    q = dissolved_species.reshape(tracer_count, level_count, sub_rows, 1, tile_cols)
    parts = levels // SUB
    every = parts * blocks
    sizes = [every - 5 * every // 8, 3 * every // 8, every // 4]
    cuts = [(sum(sizes[:i]), size) for i, size in enumerate(sizes)]
    scalars_of_uptake = (
        peak_intake_speed,
        feedstock_midpoint_constant,
        photon_midpoint_constant,
    )

    def rims(own):
        return own, (from_block_after(own[0]), from_block_before(own[1]))

    def sides(x):
        return (x, *from_sides(x))

    packed, edges, ocean_rows = pack_ocean(flat, sea, levels)
    ranges = [(first * SUB, size * SUB) for first, size in cuts]
    chunks = [rims(cut_rows(q, ranges[:1], []))]
    later = cut_rows(q, ranges[1:], chunks[0][0][:1])
    up, down, packed = ocean_sides(packed, *from_sides(packed), edges)
    after, before = from_after(up, "gx"), from_before(down, "gx")
    smix, mixed, send, local, faces, depths = ocean_phase(
        blocks, levels, ocean_rows, sea, packed, after, before, later[:1]
    )
    received = lax.all_to_all(send, "comp", split_axis=0, concat_axis=0, tiled=True)
    east_new, north_new, finished = velocities(local, faces, received)
    matrix = call_once(
        spread_kernel,
        [stoichiometry_matrix],
        [shaped(SUB * tracer_count, SUB * tracer_count)],
        after=[depths],
        cost=COVER,
    )[0]
    chunks.append(rims(held_until(later[:2], [matrix])))
    own = pack_tracers(*chunks[0], [matrix])

    surface = topmost_sunshine.reshape(sub_rows, tile_cols)
    carry, heat, result = None, None, None
    near = sides(own)
    for i, cut in enumerate(cuts):
        moved, light, heat, carry = advection(
            cut,
            level_count,
            attenuation_coefficient,
            surface,
            depths,
            received,
            *chunks[i],
            near,
            carry,
            heat,
            [] if i == 0 else [token, finished],
        )
        if i > 0 and i + 1 < len(cuts):
            near = sides(pack_tracers(*chunks[i + 1], [carry]))
        result, token = uptake(
            cut,
            level_count * sub_rows,
            scalars_of_uptake,
            matrix,
            depths,
            moved,
            light,
            result,
        )
        if i + 2 < len(cuts):
            at = 2 * (i + 1)
            chunks.append(rims(held_until(later[at : at + 2], [token])))
        if i == 0:
            near = sides(pack_tracers(*chunks[1], [token]))
    heat = lax.all_to_all(heat, "comp", split_axis=0, concat_axis=0, tiled=True)
    warmed_result, buoyancy = warming(heat, mixed, sea)
    fields = (east_new, north_new, warmed_result, smix, buoyancy)
    return (
        *[x.reshape(zonal_flow_speed.shape) for x in fields],
        result.reshape(dissolved_species.shape),
    )


def solution(mesh):
    return jax.shard_map(
        on_device,
        mesh=mesh,
        in_specs=(
            P("comp", "gx", "gy"),
            P("comp", "gx", "gy"),
            P("comp", "gx", "gy"),
            P("comp", "gx", "gy"),
            P("gx", "gy"),
            P("gx", "gy"),
            P(None, None, "gx", "comp", None, "gy"),
            P("gx", "comp", None, "gy"),
            P(),
            P(),
            P(),
            P(),
            P(),
        ),
        out_specs=(
            P("comp", "gx", "gy"),
            P("comp", "gx", "gy"),
            P("comp", "gx", "gy"),
            P("comp", "gx", "gy"),
            P("comp", "gx", "gy"),
            P(None, None, "gx", "comp", None, "gy"),
        ),
        check_vma=False,
    )
```

```python
import functools

import jax
import jax.numpy as jnp
from jax import lax
from jax.experimental import pallas as pl
from jax.experimental.pallas import tpu as pltpu
from jax.sharding import PartitionSpec as P

NSUB = 2
SLOTS = 4 * NSUB
SUB = 8
GROUP = 24
HALF = 64
ENTRIES = 18

DT_FLOW = 0.1
CORIOLIS = 0.3
MIXING = 0.15
COURANT = 0.24
DT_BIO = 0.5
WARMING_FACTOR = 0.5
CLEAR_WATER = 0.5
VMEM_LIMIT = 10 * 1024 * 1024
COVER = pl.CostEstimate(flops=0, bytes_accessed=200_000_000, transcendentals=0)
VMEM_MOST = 62 * 1024 * 1024


def lanes_of(shape):
    return lax.broadcasted_iota(jnp.int32, shape, len(shape) - 1)


def subs_of(shape):
    return lax.broadcasted_iota(jnp.int32, shape, len(shape) - 2)


def turn(x, by, axis):
    by = by % x.shape[axis]
    return x if by == 0 else pltpu.roll(x, by, axis)


def params(limit=VMEM_LIMIT):
    return pltpu.CompilerParams(vmem_limit_bytes=limit)


def whole(shape):
    return pl.BlockSpec(shape, lambda *_: (0,) * len(shape))


def smem():
    return pl.BlockSpec(memory_space=pltpu.SMEM)


def shaped(*shape):
    return jax.ShapeDtypeStruct(shape, jnp.float32)


def halves(x):
    high = x.astype(jnp.bfloat16)
    return high, (x - high.astype(jnp.float32)).astype(jnp.bfloat16)


def sums_above(x):
    sub = subs_of(x.shape)
    running, total = x, x
    by = 1
    while by < x.shape[0]:
        running = running + jnp.where(sub >= by, turn(running, by, 0), 0.0)
        total = total + turn(total, by, 0)
        by *= 2
    return jnp.where(sub >= 1, turn(running, 1, 0), 0.0), total


def cut_kernel(cuts, q_ref, *refs):
    outs, sems = refs[-2 * len(cuts) - 1 : -1], refs[-1]
    rows = q_ref.shape[2]
    copies = [
        pltpu.make_async_copy(
            q_ref.at[:, pl.ds(start, size), r],
            outs[2 * i + r // NSUB].at[:, r % NSUB],
            sems.at[rows * i + r],
        )
        for i, (start, size) in enumerate(cuts)
        for r in range(rows)
    ]
    for copy in copies:
        copy.start()
    for copy in copies:
        copy.wait()


def cut_rows(q, cuts, after):
    tracers, _, rows, _, cols = q.shape
    anywhere = pl.BlockSpec(memory_space=pl.ANY)
    outs = [shaped(tracers, NSUB, size, 1, cols) for _, size in cuts for _ in range(2)]
    outs = pl.pallas_call(
        functools.partial(cut_kernel, cuts),
        in_specs=[anywhere] * (1 + len(after)),
        out_specs=[anywhere] * len(outs),
        out_shape=outs,
        scratch_shapes=[pltpu.SemaphoreType.DMA((rows * len(cuts),))],
        compiler_params=params(),
    )(q, *after)
    return [x.reshape(tracers, NSUB, x.shape[2], cols) for x in outs]


def hold_kernel(*refs):
    pass


def held_until(arrays, after):
    anywhere = pl.BlockSpec(memory_space=pl.ANY)
    return pl.pallas_call(
        hold_kernel,
        in_specs=[anywhere] * (len(arrays) + len(after)),
        out_specs=[anywhere] * len(arrays),
        out_shape=[shaped(*x.shape) for x in arrays],
        input_output_aliases={i: i for i in range(len(arrays))},
        compiler_params=params(),
    )(*arrays, *after)


def both_ends(acc):
    return jnp.where(lanes_of(acc.shape) % SLOTS < SLOTS // 2, acc, turn(acc, SLOTS // 2, 1))


def pack_tracers_kernel(low_ref, high_ref, after_ref, before_ref, packed_ref):
    tracers, _, _, cols = low_ref.shape
    lane = lanes_of((SUB, cols))
    for pair in range(tracers // 2):
        acc = jnp.zeros((SUB, cols), jnp.float32)
        for odd in range(2):
            t = 2 * pair + odd
            rows = [before_ref[t, 1], low_ref[t, 0], low_ref[t, 1], high_ref[t, 0], high_ref[t, 1]]
            for r, x in enumerate(rows + [after_ref[t, 0]]):
                at = HALF * odd + SLOTS * (r + 1)
                acc = jnp.where(lane // SLOTS == at // SLOTS, turn(x, at + NSUB, 1), acc)
        packed_ref[pair] = both_ends(acc)


def pack_tracers(own, rim, after):
    tracers, _, levels, cols = own[0].shape
    rows = pl.BlockSpec((tracers, NSUB, SUB, cols), lambda i: (0, 0, i, 0))
    return pl.pallas_call(
        functools.partial(ignoring, len(after), pack_tracers_kernel),
        grid=(levels // SUB,),
        in_specs=[pl.BlockSpec(memory_space=pl.ANY)] * len(after) + [rows] * 4,
        out_specs=pl.BlockSpec((tracers // 2, SUB, cols), lambda i: (0, i, 0)),
        out_shape=shaped(tracers // 2, levels, cols),
        compiler_params=params(),
    )(*after, *own, *rim)


def ignoring(count, kernel, *refs):
    kernel(*refs[count:])


def call_once(kernel, operands, outs, scratch=(), scalars=(), after=(), limit=VMEM_LIMIT, cost=None):
    return pl.pallas_call(
        functools.partial(ignoring, len(after), kernel),
        grid=(1,),
        in_specs=[pl.BlockSpec(memory_space=pl.ANY)] * len(after)
        + [smem()] * len(scalars)
        + [whole(x.shape) for x in operands],
        out_specs=[whole(x.shape) for x in outs],
        out_shape=outs,
        scratch_shapes=list(scratch),
        compiler_params=params(limit),
        cost_estimate=cost,
    )(*after, *scalars, *operands)


def pack_ocean_kernel(levels, *refs):
    u_ref, v_ref, t_ref, s_ref, sea_ref, floor_ref, packed_ref, edges_ref, row_ref = refs
    edge_low_ref, edge_high_ref = edges_ref.at[0], edges_ref.at[1]
    tile_rows, cols = sea_ref.shape
    lane = lanes_of((levels, cols))
    edge_low_ref[4 * NSUB] = jnp.zeros((levels, cols), jnp.float32)
    edge_high_ref[4 * NSUB] = jnp.zeros((levels, cols), jnp.float32)
    for f, ref in enumerate((u_ref, v_ref, t_ref, s_ref)):
        acc = jnp.zeros((levels, cols), jnp.float32)
        for r in range(tile_rows):
            x = ref[pl.ds(r, levels, stride=tile_rows), :]
            row_ref[f, r] = x
            acc = jnp.where(lane // SLOTS == r, turn(x, SLOTS * r + NSUB, 1), acc)
            if r < NSUB:
                edge_low_ref[NSUB * f + r] = x
            if r >= tile_rows - NSUB:
                edge_high_ref[NSUB * f + r - tile_rows + NSUB] = x
        packed_ref[f] = both_ends(acc)
    depth = jnp.where(sea_ref[...] == 1, floor_ref[...], 0).astype(jnp.float32)
    acc = jnp.zeros((levels, cols), jnp.float32)
    for r in range(tile_rows):
        x = jnp.broadcast_to(depth[r : r + 1], (levels, cols))
        acc = jnp.where(lane // SLOTS == r, turn(x, SLOTS * r + NSUB, 1), acc)
    packed_ref[4] = both_ends(acc)
    edge_low_ref[4 * NSUB, 0:NSUB, :] = depth[0:NSUB]
    edge_high_ref[4 * NSUB, 0:NSUB, :] = depth[tile_rows - NSUB :]


def pack_ocean(flat, sea, levels):
    cols = sea[0].shape[1]
    edges = shaped(2, 4 * NSUB + 1, levels, cols)
    return call_once(
        functools.partial(pack_ocean_kernel, levels),
        [*flat, *sea],
        [shaped(5, levels, cols), edges, shaped(4, sea[0].shape[0], levels, cols)],
        limit=VMEM_MOST,
    )


def with_sides(own, left, right):
    slot = lanes_of(own.shape) % SLOTS
    ends = jnp.where(slot < NSUB, left, right)
    return jnp.where((slot < NSUB) | (slot >= SLOTS - NSUB), ends, own)


def ocean_sides_kernel(own_ref, left_ref, right_ref, edges_ref, up_ref, down_ref, out_ref):
    _, levels, cols = own_ref.shape
    rows = edges_ref.shape[1]
    up_ref[0:rows] = edges_ref[0]
    down_ref[0:rows] = edges_ref[1]
    slot = lanes_of((levels, cols)) % SLOTS
    place = lax.axis_index("gy")
    first, last = place == 0, place == lax.axis_size("gy") - 1
    for f in range(5):
        x = with_sides(own_ref[f], left_ref[f], right_ref[f])
        if f == 4:
            x = jnp.where((slot < NSUB) & first, 0.0, x)
            x = jnp.where((slot >= SLOTS - NSUB) & last, 0.0, x)
        out_ref[f] = x
        up_ref[rows + f] = x
        down_ref[rows + f] = x


def ocean_sides(own, left, right, edges):
    edge = shaped(edges.shape[1] + 5, *edges.shape[2:])
    return call_once(
        ocean_sides_kernel,
        [own, left, right, edges],
        [edge, edge, shaped(*own.shape)],
    )


def ocean_kernel(blocks, levels, *refs):
    own_ref, sea_ref, floor_ref, packed_ref, after_ref, before_ref = refs[:6]
    smix_ref, mixed_ref, send_ref, local_ref, faces_ref, depths_ref, press_ref, total_ref = refs[6:]
    tile_rows, cols = sea_ref.shape
    sub_rows = tile_rows // blocks
    shape = (levels, cols)
    lane = lanes_of(shape)
    first, last = lane == 0, lane == cols - 1
    base = lax.axis_index("comp") * levels
    level = (base + subs_of(shape)).astype(jnp.float32)
    rims = after_ref.shape[0] - 5

    def packed(f):
        after, before = after_ref[rims + f], before_ref[rims + f]
        rim = jnp.where(lane < NSUB * SLOTS, after, jnp.where(lane >= cols - NSUB * SLOTS, before, 0.0))
        return jnp.concatenate([packed_ref[f], rim], axis=1)

    def row_after(x):
        return turn(x, -SLOTS, 1)

    def row_before(x):
        return turn(x, SLOTS, 1)

    up, vp, tp, sp, dp = [packed(f) for f in range(5)]
    wide = jnp.concatenate([level, level], axis=1)
    wet = (wide < dp).astype(jnp.float32)
    heavy = wet * (-0.2 * tp + 0.8 * sp)
    above, total = sums_above(heavy)
    press = above + 0.5 * heavy
    east = up + DT_FLOW * (CORIOLIS * vp - (row_after(press) - press))
    north = vp + DT_FLOW * (-CORIOLIS * up - (turn(press, -1, 1) - press))
    open_n = wet * turn(wet, -1, 1)
    flux_t = open_n * (turn(tp, -1, 1) - tp)
    flux_s = open_n * (turn(sp, -1, 1) - sp)
    total_e, total_n = row_after(total) - total, turn(total, -1, 1) - total
    depth_e, depth_n = jnp.minimum(dp, row_after(dp)), jnp.minimum(dp, turn(dp, -1, 1))

    def window(x, g):
        x = turn(x, -SLOTS * (sub_rows * g - NSUB), 1)[:, 0:cols]
        return jnp.where(lane < HALF, x, turn(x, HALF, 1))

    for g in range(blocks):
        send_ref[g, 13] = window(east, g)
        send_ref[g, 14] = window(north, g)
        send_ref[g, 15, 13:14, :] = window(total_e, g)[0:1]
        send_ref[g, 15, 14:15, :] = window(total_n, g)[0:1]
        send_ref[g, 15, 15:16, :] = jnp.zeros((1, cols), jnp.float32)
        depths_ref[g, 24:25, :] = window(depth_e, g)[0:1]
        depths_ref[g, 25:26, :] = window(depth_n, g)[0:1]
        depths_ref[g, 26:27, :] = window(dp, g)[0:1]

    slot = lanes_of(tp.shape) % SLOTS

    def edges(x, other):
        x = jnp.where(slot == 0, turn(x, -6, 1), other)
        return x[:, 0:cols], x[:, cols:]

    edge_p, edge_w = edges(press, press), edges(wet, wet)
    edge_t, edge_s = edges(tp, flux_t), edges(sp, flux_s)
    edge_total, edge_depth = edges(total, total), edges(dp, dp)

    def edge(pair, r):
        at = r % tile_rows
        return turn(pair[0] if 0 <= r < tile_rows else pair[1], -(SLOTS * at + 1), 1)

    depth = jnp.where(sea_ref[...] == 1, floor_ref[...], 0).astype(jnp.float32)

    def row_of(f, r):
        if r < 0:
            return before_ref[NSUB * f + r + NSUB]
        if r >= tile_rows:
            return after_ref[NSUB * f + r - tile_rows]
        return own_ref[f, r]

    def depth_of(r):
        if r < 0:
            x = before_ref[4 * NSUB, r + NSUB : r + NSUB + 1, :]
        elif r >= tile_rows:
            x = after_ref[4 * NSUB, r - tile_rows : r - tile_rows + 1, :]
        else:
            x = depth[r : r + 1]
        return jnp.broadcast_to(x, shape)

    lo, hi = -NSUB, tile_rows + NSUB
    for r in range(lo, hi):
        heavy = (level < depth_of(r)).astype(jnp.float32) * (-0.2 * row_of(2, r) + 0.8 * row_of(3, r))
        above, total = sums_above(heavy)
        press_ref[r - lo] = above + 0.5 * heavy
        total_ref[r - lo] = total

    def windows(r, before):
        for g in range(blocks):
            j = r - (sub_rows * g - before)
            if 0 <= j < sub_rows + 1 + before:
                yield g, j

    flux_before = [None, None]
    for r in range(lo, hi - 1):
        press, press_e = press_ref[r - lo], press_ref[r - lo + 1]
        total, total_a = total_ref[r - lo], total_ref[r - lo + 1]
        d, d_e = depth_of(r), depth_of(r + 1)
        d_n = jnp.where(last, edge(edge_depth, r), turn(d, -1, 1))
        face_e, face_n = jnp.minimum(d, d_e), jnp.minimum(d, d_n)
        u, v = row_of(0, r), row_of(1, r)
        east = u + DT_FLOW * (CORIOLIS * v - (press_e - press))
        press_n = jnp.where(last, edge(edge_p, r), turn(press, -1, 1))
        north = v + DT_FLOW * (-CORIOLIS * u - (press_n - press))
        total_e = total_a - total
        total_n = jnp.where(last, edge(edge_total, r), turn(total, -1, 1)) - total
        for g, j in windows(r, 2):
            send_ref[g, j] = east
            send_ref[g, 15, j : j + 1, :] = total_e[0:1]
            depths_ref[g, j : j + 1, :] = face_e[0:1]
        for g, j in windows(r, 1):
            send_ref[g, 7 + j] = north
            send_ref[g, 15, 7 + j : 8 + j, :] = total_n[0:1]
            depths_ref[g, 8 + j : 9 + j, :] = face_n[0:1]
            depths_ref[g, 16 + j : 17 + j, :] = d[0:1]
        if 0 <= r < tile_rows:
            local_ref[0, r] = east
            local_ref[1, r] = north
            faces_ref[0, r : r + 1, :] = face_e[0:1]
            faces_ref[1, r : r + 1, :] = face_n[0:1]
            for g in range(blocks):
                send_ref[g, 16, r : r + 1, :] = total_e[0:1]
                send_ref[g, 17, r : r + 1, :] = total_n[0:1]
        if r < -1 or r >= tile_rows:
            continue
        open_e = (level < face_e).astype(jnp.float32)
        open_n = (level < face_n).astype(jnp.float32)
        for i, (f, ends) in enumerate(((2, edge_t), (3, edge_s))):
            x = row_of(f, r)
            flux_e = open_e * (row_of(f, r + 1) - x)
            if r >= 0:
                ending = edge(ends, r)
                flux_n = open_n * (jnp.where(last, ending, turn(x, -1, 1)) - x)
                flux_b = jnp.where(first, ending, turn(flux_n, 1, 1))
                mixed = x + MIXING * ((flux_e - flux_before[i]) + (flux_n - flux_b))
                mixed_ref[i, r] = mixed
                if i == 1:
                    smix_ref[pl.ds(r, levels, stride=tile_rows), :] = mixed
            flux_before[i] = flux_e


def ocean_phase(blocks, levels, own, sea, packed, rim_after, rim_before, after):
    tile_rows, cols = sea[0].shape
    outs = [
        shaped(levels * tile_rows, cols),
        shaped(2, tile_rows, levels, cols),
        shaped(blocks, ENTRIES, levels, cols),
        shaped(2, tile_rows, levels, cols),
        shaped(2, tile_rows, cols),
        shaped(blocks, 32, cols),
    ]
    tall = tile_rows + 2 * NSUB
    return call_once(
        functools.partial(ocean_kernel, blocks, levels),
        [own, *sea, packed, rim_after, rim_before],
        outs,
        [pltpu.VMEM((tall, levels, cols), jnp.float32)] * 2,
        after=after,
    )


def velocity_kernel(local_ref, faces_ref, received_ref, east_ref, north_ref, token_ref):
    blocks = received_ref.shape[0]
    _, tile_rows, levels, cols = local_ref.shape
    token_ref[...] = jnp.zeros_like(token_ref)
    group = lax.axis_index("comp")
    level = (group * levels + subs_of((levels, cols))).astype(jnp.float32)
    for f, out_ref in enumerate((east_ref, north_ref)):
        above = jnp.zeros((tile_rows, cols), jnp.float32)
        for s in range(blocks - 1):
            above = above + jnp.where(s < group, received_ref[s, f], 0.0)
        for r in range(tile_rows):
            x = local_ref[f, r] - DT_FLOW * jnp.broadcast_to(above[r : r + 1], (levels, cols))
            x = jnp.where(level < faces_ref[f, r : r + 1, :], x, 0.0)
            out_ref[pl.ds(r, levels, stride=tile_rows), :] = x


def velocities(local, faces, received):
    blocks = received.shape[0]
    _, tile_rows, levels, cols = local.shape
    out = shaped(levels * tile_rows, cols)
    return pl.pallas_call(
        velocity_kernel,
        grid=(1,),
        in_specs=[
            whole(local.shape),
            whole(faces.shape),
            pl.BlockSpec((blocks, 2, levels, cols), lambda i: (0, ENTRIES // 2 - 1, 0, 0)),
        ],
        out_specs=[whole(out.shape)] * 2 + [whole((SUB, cols))],
        out_shape=[out] * 2 + [shaped(SUB, cols)],
        compiler_params=params(),
    )(local, faces, received)


def advection_kernel(first_part, parts, level_count, *refs):
    (
        absorb_ref,
        surface_ref,
        depth_ref,
        totals_ref,
        courant_ref,
        low_ref,
        high_ref,
        after_ref,
        before_ref,
        side_ref,
        left_ref,
        right_ref,
    ) = refs[:12]
    moved_ref, light_ref, heat_ref, carry_out_ref = refs[-10:-6]
    coef_ref, side_coef_ref, edge_ref, running_ref, above_ref, shift_ref = refs[-6:]
    depth_ref = depth_ref.at[lax.axis_index("comp")]
    step = pl.program_id(0)
    tracers, _, _, cols = low_ref.shape
    levels = courant_ref.shape[2]
    sub_rows = surface_ref.shape[0]
    rows = sub_rows + 2
    shape = (levels, cols)
    lane = lanes_of(shape)
    first, last = lane == 0, lane == cols - 1
    first8, last8 = first[0:SUB], last[0:SUB]
    slot = lane % SLOTS

    @pl.when(step == 0)
    def _():
        running_ref[...] = refs[12][...] if first_part else jnp.zeros_like(running_ref)
        size = (2 * cols, 2 * cols)
        source, to = subs_of(size) % cols, lanes_of(size)
        hit = ((to < cols) & (source == to + 1)) | ((to >= cols) & (source == to - cols - 1))
        shift_ref[...] = hit.astype(jnp.float32).astype(jnp.bfloat16)

    part = first_part + step
    above = jnp.zeros(above_ref.shape, jnp.float32)
    for s in range(totals_ref.shape[0] - 1):
        above = above + jnp.where(s < part // parts, totals_ref[s, 0], 0.0)
    above_ref[...] = above
    level = (part * levels + subs_of(shape)).astype(jnp.float32)

    def spread(ref, r):
        return jnp.broadcast_to(ref[r : r + 1, :], shape)

    def courant(entry, face):
        x = courant_ref[0, entry] - DT_FLOW * spread(above_ref, entry)
        return COURANT * jnp.tanh(jnp.where(level < spread(depth_ref, face), x, 0.0))

    def coefficients(wet, ce, ce_b, cn, cn_b):
        return (
            wet
            * (
                1.0
                - jnp.maximum(ce, 0.0)
                + jnp.minimum(ce_b, 0.0)
                - jnp.maximum(cn, 0.0)
                + jnp.minimum(cn_b, 0.0)
            ),
            -wet * jnp.minimum(ce, 0.0),
            wet * jnp.maximum(ce_b, 0.0),
            -wet * jnp.minimum(cn, 0.0),
            wet * jnp.maximum(cn_b, 0.0),
        )

    side_e, side_n = courant(13, 24), courant(14, 25)
    wet = (level < spread(depth_ref, 26)).astype(jnp.float32)
    packed_coef = coefficients(wet, side_e, turn(side_e, SLOTS, 1), side_n, turn(side_n, 1, 1))
    for i in range(5):
        side_coef_ref[i] = packed_coef[i]
    ce_b = courant(0, 0)
    for j in range(rows):
        ce, cn = courant(1 + j, 1 + j), courant(7 + j, 8 + j)
        cn_b = jnp.where(first, turn(side_n, -(SLOTS * (j + 1) + 1), 1), turn(cn, 1, 1))
        wet = (level < spread(depth_ref, 16 + j)).astype(jnp.float32)
        for i, x in enumerate(coefficients(wet, ce, ce_b, cn, cn_b)):
            coef_ref[5 * j + i] = x
        ce_b = ce
    for i in range(side_ref.shape[0]):
        x = with_sides(side_ref[i], left_ref[i], right_ref[i])
        edge_ref[i, 0] = jnp.where(slot == 0, turn(x, -6, 1), x)
        x = (
            (side_coef_ref[0] * x + side_coef_ref[1] * turn(x, -SLOTS, 1))
            + (side_coef_ref[2] * turn(x, SLOTS, 1) + side_coef_ref[3] * turn(x, -1, 1))
            + side_coef_ref[4] * turn(x, 1, 1)
        )
        edge_ref[i, 1] = jnp.where(slot == 0, turn(x, -6, 1), x)

    layer = 2.0 / level_count
    zero = jnp.zeros((SUB, cols), jnp.float32)
    for k in range(0, levels, SUB):
        at = slice(k, k + SUB)

        def shifted(tiles):
            high, low = halves(jnp.concatenate(tiles, axis=0))
            return jnp.dot(
                jnp.concatenate([high, low], axis=1),
                shift_ref[...],
                preferred_element_type=jnp.float32,
            )

        def stencil(x, coef, edge, beside):
            north = jnp.where(last8, edge, beside[:, :cols])
            south = jnp.where(first8, edge, beside[:, cols:])
            return (
                (coef[0] * x[1] + coef[1] * x[2])
                + (coef[2] * x[0] + coef[3] * north)
                + coef[4] * south
            )

        def advect(i, sums):
            sums = list(sums)
            fields = []
            for t in range(GROUP):
                t = GROUP * i + t
                rows_of = (before_ref, low_ref, high_ref, after_ref)
                x = [ref[t, n, at] for ref in rows_of for n in range(NSUB)]
                fields.append(x)
            for stage in range(NSUB):
                inner = range(1 + stage, rows + 1 - stage)
                beside = shifted([x[j - stage] for j in inner for x in fields])
                fresh = [[] for _ in fields]
                for n, j in enumerate(inner):
                    coef = [coef_ref[5 * (j - 1) + c, at] for c in range(5)]
                    for t, x in enumerate(fields):
                        edges = edge_ref[GROUP // 2 * i + t // 2, stage, at]
                        edge = turn(edges, -(HALF * (t % 2) + SLOTS * j + 1), 1)
                        row = SUB * (len(fields) * n + t)
                        fresh[t].append(
                            stencil(x[n : n + 3], coef, edge, beside[row : row + SUB])
                        )
                fields = fresh
            for t, x in enumerate(fields):
                for r in range(sub_rows):
                    moved_ref[GROUP * i + t, r, at] = x[r]
                    sums[r] = sums[r] + absorb_ref[GROUP * i + t] * x[r]
            return tuple(sums)

        sums = (zero,) * sub_rows
        for i in range(tracers // GROUP):
            sums = advect(i, sums)
        for r in range(sub_rows):
            optical = layer * (CLEAR_WATER + sums[r])
            above, total = sums_above(optical)
            through = jnp.exp(-(running_ref[r] + above))
            running_ref[r] = running_ref[r] + total
            surface = jnp.broadcast_to(surface_ref[r : r + 1, :], (SUB, cols))
            light_ref[r, at] = surface * through * jnp.exp(-0.5 * optical)
            wet = (level[at] < jnp.broadcast_to(depth_ref[17 + r : 18 + r, :], (SUB, cols))).astype(
                jnp.float32
            )
            heat_ref[0, r, at] = wet * surface * through * (1.0 - jnp.exp(-optical)) / layer
    carry_out_ref[...] = running_ref[...]


def advection(cut, level_count, absorb, surface, depth, received, own, rim, sides, carry, heat, after):
    first_part, count = cut
    tracers, _, _, cols = own[0].shape
    every, _, levels, _ = received.shape
    parts = levels // SUB
    sub_rows = surface.shape[0]
    rows = pl.BlockSpec((tracers, NSUB, SUB, cols), lambda i: (0, 0, i, 0))
    side = pl.BlockSpec((tracers // 2, SUB, cols), lambda i: (0, i, 0))
    operands = [absorb, surface, depth, received, received, *own, *rim, *sides]
    in_specs = [
        smem(),
        whole(surface.shape),
        whole(depth.shape),
        pl.BlockSpec((every, 1, levels, cols), lambda i: (0, 15, 0, 0)),
        pl.BlockSpec(
            (1, ENTRIES, SUB, cols),
            lambda i: ((first_part + i) // parts, 0, (first_part + i) % parts, 0),
        ),
        rows,
        rows,
        rows,
        rows,
        side,
        side,
        side,
    ]
    aliases = {}
    carry_shape = (sub_rows, SUB, cols)
    if carry is not None:
        operands.append(carry)
        in_specs.append(whole(carry_shape))
        aliases = {len(operands): 2}
        operands.append(heat)
    operands += after
    in_specs += [pl.BlockSpec(memory_space=pl.ANY)] * (len(operands) - len(in_specs))
    outs = [
        shaped(tracers, sub_rows, count * SUB, cols),
        shaped(sub_rows, count * SUB, cols),
        shaped(every, sub_rows, levels, cols),
        shaped(*carry_shape),
    ]
    return pl.pallas_call(
        functools.partial(advection_kernel, first_part, parts, level_count),
        grid=(count,),
        in_specs=in_specs,
        out_specs=[
            pl.BlockSpec((tracers, sub_rows, SUB, cols), lambda i: (0, 0, i, 0)),
            pl.BlockSpec((sub_rows, SUB, cols), lambda i: (0, i, 0)),
            pl.BlockSpec(
                (1, sub_rows, SUB, cols),
                lambda i: ((first_part + i) // parts, 0, (first_part + i) % parts, 0),
            ),
            whole(carry_shape),
        ],
        out_shape=outs,
        scratch_shapes=[
            pltpu.VMEM((5 * (sub_rows + 2), SUB, cols), jnp.float32),
            pltpu.VMEM((5, SUB, cols), jnp.float32),
            pltpu.VMEM((tracers // 2, 2, SUB, cols), jnp.float32),
            pltpu.VMEM((sub_rows, SUB, cols), jnp.float32),
            pltpu.VMEM((levels, cols), jnp.float32),
            pltpu.VMEM((2 * cols, 2 * cols), jnp.bfloat16),
        ],
        input_output_aliases=aliases,
        compiler_params=params(),
    )(*operands)


def spread_kernel(matrix_ref, out_ref):
    tracers = matrix_ref.shape[0]
    size = tracers * SUB
    tall = (subs_of((size, tracers)) // SUB == lanes_of((size, tracers))).astype(jnp.float32)
    wide = (lanes_of((tracers, size)) // SUB == subs_of((tracers, size))).astype(jnp.float32)
    exact = functools.partial(
        jnp.dot, precision=lax.Precision.HIGHEST, preferred_element_type=jnp.float32
    )
    same = subs_of((size, size)) % SUB == lanes_of((size, size)) % SUB
    out_ref[...] = jnp.where(same, exact(exact(tall, matrix_ref[...]), wide), 0.0)


def uptake_kernel(first_level, *refs):
    growth_ref, half_ref, dim_ref, matrix_ref, depth_ref, moved_ref, light_ref = refs[:7]
    depth_ref = depth_ref.at[lax.axis_index("comp")]
    result_ref, token_ref, uptake_ref = refs[-3:]
    token_ref[...] = jnp.zeros_like(token_ref)
    tracers, sub_rows, levels, cols = moved_ref.shape
    step = pl.program_id(0)
    matrix_high, matrix_low = halves(matrix_ref[...])
    for k in range(0, levels, SUB):
        at = slice(k, k + SUB)
        level = (first_level + step * levels + k + subs_of((SUB, cols))).astype(jnp.float32)
        light = [light_ref[r, at] for r in range(sub_rows)]
        food = [moved_ref[0, r, at] for r in range(sub_rows)]
        both = [light[r] * food[r] for r in range(sub_rows)]

        def uptake(t, _):
            for r in range(sub_rows):
                scale = (half_ref[t] + food[r]) * (light[r] + dim_ref[t])
                value = growth_ref[t] * moved_ref[t, r, at] * (both[r] / scale)
                uptake_ref[pl.ds(t * SUB, SUB), r * cols : (r + 1) * cols] = value
            return _

        lax.fori_loop(0, tracers, uptake, 0, unroll=4)
        amount = uptake_ref[...]
        high, low = halves(amount)
        dot = functools.partial(jnp.dot, preferred_element_type=jnp.float32)
        change = dot(matrix_high, high) + (dot(matrix_high, low) + dot(matrix_low, high))
        for r in range(sub_rows):
            depth = jnp.broadcast_to(depth_ref[17 + r : 18 + r, :], (SUB, cols))
            scale = DT_BIO * (level < depth).astype(jnp.float32)
            for t in range(tracers):
                result_ref[t, pl.ds(sub_rows * k + r, SUB, stride=sub_rows), :] = (
                    moved_ref[t, r, at]
                    + scale * change[SUB * t : SUB * (t + 1), r * cols : (r + 1) * cols]
                )


def uptake(cut, all_rows, scalars, matrix, depth, moved, light, result):
    first_part, count = cut
    tracers, sub_rows, _, cols = moved.shape
    operands = [*scalars, matrix, depth, moved, light]
    in_specs = [smem()] * 3 + [
        whole(matrix.shape),
        whole(depth.shape),
        pl.BlockSpec((tracers, sub_rows, SUB, cols), lambda i: (0, 0, i, 0)),
        pl.BlockSpec((sub_rows, SUB, cols), lambda i: (0, i, 0)),
    ]
    aliases = {}
    if result is not None:
        aliases = {len(operands): 0}
        operands.append(result)
        in_specs.append(pl.BlockSpec(memory_space=pl.ANY))
    return pl.pallas_call(
        functools.partial(uptake_kernel, first_part * SUB),
        grid=(count,),
        in_specs=in_specs,
        out_specs=[
            pl.BlockSpec((tracers, SUB * sub_rows, cols), lambda i: (0, first_part + i, 0)),
            whole((SUB, cols)),
        ],
        out_shape=[shaped(tracers, all_rows, cols), shaped(SUB, cols)],
        scratch_shapes=[pltpu.VMEM((tracers * SUB, sub_rows * cols), jnp.float32)],
        input_output_aliases=aliases,
        compiler_params=params(),
    )(*operands)


def warming_kernel(sea_ref, floor_ref, heat_ref, mixed_ref, warm_ref, buoyant_ref):
    blocks, sub_rows, levels, cols = heat_ref.shape
    tile_rows = blocks * sub_rows
    base = lax.axis_index("comp") * levels
    level = (base + subs_of((levels, cols))).astype(jnp.float32)
    depth = jnp.where(sea_ref[...] == 1, floor_ref[...], 0).astype(jnp.float32)
    for r in range(tile_rows):
        at = pl.ds(r, levels, stride=tile_rows)
        warm = mixed_ref[0, r] + WARMING_FACTOR * heat_ref[r // sub_rows, r % sub_rows]
        wet = (level < depth[r : r + 1]).astype(jnp.float32)
        warm_ref[at, :] = warm
        buoyant_ref[at, :] = wet * (0.2 * warm - 0.8 * mixed_ref[1, r])


def warming(heat, mixed, sea):
    _, tile_rows, levels, cols = mixed.shape
    outs = [shaped(levels * tile_rows, cols)] * 2
    return call_once(warming_kernel, [*sea, heat, mixed], outs)


def from_before(x, axis):
    return lax.ppermute(x, axis, [(i, i + 1) for i in range(lax.axis_size(axis) - 1)])


def from_after(x, axis):
    return lax.ppermute(x, axis, [(i + 1, i) for i in range(lax.axis_size(axis) - 1)])


def row_pairs():
    blocks, tiles = lax.axis_size("comp"), lax.axis_size("gx")
    places = [b * tiles + tile for tile in range(tiles) for b in range(blocks)]
    return list(zip(places[:-1], places[1:]))


def from_block_before(x):
    return lax.ppermute(x, ("comp", "gx"), row_pairs())


def from_block_after(x):
    return lax.ppermute(x, ("comp", "gx"), [(later, own) for own, later in row_pairs()])


def from_sides(x):
    if lax.axis_size("gy") == 2:
        other = lax.ppermute(x, "gy", [(0, 1), (1, 0)])
        return other, other
    return from_before(x, "gy"), from_after(x, "gy")


def on_device(
    zonal_flow_speed,
    meridional_flow_speed,
    thermal_anomaly,
    brine_anomaly_values,
    marine_indicator,
    seafloor_layer,
    dissolved_species,
    topmost_sunshine,
    attenuation_coefficient,
    peak_intake_speed,
    feedstock_midpoint_constant,
    photon_midpoint_constant,
    stoichiometry_matrix,
):
    blocks = lax.axis_size("comp")
    levels, tile_rows, tile_cols = zonal_flow_speed.shape
    tracer_count, level_count = dissolved_species.shape[:2]
    sub_rows = dissolved_species.shape[4]
    ocean = (zonal_flow_speed, meridional_flow_speed, thermal_anomaly, brine_anomaly_values)
    sea = (marine_indicator, seafloor_layer)
    flat = [x.reshape(levels * tile_rows, tile_cols) for x in ocean]
    q = dissolved_species.reshape(tracer_count, level_count, sub_rows, 1, tile_cols)
    parts = levels // SUB
    every = parts * blocks
    sizes = [every - 5 * every // 8, 3 * every // 8, every // 4]
    cuts = [(sum(sizes[:i]), size) for i, size in enumerate(sizes)]
    scalars_of_uptake = (
        peak_intake_speed,
        feedstock_midpoint_constant,
        photon_midpoint_constant,
    )

    def rims(own):
        return own, (from_block_after(own[0]), from_block_before(own[1]))

    def sides(x):
        return (x, *from_sides(x))

    packed, edges, ocean_rows = pack_ocean(flat, sea, levels)
    ranges = [(first * SUB, size * SUB) for first, size in cuts]
    up, down, packed = ocean_sides(packed, *from_sides(packed), edges)
    after, before = from_after(up, "gx"), from_before(down, "gx")
    chunks = [rims(cut_rows(q, ranges[:1], [up]))]
    later = cut_rows(q, ranges[1:], chunks[0][0][:1])
    smix, mixed, send, local, faces, depths = ocean_phase(
        blocks, levels, ocean_rows, sea, packed, after, before, later[:1]
    )
    received = lax.all_to_all(send, "comp", split_axis=0, concat_axis=0, tiled=True)
    east_new, north_new, finished = velocities(local, faces, received)
    matrix = call_once(
        spread_kernel,
        [stoichiometry_matrix],
        [shaped(SUB * tracer_count, SUB * tracer_count)],
        after=[depths],
        cost=COVER,
    )[0]
    chunks.append(rims(held_until(later[:2], [matrix])))
    own = pack_tracers(*chunks[0], [matrix])

    surface = topmost_sunshine.reshape(sub_rows, tile_cols)
    carry, heat, result = None, None, None
    near = sides(own)
    for i, cut in enumerate(cuts):
        moved, light, heat, carry = advection(
            cut,
            level_count,
            attenuation_coefficient,
            surface,
            depths,
            received,
            *chunks[i],
            near,
            carry,
            heat,
            [] if i == 0 else [token, finished],
        )
        if i > 0 and i + 1 < len(cuts):
            near = sides(pack_tracers(*chunks[i + 1], [carry]))
        result, token = uptake(
            cut,
            level_count * sub_rows,
            scalars_of_uptake,
            matrix,
            depths,
            moved,
            light,
            result,
        )
        if i + 2 < len(cuts):
            at = 2 * (i + 1)
            chunks.append(rims(held_until(later[at : at + 2], [token])))
        if i == 0:
            near = sides(pack_tracers(*chunks[1], [token]))
    heat = lax.all_to_all(heat, "comp", split_axis=0, concat_axis=0, tiled=True)
    warmed_result, buoyancy = warming(heat, mixed, sea)
    fields = (east_new, north_new, warmed_result, smix, buoyancy)
    return (
        *[x.reshape(zonal_flow_speed.shape) for x in fields],
        result.reshape(dissolved_species.shape),
    )


def solution(mesh):
    return jax.shard_map(
        on_device,
        mesh=mesh,
        in_specs=(
            P("comp", "gx", "gy"),
            P("comp", "gx", "gy"),
            P("comp", "gx", "gy"),
            P("comp", "gx", "gy"),
            P("gx", "gy"),
            P("gx", "gy"),
            P(None, None, "gx", "comp", None, "gy"),
            P("gx", "comp", None, "gy"),
            P(),
            P(),
            P(),
            P(),
            P(),
        ),
        out_specs=(
            P("comp", "gx", "gy"),
            P("comp", "gx", "gy"),
            P("comp", "gx", "gy"),
            P("comp", "gx", "gy"),
            P("comp", "gx", "gy"),
            P(None, None, "gx", "comp", None, "gy"),
        ),
        check_vma=False,
    )
```
